32 devices in a mesh: hst: 8 (over z, y), dev: 4 (over x, core).
Axes of the slice: x: 2, y: 2, z: 4, core: 2. Of those that a mesh axis runs over, the one named last changes fastest.
Arguments:
- features: bfloat16 [8192, 256], P(('hst', 'dev')), may hold values from -6 to 6
- send_list: int32 [8, 4, 8, 8], P('hst', 'dev'), may hold values from 0 to 255
- tile_dst: int32 [2048], P(('hst', 'dev')), may hold values from 0 to 1
- tile_src: int32 [2048], P(('hst', 'dev')), may hold values from 0 to 9, as said below
- tile_rows: int32 [2048], P(('hst', 'dev')), may hold values from 1 to 128, as said below
- tile_val: bfloat16 [2048, 128, 128], P(('hst', 'dev')), may hold values from -0.09375 to 0.09375
- self_one: bfloat16 [256, 256], replicated, may hold values from -0.375 to 0.375
- neigh_one: bfloat16 [256, 256], replicated, may hold values from -0.375 to 0.375
- bias_one: float32 [256], replicated, may hold values from -2.5 to 2.5
- self_two: bfloat16 [256, 256], replicated, may hold values from -0.375 to 0.375
- neigh_two: bfloat16 [256, 256], replicated, may hold values from -0.375 to 0.375
- bias_two: float32 [256], replicated, may hold values from -2.5 to 2.5
- cotangent: bfloat16 [8192, 256], P(('hst', 'dev')), may hold values from -6 to 6
Outputs:
- output: bfloat16 [8192, 256], P(('hst', 'dev'))
- grad_features: float32 [8192, 256], P(('hst', 'dev'))
The draws below stay inside these ranges and needn't reach their ends.
Inputs may be any that keep to these rules, and one draw needn't show every extreme that they name: `tile_src`: among the tiles of each host, every one of the host's 10 source blocks is named at least once. `tile_rows`: each device has a tile whose 128 rows are all live.
All inputs are finite; a program needn't handle non-finite values.
Results may differ from the reference program's by a relative error of at most 0.005.
Values may be sent and summed in bfloat16 or wider, within the bound.
No kernel may reach another device: no remote copies, remote signals or barrier semaphores. Data moves between devices by JAX's collectives and lax.ppermute only.
A program may use at most 64 MiB of HBM per device.

```python
import jax
import jax.numpy as jnp
from jax import lax

WIDTH = 256
BLK = 128
NODE_DEV = 256
TILES = 64
SEND = 8
BPD = 2
HOSTROWS = 1024
SRCBLK = 10
TOTAL = 8192
TILES_ALL = 2048
N_HST = 8
N_DEV = 4


def host_order(subkey):
    return jax.random.permutation(subkey, N_DEV * TILES)


def draw_tile_src(key, part):
    key = jax.random.fold_in(key, 11)
    host_keys = jax.random.split(jax.random.fold_in(key, 1), N_HST)
    orders = jax.vmap(host_order)(host_keys).astype(jnp.int32)
    shifts = jax.random.randint(jax.random.fold_in(key, 2), (N_HST, 1), 0, SRCBLK)
    covering = (orders + shifts) % SRCBLK
    loose = jax.random.randint(jax.random.fold_in(key, 3), (N_HST, N_DEV * TILES), 0, SRCBLK)
    return jnp.where(orders < SRCBLK, covering, loose).reshape(-1).astype(jnp.int32)


def draw_tile_rows(key, part):
    key = jax.random.fold_in(key, 23)
    ceilings = jax.random.randint(jax.random.fold_in(key, 1), (N_HST * N_DEV, 1), 16, BLK + 1)
    raw_draws = jax.random.randint(jax.random.fold_in(key, 2), (N_HST * N_DEV, TILES), 0, 1 << 20)
    live_rows = 1 + raw_draws % ceilings
    full_slot = jax.random.randint(jax.random.fold_in(key, 3), (N_HST * N_DEV, 1), 0, TILES)
    slot_index = lax.broadcasted_iota(jnp.int32, (N_HST * N_DEV, TILES), 1)
    live_rows = jnp.where(slot_index == full_slot, BLK, live_rows)
    return live_rows.reshape(-1).astype(jnp.int32)


def place_ends(array, rng, least, high):
    longest = array.shape.index(max(array.shape))
    spots = []
    for shift in (0, 1):
        where = [jax.random.randint(jax.random.fold_in(rng, axis), (), 0, length) for axis, length in enumerate(array.shape)]
        where[longest] = (where[longest] + shift) % array.shape[longest]
        spots.append(tuple(where))
    return array.at[spots[0]].set(least).at[spots[1]].set(high)


def shard_levels(own_key, dims, shards, least, high):
    loudness = 1.0
    for position, shards_of in shards:
        steps = jax.random.uniform(jax.random.fold_in(jax.random.fold_in(own_key, 6), position), (shards_of,), jnp.float32, least / len(shards), high / len(shards))
        loudness = loudness * jnp.repeat(jnp.exp(steps), dims[position] // shards_of).reshape((-1,) + (1,) * (len(dims) - 1 - position))
    return loudness


def gaussian(rng, extent, scale, reach, shards=(), kind=jnp.bfloat16):
    values = jax.random.normal(rng, extent, jnp.float32) * scale
    if len(shards) > 0:
        values = shard_levels(rng, extent, shards, -0.22, 0.18) * values
    return jnp.clip(values, min=-reach, max=reach).astype(kind)


def setup_inputs(seed: int = 0) -> dict:
    streams_of = jax.random.split(jax.random.key(seed), 14)
    features = gaussian(streams_of[0], (TOTAL, WIDTH), 1.0, 6.0, ((0, 32),))
    send_list = place_ends(jax.random.randint(streams_of[1], (N_HST, N_DEV, N_HST, SEND), 0, NODE_DEV), jax.random.fold_in(streams_of[1], 1), 0, NODE_DEV - 1).astype(jnp.int32)
    tile_dst = place_ends(jax.random.randint(streams_of[2], (TILES_ALL,), 0, BPD), jax.random.fold_in(streams_of[2], 1), 0, BPD - 1).astype(jnp.int32)
    tile_src = draw_tile_src(jax.random.fold_in(streams_of[13], 71), 0)
    tile_rows = draw_tile_rows(jax.random.fold_in(streams_of[13], 71), 0)
    tile_val = gaussian(streams_of[5], (TILES_ALL, BLK, BLK), (TILES * BLK // BPD) ** -0.5, 0.09375, ((0, 32),))
    self_one = gaussian(streams_of[6], (WIDTH, WIDTH), WIDTH ** -0.5, 0.375)
    neigh_one = gaussian(streams_of[7], (WIDTH, WIDTH), WIDTH ** -0.5, 0.375)
    bias_one = gaussian(streams_of[8], (WIDTH,), 0.5, 2.5, (), jnp.float32)
    self_two = gaussian(streams_of[9], (WIDTH, WIDTH), WIDTH ** -0.5, 0.375)
    neigh_two = gaussian(streams_of[10], (WIDTH, WIDTH), WIDTH ** -0.5, 0.375)
    bias_two = gaussian(streams_of[11], (WIDTH,), 0.5, 2.5, (), jnp.float32)
    cotangent = gaussian(streams_of[12], (TOTAL, WIDTH), 1.0, 6.0, ((0, 32),))
    return dict(features=features, send_list=send_list, tile_dst=tile_dst, tile_src=tile_src, tile_rows=tile_rows, tile_val=tile_val, self_one=self_one, neigh_one=neigh_one, bias_one=bias_one, self_two=self_two, neigh_two=neigh_two, bias_two=bias_two, cotangent=cotangent)


def live_tiles(tile_val, tile_rows):
    row_place = lax.broadcasted_iota(jnp.int32, tile_val.shape, 1)
    return jnp.where(row_place < tile_rows[:, None, None], tile_val, jnp.zeros_like(tile_val))


def halo_rows(send_list, host_index):
    pair_lists = lax.dynamic_index_in_dim(send_list, host_index, 2, keepdims=False).astype(jnp.int32)
    source = lax.broadcasted_iota(jnp.int32, pair_lists.shape, 0)
    device = lax.broadcasted_iota(jnp.int32, pair_lists.shape, 1)
    row_index = source * HOSTROWS + device * NODE_DEV + pair_lists
    return jnp.transpose(row_index, (1, 0, 2)).reshape(-1)


def host_row_index(send_list, host_index):
    own_rows = host_index * HOSTROWS + jnp.arange(HOSTROWS, dtype=jnp.int32)
    return jnp.concatenate([own_rows, halo_rows(send_list, host_index)], 0)


def aggregate(values, send_list, tile_dst, tile_src, masked):
    def device_rows(device_slot):
        host_index = device_slot // N_DEV
        source_rows = jnp.take(values, host_row_index(send_list, host_index), axis=0)
        source_rows = source_rows.reshape(SRCBLK, BLK, WIDTH)
        targets = lax.dynamic_slice_in_dim(tile_dst, device_slot * TILES, TILES, 0)
        sources = lax.dynamic_slice_in_dim(tile_src, device_slot * TILES, TILES, 0)
        weights = lax.dynamic_slice_in_dim(masked, device_slot * TILES, TILES, 0)
        picked = jnp.take(source_rows, sources, axis=0)
        products = jnp.einsum("tij,tjf->tif", weights.astype(jnp.float32), picked.astype(jnp.float32))
        blocks = jnp.zeros((BPD, BLK, WIDTH), jnp.float32).at[targets].add(products)
        return blocks.reshape(NODE_DEV, WIDTH)

    device_slots = jnp.arange(N_HST * N_DEV, dtype=jnp.int32)
    return lax.map(device_rows, device_slots).reshape(TOTAL, WIDTH)


def spread(upstream, send_list, tile_dst, tile_src, masked):
    def add_device(totals, device_slot):
        host_index = device_slot // N_DEV
        targets = lax.dynamic_slice_in_dim(tile_dst, device_slot * TILES, TILES, 0)
        sources = lax.dynamic_slice_in_dim(tile_src, device_slot * TILES, TILES, 0)
        weights = lax.dynamic_slice_in_dim(masked, device_slot * TILES, TILES, 0)
        mine = lax.dynamic_slice_in_dim(upstream, device_slot * NODE_DEV, NODE_DEV, 0).reshape(BPD, BLK, WIDTH)
        seen = jnp.take(mine, targets, axis=0)
        products = jnp.einsum("tij,tif->tjf", weights.astype(jnp.float32), seen.astype(jnp.float32))
        gathered = jnp.zeros((SRCBLK, BLK, WIDTH), jnp.float32).at[sources].add(products)
        gathered = gathered.reshape(SRCBLK * BLK, WIDTH)
        totals = totals.at[host_row_index(send_list, host_index)].add(gathered)
        return totals, None

    device_slots = jnp.arange(N_HST * N_DEV, dtype=jnp.int32)
    totals, unused = lax.scan(add_device, jnp.zeros((TOTAL, WIDTH), jnp.float32), device_slots)
    return totals


def reference(features, send_list, tile_dst, tile_src, tile_rows, tile_val, self_one, neigh_one, bias_one, self_two, neigh_two, bias_two, cotangent):
    masked = live_tiles(tile_val, tile_rows)
    agg_one = aggregate(features, send_list, tile_dst, tile_src, masked).astype(jnp.bfloat16)
    pre = jnp.dot(features, self_one, preferred_element_type=jnp.float32)
    pre = pre + jnp.dot(agg_one, neigh_one, preferred_element_type=jnp.float32) + bias_one
    hidden = jax.nn.silu(pre).astype(jnp.bfloat16)
    agg_two = aggregate(hidden, send_list, tile_dst, tile_src, masked).astype(jnp.bfloat16)
    result = jnp.dot(hidden, self_two, preferred_element_type=jnp.float32)
    result = result + jnp.dot(agg_two, neigh_two, preferred_element_type=jnp.float32) + bias_two
    output = result.astype(jnp.bfloat16)
    back_two = jnp.dot(cotangent, neigh_two.T, preferred_element_type=jnp.float32).astype(jnp.bfloat16)
    grad_hidden = jnp.dot(cotangent, self_two.T, preferred_element_type=jnp.float32)
    grad_hidden = grad_hidden + spread(back_two, send_list, tile_dst, tile_src, masked)
    sigmoid = jax.nn.sigmoid(pre)
    grad_pre = (grad_hidden * sigmoid * (1.0 + pre * (1.0 - sigmoid))).astype(jnp.bfloat16)
    back_one = jnp.dot(grad_pre, neigh_one.T, preferred_element_type=jnp.float32).astype(jnp.bfloat16)
    grad_features = jnp.dot(grad_pre, self_one.T, preferred_element_type=jnp.float32)
    grad_features = grad_features + spread(back_one, send_list, tile_dst, tile_src, masked)
    return output, grad_features
```

```python
import functools

import jax
import jax.numpy as jnp
from jax import lax
from jax.experimental import pallas as pl
from jax.experimental.pallas import tpu as pltpu
from jax.sharding import PartitionSpec as P

F32 = jnp.float32
BF16 = jnp.bfloat16
VMEM_LIMIT = 40 * 1024 * 1024
CHUNKS = 8


def dot(a, b):
    return jnp.dot(a, b, preferred_element_type=F32)


def dot_nt(a, b):
    return lax.dot_general(a, b, (((1,), (1,)), ((), ())), preferred_element_type=F32)


def dot_tn(a, b):
    return lax.dot_general(a, b, (((0,), (0,)), ((), ())), preferred_element_type=F32)


def pick_matrix(send_ref, rows):
    hosts, send = send_ref.shape[2], send_ref.shape[3]
    place = lax.broadcasted_iota(jnp.int32, (send, rows), 0)
    column = lax.broadcasted_iota(jnp.int32, (send, rows), 1)
    parts = []
    for g in range(hosts):
        index = jnp.zeros((send, rows), jnp.int32)
        for s in range(send):
            index = jnp.where(place == s, send_ref[0, 0, g, s], index)
        parts.append(jnp.where(index == column, 1.0, 0.0).astype(F32))
    return jnp.concatenate(parts, 0).astype(BF16)


def pack(picked, far, msg_ref, hosts, devs):
    send = picked.shape[0] // hosts
    for g in range(hosts):
        for d in range(devs):
            low = (d * hosts + g) * send
            both = jnp.concatenate(
                [picked[g * send : (g + 1) * send], far[low : low + send]], 0
            )
            msg_ref[g * devs + d] = both.astype(BF16)


def unpack(recv_ref, hosts, devs):
    send = recv_ref.shape[1] // 2
    halo, back = [], []
    for d in range(devs):
        for g in range(hosts):
            both = recv_ref[g * devs + d].astype(F32)
            halo.append(both[:send])
            back.append(both[send:])
    return jnp.concatenate(halo, 0).astype(BF16), jnp.concatenate(back, 0).astype(BF16)


def spread_parts(adj, u, own_ref, own_rows):
    own_ref[...] = dot_tn(adj[:, :own_rows], u).astype(BF16)
    return dot_tn(adj[:, own_rows:], u)


def prep_kernel(
    hosts,
    devs,
    dst_ref,
    src_ref,
    rows_ref,
    send_ref,
    tile_hbm,
    features_ref,
    cot_ref,
    neigh_two_ref,
    adj_ref,
    msg_ref,
    own_ref,
    tile_buf,
    acc,
    sems,
):
    tiles, blk = tile_buf.shape[0], tile_buf.shape[1]
    each = tiles // CHUNKS
    copies = [
        pltpu.make_async_copy(
            tile_hbm.at[pl.ds(c * each, each)], tile_buf.at[pl.ds(c * each, each)], sems.at[c]
        )
        for c in range(CHUNKS)
    ]
    for copy in copies:
        copy.start()
    rows = features_ref.shape[0]
    bpd = rows // blk
    slots = acc.shape[0]
    sources = slots // bpd
    acc[...] = jnp.zeros_like(acc)
    picked = dot(pick_matrix(send_ref, rows), features_ref[...])
    u = dot_nt(cot_ref[...], neigh_two_ref[...]).astype(BF16)
    place = lax.broadcasted_iota(jnp.int32, (blk, blk), 0)
    for c in range(CHUNKS):
        copies[c].wait()

        def add(t, carry):
            slot = dst_ref[t] * sources + src_ref[t]
            live = jnp.where(place < rows_ref[t], tile_buf[t].astype(F32), 0.0)
            acc[slot] = acc[slot] + live
            return carry

        lax.fori_loop(c * each, (c + 1) * each, add, 0, unroll=True)
    for b in range(bpd):
        for j in range(sources):
            adj_ref[b * blk : (b + 1) * blk, j * blk : (j + 1) * blk] = acc[
                b * sources + j
            ].astype(BF16)
    far = spread_parts(adj_ref[...], u, own_ref, devs * rows)
    pack(picked, far, msg_ref, hosts, devs)


def middle_kernel(
    hosts,
    devs,
    send_ref,
    adj_ref,
    wide_ref,
    recv_ref,
    terms_ref,
    features_ref,
    cot_ref,
    self_one_ref,
    neigh_one_ref,
    bias_ref,
    self_two_ref,
    hidden_ref,
    grad_pre_ref,
    msg_ref,
    own_ref,
):
    rows = features_ref.shape[0]
    own_rows = devs * rows
    pick = pick_matrix(send_ref, rows)
    halo, back = unpack(recv_ref, hosts, devs)
    adj = adj_ref[...]
    agg = dot(adj[:, :own_rows], wide_ref[...]) + dot(adj[:, own_rows:], halo)
    pre = dot(features_ref[...], self_one_ref[...])
    pre = pre + dot(agg.astype(BF16), neigh_one_ref[...]) + bias_ref[...].reshape(1, -1)
    sigmoid = jax.nn.sigmoid(pre)
    hidden = (pre * sigmoid).astype(BF16)
    hidden_ref[...] = hidden
    grad = dot_nt(cot_ref[...], self_two_ref[...])
    grad = grad + dot_tn(jnp.concatenate([pick] * devs, 0), back)
    for d in range(devs):
        grad = grad + terms_ref[d * rows : (d + 1) * rows, :].astype(F32)
    grad_pre = (grad * sigmoid * (1.0 + pre * (1.0 - sigmoid))).astype(BF16)
    grad_pre_ref[...] = grad_pre
    u = dot_nt(grad_pre, neigh_one_ref[...]).astype(BF16)
    far = spread_parts(adj, u, own_ref, own_rows)
    pack(dot(pick, hidden), far, msg_ref, hosts, devs)


def last_kernel(
    hosts,
    devs,
    send_ref,
    adj_ref,
    wide_ref,
    recv_ref,
    terms_ref,
    hidden_ref,
    grad_pre_ref,
    self_one_ref,
    self_two_ref,
    neigh_two_ref,
    bias_ref,
    output_ref,
    grad_ref,
):
    rows = hidden_ref.shape[0]
    own_rows = devs * rows
    pick = pick_matrix(send_ref, rows)
    halo, back = unpack(recv_ref, hosts, devs)
    adj = adj_ref[...]
    agg = dot(adj[:, :own_rows], wide_ref[...]) + dot(adj[:, own_rows:], halo)
    result = dot(hidden_ref[...], self_two_ref[...])
    result = result + dot(agg.astype(BF16), neigh_two_ref[...]) + bias_ref[...].reshape(1, -1)
    output_ref[...] = result.astype(BF16)
    grad = dot_nt(grad_pre_ref[...], self_one_ref[...])
    grad = grad + dot_tn(jnp.concatenate([pick] * devs, 0), back)
    for d in range(devs):
        grad = grad + terms_ref[d * rows : (d + 1) * rows, :].astype(F32)
    grad_ref[...] = grad


VMEM = pl.BlockSpec(memory_space=pltpu.VMEM)
SMEM = pl.BlockSpec(memory_space=pltpu.SMEM)
PARAMS = pltpu.CompilerParams(vmem_limit_bytes=VMEM_LIMIT)


def exchange(value, msg, own):
    wide = lax.all_gather(value, "dev", axis=0, tiled=True)
    recv = lax.all_to_all(msg, ("hst", "dev"), split_axis=0, concat_axis=0, tiled=True)
    terms = lax.all_to_all(own, "dev", split_axis=0, concat_axis=0, tiled=True)
    return wide, recv, terms


def body(
    features,
    send_list,
    tile_dst,
    tile_src,
    tile_rows,
    tile_val,
    self_one,
    neigh_one,
    bias_one,
    self_two,
    neigh_two,
    bias_two,
    cotangent,
):
    devs = lax.axis_size("dev")
    hosts = lax.axis_size("hst")
    rows, width = features.shape
    tiles, blk = tile_val.shape[:2]
    send = send_list.shape[3]
    own_rows = devs * rows
    all_rows = own_rows + devs * hosts * send
    bpd = rows // blk
    adj_shape = jax.ShapeDtypeStruct((rows, all_rows), BF16)
    msg_shape = jax.ShapeDtypeStruct((hosts * devs, 2 * send, width), BF16)
    own_shape = jax.ShapeDtypeStruct((own_rows, width), BF16)
    rows_shape = jax.ShapeDtypeStruct((rows, width), BF16)

    adj, msg, own = pl.pallas_call(
        functools.partial(prep_kernel, hosts, devs),
        out_shape=(adj_shape, msg_shape, own_shape),
        in_specs=[SMEM] * 4 + [pl.BlockSpec(memory_space=pl.ANY)] + [VMEM] * 3,
        out_specs=(VMEM,) * 3,
        scratch_shapes=[
            pltpu.VMEM((tiles, blk, blk), BF16),
            pltpu.VMEM((bpd * (all_rows // blk), blk, blk), F32),
            pltpu.SemaphoreType.DMA((CHUNKS,)),
        ],
        compiler_params=PARAMS,
        name="prep",
    )(tile_dst, tile_src, tile_rows, send_list, tile_val, features, cotangent, neigh_two)

    wide, recv, terms = exchange(features, msg, own)
    hidden, grad_pre, msg, own = pl.pallas_call(
        functools.partial(middle_kernel, hosts, devs),
        out_shape=(rows_shape, rows_shape, msg_shape, own_shape),
        in_specs=[SMEM] + [VMEM] * 10,
        out_specs=(VMEM,) * 4,
        compiler_params=PARAMS,
        name="middle",
    )(
        send_list,
        adj,
        wide,
        recv,
        terms,
        features,
        cotangent,
        self_one,
        neigh_one,
        bias_one,
        self_two,
    )

    wide, recv, terms = exchange(hidden, msg, own)
    return pl.pallas_call(
        functools.partial(last_kernel, hosts, devs),
        out_shape=(rows_shape, jax.ShapeDtypeStruct((rows, width), F32)),
        in_specs=[SMEM] + [VMEM] * 10,
        out_specs=(VMEM,) * 2,
        compiler_params=PARAMS,
        name="last",
    )(
        send_list,
        adj,
        wide,
        recv,
        terms,
        hidden,
        grad_pre,
        self_one,
        self_two,
        neigh_two,
        bias_two,
    )


def solution(mesh):
    split = P(("hst", "dev"))
    return jax.shard_map(
        body,
        mesh=mesh,
        in_specs=(
            P(("hst", "dev"), None),
            P("hst", "dev", None, None),
            split,
            split,
            split,
            P(("hst", "dev"), None, None),
            P(),
            P(),
            P(),
            P(),
            P(),
            P(),
            P(("hst", "dev"), None),
        ),
        out_specs=(P(("hst", "dev"), None), P(("hst", "dev"), None)),
        check_vma=False,
    )
```

```python
import functools

import jax
import jax.numpy as jnp
from jax import lax
from jax.experimental import pallas as pl
from jax.experimental.pallas import tpu as pltpu
from jax.sharding import PartitionSpec as P

F32 = jnp.float32
BF16 = jnp.bfloat16
MIB = 1024 * 1024
CHUNKS = 8
CORES = 2

VMEM = pl.BlockSpec(memory_space=pltpu.VMEM)
SMEM = pl.BlockSpec(memory_space=pltpu.SMEM)
ANY = pl.BlockSpec(memory_space=pl.ANY)


def dot(a, b):
    return jnp.dot(a, b, preferred_element_type=F32)


def dot_nt(a, b):
    return lax.dot_general(a, b, (((1,), (1,)), ((), ())), preferred_element_type=F32)


def dot_tn(a, b):
    return lax.dot_general(a, b, (((0,), (0,)), ((), ())), preferred_element_type=F32)


def place_of(devs):
    dev = lax.axis_index("dev")
    return lax.div(dev, CORES), lax.rem(dev, CORES)


def pick_rows(send_ref, host, rows):
    send = send_ref.shape[3]
    place = lax.broadcasted_iota(jnp.int32, (send, rows), 0)
    column = lax.broadcasted_iota(jnp.int32, (send, rows), 1)
    index = jnp.zeros((send, rows), jnp.int32)
    for s in range(send):
        index = jnp.where(place == s, send_ref[0, 0, host, s], index)
    return jnp.where(index == column, 1.0, 0.0).astype(F32)


def pick_matrix(send_ref, rows, sign):
    hosts = send_ref.shape[2]
    me = lax.axis_index("hst")
    order = [lax.rem(me + sign * k + hosts, hosts) for k in range(hosts)]
    return jnp.concatenate([pick_rows(send_ref, g, rows) for g in order], 0).astype(BF16)


def put_picked(send_ref, value, out_refs):
    send = send_ref.shape[3]
    picked = dot(pick_matrix(send_ref, value.shape[0], 1), value)
    for k, out in enumerate(out_refs):
        out[...] = picked[k * send : (k + 1) * send].astype(BF16)


def spread_parts(devs, far, adj, u, whole, keep_ref, give_ref):
    rows = u.shape[0]
    own_rows = devs * rows
    whole[...] = dot_tn(adj, u).astype(BF16)
    chip, core = place_of(devs)
    for side, ref in ((core, keep_ref), (1 - core, give_ref)):
        for x in range(devs // CORES):
            d = x * CORES + side
            low = pl.multiple_of(d * rows, rows)
            ref[x, :rows, :] = whole[pl.ds(low, rows), :]
            low = pl.multiple_of(own_rows + d * far, far)
            ref[x, rows:, :] = whole[pl.ds(low, far), :]


def prep_kernel(
    devs,
    dst_ref,
    src_ref,
    rows_ref,
    send_ref,
    tile_hbm,
    features_ref,
    cot_ref,
    neigh_two_ref,
    adj_ref,
    keep_ref,
    give_ref,
    *rest,
):
    picked_refs, (tile_buf, acc, whole, sems) = rest[:-4], rest[-4:]
    tiles, blk = tile_buf.shape[0], tile_buf.shape[1]
    each = tiles // CHUNKS
    copies = [
        pltpu.make_async_copy(
            tile_hbm.at[pl.ds(c * each, each)], tile_buf.at[pl.ds(c * each, each)], sems.at[c]
        )
        for c in range(CHUNKS)
    ]
    for copy in copies:
        copy.start()
    rows = features_ref.shape[0]
    bpd = rows // blk
    sources = acc.shape[0] // bpd
    far = send_ref.shape[2] * send_ref.shape[3]
    acc[...] = jnp.zeros_like(acc)
    put_picked(send_ref, features_ref[...], picked_refs)
    u = dot_nt(cot_ref[...], neigh_two_ref[...]).astype(BF16)
    place = lax.broadcasted_iota(jnp.int32, (blk, blk), 0)
    for c in range(CHUNKS):
        copies[c].wait()

        def add(t, carry):
            slot = dst_ref[t] * sources + src_ref[t]
            live = jnp.where(place < rows_ref[t], tile_buf[t].astype(F32), 0.0)
            acc[slot] = acc[slot] + live
            return carry

        lax.fori_loop(c * each, (c + 1) * each, add, 0, unroll=True)
    for b in range(bpd):
        for j in range(sources):
            adj_ref[b * blk : (b + 1) * blk, j * blk : (j + 1) * blk] = acc[
                b * sources + j
            ].astype(BF16)
    spread_parts(devs, far, adj_ref[...], u, whole, keep_ref, give_ref)


def core_sum_kernel(devs, keep_ref, came_ref, mine_ref, *to_refs):
    chips = devs // CORES
    chip, _ = place_of(devs)
    mine_ref[...] = keep_ref[chip].astype(F32) + came_ref[chip].astype(F32)
    for k, ref in enumerate(to_refs):
        other = lax.rem(chip + k + 1, chips)
        ref[...] = (keep_ref[other].astype(F32) + came_ref[other].astype(F32)).astype(BF16)


def chip_sum_kernel(hosts, send, count, *refs):
    mine_ref, came, own_ref, outs = refs[0], refs[1 : 1 + count], refs[1 + count], refs[2 + count : -1]
    far_buf = refs[-1]
    total = mine_ref[...]
    for ref in came:
        total = total + ref[...].astype(F32)
    rows = own_ref.shape[0]
    own_ref[...] = total[:rows]
    far_buf[...] = total[rows:]
    me = lax.axis_index("hst")
    for k, out in enumerate(outs):
        low = pl.multiple_of(lax.rem(me + k, hosts) * send, send)
        out[...] = far_buf[pl.ds(low, send), :].astype(BF16)


def join_kernel(hosts, send, *refs):
    outs, buf = refs[-2], refs[-1]
    me = lax.axis_index("hst")
    for k in range(hosts):
        low = pl.multiple_of(lax.rem(me - k + hosts, hosts) * send, send)
        buf[pl.ds(low, send), :] = refs[k][...].astype(F32)
    outs[...] = buf[...].astype(BF16)


def gather_sources(devs, wide_refs, halo_refs, space):
    chips = devs // CORES
    chip, core = place_of(devs)
    rows, far = wide_refs[0].shape[0], halo_refs[0].shape[0]
    for k in range(chips):
        for i, side in enumerate((core, 1 - core)):
            d = lax.rem(chip - k + chips, chips) * CORES + side
            space[pl.ds(pl.multiple_of(d * rows, rows), rows), :] = wide_refs[k * CORES + i][...]
            low = pl.multiple_of(devs * rows + d * far, far)
            space[pl.ds(low, far), :] = halo_refs[k * CORES + i][...]


def forward_one_kernel(
    devs, send_ref, adj_ref, self_ref, neigh_ref, bias_ref, *refs
):
    wide, halo, rest = refs[:devs], refs[devs : 2 * devs], refs[2 * devs :]
    pre_ref, hidden_ref, picked_refs, space = rest[0], rest[1], rest[2:-1], rest[-1]
    gather_sources(devs, wide, halo, space)
    agg = dot(adj_ref[...], space[...]).astype(BF16)
    pre = dot(wide[0][...], self_ref[...])
    pre = pre + dot(agg, neigh_ref[...]) + bias_ref[...].reshape(1, -1)
    pre_ref[...] = pre
    hidden = (pre * jax.nn.sigmoid(pre)).astype(BF16)
    hidden_ref[...] = hidden
    put_picked(send_ref, hidden, picked_refs)


def forward_two_kernel(devs, adj_ref, self_ref, neigh_ref, bias_ref, *refs):
    wide, halo, out_ref, space = refs[:devs], refs[devs : 2 * devs], refs[-2], refs[-1]
    gather_sources(devs, wide, halo, space)
    agg = dot(adj_ref[...], space[...]).astype(BF16)
    result = dot(wide[0][...], self_ref[...])
    result = result + dot(agg, neigh_ref[...]) + bias_ref[...].reshape(1, -1)
    out_ref[...] = result.astype(BF16)


def spread_total(send_ref, own_ref, back_refs):
    back = jnp.concatenate([ref[...].astype(F32) for ref in back_refs], 0).astype(BF16)
    return own_ref[...] + dot_tn(pick_matrix(send_ref, own_ref.shape[0], -1), back)


def backward_two_kernel(
    devs,
    hosts,
    send_ref,
    adj_ref,
    pre_ref,
    cot_ref,
    self_two_ref,
    neigh_one_ref,
    own_ref,
    *refs,
):
    back, (grad_pre_ref, keep_ref, give_ref, whole) = refs[:hosts], refs[hosts:]
    pre = pre_ref[...]
    sigmoid = jax.nn.sigmoid(pre)
    grad = dot_nt(cot_ref[...], self_two_ref[...]) + spread_total(send_ref, own_ref, back)
    grad_pre = (grad * sigmoid * (1.0 + pre * (1.0 - sigmoid))).astype(BF16)
    grad_pre_ref[...] = grad_pre
    u = dot_nt(grad_pre, neigh_one_ref[...]).astype(BF16)
    far = send_ref.shape[2] * send_ref.shape[3]
    spread_parts(devs, far, adj_ref[...], u, whole, keep_ref, give_ref)


def backward_one_kernel(hosts, send_ref, grad_pre_ref, self_one_ref, own_ref, *refs):
    back, grad_ref = refs[:hosts], refs[hosts]
    grad_ref[...] = dot_nt(grad_pre_ref[...], self_one_ref[...]) + spread_total(
        send_ref, own_ref, back
    )


def call(kernel, name, out_shape, in_specs, args, scratch=(), limit=40):
    return pl.pallas_call(
        kernel,
        out_shape=out_shape,
        in_specs=in_specs,
        out_specs=jax.tree.map(lambda _: VMEM, out_shape),
        scratch_shapes=scratch,
        compiler_params=pltpu.CompilerParams(vmem_limit_bytes=limit * MIB),
        name=name,
    )(*args)


def core_permute(value):
    devs = lax.axis_size("dev")
    return lax.ppermute(value, "dev", [(d, d ^ 1) for d in range(devs)])


def chip_permute(value, k):
    devs = lax.axis_size("dev")
    return lax.ppermute(value, "dev", [(d, (d + k * CORES) % devs) for d in range(devs)])


def host_permute(value, k):
    hosts = lax.axis_size("hst")
    return lax.ppermute(value, "hst", [(h, (h + k) % hosts) for h in range(hosts)])


def across_hosts(blocks):
    return [blocks[0]] + [host_permute(blocks[k], k) for k in range(1, len(blocks))]


def across_devs(value):
    chips = lax.axis_size("dev") // CORES
    held = [value] + [chip_permute(value, k) for k in range(1, chips)]
    out = []
    for block in held:
        out += [block, core_permute(block)]
    return out


def shape(rows, width, kind=BF16):
    return jax.ShapeDtypeStruct((rows, width), kind)


def body(
    features,
    send_list,
    tile_dst,
    tile_src,
    tile_rows,
    tile_val,
    self_one,
    neigh_one,
    bias_one,
    self_two,
    neigh_two,
    bias_two,
    cotangent,
):
    devs = lax.axis_size("dev")
    hosts = lax.axis_size("hst")
    chips = devs // CORES
    rows, width = features.shape
    tiles, blk = tile_val.shape[:2]
    send = send_list.shape[3]
    far = hosts * send
    all_rows = devs * (rows + far)
    half = jax.ShapeDtypeStruct((chips, rows + far, width), BF16)
    blocks = (shape(send, width),) * hosts
    space = pltpu.VMEM((all_rows, width), BF16)

    def halo_of(picked):
        arrived = across_hosts(picked)
        joined = call(
            functools.partial(join_kernel, hosts, send),
            "join",
            shape(far, width),
            [VMEM] * hosts,
            arrived,
            [pltpu.VMEM((far, width), F32)],
        )
        return across_devs(joined)

    def reduced(keep, give):
        came = core_permute(give)
        sums = call(
            functools.partial(core_sum_kernel, devs),
            "core_sum",
            (shape(rows + far, width, F32),) + (shape(rows + far, width),) * (chips - 1),
            [VMEM] * 2,
            (keep, came),
        )
        terms = [chip_permute(sums[k], k) for k in range(1, chips)]
        sums = call(
            functools.partial(chip_sum_kernel, hosts, send, chips - 1),
            "chip_sum",
            (shape(rows, width, F32),) + blocks,
            [VMEM] * chips,
            (sums[0], *terms),
            [pltpu.VMEM((far, width), F32)],
        )
        return sums[0], across_hosts(sums[1:])

    wide = across_devs(features)
    adj, keep, give, *picked = call(
        functools.partial(prep_kernel, devs),
        "prep",
        (shape(rows, all_rows), half, half) + blocks,
        [SMEM] * 4 + [ANY] + [VMEM] * 3,
        (tile_dst, tile_src, tile_rows, send_list, tile_val, features, cotangent, neigh_two),
        [
            pltpu.VMEM((tiles, blk, blk), BF16),
            pltpu.VMEM(((rows // blk) * (all_rows // blk), blk, blk), F32),
            space,
            pltpu.SemaphoreType.DMA((CHUNKS,)),
        ],
        limit=56,
    )
    halo = halo_of(picked)
    own, back = reduced(keep, give)
    pre, hidden, *picked = call(
        functools.partial(forward_one_kernel, devs),
        "forward_one",
        (shape(rows, width, F32), shape(rows, width)) + blocks,
        [SMEM] + [VMEM] * (4 + 2 * devs),
        (send_list, adj, self_one, neigh_one, bias_one, *wide, *halo),
        [space],
    )
    wide = across_devs(hidden)
    halo = halo_of(picked)
    grad_pre, keep, give = call(
        functools.partial(backward_two_kernel, devs, hosts),
        "backward_two",
        (shape(rows, width), half, half),
        [SMEM] + [VMEM] * (6 + hosts),
        (send_list, adj, pre, cotangent, self_two, neigh_one, own, *back),
        [space],
    )
    own, back = reduced(keep, give)
    output = call(
        functools.partial(forward_two_kernel, devs),
        "forward_two",
        shape(rows, width),
        [VMEM] * (4 + 2 * devs),
        (adj, self_two, neigh_two, bias_two, *wide, *halo),
        [space],
    )
    grad = call(
        functools.partial(backward_one_kernel, hosts),
        "backward_one",
        shape(rows, width, F32),
        [SMEM] + [VMEM] * (3 + hosts),
        (send_list, grad_pre, self_one, own, *back),
    )
    return output, grad


def solution(mesh):
    split = P(("hst", "dev"))
    return jax.shard_map(
        body,
        mesh=mesh,
        in_specs=(
            P(("hst", "dev"), None),
            P("hst", "dev", None, None),
            split,
            split,
            split,
            P(("hst", "dev"), None, None),
            P(),
            P(),
            P(),
            P(),
            P(),
            P(),
            P(("hst", "dev"), None),
        ),
        out_specs=(P(("hst", "dev"), None), P(("hst", "dev"), None)),
        check_vma=False,
    )
```

```python
import functools

import jax
import jax.numpy as jnp
from jax import lax
from jax.experimental import pallas as pl
from jax.experimental.pallas import tpu as pltpu
from jax.sharding import Mesh, PartitionSpec as P

F32 = jnp.float32
BF16 = jnp.bfloat16
MIB = 1024 * 1024
CHUNKS = 8
CORES = 2

VMEM = pl.BlockSpec(memory_space=pltpu.VMEM)
SMEM = pl.BlockSpec(memory_space=pltpu.SMEM)
HBM = pl.BlockSpec(memory_space=pltpu.HBM)


def dot(a, b):
    return jnp.dot(a, b, preferred_element_type=F32)


def dot_nt(a, b):
    return lax.dot_general(a, b, (((1,), (1,)), ((), ())), preferred_element_type=F32)


def dot_tn(a, b):
    return lax.dot_general(a, b, (((0,), (0,)), ((), ())), preferred_element_type=F32)


def pick_matrix(send_ref, rows):
    hosts, send = send_ref.shape[2], send_ref.shape[3]
    place = lax.broadcasted_iota(jnp.int32, (send, rows), 0)
    column = lax.broadcasted_iota(jnp.int32, (send, rows), 1)
    parts = []
    for g in range(hosts):
        index = jnp.zeros((send, rows), jnp.int32)
        for s in range(send):
            index = jnp.where(place == s, send_ref[0, 0, g, s], index)
        parts.append(jnp.where(index == column, 1.0, 0.0).astype(F32))
    return jnp.concatenate(parts, 0).astype(BF16)


def spread_parts(chips, far, adj_t, u, value, whole, keep_ref, give_ref):
    rows = u.shape[0]
    own_rows = chips * CORES * rows
    whole[...] = dot(adj_t, u).astype(BF16)
    core = lax.axis_index("core")
    each = rows + far
    for side, ref in ((core, keep_ref), (1 - core, give_ref)):
        for x in range(chips):
            d = x * CORES + side
            low = pl.multiple_of(d * rows, rows)
            ref[x * each : x * each + rows, :] = whole[pl.ds(low, rows), :]
            low = pl.multiple_of(own_rows + d * far, far)
            ref[x * each + rows : (x + 1) * each, :] = whole[pl.ds(low, far), :]
    give_ref[chips * each :, :] = value


def prep_kernel(
    chips,
    dst_hbm,
    src_hbm,
    rows_hbm,
    send_hbm,
    tile_hbm,
    features_hbm,
    cot_hbm,
    neigh_two_hbm,
    adj_ref,
    adj_t_ref,
    keep_ref,
    give_ref,
    picked_ref,
    dst_ref,
    src_ref,
    rows_ref,
    send_ref,
    tile_buf,
    features_ref,
    cot_ref,
    neigh_two_ref,
    acc,
    whole,
    sems,
):
    tiles, blk = tile_buf.shape[0], tile_buf.shape[1]
    each = tiles // CHUNKS
    pairs = [
        (cot_hbm, cot_ref),
        (neigh_two_hbm, neigh_two_ref),
        (features_hbm, features_ref),
        (send_hbm, send_ref),
        (dst_hbm, dst_ref),
        (src_hbm, src_ref),
        (rows_hbm, rows_ref),
    ]
    pairs += [
        (tile_hbm.at[pl.ds(c * each, each)], tile_buf.at[pl.ds(c * each, each)])
        for c in range(CHUNKS)
    ]
    copies = [pltpu.make_async_copy(a, b, sems.at[i]) for i, (a, b) in enumerate(pairs)]
    for copy in copies:
        copy.start()
    rows = features_ref.shape[0]
    bpd = rows // blk
    sources = acc.shape[0] // bpd
    far = send_ref.shape[2] * send_ref.shape[3]
    acc[...] = jnp.zeros_like(acc)
    copies[0].wait()
    copies[1].wait()
    u = dot_nt(cot_ref[...], neigh_two_ref[...]).astype(BF16)
    copies[2].wait()
    copies[3].wait()
    picked_ref[...] = dot(pick_matrix(send_ref, rows), features_ref[...]).astype(BF16)
    for copy in copies[4:7]:
        copy.wait()
    place = lax.broadcasted_iota(jnp.int32, (blk, blk), 0)
    for c in range(CHUNKS):
        copies[7 + c].wait()

        def add(t, carry):
            slot = dst_ref[t] * sources + src_ref[t]
            live = jnp.where(place < rows_ref[t], tile_buf[t].astype(F32), 0.0)
            acc[slot] = acc[slot] + live
            return carry

        lax.fori_loop(c * each, (c + 1) * each, add, 0, unroll=True)
    for b in range(bpd):
        for j in range(sources):
            block = acc[b * sources + j].astype(BF16)
            adj_ref[b * blk : (b + 1) * blk, j * blk : (j + 1) * blk] = block
            adj_t_ref[j * blk : (j + 1) * blk, b * blk : (b + 1) * blk] = block.T
    spread_parts(
        chips, far, adj_t_ref[...], u, features_ref[...], whole, keep_ref, give_ref
    )


def core_sum_kernel(
    chips, hosts, keep_ref, came_ref, value_ref, picked_ref, mine_ref, msg_ref, *rest
):
    to_refs, total = rest[:-1], rest[-1]
    rows = value_ref.shape[0]
    far = picked_ref.shape[0]
    send = far // hosts
    each = rows + far
    chip = lax.axis_index("chip")
    total[...] = keep_ref[...].astype(F32) + came_ref[: chips * each, :].astype(F32)
    mine_ref[...] = total[pl.ds(pl.multiple_of(chip * each, 8), rows), :]
    for k, ref in enumerate(to_refs):
        other = lax.rem(chip + k + 1, chips)
        ref[:rows, :] = total[pl.ds(pl.multiple_of(other * each, 8), rows), :].astype(BF16)
        ref[rows:, :] = value_ref[...]
    picked = picked_ref[...].astype(F32)
    for g in range(hosts):
        for x in range(chips):
            low = x * each + rows + g * send
            both = jnp.concatenate(
                [picked[g * send : (g + 1) * send], total[low : low + send, :]], 0
            )
            msg_ref[g * chips + x] = both.astype(BF16)


def halo_part(recv_ref, hosts, chips, part):
    send = recv_ref.shape[1] // 2
    low = part * send
    blocks = [
        recv_ref[g * chips + x].astype(F32)[low : low + send]
        for x in range(chips)
        for g in range(hosts)
    ]
    return jnp.concatenate(blocks, 0).astype(BF16)


def merge_kernel(chips, hosts, recv_ref, *refs):
    came, out_ref = refs[:-1], refs[-1]
    rows = came[0].shape[0] // 2
    for k, ref in enumerate(came):
        out_ref[k * rows : (k + 1) * rows, :] = ref[rows:, :]
    out_ref[len(came) * rows :, :] = halo_part(recv_ref, hosts, chips, 0)


def gather_sources(chips, hosts, value, came_ref, chip_refs, recv_ref, shared_ref, space):
    rows = value.shape[0]
    chip, core = lax.axis_index("chip"), lax.axis_index("core")
    far_rows = recv_ref.shape[0] // chips * recv_ref.shape[1] // 2

    def put(x, side, block):
        low = pl.multiple_of((x * CORES + side) * rows, rows)
        space[pl.ds(low, rows), :] = block

    put(chip, core, value)
    put(chip, 1 - core, came_ref[came_ref.shape[0] - rows :, :])
    for k, ref in enumerate(chip_refs):
        x = lax.rem(chip - k - 1 + chips, chips)
        put(x, core, ref[rows:, :])
        put(x, 1 - core, shared_ref[k * rows : (k + 1) * rows, :])
    base = chips * CORES * rows
    here = halo_part(recv_ref, hosts, chips, 0)
    there = shared_ref[(chips - 1) * rows :, :]
    for x in range(chips):
        for side, block in ((core, here), (1 - core, there)):
            low = pl.multiple_of(base + (x * CORES + side) * far_rows, far_rows)
            space[pl.ds(low, far_rows), :] = block[x * far_rows : (x + 1) * far_rows]


def spread_total(pick, chips, hosts, mine_ref, chip_refs, recv_ref):
    total = mine_ref[...]
    rows = total.shape[0]
    for ref in chip_refs:
        total = total + ref[:rows, :].astype(F32)
    back = halo_part(recv_ref, hosts, chips, 1)
    return total + dot_tn(jnp.concatenate([pick] * chips, 0), back)


def middle_kernel(
    chips,
    hosts,
    send_ref,
    adj_ref,
    adj_t_ref,
    features_ref,
    cot_ref,
    self_one_ref,
    neigh_one_ref,
    bias_ref,
    self_two_ref,
    mine_ref,
    came_ref,
    recv_ref,
    shared_ref,
    *refs,
):
    chip_refs = refs[: chips - 1]
    hidden_ref, grad_pre_ref, keep_ref, give_ref, picked_ref, space = refs[chips - 1 :]
    rows = features_ref.shape[0]
    far = send_ref.shape[2] * send_ref.shape[3]
    pick = pick_matrix(send_ref, rows)
    gather_sources(
        chips, hosts, features_ref[...], came_ref, chip_refs, recv_ref, shared_ref, space
    )
    agg = dot(adj_ref[...], space[...]).astype(BF16)
    pre = dot(features_ref[...], self_one_ref[...])
    pre = pre + dot(agg, neigh_one_ref[...]) + bias_ref[...].reshape(1, -1)
    sigmoid = jax.nn.sigmoid(pre)
    hidden = (pre * sigmoid).astype(BF16)
    hidden_ref[...] = hidden
    picked_ref[...] = dot(pick, hidden).astype(BF16)
    grad = dot_nt(cot_ref[...], self_two_ref[...])
    grad = grad + spread_total(pick, chips, hosts, mine_ref, chip_refs, recv_ref)
    grad_pre = (grad * sigmoid * (1.0 + pre * (1.0 - sigmoid))).astype(BF16)
    grad_pre_ref[...] = grad_pre
    u = dot_nt(grad_pre, neigh_one_ref[...]).astype(BF16)
    spread_parts(chips, far, adj_t_ref[...], u, hidden, space, keep_ref, give_ref)


def last_kernel(
    chips,
    hosts,
    send_ref,
    adj_ref,
    hidden_ref,
    grad_pre_ref,
    self_one_ref,
    self_two_ref,
    neigh_two_ref,
    bias_ref,
    mine_ref,
    came_ref,
    recv_ref,
    shared_ref,
    *refs,
):
    chip_refs = refs[: chips - 1]
    output_ref, grad_ref, space = refs[chips - 1 :]
    rows = hidden_ref.shape[0]
    pick = pick_matrix(send_ref, rows)
    gather_sources(
        chips, hosts, hidden_ref[...], came_ref, chip_refs, recv_ref, shared_ref, space
    )
    agg = dot(adj_ref[...], space[...]).astype(BF16)
    result = dot(hidden_ref[...], self_two_ref[...])
    result = result + dot(agg, neigh_two_ref[...]) + bias_ref[...].reshape(1, -1)
    output_ref[...] = result.astype(BF16)
    grad = dot_nt(grad_pre_ref[...], self_one_ref[...])
    grad_ref[...] = grad + spread_total(pick, chips, hosts, mine_ref, chip_refs, recv_ref)


def call(kernel, name, out_shape, in_specs, args, scratch=(), limit=32):
    return pl.pallas_call(
        kernel,
        out_shape=out_shape,
        in_specs=in_specs,
        out_specs=jax.tree.map(lambda _: VMEM, out_shape),
        scratch_shapes=scratch,
        compiler_params=pltpu.CompilerParams(vmem_limit_bytes=limit * MIB),
        name=name,
    )(*args)


def shift(value, axis, k):
    size = lax.axis_size(axis)
    return lax.ppermute(value, axis, [(i, (i + k) % size) for i in range(size)])


def shape(rows, width, kind=BF16):
    return jax.ShapeDtypeStruct((rows, width), kind)


def body(
    features,
    send_list,
    tile_dst,
    tile_src,
    tile_rows,
    tile_val,
    self_one,
    neigh_one,
    bias_one,
    self_two,
    neigh_two,
    bias_two,
    cotangent,
):
    chips = lax.axis_size("chip")
    hosts = lax.axis_size("hst")
    rows, width = features.shape
    tiles, blk = tile_val.shape[:2]
    send = send_list.shape[3]
    far = hosts * send
    all_rows = chips * CORES * (rows + far)
    keep_shape = shape(chips * (rows + far), width)
    give_shape = shape(chips * (rows + far) + rows, width)
    picked_shape = shape(far, width)
    rows_shape = shape(rows, width)
    space = pltpu.VMEM((all_rows, width), BF16)

    def exchange(keep, give, value, picked):
        came = shift(give, "core", 1)
        mine, msg, *to = call(
            functools.partial(core_sum_kernel, chips, hosts),
            "core_sum",
            (
                shape(rows, width, F32),
                jax.ShapeDtypeStruct((hosts * chips, 2 * send, width), BF16),
            )
            + (shape(2 * rows, width),) * (chips - 1),
            [VMEM] * 4,
            (keep, came, value, picked),
            [pltpu.VMEM(keep_shape.shape, F32)],
        )
        terms = [shift(block, "chip", k + 1) for k, block in enumerate(to)]
        recv = lax.all_to_all(msg, ("hst", "chip"), split_axis=0, concat_axis=0, tiled=True)
        merged = call(
            functools.partial(merge_kernel, chips, hosts),
            "merge",
            shape((chips - 1) * rows + chips * far, width),
            [VMEM] * chips,
            (recv, *terms),
        )
        shared = shift(merged, "core", 1)
        return mine, came, recv, shared, *terms

    adj, adj_t, keep, give, picked = call(
        functools.partial(prep_kernel, chips),
        "prep",
        (shape(rows, all_rows), shape(all_rows, rows), keep_shape, give_shape, picked_shape),
        [HBM] * 8,
        [
            pltpu.with_memory_space_constraint(value, pltpu.HBM)
            for value in (
                tile_dst,
                tile_src,
                tile_rows,
                send_list,
                tile_val,
                features,
                cotangent,
                neigh_two,
            )
        ],
        [
            pltpu.SMEM(tile_dst.shape, jnp.int32),
            pltpu.SMEM(tile_src.shape, jnp.int32),
            pltpu.SMEM(tile_rows.shape, jnp.int32),
            pltpu.SMEM(send_list.shape, jnp.int32),
            pltpu.VMEM(tile_val.shape, BF16),
            pltpu.VMEM(features.shape, BF16),
            pltpu.VMEM(cotangent.shape, BF16),
            pltpu.VMEM(neigh_two.shape, BF16),
            pltpu.VMEM(((rows // blk) * (all_rows // blk), blk, blk), F32),
            space,
            pltpu.SemaphoreType.DMA((7 + CHUNKS,)),
        ],
    )
    came = exchange(keep, give, features, picked)
    hidden, grad_pre, keep, give, picked = call(
        functools.partial(middle_kernel, chips, hosts),
        "middle",
        (rows_shape, rows_shape, keep_shape, give_shape, picked_shape),
        [SMEM] + [VMEM] * (11 + chips),
        (
            send_list,
            adj,
            adj_t,
            features,
            cotangent,
            self_one,
            neigh_one,
            bias_one,
            self_two,
            *came,
        ),
        [space],
    )
    came = exchange(keep, give, hidden, picked)
    return call(
        functools.partial(last_kernel, chips, hosts),
        "last",
        (rows_shape, shape(rows, width, F32)),
        [SMEM] + [VMEM] * (10 + chips),
        (
            send_list,
            adj,
            hidden,
            grad_pre,
            self_one,
            self_two,
            neigh_two,
            bias_two,
            *came,
        ),
        [space],
    )


def solution(mesh):
    hosts, devs = mesh.devices.shape
    mesh = Mesh(mesh.devices.reshape(hosts, devs // CORES, CORES), ("hst", "chip", "core"))
    dev = ("chip", "core")
    every = ("hst", "chip", "core")
    return jax.shard_map(
        body,
        mesh=mesh,
        in_specs=(
            P(every, None),
            P("hst", dev, None, None),
            P(every),
            P(every),
            P(every),
            P(every, None, None),
            P(),
            P(),
            P(),
            P(),
            P(),
            P(),
            P(every, None),
        ),
        out_specs=(P(every, None), P(every, None)),
        check_vma=False,
    )
```

```python
import functools

import jax
import jax.numpy as jnp
from jax import lax
from jax.experimental import pallas as pl
from jax.experimental.pallas import tpu as pltpu
from jax.sharding import Mesh, PartitionSpec as P

F32 = jnp.float32
BF16 = jnp.bfloat16
MIB = 1024 * 1024
CHUNKS = 8
CORES = 2

VMEM = pl.BlockSpec(memory_space=pltpu.VMEM)
SMEM = pl.BlockSpec(memory_space=pltpu.SMEM)
HBM = pl.BlockSpec(memory_space=pltpu.HBM)


def dot(a, b):
    return jnp.dot(a, b, preferred_element_type=F32)


def dot_nt(a, b):
    return lax.dot_general(a, b, (((1,), (1,)), ((), ())), preferred_element_type=F32)


def dot_tn(a, b):
    return lax.dot_general(a, b, (((0,), (0,)), ((), ())), preferred_element_type=F32)


def pick_matrix(send_ref, rows):
    hosts, send = send_ref.shape[2], send_ref.shape[3]
    place = lax.broadcasted_iota(jnp.int32, (send, rows), 0)
    column = lax.broadcasted_iota(jnp.int32, (send, rows), 1)
    parts = []
    for g in range(hosts):
        index = jnp.zeros((send, rows), jnp.int32)
        for s in range(send):
            index = jnp.where(place == s, send_ref[0, 0, g, s], index)
        parts.append(jnp.where(index == column, 1.0, 0.0).astype(F32))
    return jnp.concatenate(parts, 0).astype(BF16)


def spread_parts(chips, far, adj_t, u, value, whole, keep_ref, give_ref):
    rows = u.shape[0]
    own_rows = chips * CORES * rows
    whole[...] = dot(adj_t, u).astype(BF16)
    core = lax.axis_index("core")
    each = rows + far
    for side, ref in ((core, keep_ref), (1 - core, give_ref)):
        for x in range(chips):
            d = x * CORES + side
            low = pl.multiple_of(d * rows, rows)
            ref[x * each : x * each + rows, :] = whole[pl.ds(low, rows), :]
            low = pl.multiple_of(own_rows + d * far, far)
            ref[x * each + rows : (x + 1) * each, :] = whole[pl.ds(low, far), :]
    give_ref[chips * each :, :] = value


def prep_kernel(
    chips,
    dst_hbm,
    src_hbm,
    rows_hbm,
    send_hbm,
    tile_hbm,
    features_hbm,
    cot_hbm,
    neigh_two_hbm,
    adj_ref,
    adj_t_ref,
    keep_ref,
    give_ref,
    picked_ref,
    dst_ref,
    src_ref,
    rows_ref,
    send_ref,
    tile_buf,
    features_ref,
    cot_ref,
    neigh_two_ref,
    acc,
    whole,
    sems,
):
    tiles, blk = tile_buf.shape[0], tile_buf.shape[1]
    each = tiles // CHUNKS
    pairs = [
        (cot_hbm, cot_ref),
        (neigh_two_hbm, neigh_two_ref),
        (features_hbm, features_ref),
        (send_hbm, send_ref),
        (dst_hbm, dst_ref),
        (src_hbm, src_ref),
        (rows_hbm, rows_ref),
    ]
    pairs += [
        (tile_hbm.at[pl.ds(c * each, each)], tile_buf.at[pl.ds(c * each, each)])
        for c in range(CHUNKS)
    ]
    copies = [pltpu.make_async_copy(a, b, sems.at[i]) for i, (a, b) in enumerate(pairs)]
    for copy in copies:
        copy.start()
    rows = features_ref.shape[0]
    bpd = rows // blk
    sources = acc.shape[0] // bpd
    far = send_ref.shape[2] * send_ref.shape[3]
    acc[...] = jnp.zeros_like(acc)
    copies[0].wait()
    copies[1].wait()
    u = dot_nt(cot_ref[...], neigh_two_ref[...]).astype(BF16)
    copies[2].wait()
    copies[3].wait()
    picked_ref[...] = dot(pick_matrix(send_ref, rows), features_ref[...]).astype(BF16)
    for copy in copies[4:7]:
        copy.wait()
    place = lax.broadcasted_iota(jnp.int32, (blk, blk), 0)
    for c in range(CHUNKS):
        copies[7 + c].wait()

        def add(t, carry):
            slot = dst_ref[t] * sources + src_ref[t]
            live = jnp.where(place < rows_ref[t], tile_buf[t].astype(F32), 0.0)
            acc[slot] = acc[slot] + live
            return carry

        lax.fori_loop(c * each, (c + 1) * each, add, 0, unroll=True)
    for b in range(bpd):
        for j in range(sources):
            block = acc[b * sources + j].astype(BF16)
            adj_ref[b * blk : (b + 1) * blk, j * blk : (j + 1) * blk] = block
            adj_t_ref[j * blk : (j + 1) * blk, b * blk : (b + 1) * blk] = block.T
    spread_parts(
        chips, far, adj_t_ref[...], u, features_ref[...], whole, keep_ref, give_ref
    )


def core_sum_kernel(
    chips, keep_ref, came_ref, value_ref, picked_ref, mine_ref, far_ref, *rest
):
    small_refs, big_refs, total = rest[: chips - 1], rest[chips - 1 : -1], rest[-1]
    rows = value_ref.shape[0]
    far = picked_ref.shape[0]
    each = rows + far
    chip = lax.axis_index("chip")
    total[...] = keep_ref[...].astype(F32) + came_ref[: chips * each, :].astype(F32)
    low = pl.multiple_of(chip * each, 8)
    mine_ref[...] = total[pl.ds(low, rows), :]
    far_ref[...] = total[pl.ds(low + rows, far), :]
    for k in range(chips - 1):
        other = lax.rem(chip + k + 1, chips)
        low = pl.multiple_of(other * each, 8)
        small_refs[k][:far, :] = total[pl.ds(low + rows, far), :].astype(BF16)
        small_refs[k][far:, :] = picked_ref[...]
        big_refs[k][:rows, :] = total[pl.ds(low, rows), :].astype(BF16)
        big_refs[k][rows:, :] = value_ref[...]


def halves(hosts, bit):
    stay = [r for r in range(hosts) if not r & bit]
    return stay, [r for r in range(hosts) if r & bit]


def deal_kernel(chips, hosts, picked_ref, far_ref, *refs):
    came, (stay_ref, go_ref, buf) = refs[: chips - 1], refs[chips - 1 :]
    far = far_ref.shape[0]
    send = far // hosts
    chip, me = lax.axis_index("chip"), lax.axis_index("hst")

    def put(x, value):
        buf[pl.ds(pl.multiple_of(x * far, far), far), :] = value

    total = far_ref[...]
    put(chip, picked_ref[...].astype(F32))
    for k, ref in enumerate(came):
        total = total + ref[:far, :].astype(F32)
        put(lax.rem(chip - k - 1 + chips, chips), ref[far:, :].astype(F32))
    buf[chips * far :, :] = total
    for blocks, ref in zip(halves(hosts, 1), (stay_ref, go_ref)):
        parts = []
        for r in blocks:
            host = lax.bitwise_xor(me, r)
            for x in range(chips + 1):
                parts.append(buf[pl.ds(pl.multiple_of(x * far + host * send, send), send), :])
        ref[...] = jnp.concatenate(parts, 0).astype(BF16)


def regroup(hosts, bit, stay_ref, came_ref):
    size = stay_ref.shape[0] // (hosts // 2)
    out = {}
    for blocks, ref in zip(halves(hosts, bit), (stay_ref, came_ref)):
        value = ref[...].astype(F32)
        for i, r in enumerate(blocks):
            out[r] = value[i * size : (i + 1) * size]
    return out


def pass_kernel(hosts, bit, stay_ref, came_ref, stay_out, go_out):
    held = regroup(hosts, bit, stay_ref, came_ref)
    for blocks, ref in zip(halves(hosts, 2 * bit), (stay_out, go_out)):
        ref[...] = jnp.concatenate([held[r] for r in blocks], 0).astype(BF16)


def merge_kernel(chips, hosts, stay_ref, came_ref, *refs):
    came, (out_ref, back_ref, buf) = refs[: chips - 1], refs[chips - 1 :]
    rows = came[0].shape[0] // 2
    far = back_ref.shape[0]
    send = far // hosts
    held = regroup(hosts, hosts // 2, stay_ref, came_ref)
    me = lax.axis_index("hst")
    for r, value in held.items():
        host = lax.bitwise_xor(me, r)
        for x in range(chips + 1):
            low = pl.multiple_of(x * far + host * send, send)
            buf[pl.ds(low, send), :] = value[x * send : (x + 1) * send]
    for k, ref in enumerate(came):
        out_ref[k * rows : (k + 1) * rows, :] = ref[rows:, :]
    out_ref[len(came) * rows :, :] = buf[: chips * far, :].astype(BF16)
    back_ref[...] = buf[chips * far :, :].astype(BF16)


def gather_sources(chips, value, came_ref, chip_refs, here_ref, shared_ref, space):
    rows = value.shape[0]
    chip, core = lax.axis_index("chip"), lax.axis_index("core")
    far = (here_ref.shape[0] - (chips - 1) * rows) // chips

    def put(x, side, block):
        low = pl.multiple_of((x * CORES + side) * rows, rows)
        space[pl.ds(low, rows), :] = block

    put(chip, core, value)
    put(chip, 1 - core, came_ref[came_ref.shape[0] - rows :, :])
    for k, ref in enumerate(chip_refs):
        x = lax.rem(chip - k - 1 + chips, chips)
        put(x, core, ref[rows:, :])
        put(x, 1 - core, shared_ref[k * rows : (k + 1) * rows, :])
    base = chips * CORES * rows
    for x in range(chips):
        at = (chips - 1) * rows + x * far
        for side, ref in ((core, here_ref), (1 - core, shared_ref)):
            low = pl.multiple_of(base + (x * CORES + side) * far, far)
            space[pl.ds(low, far), :] = ref[at : at + far, :]


def spread_total(pick, mine_ref, chip_refs, back_ref):
    total = mine_ref[...]
    rows = total.shape[0]
    for ref in chip_refs:
        total = total + ref[:rows, :].astype(F32)
    return total + dot_tn(pick, back_ref[...])


def middle_kernel(
    chips,
    send_ref,
    adj_ref,
    adj_t_ref,
    features_ref,
    cot_ref,
    self_one_ref,
    neigh_one_ref,
    bias_ref,
    self_two_ref,
    mine_ref,
    came_ref,
    here_ref,
    back_ref,
    shared_ref,
    *refs,
):
    chip_refs = refs[: chips - 1]
    hidden_ref, grad_pre_ref, keep_ref, give_ref, picked_ref, space = refs[chips - 1 :]
    rows = features_ref.shape[0]
    far = send_ref.shape[2] * send_ref.shape[3]
    pick = pick_matrix(send_ref, rows)
    gather_sources(
        chips, features_ref[...], came_ref, chip_refs, here_ref, shared_ref, space
    )
    agg = dot(adj_ref[...], space[...]).astype(BF16)
    pre = dot(features_ref[...], self_one_ref[...])
    pre = pre + dot(agg, neigh_one_ref[...]) + bias_ref[...].reshape(1, -1)
    sigmoid = jax.nn.sigmoid(pre)
    hidden = (pre * sigmoid).astype(BF16)
    hidden_ref[...] = hidden
    picked_ref[...] = dot(pick, hidden).astype(BF16)
    grad = dot_nt(cot_ref[...], self_two_ref[...])
    grad = grad + spread_total(pick, mine_ref, chip_refs, back_ref)
    grad_pre = (grad * sigmoid * (1.0 + pre * (1.0 - sigmoid))).astype(BF16)
    grad_pre_ref[...] = grad_pre
    u = dot_nt(grad_pre, neigh_one_ref[...]).astype(BF16)
    spread_parts(chips, far, adj_t_ref[...], u, hidden, space, keep_ref, give_ref)


def last_kernel(
    chips,
    send_ref,
    adj_ref,
    hidden_ref,
    grad_pre_ref,
    self_one_ref,
    self_two_ref,
    neigh_two_ref,
    bias_ref,
    mine_ref,
    came_ref,
    here_ref,
    back_ref,
    shared_ref,
    *refs,
):
    chip_refs = refs[: chips - 1]
    output_ref, grad_ref, space = refs[chips - 1 :]
    rows = hidden_ref.shape[0]
    pick = pick_matrix(send_ref, rows)
    gather_sources(
        chips, hidden_ref[...], came_ref, chip_refs, here_ref, shared_ref, space
    )
    agg = dot(adj_ref[...], space[...]).astype(BF16)
    result = dot(hidden_ref[...], self_two_ref[...])
    result = result + dot(agg, neigh_two_ref[...]) + bias_ref[...].reshape(1, -1)
    output_ref[...] = result.astype(BF16)
    grad = dot_nt(grad_pre_ref[...], self_one_ref[...])
    grad_ref[...] = grad + spread_total(pick, mine_ref, chip_refs, back_ref)


def call(kernel, name, out_shape, in_specs, args, scratch=(), limit=32):
    return pl.pallas_call(
        kernel,
        out_shape=out_shape,
        in_specs=in_specs,
        out_specs=jax.tree.map(lambda _: VMEM, out_shape),
        scratch_shapes=scratch,
        compiler_params=pltpu.CompilerParams(vmem_limit_bytes=limit * MIB),
        name=name,
    )(*args)


def shift(value, axis, k):
    size = lax.axis_size(axis)
    return lax.ppermute(value, axis, [(i, (i + k) % size) for i in range(size)])


def flip(value, axis, bit):
    size = lax.axis_size(axis)
    return lax.ppermute(value, axis, [(i, i ^ bit) for i in range(size)])


def shape(rows, width, kind=BF16):
    return jax.ShapeDtypeStruct((rows, width), kind)


def body(
    features,
    send_list,
    tile_dst,
    tile_src,
    tile_rows,
    tile_val,
    self_one,
    neigh_one,
    bias_one,
    self_two,
    neigh_two,
    bias_two,
    cotangent,
):
    chips = lax.axis_size("chip")
    hosts = lax.axis_size("hst")
    rows, width = features.shape
    tiles, blk = tile_val.shape[:2]
    send = send_list.shape[3]
    far = hosts * send
    all_rows = chips * CORES * (rows + far)
    keep_shape = shape(chips * (rows + far), width)
    give_shape = shape(chips * (rows + far) + rows, width)
    picked_shape = shape(far, width)
    rows_shape = shape(rows, width)
    space = pltpu.VMEM((all_rows, width), BF16)

    def exchange(keep, give, value, picked):
        came = shift(give, "core", 1)
        mine, far_sum, *to = call(
            functools.partial(core_sum_kernel, chips),
            "core_sum",
            (shape(rows, width, F32), shape(far, width, F32))
            + (shape(2 * far, width),) * (chips - 1)
            + (shape(2 * rows, width),) * (chips - 1),
            [VMEM] * 4,
            (keep, came, value, picked),
            [pltpu.VMEM(keep_shape.shape, F32)],
        )
        small = [shift(block, "chip", k + 1) for k, block in enumerate(to[: chips - 1])]
        small, big = lax.optimization_barrier((small, to[chips - 1 :]))
        block_buf = pltpu.VMEM(((chips + 1) * far, width), F32)
        half = (shape((chips + 1) * far // 2, width),) * 2
        stay, go = call(
            functools.partial(deal_kernel, chips, hosts),
            "deal",
            half,
            [VMEM] * (1 + chips),
            (picked, far_sum, *small),
            [block_buf],
        )
        terms = [shift(block, "chip", k + 1) for k, block in enumerate(big)]
        bit = 1
        got = flip(go, "hst", bit)
        while 2 * bit < hosts:
            stay, go = call(
                functools.partial(pass_kernel, hosts, bit), "pass_on", half, [VMEM] * 2, (stay, got)
            )
            bit *= 2
            got = flip(go, "hst", bit)
        here, back = call(
            functools.partial(merge_kernel, chips, hosts),
            "merge",
            (shape((chips - 1) * rows + chips * far, width), shape(far, width)),
            [VMEM] * (1 + chips),
            (stay, got, *terms),
            [block_buf],
        )
        shared = shift(here, "core", 1)
        return mine, came, here, back, shared, *terms

    adj, adj_t, keep, give, picked = call(
        functools.partial(prep_kernel, chips),
        "prep",
        (shape(rows, all_rows), shape(all_rows, rows), keep_shape, give_shape, picked_shape),
        [HBM] * 8,
        [
            pltpu.with_memory_space_constraint(value, pltpu.HBM)
            for value in (
                tile_dst,
                tile_src,
                tile_rows,
                send_list,
                tile_val,
                features,
                cotangent,
                neigh_two,
            )
        ],
        [
            pltpu.SMEM(tile_dst.shape, jnp.int32),
            pltpu.SMEM(tile_src.shape, jnp.int32),
            pltpu.SMEM(tile_rows.shape, jnp.int32),
            pltpu.SMEM(send_list.shape, jnp.int32),
            pltpu.VMEM(tile_val.shape, BF16),
            pltpu.VMEM(features.shape, BF16),
            pltpu.VMEM(cotangent.shape, BF16),
            pltpu.VMEM(neigh_two.shape, BF16),
            pltpu.VMEM(((rows // blk) * (all_rows // blk), blk, blk), F32),
            space,
            pltpu.SemaphoreType.DMA((7 + CHUNKS,)),
        ],
    )
    came = exchange(keep, give, features, picked)
    hidden, grad_pre, keep, give, picked = call(
        functools.partial(middle_kernel, chips),
        "middle",
        (rows_shape, rows_shape, keep_shape, give_shape, picked_shape),
        [SMEM] + [VMEM] * (12 + chips),
        (
            send_list,
            adj,
            adj_t,
            features,
            cotangent,
            self_one,
            neigh_one,
            bias_one,
            self_two,
            *came,
        ),
        [space],
    )
    came = exchange(keep, give, hidden, picked)
    return call(
        functools.partial(last_kernel, chips),
        "last",
        (rows_shape, shape(rows, width, F32)),
        [SMEM] + [VMEM] * (11 + chips),
        (
            send_list,
            adj,
            hidden,
            grad_pre,
            self_one,
            self_two,
            neigh_two,
            bias_two,
            *came,
        ),
        [space],
    )


def solution(mesh):
    hosts, devs = mesh.devices.shape
    mesh = Mesh(mesh.devices.reshape(hosts, devs // CORES, CORES), ("hst", "chip", "core"))
    dev = ("chip", "core")
    every = ("hst", "chip", "core")
    return jax.shard_map(
        body,
        mesh=mesh,
        in_specs=(
            P(every, None),
            P("hst", dev, None, None),
            P(every),
            P(every),
            P(every),
            P(every, None, None),
            P(),
            P(),
            P(),
            P(),
            P(),
            P(),
            P(every, None),
        ),
        out_specs=(P(every, None), P(every, None)),
        check_vma=False,
    )
```

```python
import functools

import jax
import jax.numpy as jnp
from jax import lax
from jax.experimental import pallas as pl
from jax.experimental.pallas import tpu as pltpu
from jax.sharding import Mesh, PartitionSpec as P

F32 = jnp.float32
BF16 = jnp.bfloat16
MIB = 1024 * 1024
CHUNKS = 8
CORES = 2

VMEM = pl.BlockSpec(memory_space=pltpu.VMEM)
HBM = pl.BlockSpec(memory_space=pltpu.HBM)


def dot(a, b):
    return jnp.dot(a, b, preferred_element_type=F32)


def dot_nt(a, b):
    return lax.dot_general(a, b, (((1,), (1,)), ((), ())), preferred_element_type=F32)


def dot_tn(a, b):
    return lax.dot_general(a, b, (((0,), (0,)), ((), ())), preferred_element_type=F32)


def pick_matrix(send_ref, rows):
    hosts, send = send_ref.shape[2], send_ref.shape[3]
    place = lax.broadcasted_iota(jnp.int32, (send, rows), 0)
    column = lax.broadcasted_iota(jnp.int32, (send, rows), 1)
    parts = []
    for g in range(hosts):
        index = jnp.zeros((send, rows), jnp.int32)
        for s in range(send):
            index = jnp.where(place == s, send_ref[0, 0, g, s], index)
        parts.append(jnp.where(index == column, 1.0, 0.0).astype(F32))
    return jnp.concatenate(parts, 0).astype(BF16)


def spread_parts(chips, far, adj_t, u, value, whole, keep_ref, give_ref):
    rows = u.shape[0]
    own_rows = chips * CORES * rows
    whole[...] = dot(adj_t, u).astype(BF16)
    core = lax.axis_index("core")
    each = rows + far
    for side, ref in ((core, keep_ref), (1 - core, give_ref)):
        for x in range(chips):
            d = x * CORES + side
            low = pl.multiple_of(d * rows, rows)
            ref[x * each : x * each + rows, :] = whole[pl.ds(low, rows), :]
            low = pl.multiple_of(own_rows + d * far, far)
            ref[x * each + rows : (x + 1) * each, :] = whole[pl.ds(low, far), :]
    give_ref[chips * each :, :] = value


def prep_kernel(
    chips,
    dst_hbm,
    src_hbm,
    rows_hbm,
    send_hbm,
    tile_hbm,
    features_hbm,
    cot_hbm,
    neigh_two_hbm,
    adj_ref,
    adj_t_ref,
    keep_ref,
    give_ref,
    picked_ref,
    pick_ref,
    dst_ref,
    src_ref,
    rows_ref,
    send_ref,
    tile_buf,
    features_ref,
    cot_ref,
    neigh_two_ref,
    acc,
    whole,
    sems,
):
    tiles, blk = tile_buf.shape[0], tile_buf.shape[1]
    each = tiles // CHUNKS
    pairs = [
        (cot_hbm, cot_ref),
        (neigh_two_hbm, neigh_two_ref),
        (features_hbm, features_ref),
        (send_hbm, send_ref),
        (dst_hbm, dst_ref),
        (src_hbm, src_ref),
        (rows_hbm, rows_ref),
    ]
    pairs += [
        (tile_hbm.at[pl.ds(c * each, each)], tile_buf.at[pl.ds(c * each, each)])
        for c in range(CHUNKS)
    ]
    copies = [pltpu.make_async_copy(a, b, sems.at[i]) for i, (a, b) in enumerate(pairs)]
    for copy in copies:
        copy.start()
    rows = features_ref.shape[0]
    bpd = rows // blk
    sources = acc.shape[0] // bpd
    far = send_ref.shape[2] * send_ref.shape[3]
    acc[...] = jnp.zeros_like(acc)
    copies[0].wait()
    copies[1].wait()
    u = dot_nt(cot_ref[...], neigh_two_ref[...]).astype(BF16)
    copies[2].wait()
    copies[3].wait()
    pick_ref[...] = pick_matrix(send_ref, rows)
    picked_ref[...] = dot(pick_ref[...], features_ref[...]).astype(BF16)
    for copy in copies[4:7]:
        copy.wait()
    place = lax.broadcasted_iota(jnp.int32, (blk, blk), 0)
    for c in range(CHUNKS):
        copies[7 + c].wait()

        def add(t, carry):
            slot = dst_ref[t] * sources + src_ref[t]
            live = jnp.where(place < rows_ref[t], tile_buf[t].astype(F32), 0.0)
            acc[slot] = acc[slot] + live
            return carry

        lax.fori_loop(c * each, (c + 1) * each, add, 0, unroll=True)
    for b in range(bpd):
        for j in range(sources):
            block = acc[b * sources + j].astype(BF16)
            adj_ref[b * blk : (b + 1) * blk, j * blk : (j + 1) * blk] = block
            adj_t_ref[j * blk : (j + 1) * blk, b * blk : (b + 1) * blk] = block.T
    spread_parts(
        chips, far, adj_t_ref[...], u, features_ref[...], whole, keep_ref, give_ref
    )


def core_sum_kernel(
    chips, hosts, keep_ref, came_ref, value_ref, picked_ref, mine_ref, msg_ref, *rest
):
    to_refs, total = rest[:-1], rest[-1]
    rows = value_ref.shape[0]
    far = picked_ref.shape[0]
    send = far // hosts
    each = rows + far
    chip = lax.axis_index("chip")
    total[...] = keep_ref[...].astype(F32) + came_ref[: chips * each, :].astype(F32)
    mine_ref[...] = total[pl.ds(pl.multiple_of(chip * each, 8), rows), :]
    for k, ref in enumerate(to_refs):
        other = lax.rem(chip + k + 1, chips)
        ref[:rows, :] = total[pl.ds(pl.multiple_of(other * each, 8), rows), :].astype(BF16)
        ref[rows:, :] = value_ref[...]
    picked = picked_ref[...].astype(F32)
    for g in range(hosts):
        for x in range(chips):
            low = x * each + rows + g * send
            both = jnp.concatenate(
                [picked[g * send : (g + 1) * send], total[low : low + send, :]], 0
            )
            msg_ref[g * chips + x] = both.astype(BF16)


def halo_part(recv_ref, hosts, chips, part):
    send = recv_ref.shape[1] // 2
    low = part * send
    blocks = [
        recv_ref[g * chips + x].astype(F32)[low : low + send]
        for x in range(chips)
        for g in range(hosts)
    ]
    return jnp.concatenate(blocks, 0).astype(BF16)


def merge_kernel(chips, hosts, recv_ref, *refs):
    came, out_ref = refs[:-1], refs[-1]
    rows = came[0].shape[0] // 2
    for k, ref in enumerate(came):
        out_ref[k * rows : (k + 1) * rows, :] = ref[rows:, :]
    out_ref[len(came) * rows :, :] = halo_part(recv_ref, hosts, chips, 0)


def early_kernel(
    chips, adj_ref, value_ref, came_ref, self_ref, bias_ref, up_ref, weight_ref, mine_ref,
    agg_ref, direct_ref, grad_ref,
):
    value = value_ref[...]
    rows = value.shape[0]
    chip, core = lax.axis_index("chip"), lax.axis_index("core")
    there = came_ref[came_ref.shape[0] - rows :, :]
    total = 0.0
    for side, block in ((core, value), (1 - core, there)):
        low = pl.multiple_of((chip * CORES + side) * rows, rows)
        total = total + dot(adj_ref[:, pl.ds(low, rows)], block)
    agg_ref[...] = total
    direct_ref[...] = dot(value, self_ref[...]) + bias_ref[...].reshape(1, -1)
    grad_ref[...] = dot_nt(up_ref[...], weight_ref[...]) + mine_ref[...]


def mid_kernel(chips, hosts, adj_ref, agg_ref, part_ref, pick_ref, recv_ref, *refs):
    came, (agg_out, grad_ref) = refs[: chips - 1], refs[chips - 1 :]
    rows = part_ref.shape[0]
    chip, core = lax.axis_index("chip"), lax.axis_index("core")
    agg, grad = agg_ref[...], part_ref[...]
    for k, ref in enumerate(came):
        grad = grad + ref[:rows, :].astype(F32)
        x = lax.rem(chip - k - 1 + chips, chips)
        low = pl.multiple_of((x * CORES + core) * rows, rows)
        agg = agg + dot(adj_ref[:, pl.ds(low, rows)], ref[rows:, :])
    back = halo_part(recv_ref, hosts, chips, 1)
    grad_ref[...] = grad + dot_tn(jnp.concatenate([pick_ref[...]] * chips, 0), back)
    agg_out[...] = agg


def full_aggregate(chips, adj_ref, agg_ref, here_ref, shared_ref, halo):
    rows = agg_ref.shape[0]
    far = halo.shape[0] // (chips * CORES)
    chip, core = lax.axis_index("chip"), lax.axis_index("core")
    at = (chips - 1) * rows
    for x in range(chips):
        for side, ref in ((core, here_ref), (1 - core, shared_ref)):
            low = pl.multiple_of((x * CORES + side) * far, far)
            halo[pl.ds(low, far), :] = ref[at + x * far : at + (x + 1) * far, :]
    agg = agg_ref[...]
    for k in range(chips - 1):
        x = lax.rem(chip - k - 1 + chips, chips)
        low = pl.multiple_of((x * CORES + 1 - core) * rows, rows)
        agg = agg + dot(adj_ref[:, pl.ds(low, rows)], shared_ref[k * rows : (k + 1) * rows, :])
    return agg + dot(adj_ref[:, chips * CORES * rows :], halo[...])


def middle_kernel(
    chips,
    adj_ref,
    adj_t_ref,
    agg_ref,
    direct_ref,
    grad_ref,
    pick_ref,
    here_ref,
    shared_ref,
    neigh_one_ref,
    hidden_ref,
    grad_pre_ref,
    keep_ref,
    give_ref,
    picked_ref,
    halo,
    whole,
):
    agg = full_aggregate(chips, adj_ref, agg_ref, here_ref, shared_ref, halo).astype(BF16)
    pre = direct_ref[...] + dot(agg, neigh_one_ref[...])
    sigmoid = jax.nn.sigmoid(pre)
    hidden = (pre * sigmoid).astype(BF16)
    hidden_ref[...] = hidden
    picked_ref[...] = dot(pick_ref[...], hidden).astype(BF16)
    grad_pre = (grad_ref[...] * sigmoid * (1.0 + pre * (1.0 - sigmoid))).astype(BF16)
    grad_pre_ref[...] = grad_pre
    u = dot_nt(grad_pre, neigh_one_ref[...]).astype(BF16)
    spread_parts(
        chips, pick_ref.shape[0], adj_t_ref[...], u, hidden, whole, keep_ref, give_ref
    )


def last_kernel(
    chips, adj_ref, agg_ref, direct_ref, here_ref, shared_ref, neigh_two_ref, output_ref, halo
):
    agg = full_aggregate(chips, adj_ref, agg_ref, here_ref, shared_ref, halo).astype(BF16)
    output_ref[...] = (direct_ref[...] + dot(agg, neigh_two_ref[...])).astype(BF16)


def call(kernel, name, out_shape, in_specs, args, scratch=(), limit=32, flops=0):
    return pl.pallas_call(
        kernel,
        out_shape=out_shape,
        in_specs=in_specs,
        out_specs=jax.tree.map(lambda _: VMEM, out_shape),
        scratch_shapes=scratch,
        compiler_params=pltpu.CompilerParams(vmem_limit_bytes=limit * MIB),
        cost_estimate=pl.CostEstimate(
            flops=flops, bytes_accessed=flops // 1024, transcendentals=0
        ),
        name=name,
    )(*args)


def shift(value, axis, k):
    size = lax.axis_size(axis)
    return lax.ppermute(value, axis, [(i, (i + k) % size) for i in range(size)])


def shape(rows, width, kind=BF16):
    return jax.ShapeDtypeStruct((rows, width), kind)


def body(
    features,
    send_list,
    tile_dst,
    tile_src,
    tile_rows,
    tile_val,
    self_one,
    neigh_one,
    bias_one,
    self_two,
    neigh_two,
    bias_two,
    cotangent,
):
    chips = lax.axis_size("chip")
    hosts = lax.axis_size("hst")
    rows, width = features.shape
    tiles, blk = tile_val.shape[:2]
    send = send_list.shape[3]
    far = hosts * send
    all_rows = chips * CORES * (rows + far)
    keep_shape = shape(chips * (rows + far), width)
    give_shape = shape(chips * (rows + far) + rows, width)
    picked_shape = shape(far, width)
    rows_shape = shape(rows, width)
    space = pltpu.VMEM((all_rows, width), BF16)

    square = 2 * rows * width * width
    halo = pltpu.VMEM((chips * CORES * far, width), BF16)
    sum_shape = shape(rows, width, F32)

    def exchange(adj, pick, keep, give, picked, value, self_weight, bias, up, weight):
        came = shift(give, "core", 1)
        mine, msg, *to = call(
            functools.partial(core_sum_kernel, chips, hosts),
            "core_sum",
            (sum_shape, jax.ShapeDtypeStruct((hosts * chips, 2 * send, width), BF16))
            + (shape(2 * rows, width),) * (chips - 1),
            [VMEM] * 4,
            (keep, came, value, picked),
            [pltpu.VMEM(keep_shape.shape, F32)],
        )
        terms = [shift(block, "chip", k + 1) for k, block in enumerate(to)]
        recv = lax.all_to_all(msg, ("hst", "chip"), split_axis=0, concat_axis=0, tiled=True)
        agg, direct, grad = call(
            functools.partial(early_kernel, chips),
            "early",
            (sum_shape,) * 3,
            [VMEM] * 8,
            (adj, value, came, self_weight, bias, up, weight, mine),
            flops=4 * square,
        )
        here = call(
            functools.partial(merge_kernel, chips, hosts),
            "merge",
            shape((chips - 1) * rows + chips * far, width),
            [VMEM] * chips,
            (recv, *terms),
        )
        shared = shift(here, "core", 1)
        agg, grad = call(
            functools.partial(mid_kernel, chips, hosts),
            "mid",
            (sum_shape,) * 2,
            [VMEM] * (4 + chips),
            (adj, agg, grad, pick, recv, *terms),
            flops=2 * square,
        )
        return agg, direct, grad, here, shared

    adj, adj_t, keep, give, picked, pick = call(
        functools.partial(prep_kernel, chips),
        "prep",
        (shape(rows, all_rows), shape(all_rows, rows), keep_shape, give_shape)
        + (picked_shape, shape(far, rows)),
        [HBM] * 8,
        [
            pltpu.with_memory_space_constraint(value, pltpu.HBM)
            for value in (
                tile_dst,
                tile_src,
                tile_rows,
                send_list,
                tile_val,
                features,
                cotangent,
                neigh_two,
            )
        ],
        [
            pltpu.SMEM(tile_dst.shape, jnp.int32),
            pltpu.SMEM(tile_src.shape, jnp.int32),
            pltpu.SMEM(tile_rows.shape, jnp.int32),
            pltpu.SMEM(send_list.shape, jnp.int32),
            pltpu.VMEM(tile_val.shape, BF16),
            pltpu.VMEM(features.shape, BF16),
            pltpu.VMEM(cotangent.shape, BF16),
            pltpu.VMEM(neigh_two.shape, BF16),
            pltpu.VMEM(((rows // blk) * (all_rows // blk), blk, blk), F32),
            space,
            pltpu.SemaphoreType.DMA((7 + CHUNKS,)),
        ],
    )
    agg, direct, grad, here, shared = exchange(
        adj, pick, keep, give, picked, features, self_one, bias_one, cotangent, self_two
    )
    hidden, grad_pre, keep, give, picked = call(
        functools.partial(middle_kernel, chips),
        "middle",
        (rows_shape, rows_shape, keep_shape, give_shape, picked_shape),
        [VMEM] * 9,
        (adj, adj_t, agg, direct, grad, pick, here, shared, neigh_one),
        [halo, space],
        flops=9 * square,
    )
    agg, direct, grad, here, shared = exchange(
        adj, pick, keep, give, picked, hidden, self_two, bias_two, grad_pre, self_one
    )
    output = call(
        functools.partial(last_kernel, chips),
        "last",
        rows_shape,
        [VMEM] * 6,
        (adj, agg, direct, here, shared, neigh_two),
        [halo],
        flops=3 * square,
    )
    return output, grad


def solution(mesh):
    hosts, devs = mesh.devices.shape
    mesh = Mesh(mesh.devices.reshape(hosts, devs // CORES, CORES), ("hst", "chip", "core"))
    dev = ("chip", "core")
    every = ("hst", "chip", "core")
    return jax.shard_map(
        body,
        mesh=mesh,
        in_specs=(
            P(every, None),
            P("hst", dev, None, None),
            P(every),
            P(every),
            P(every),
            P(every, None, None),
            P(),
            P(),
            P(),
            P(),
            P(),
            P(),
            P(every, None),
        ),
        out_specs=(P(every, None), P(every, None)),
        check_vma=False,
    )
```

```python
import functools

import jax
import jax.numpy as jnp
from jax import lax
from jax.experimental import pallas as pl
from jax.experimental.pallas import tpu as pltpu
from jax.sharding import Mesh, PartitionSpec as P

F32 = jnp.float32
BF16 = jnp.bfloat16
MIB = 1024 * 1024
CHUNKS = 8
PARTS = 4
CORES = 2

VMEM = pl.BlockSpec(memory_space=pltpu.VMEM)
HBM = pl.BlockSpec(memory_space=pltpu.HBM)


def dot(a, b):
    return jnp.dot(a, b, preferred_element_type=F32)


def dot_nt(a, b):
    return lax.dot_general(a, b, (((1,), (1,)), ((), ())), preferred_element_type=F32)


def dot_tn(a, b):
    return lax.dot_general(a, b, (((0,), (0,)), ((), ())), preferred_element_type=F32)


def pick_matrix(send_ref, rows):
    hosts, send = send_ref.shape[2], send_ref.shape[3]
    place = lax.broadcasted_iota(jnp.int32, (send, rows), 0)
    column = lax.broadcasted_iota(jnp.int32, (send, rows), 1)
    parts = []
    for g in range(hosts):
        index = jnp.zeros((send, rows), jnp.int32)
        for s in range(send):
            index = jnp.where(place == s, send_ref[0, 0, g, s], index)
        parts.append(jnp.where(index == column, 1.0, 0.0).astype(F32))
    return jnp.concatenate(parts, 0).astype(BF16)


def spread_parts(chips, far, adj_t, u, value, whole, keep_ref, give_ref):
    rows = u.shape[0]
    own_rows = chips * CORES * rows
    whole[...] = dot(adj_t, u).astype(BF16)
    core = lax.axis_index("core")
    each = rows + far
    for side, ref in ((core, keep_ref), (1 - core, give_ref)):
        for x in range(chips):
            d = x * CORES + side
            low = pl.multiple_of(d * rows, rows)
            ref[x * each : x * each + rows, :] = whole[pl.ds(low, rows), :]
            low = pl.multiple_of(own_rows + d * far, far)
            ref[x * each + rows : (x + 1) * each, :] = whole[pl.ds(low, far), :]
    give_ref[chips * each :, :] = value


def prep_kernel(
    chips,
    dst_hbm,
    src_hbm,
    rows_hbm,
    send_hbm,
    tile_hbm,
    features_hbm,
    cot_hbm,
    neigh_two_hbm,
    adj_ref,
    adj_t_ref,
    keep_ref,
    give_ref,
    picked_ref,
    pick_ref,
    dst_ref,
    src_ref,
    rows_ref,
    send_ref,
    tile_buf,
    features_ref,
    cot_ref,
    neigh_two_ref,
    whole,
    sems,
    *accs,
):
    tiles, blk = tile_buf.shape[0], tile_buf.shape[1]
    each = tiles // CHUNKS
    pairs = [
        (cot_hbm, cot_ref),
        (neigh_two_hbm, neigh_two_ref),
        (features_hbm, features_ref),
        (send_hbm, send_ref),
        (dst_hbm, dst_ref),
        (src_hbm, src_ref),
        (rows_hbm, rows_ref),
    ]
    pairs += [
        (tile_hbm.at[pl.ds(c * each, each)], tile_buf.at[pl.ds(c * each, each)])
        for c in range(CHUNKS)
    ]
    copies = [pltpu.make_async_copy(a, b, sems.at[i]) for i, (a, b) in enumerate(pairs)]
    for copy in copies:
        copy.start()
    rows = features_ref.shape[0]
    bpd = rows // blk
    sources = accs[0].shape[0] // bpd
    far = send_ref.shape[2] * send_ref.shape[3]
    part = accs[0].shape[1]
    for acc in accs:
        acc[...] = jnp.zeros_like(acc)
    copies[0].wait()
    copies[1].wait()
    u = dot_nt(cot_ref[...], neigh_two_ref[...]).astype(BF16)
    copies[2].wait()
    copies[3].wait()
    pick_ref[...] = pick_matrix(send_ref, rows)
    picked_ref[...] = dot(pick_ref[...], features_ref[...]).astype(BF16)
    for copy in copies[4:7]:
        copy.wait()
    place = lax.broadcasted_iota(jnp.int32, (part, blk), 0)
    for c in range(CHUNKS):
        copies[7 + c].wait()

        def add(t, carry):
            slot = dst_ref[t] * sources + src_ref[t]
            for i, acc in enumerate(accs):
                value = tile_buf[t, i * part : (i + 1) * part, :].astype(F32)
                acc[slot] += jnp.where(place < rows_ref[t] - i * part, value, 0.0)
            return carry

        lax.fori_loop(c * each, (c + 1) * each, add, 0, unroll=True)
    for b in range(bpd):
        for j in range(sources):
            block = jnp.concatenate([acc[b * sources + j] for acc in accs], 0).astype(BF16)
            adj_ref[b * blk : (b + 1) * blk, j * blk : (j + 1) * blk] = block
            adj_t_ref[j * blk : (j + 1) * blk, b * blk : (b + 1) * blk] = block.T
    spread_parts(
        chips, far, adj_t_ref[...], u, features_ref[...], whole, keep_ref, give_ref
    )


def core_sum_kernel(
    chips, hosts, keep_ref, came_ref, picked_ref, mine_ref, msg_ref, *rest
):
    to_refs, total = rest[:-1], rest[-1]
    rows = mine_ref.shape[0]
    far = picked_ref.shape[0]
    send = far // hosts
    each = rows + far
    chip = lax.axis_index("chip")
    total[...] = keep_ref[...].astype(F32) + came_ref[: chips * each, :].astype(F32)
    mine_ref[...] = total[pl.ds(pl.multiple_of(chip * each, 8), rows), :]
    for k, ref in enumerate(to_refs):
        other = lax.rem(chip + k + 1, chips)
        ref[...] = total[pl.ds(pl.multiple_of(other * each, 8), rows), :].astype(BF16)
    picked = picked_ref[...].astype(F32)
    for g in range(hosts):
        for x in range(chips):
            low = x * each + rows + g * send
            both = jnp.concatenate(
                [picked[g * send : (g + 1) * send], total[low : low + send, :]], 0
            )
            msg_ref[g * chips + x] = both.astype(BF16)


def halo_part(recv_ref, hosts, chips, part):
    send = recv_ref.shape[1] // 2
    low = part * send
    blocks = [
        recv_ref[g * chips + x].astype(F32)[low : low + send]
        for x in range(chips)
        for g in range(hosts)
    ]
    return jnp.concatenate(blocks, 0).astype(BF16)


def merge_kernel(chips, hosts, recv_ref, mine_ref, *refs):
    terms, came, (out_ref, sum_ref) = refs[: chips - 1], refs[chips - 1 : -2], refs[-2:]
    rows = came[0].shape[0]
    total = mine_ref[...]
    for ref in terms:
        total = total + ref[...].astype(F32)
    sum_ref[...] = total
    for k, ref in enumerate(came):
        out_ref[k * rows : (k + 1) * rows, :] = ref[...]
    out_ref[len(came) * rows :, :] = halo_part(recv_ref, hosts, chips, 0)


def early_kernel(
    chips, adj_ref, value_ref, came_ref, self_ref, bias_ref, up_ref, weight_ref,
    agg_ref, direct_ref, grad_ref,
):
    value = value_ref[...]
    rows = value.shape[0]
    chip, core = lax.axis_index("chip"), lax.axis_index("core")
    there = came_ref[came_ref.shape[0] - rows :, :]
    total = 0.0
    for side, block in ((core, value), (1 - core, there)):
        low = pl.multiple_of((chip * CORES + side) * rows, rows)
        total = total + dot(adj_ref[:, pl.ds(low, rows)], block)
    agg_ref[...] = total
    direct_ref[...] = dot(value, self_ref[...]) + bias_ref[...].reshape(1, -1)
    grad_ref[...] = dot_nt(up_ref[...], weight_ref[...])


def mid_kernel(chips, hosts, adj_ref, agg_ref, part_ref, sum_ref, pick_ref, recv_ref, *refs):
    came, (agg_out, grad_ref) = refs[:-2], refs[-2:]
    rows = part_ref.shape[0]
    chip, core = lax.axis_index("chip"), lax.axis_index("core")
    agg, grad = agg_ref[...], part_ref[...] + sum_ref[...]
    for k, ref in enumerate(came):
        x = lax.rem(chip - k - 1 + chips, chips)
        low = pl.multiple_of((x * CORES + core) * rows, rows)
        agg = agg + dot(adj_ref[:, pl.ds(low, rows)], ref[...])
    back = halo_part(recv_ref, hosts, chips, 1)
    grad_ref[...] = grad + dot_tn(jnp.concatenate([pick_ref[...]] * chips, 0), back)
    agg_out[...] = agg


def full_aggregate(chips, adj_ref, agg_ref, here_ref, shared_ref, halo):
    rows = agg_ref.shape[0]
    far = halo.shape[0] // (chips * CORES)
    chip, core = lax.axis_index("chip"), lax.axis_index("core")
    at = (chips - 1) * rows
    for x in range(chips):
        for side, ref in ((core, here_ref), (1 - core, shared_ref)):
            low = pl.multiple_of((x * CORES + side) * far, far)
            halo[pl.ds(low, far), :] = ref[at + x * far : at + (x + 1) * far, :]
    agg = agg_ref[...]
    for k in range(chips - 1):
        x = lax.rem(chip - k - 1 + chips, chips)
        low = pl.multiple_of((x * CORES + 1 - core) * rows, rows)
        agg = agg + dot(adj_ref[:, pl.ds(low, rows)], shared_ref[k * rows : (k + 1) * rows, :])
    return agg + dot(adj_ref[:, chips * CORES * rows :], halo[...])


def middle_kernel(
    chips,
    adj_ref,
    adj_t_ref,
    agg_ref,
    direct_ref,
    grad_ref,
    pick_ref,
    here_ref,
    shared_ref,
    neigh_one_ref,
    hidden_ref,
    grad_pre_ref,
    keep_ref,
    give_ref,
    picked_ref,
    halo,
    whole,
):
    agg = full_aggregate(chips, adj_ref, agg_ref, here_ref, shared_ref, halo).astype(BF16)
    pre = direct_ref[...] + dot(agg, neigh_one_ref[...])
    sigmoid = jax.nn.sigmoid(pre)
    hidden = (pre * sigmoid).astype(BF16)
    hidden_ref[...] = hidden
    picked_ref[...] = dot(pick_ref[...], hidden).astype(BF16)
    grad_pre = (grad_ref[...] * sigmoid * (1.0 + pre * (1.0 - sigmoid))).astype(BF16)
    grad_pre_ref[...] = grad_pre
    u = dot_nt(grad_pre, neigh_one_ref[...]).astype(BF16)
    spread_parts(
        chips, pick_ref.shape[0], adj_t_ref[...], u, hidden, whole, keep_ref, give_ref
    )


def last_kernel(
    chips, adj_ref, agg_ref, direct_ref, here_ref, shared_ref, neigh_two_ref, output_ref, halo
):
    agg = full_aggregate(chips, adj_ref, agg_ref, here_ref, shared_ref, halo).astype(BF16)
    output_ref[...] = (direct_ref[...] + dot(agg, neigh_two_ref[...])).astype(BF16)


def call(kernel, name, out_shape, in_specs, args, scratch=(), limit=32, flops=0):
    return pl.pallas_call(
        kernel,
        out_shape=out_shape,
        in_specs=in_specs,
        out_specs=jax.tree.map(lambda _: VMEM, out_shape),
        scratch_shapes=scratch,
        compiler_params=pltpu.CompilerParams(vmem_limit_bytes=limit * MIB),
        cost_estimate=pl.CostEstimate(
            flops=flops, bytes_accessed=flops // 1024, transcendentals=0
        ),
        name=name,
    )(*args)


def shift(value, axis, k):
    size = lax.axis_size(axis)
    return lax.ppermute(value, axis, [(i, (i + k) % size) for i in range(size)])


def shape(rows, width, kind=BF16):
    return jax.ShapeDtypeStruct((rows, width), kind)


def body(
    features,
    send_list,
    tile_dst,
    tile_src,
    tile_rows,
    tile_val,
    self_one,
    neigh_one,
    bias_one,
    self_two,
    neigh_two,
    bias_two,
    cotangent,
):
    chips = lax.axis_size("chip")
    hosts = lax.axis_size("hst")
    rows, width = features.shape
    tiles, blk = tile_val.shape[:2]
    send = send_list.shape[3]
    far = hosts * send
    all_rows = chips * CORES * (rows + far)
    keep_shape = shape(chips * (rows + far), width)
    give_shape = shape(chips * (rows + far) + rows, width)
    picked_shape = shape(far, width)
    rows_shape = shape(rows, width)
    space = pltpu.VMEM((all_rows, width), BF16)

    square = 2 * rows * width * width
    halo = pltpu.VMEM((chips * CORES * far, width), BF16)
    sum_shape = shape(rows, width, F32)

    def exchange(adj, pick, keep, give, picked, value, self_weight, bias, up, weight):
        came = shift(give, "core", 1)
        moved = [shift(value, "chip", k) for k in range(1, chips)]
        mine, msg, *to = call(
            functools.partial(core_sum_kernel, chips, hosts),
            "core_sum",
            (sum_shape, jax.ShapeDtypeStruct((hosts * chips, 2 * send, width), BF16))
            + (rows_shape,) * (chips - 1),
            [VMEM] * 3,
            (keep, came, picked),
            [pltpu.VMEM(keep_shape.shape, F32)],
        )
        terms = [shift(block, "chip", k + 1) for k, block in enumerate(to)]
        recv = lax.all_to_all(msg, ("hst", "chip"), split_axis=0, concat_axis=0, tiled=True)
        agg, direct, grad = call(
            functools.partial(early_kernel, chips),
            "early",
            (sum_shape,) * 3,
            [VMEM] * 7,
            (adj, value, came, self_weight, bias, up, weight),
            flops=4 * square,
        )
        here, total = call(
            functools.partial(merge_kernel, chips, hosts),
            "merge",
            (shape((chips - 1) * rows + chips * far, width), sum_shape),
            [VMEM] * (2 * chips),
            (recv, mine, *terms, *moved),
        )
        shared = shift(here, "core", 1)
        agg, grad = call(
            functools.partial(mid_kernel, chips, hosts),
            "mid",
            (sum_shape,) * 2,
            [VMEM] * (5 + chips),
            (adj, agg, grad, total, pick, recv, *moved),
            flops=2 * square,
        )
        return agg, direct, grad, here, shared

    adj, adj_t, keep, give, picked, pick = call(
        functools.partial(prep_kernel, chips),
        "prep",
        (shape(rows, all_rows), shape(all_rows, rows), keep_shape, give_shape)
        + (picked_shape, shape(far, rows)),
        [HBM] * 8,
        [
            pltpu.with_memory_space_constraint(value, pltpu.HBM)
            for value in (
                tile_dst,
                tile_src,
                tile_rows,
                send_list,
                tile_val,
                features,
                cotangent,
                neigh_two,
            )
        ],
        [
            pltpu.SMEM(tile_dst.shape, jnp.int32),
            pltpu.SMEM(tile_src.shape, jnp.int32),
            pltpu.SMEM(tile_rows.shape, jnp.int32),
            pltpu.SMEM(send_list.shape, jnp.int32),
            pltpu.VMEM(tile_val.shape, BF16),
            pltpu.VMEM(features.shape, BF16),
            pltpu.VMEM(cotangent.shape, BF16),
            pltpu.VMEM(neigh_two.shape, BF16),
            space,
            pltpu.SemaphoreType.DMA((7 + CHUNKS,)),
        ]
        + [pltpu.VMEM(((rows // blk) * (all_rows // blk), blk // PARTS, blk), F32)] * PARTS,
    )
    agg, direct, grad, here, shared = exchange(
        adj, pick, keep, give, picked, features, self_one, bias_one, cotangent, self_two
    )
    hidden, grad_pre, keep, give, picked = call(
        functools.partial(middle_kernel, chips),
        "middle",
        (rows_shape, rows_shape, keep_shape, give_shape, picked_shape),
        [VMEM] * 9,
        (adj, adj_t, agg, direct, grad, pick, here, shared, neigh_one),
        [halo, space],
        flops=9 * square,
    )
    agg, direct, grad, here, shared = exchange(
        adj, pick, keep, give, picked, hidden, self_two, bias_two, grad_pre, self_one
    )
    output = call(
        functools.partial(last_kernel, chips),
        "last",
        rows_shape,
        [VMEM] * 6,
        (adj, agg, direct, here, shared, neigh_two),
        [halo],
        flops=3 * square,
    )
    return output, grad


def solution(mesh):
    hosts, devs = mesh.devices.shape
    mesh = Mesh(mesh.devices.reshape(hosts, devs // CORES, CORES), ("hst", "chip", "core"))
    dev = ("chip", "core")
    every = ("hst", "chip", "core")
    return jax.shard_map(
        body,
        mesh=mesh,
        in_specs=(
            P(every, None),
            P("hst", dev, None, None),
            P(every),
            P(every),
            P(every),
            P(every, None, None),
            P(),
            P(),
            P(),
            P(),
            P(),
            P(),
            P(every, None),
        ),
        out_specs=(P(every, None), P(every, None)),
        check_vma=False,
    )
```

```python
import functools

import jax
import jax.numpy as jnp
from jax import lax
from jax.experimental import pallas as pl
from jax.experimental.pallas import tpu as pltpu
from jax.sharding import Mesh, PartitionSpec as P

F32 = jnp.float32
BF16 = jnp.bfloat16
MIB = 1024 * 1024
CHUNKS = 8
PARTS = 4
CORES = 2

VMEM = pl.BlockSpec(memory_space=pltpu.VMEM)
HBM = pl.BlockSpec(memory_space=pltpu.HBM)


def dot(a, b):
    return jnp.dot(a, b, preferred_element_type=F32)


def dot_nt(a, b):
    return lax.dot_general(a, b, (((1,), (1,)), ((), ())), preferred_element_type=F32)


def dot_tn(a, b):
    return lax.dot_general(a, b, (((0,), (0,)), ((), ())), preferred_element_type=F32)


def pick_matrix(send_ref, rows):
    hosts, send = send_ref.shape[2], send_ref.shape[3]
    place = lax.broadcasted_iota(jnp.int32, (send, rows), 0)
    column = lax.broadcasted_iota(jnp.int32, (send, rows), 1)
    parts = []
    for g in range(hosts):
        index = jnp.zeros((send, rows), jnp.int32)
        for s in range(send):
            index = jnp.where(place == s, send_ref[0, 0, g, s], index)
        parts.append(jnp.where(index == column, 1.0, 0.0).astype(F32))
    return jnp.concatenate(parts, 0).astype(BF16)


def column(chips, far, rows, side, whole_ref, out_ref):
    each = rows + far
    for x in range(chips):
        d = x * CORES + side
        low = pl.multiple_of(d * rows, rows)
        out_ref[x * each : x * each + rows, :] = whole_ref[pl.ds(low, rows), :]
        low = pl.multiple_of(chips * CORES * rows + d * far, far)
        out_ref[x * each + rows : (x + 1) * each, :] = whole_ref[pl.ds(low, far), :]


def prep_kernel(
    chips,
    dst_hbm,
    src_hbm,
    rows_hbm,
    send_hbm,
    tile_hbm,
    features_hbm,
    cot_hbm,
    neigh_two_hbm,
    adj_t_ref,
    give_ref,
    up_ref,
    picked_ref,
    pick_ref,
    dst_ref,
    src_ref,
    rows_ref,
    send_ref,
    tile_buf,
    features_ref,
    cot_ref,
    neigh_two_ref,
    col,
    sems,
    *accs,
):
    tiles, blk = tile_buf.shape[0], tile_buf.shape[1]
    each = tiles // CHUNKS
    pairs = [
        (cot_hbm, cot_ref),
        (neigh_two_hbm, neigh_two_ref),
        (features_hbm, features_ref),
        (send_hbm, send_ref),
        (dst_hbm, dst_ref),
        (src_hbm, src_ref),
        (rows_hbm, rows_ref),
    ]
    pairs += [
        (tile_hbm.at[pl.ds(c * each, each)], tile_buf.at[pl.ds(c * each, each)])
        for c in range(CHUNKS)
    ]
    copies = [pltpu.make_async_copy(a, b, sems.at[i]) for i, (a, b) in enumerate(pairs)]
    for copy in copies:
        copy.start()
    rows = features_ref.shape[0]
    bpd = rows // blk
    sources = accs[0].shape[0] // bpd
    part = accs[0].shape[1]
    far = send_ref.shape[2] * send_ref.shape[3]
    for acc in accs:
        acc[...] = jnp.zeros_like(acc)
    copies[0].wait()
    copies[1].wait()
    u = dot_nt(cot_ref[...], neigh_two_ref[...]).astype(BF16)
    up_ref[...] = u
    copies[2].wait()
    copies[3].wait()
    pick_ref[...] = pick_matrix(send_ref, rows)
    picked_ref[...] = dot(pick_ref[...], features_ref[...]).astype(BF16)
    give_ref[chips * (rows + far) :, :] = features_ref[...]
    for copy in copies[4:7]:
        copy.wait()
    place = lax.broadcasted_iota(jnp.int32, (part, blk), 0)
    for c in range(CHUNKS):
        copies[7 + c].wait()

        def add(t, carry):
            slot = dst_ref[t] * sources + src_ref[t]
            for i, acc in enumerate(accs):
                value = tile_buf[t, i * part : (i + 1) * part, :].astype(F32)
                acc[slot] += jnp.where(place < rows_ref[t] - i * part, value, 0.0)
            return carry

        lax.fori_loop(c * each, (c + 1) * each, add, 0, unroll=True)
    for b in range(bpd):
        for j in range(sources):
            block = jnp.concatenate([acc[b * sources + j] for acc in accs], 0).astype(BF16)
            adj_t_ref[j * blk : (j + 1) * blk, b * blk : (b + 1) * blk] = block.T
    column(chips, far, rows, 1 - lax.axis_index("core"), adj_t_ref, col)
    give_ref[: chips * (rows + far), :] = dot(col[...], u).astype(BF16)


def rest_kernel(chips, adj_t_ref, up_ref, cot_ref, pick_ref, adj_ref, col_ref, keep_ref, lend_ref):
    far, rows = pick_ref.shape
    core = lax.axis_index("core")
    count = chips * (rows + far)
    column(chips, far, rows, core, adj_t_ref, col_ref)
    column(chips, far, rows, 1 - core, adj_t_ref, lend_ref)
    lend_ref[count : count + rows, :] = cot_ref[...]
    lend_ref[count + rows :, :] = pick_ref[...]
    keep_ref[...] = dot(col_ref[...], up_ref[...]).astype(BF16)
    for j in range(adj_t_ref.shape[0] // rows):
        adj_ref[:, j * rows : (j + 1) * rows] = adj_t_ref[j * rows : (j + 1) * rows, :].T


def deal(chips, hosts, total, picked, value, mine_ref, msg_ref, to_refs):
    rows = value.shape[0]
    far = picked.shape[0]
    send = far // hosts
    each = rows + far
    chip = lax.axis_index("chip")
    mine_ref[...] = total[pl.ds(pl.multiple_of(chip * each, 8), rows), :]
    for k, ref in enumerate(to_refs):
        other = lax.rem(chip + k + 1, chips)
        ref[:rows, :] = total[pl.ds(pl.multiple_of(other * each, 8), rows), :].astype(BF16)
        ref[rows:, :] = value
    for g in range(hosts):
        for x in range(chips):
            low = x * each + rows + g * send
            both = jnp.concatenate(
                [picked[g * send : (g + 1) * send], total[low : low + send, :]], 0
            )
            msg_ref[g * chips + x] = both.astype(BF16)


def core_sum_kernel(
    chips, hosts, keep_ref, came_ref, value_ref, picked_ref, mine_ref, msg_ref, *rest
):
    total = rest[-1]
    total[...] = keep_ref[...].astype(F32) + came_ref[: total.shape[0], :].astype(F32)
    picked = picked_ref[...].astype(F32)
    deal(chips, hosts, total, picked, value_ref[...], mine_ref, msg_ref, rest[:-1])


def halo_part(recv_ref, hosts, chips, part):
    send = recv_ref.shape[1] // 2
    low = part * send
    blocks = [
        recv_ref[g * chips + x].astype(F32)[low : low + send]
        for x in range(chips)
        for g in range(hosts)
    ]
    return jnp.concatenate(blocks, 0).astype(BF16)


def merge_kernel(chips, hosts, with_terms, recv_ref, mine_ref, *refs):
    came, (out_ref, sum_ref) = refs[: chips - 1], refs[chips - 1 :]
    rows = mine_ref.shape[0]
    total = mine_ref[...]
    for k, ref in enumerate(came):
        total = total + ref[:rows, :].astype(F32)
        out_ref[k * rows : (k + 1) * rows, :] = ref[rows:, :]
    sum_ref[...] = total
    low = len(came) * rows
    halo = halo_part(recv_ref, hosts, chips, 0)
    high = low + halo.shape[0]
    out_ref[low:high, :] = halo
    if with_terms:
        out_ref[high : high + rows, :] = total.astype(BF16)
        out_ref[high + rows :, :] = halo_part(recv_ref, hosts, chips, 1)


def own_chip(adj_refs, blocks):
    chip, core = lax.axis_index("chip"), lax.axis_index("core")
    rows = blocks[0].shape[0]
    parts = []
    for adj_ref in adj_refs:
        total = 0.0
        for side, block in ((core, blocks[0]), (1 - core, blocks[1])):
            low = pl.multiple_of((chip * CORES + side) * rows, rows)
            total = total + dot(adj_ref[:, pl.ds(low, rows)], block)
        parts.append(total)
    return jnp.concatenate(parts, 0)


def early_one_kernel(
    chips, adj_ref, adj_two_ref, value_ref, came_ref, self_ref, bias_ref, up_ref, lent_ref, weight_ref,
    agg_ref, direct_ref, grad_ref,
):
    value = value_ref[...]
    rows = value.shape[0]
    there = came_ref[came_ref.shape[0] - rows :, :]
    agg_ref[...] = own_chip((adj_ref, adj_two_ref), (value, there))
    both = jnp.concatenate([value, there], 0)
    direct_ref[...] = dot(both, self_ref[...]) + bias_ref[...].reshape(1, -1)
    count = came_ref.shape[0] - rows
    both = jnp.concatenate([up_ref[...], lent_ref[count : count + rows, :]], 0)
    grad_ref[...] = dot_nt(both, weight_ref[...])


def early_two_kernel(
    chips, adj_ref, value_ref, there_ref, self_ref, bias_ref, up_ref, weight_ref,
    agg_ref, direct_ref, grad_ref,
):
    value = value_ref[...]
    agg_ref[...] = own_chip((adj_ref,), (value, there_ref[...]))
    direct_ref[...] = dot(value, self_ref[...]) + bias_ref[...].reshape(1, -1)
    grad_ref[...] = dot_nt(up_ref[...], weight_ref[...])


def mid_kernel(chips, hosts, count, *refs):
    adj_refs, refs = refs[:count], refs[count:]
    agg_ref, part_ref, sum_ref, pick_ref, recv_ref = refs[:5]
    came, (agg_out, grad_ref) = refs[5:-2], refs[-2:]
    rows = sum_ref.shape[0]
    chip, core = lax.axis_index("chip"), lax.axis_index("core")
    for i, adj_ref in enumerate(adj_refs):
        agg = agg_ref[i * rows : (i + 1) * rows, :]
        for k, ref in enumerate(came):
            x = lax.rem(chip - k - 1 + chips, chips)
            low = pl.multiple_of((x * CORES + core) * rows, rows)
            agg = agg + dot(adj_ref[:, pl.ds(low, rows)], ref[rows:, :])
        agg_out[i * rows : (i + 1) * rows, :] = agg
    back = halo_part(recv_ref, hosts, chips, 1)
    grad = part_ref[:rows, :] + sum_ref[...]
    grad_ref[:rows, :] = grad + dot_tn(jnp.concatenate([pick_ref[...]] * chips, 0), back)
    if count > 1:
        grad_ref[rows:, :] = part_ref[rows:, :]


def full_aggregate(chips, far, adj_refs, agg_ref, here_ref, shared_ref, halo):
    rows = adj_refs[0].shape[0]
    chip, core = lax.axis_index("chip"), lax.axis_index("core")
    at = (chips - 1) * rows
    for x in range(chips):
        for side, ref in ((core, here_ref), (1 - core, shared_ref)):
            low = pl.multiple_of((x * CORES + side) * far, far)
            halo[pl.ds(low, far), :] = ref[at + x * far : at + (x + 1) * far, :]
    parts = []
    for i, adj_ref in enumerate(adj_refs):
        agg = agg_ref[i * rows : (i + 1) * rows, :]
        for k in range(chips - 1):
            x = lax.rem(chip - k - 1 + chips, chips)
            low = pl.multiple_of((x * CORES + 1 - core) * rows, rows)
            agg = agg + dot(adj_ref[:, pl.ds(low, rows)], shared_ref[k * rows : (k + 1) * rows, :])
        parts.append(agg + dot(adj_ref[:, chips * CORES * rows :], halo[...]))
    return jnp.concatenate(parts, 0).astype(BF16)


def middle_kernel(
    chips,
    hosts,
    adj_ref,
    adj_two_ref,
    col_ref,
    lent_ref,
    agg_ref,
    direct_ref,
    grad_ref,
    pick_ref,
    here_ref,
    shared_ref,
    neigh_one_ref,
    hidden_ref,
    there_ref,
    grad_pre_ref,
    mine_ref,
    msg_ref,
    *rest,
):
    to_refs, halo, total = rest[:-2], rest[-2], rest[-1]
    far, rows = pick_ref.shape
    count = total.shape[0]
    agg = full_aggregate(
        chips, far, (adj_ref, adj_two_ref), agg_ref, here_ref, shared_ref, halo
    )
    pre = direct_ref[...] + dot(agg, neigh_one_ref[...])
    sigmoid = jax.nn.sigmoid(pre)
    hidden = (pre * sigmoid).astype(BF16)
    hidden_ref[...] = hidden[:rows]
    there_ref[...] = hidden[rows:]
    low = (chips - 1) * rows + chips * far
    pick_two = lent_ref[count + rows :, :]
    add = shared_ref[low : low + rows, :].astype(F32)
    add = add + dot_tn(jnp.concatenate([pick_two] * chips, 0), shared_ref[low + rows :, :])
    grad = jnp.concatenate([grad_ref[:rows, :], grad_ref[rows:, :] + add], 0)
    grad_pre = (grad * sigmoid * (1.0 + pre * (1.0 - sigmoid))).astype(BF16)
    grad_pre_ref[...] = grad_pre[:rows]
    u = dot_nt(grad_pre, neigh_one_ref[...]).astype(BF16)
    total[...] = dot(col_ref[...], u[:rows]) + dot(lent_ref[:count, :], u[rows:])
    picked = dot(pick_ref[...], hidden[:rows])
    deal(chips, hosts, total, picked, hidden[:rows], mine_ref, msg_ref, to_refs)


def last_kernel(
    chips, far, adj_ref, agg_ref, direct_ref, here_ref, shared_ref, neigh_two_ref, output_ref, halo
):
    agg = full_aggregate(chips, far, (adj_ref,), agg_ref, here_ref, shared_ref, halo)
    output_ref[...] = (direct_ref[...] + dot(agg, neigh_two_ref[...])).astype(BF16)


def call(kernel, name, out_shape, in_specs, args, scratch=(), limit=32, flops=0):
    return pl.pallas_call(
        kernel,
        out_shape=out_shape,
        in_specs=in_specs,
        out_specs=jax.tree.map(lambda _: VMEM, out_shape),
        scratch_shapes=scratch,
        compiler_params=pltpu.CompilerParams(vmem_limit_bytes=limit * MIB),
        cost_estimate=pl.CostEstimate(
            flops=flops, bytes_accessed=flops // 1024, transcendentals=0
        ),
        name=name,
    )(*args)


def shift(value, axis, k):
    size = lax.axis_size(axis)
    return lax.ppermute(value, axis, [(i, (i + k) % size) for i in range(size)])


def shape(rows, width, kind=BF16):
    return jax.ShapeDtypeStruct((rows, width), kind)


def body(
    features,
    send_list,
    tile_dst,
    tile_src,
    tile_rows,
    tile_val,
    self_one,
    neigh_one,
    bias_one,
    self_two,
    neigh_two,
    bias_two,
    cotangent,
):
    chips = lax.axis_size("chip")
    hosts = lax.axis_size("hst")
    rows, width = features.shape
    tiles, blk = tile_val.shape[:2]
    send = send_list.shape[3]
    far = hosts * send
    all_rows = chips * CORES * (rows + far)
    count = chips * (rows + far)
    rows_shape = shape(rows, width)
    sum_shape = shape(rows, width, F32)
    both_shape = shape(CORES * rows, width, F32)
    square = 2 * rows * width * width
    halo = pltpu.VMEM((chips * CORES * far, width), BF16)
    total = pltpu.VMEM((count, width), F32)
    halo_rows = (chips - 1) * rows + chips * far
    dealt = (
        sum_shape,
        jax.ShapeDtypeStruct((hosts * chips, 2 * send, width), BF16),
    ) + (shape(2 * rows, width),) * (chips - 1)

    def across(mine, msg, to, with_terms):
        terms = [shift(block, "chip", k + 1) for k, block in enumerate(to)]
        recv = lax.all_to_all(msg, ("hst", "chip"), split_axis=0, concat_axis=0, tiled=True)
        here, summed = call(
            functools.partial(merge_kernel, chips, hosts, with_terms),
            "merge",
            (shape(halo_rows + (rows + chips * far) * with_terms, width), sum_shape),
            [VMEM] * (1 + chips),
            (recv, mine, *terms),
        )
        return terms, recv, here, summed, shift(here, "core", 1)

    adj_t, give, up, picked, pick = call(
        functools.partial(prep_kernel, chips),
        "prep",
        (
            shape(all_rows, rows),
            shape(count + rows, width),
            rows_shape,
            shape(far, width),
            shape(far, rows),
        ),
        [HBM] * 8,
        [
            pltpu.with_memory_space_constraint(value, pltpu.HBM)
            for value in (
                tile_dst,
                tile_src,
                tile_rows,
                send_list,
                tile_val,
                features,
                cotangent,
                neigh_two,
            )
        ],
        [
            pltpu.SMEM(tile_dst.shape, jnp.int32),
            pltpu.SMEM(tile_src.shape, jnp.int32),
            pltpu.SMEM(tile_rows.shape, jnp.int32),
            pltpu.SMEM(send_list.shape, jnp.int32),
            pltpu.VMEM(tile_val.shape, BF16),
            pltpu.VMEM(features.shape, BF16),
            pltpu.VMEM(cotangent.shape, BF16),
            pltpu.VMEM(neigh_two.shape, BF16),
            pltpu.VMEM((count, rows), BF16),
            pltpu.SemaphoreType.DMA((7 + CHUNKS,)),
        ]
        + [pltpu.VMEM(((rows // blk) * (all_rows // blk), blk // PARTS, blk), F32)] * PARTS,
    )
    came = shift(give, "core", 1)
    adj, col, keep, lend = call(
        functools.partial(rest_kernel, chips),
        "rest",
        (
            shape(rows, all_rows),
            shape(count, rows),
            shape(count, width),
            shape(count + rows + far, width),
        ),
        [VMEM] * 4,
        (adj_t, up, cotangent, pick),
        flops=3 * square,
    )
    adj_two = shift(adj, "core", 1)
    lent = shift(lend, "core", 1)
    mine, msg, *to = call(
        functools.partial(core_sum_kernel, chips, hosts),
        "core_sum",
        dealt,
        [VMEM] * 4,
        (keep, came, features, picked),
        [total],
    )
    terms, recv, here, summed, shared = across(mine, msg, to, 1)
    agg, direct, grad = call(
        functools.partial(early_one_kernel, chips),
        "early_one",
        (both_shape,) * 3,
        [VMEM] * 9,
        (adj, adj_two, features, came, self_one, bias_one, cotangent, lent, self_two),
        flops=8 * square,
    )
    agg, grad = call(
        functools.partial(mid_kernel, chips, hosts, 2),
        "mid_one",
        (both_shape,) * 2,
        [VMEM] * (6 + chips),
        (adj, adj_two, agg, grad, summed, pick, recv, *terms),
        flops=3 * square,
    )
    hidden, there, grad_pre, mine, msg, *to = call(
        functools.partial(middle_kernel, chips, hosts),
        "middle",
        (rows_shape,) * 3 + dealt,
        [VMEM] * 11,
        (adj, adj_two, col, lent, agg, direct, grad, pick, here, shared, neigh_one),
        [halo, total],
        flops=12 * square,
    )
    terms, recv, here, summed, shared = across(mine, msg, to, 0)
    agg, direct, grad = call(
        functools.partial(early_two_kernel, chips),
        "early_two",
        (sum_shape,) * 3,
        [VMEM] * 7,
        (adj, hidden, there, self_two, bias_two, grad_pre, self_one),
        flops=4 * square,
    )
    agg, grad = call(
        functools.partial(mid_kernel, chips, hosts, 1),
        "mid_two",
        (sum_shape,) * 2,
        [VMEM] * (5 + chips),
        (adj, agg, grad, summed, pick, recv, *terms),
        flops=2 * square,
    )
    output = call(
        functools.partial(last_kernel, chips, far),
        "last",
        rows_shape,
        [VMEM] * 6,
        (adj, agg, direct, here, shared, neigh_two),
        [halo],
        flops=3 * square,
    )
    return output, grad


def solution(mesh):
    hosts, devs = mesh.devices.shape
    mesh = Mesh(mesh.devices.reshape(hosts, devs // CORES, CORES), ("hst", "chip", "core"))
    dev = ("chip", "core")
    every = ("hst", "chip", "core")
    return jax.shard_map(
        body,
        mesh=mesh,
        in_specs=(
            P(every, None),
            P("hst", dev, None, None),
            P(every),
            P(every),
            P(every),
            P(every, None, None),
            P(),
            P(),
            P(),
            P(),
            P(),
            P(),
            P(every, None),
        ),
        out_specs=(P(every, None), P(every, None)),
        check_vma=False,
    )
```

```python
import functools

import jax
import jax.numpy as jnp
from jax import lax
from jax.experimental import pallas as pl
from jax.experimental.pallas import tpu as pltpu
from jax.sharding import Mesh, PartitionSpec as P

F32 = jnp.float32
BF16 = jnp.bfloat16
MIB = 1024 * 1024
CHUNKS = 8
PARTS = 4
CORES = 2

VMEM = pl.BlockSpec(memory_space=pltpu.VMEM)
HBM = pl.BlockSpec(memory_space=pltpu.HBM)


def dot(a, b):
    return jnp.dot(a, b, preferred_element_type=F32)


def dot_nt(a, b):
    return lax.dot_general(a, b, (((1,), (1,)), ((), ())), preferred_element_type=F32)


def dot_tn(a, b):
    return lax.dot_general(a, b, (((0,), (0,)), ((), ())), preferred_element_type=F32)


def pick_matrix(send_ref, rows):
    hosts, send = send_ref.shape[2], send_ref.shape[3]
    place = lax.broadcasted_iota(jnp.int32, (send, rows), 0)
    column = lax.broadcasted_iota(jnp.int32, (send, rows), 1)
    parts = []
    for g in range(hosts):
        index = jnp.zeros((send, rows), jnp.int32)
        for s in range(send):
            index = jnp.where(place == s, send_ref[0, 0, g, s], index)
        parts.append(jnp.where(index == column, 1.0, 0.0).astype(F32))
    return jnp.concatenate(parts, 0).astype(BF16)


def column(chips, far, rows, side, whole_ref, out_ref, base):
    each = rows + far
    for x in range(chips):
        d = x * CORES + side
        low = pl.multiple_of(d * rows, rows)
        at = base + x * each
        out_ref[at : at + rows, :] = whole_ref[pl.ds(low, rows), :]
        low = pl.multiple_of(chips * CORES * rows + d * far, far)
        out_ref[at + rows : at + each, :] = whole_ref[pl.ds(low, far), :]


def prep_kernel(
    chips,
    dst_hbm,
    src_hbm,
    rows_hbm,
    send_hbm,
    tile_hbm,
    features_hbm,
    cot_hbm,
    neigh_two_hbm,
    adj_t_ref,
    give_ref,
    up_ref,
    picked_ref,
    pick_ref,
    dst_ref,
    src_ref,
    rows_ref,
    send_ref,
    tile_buf,
    features_ref,
    cot_ref,
    neigh_two_ref,
    col,
    sems,
    *accs,
):
    tiles, blk = tile_buf.shape[0], tile_buf.shape[1]
    each = tiles // CHUNKS
    pairs = [
        (cot_hbm, cot_ref),
        (neigh_two_hbm, neigh_two_ref),
        (features_hbm, features_ref),
        (send_hbm, send_ref),
        (dst_hbm, dst_ref),
        (src_hbm, src_ref),
        (rows_hbm, rows_ref),
    ]
    pairs += [
        (tile_hbm.at[pl.ds(c * each, each)], tile_buf.at[pl.ds(c * each, each)])
        for c in range(CHUNKS)
    ]
    copies = [pltpu.make_async_copy(a, b, sems.at[i]) for i, (a, b) in enumerate(pairs)]
    for copy in copies:
        copy.start()
    rows = features_ref.shape[0]
    bpd = rows // blk
    sources = accs[0].shape[0] // bpd
    part = accs[0].shape[1]
    far = send_ref.shape[2] * send_ref.shape[3]
    for acc in accs:
        acc[...] = jnp.zeros_like(acc)
    copies[0].wait()
    copies[1].wait()
    u = dot_nt(cot_ref[...], neigh_two_ref[...]).astype(BF16)
    up_ref[...] = u
    copies[2].wait()
    copies[3].wait()
    pick_ref[...] = pick_matrix(send_ref, rows)
    picked_ref[...] = dot(pick_ref[...], features_ref[...]).astype(BF16)
    give_ref[chips * (rows + far) :, :] = features_ref[...]
    for copy in copies[4:7]:
        copy.wait()
    place = lax.broadcasted_iota(jnp.int32, (part, blk), 0)
    for c in range(CHUNKS):
        copies[7 + c].wait()

        def add(t, carry):
            slot = dst_ref[t] * sources + src_ref[t]
            for i, acc in enumerate(accs):
                value = tile_buf[t, i * part : (i + 1) * part, :].astype(F32)
                acc[slot] += jnp.where(place < rows_ref[t] - i * part, value, 0.0)
            return carry

        lax.fori_loop(c * each, (c + 1) * each, add, 0, unroll=True)
    for b in range(bpd):
        for j in range(sources):
            block = jnp.concatenate([acc[b * sources + j] for acc in accs], 0).astype(BF16)
            adj_t_ref[j * blk : (j + 1) * blk, b * blk : (b + 1) * blk] = block.T
    column(chips, far, rows, 1 - lax.axis_index("core"), adj_t_ref, col, 0)
    give_ref[: chips * (rows + far), :] = dot(col[...], u).astype(BF16)


def rest_kernel(chips, adj_t_ref, up_ref, cot_ref, pick_ref, adj_ref, col_ref, keep_ref, lend_ref):
    far, rows = pick_ref.shape
    core = lax.axis_index("core")
    all_rows = adj_t_ref.shape[0]
    count = chips * (rows + far)
    for j in range(all_rows // rows):
        block = adj_t_ref[j * rows : (j + 1) * rows, :].T
        adj_ref[j * rows : (j + 1) * rows, :] = block
        lend_ref[j * rows : (j + 1) * rows, :] = block
    column(chips, far, rows, core, adj_t_ref, col_ref, 0)
    column(chips, far, rows, 1 - core, adj_t_ref, lend_ref, all_rows)
    low = all_rows + count
    lend_ref[low : low + rows, :] = cot_ref[...]
    lend_ref[low + rows :, :] = pick_ref[...]
    keep_ref[...] = dot(col_ref[...], up_ref[...]).astype(BF16)


def deal(chips, hosts, total, picked, value, mine_ref, msg_ref, to_refs):
    rows = value.shape[0]
    far = picked.shape[0]
    send = far // hosts
    each = rows + far
    chip = lax.axis_index("chip")
    mine_ref[...] = total[pl.ds(pl.multiple_of(chip * each, 8), rows), :]
    for k, ref in enumerate(to_refs):
        other = lax.rem(chip + k + 1, chips)
        ref[:rows, :] = total[pl.ds(pl.multiple_of(other * each, 8), rows), :].astype(BF16)
        ref[rows:, :] = value
    for g in range(hosts):
        for x in range(chips):
            low = x * each + rows + g * send
            both = jnp.concatenate(
                [picked[g * send : (g + 1) * send], total[low : low + send, :]], 0
            )
            msg_ref[g * chips + x] = both.astype(BF16)


def core_sum_kernel(
    chips, hosts, keep_ref, came_ref, value_ref, picked_ref, mine_ref, msg_ref, *rest
):
    total = rest[-1]
    total[...] = keep_ref[...].astype(F32) + came_ref[: total.shape[0], :].astype(F32)
    picked = picked_ref[...].astype(F32)
    deal(chips, hosts, total, picked, value_ref[...], mine_ref, msg_ref, rest[:-1])


def halo_part(recv_ref, hosts, chips, part):
    send = recv_ref.shape[1] // 2
    low = part * send
    blocks = [
        recv_ref[g * chips + x].astype(F32)[low : low + send]
        for x in range(chips)
        for g in range(hosts)
    ]
    return jnp.concatenate(blocks, 0).astype(BF16)


def merge_kernel(chips, hosts, with_terms, recv_ref, mine_ref, *refs):
    came, (out_ref, sum_ref) = refs[: chips - 1], refs[chips - 1 :]
    rows = mine_ref.shape[0]
    total = mine_ref[...]
    for k, ref in enumerate(came):
        total = total + ref[:rows, :].astype(F32)
        out_ref[k * rows : (k + 1) * rows, :] = ref[rows:, :]
    sum_ref[...] = total
    low = len(came) * rows
    halo = halo_part(recv_ref, hosts, chips, 0)
    high = low + halo.shape[0]
    out_ref[low:high, :] = halo
    if with_terms:
        out_ref[high : high + rows, :] = total.astype(BF16)
        out_ref[high + rows :, :] = halo_part(recv_ref, hosts, chips, 1)


def own_chip(adj_refs, blocks):
    chip, core = lax.axis_index("chip"), lax.axis_index("core")
    rows = blocks[0].shape[0]
    parts = []
    for adj_ref in adj_refs:
        total = 0.0
        for side, block in ((core, blocks[0]), (1 - core, blocks[1])):
            low = pl.multiple_of((chip * CORES + side) * rows, rows)
            total = total + dot(adj_ref[pl.ds(low, rows), :], block)
        parts.append(total)
    return jnp.concatenate(parts, 0)


def early_one_kernel(
    chips, adj_ref, lent_ref, value_ref, came_ref, self_ref, bias_ref, up_ref, weight_ref,
    agg_ref, direct_ref, grad_ref,
):
    value = value_ref[...]
    rows = value.shape[0]
    there = came_ref[came_ref.shape[0] - rows :, :]
    agg_ref[...] = own_chip((adj_ref, lent_ref), (value, there))
    both = jnp.concatenate([value, there], 0)
    direct_ref[...] = dot(both, self_ref[...]) + bias_ref[...].reshape(1, -1)
    count = came_ref.shape[0] - rows
    high = lent_ref.shape[0] - (count // chips - rows)
    both = jnp.concatenate([up_ref[...], lent_ref[high - rows : high, :]], 0)
    grad_ref[...] = dot_nt(both, weight_ref[...])


def early_two_kernel(
    chips, adj_ref, value_ref, there_ref, self_ref, bias_ref, up_ref, weight_ref,
    agg_ref, direct_ref, grad_ref,
):
    value = value_ref[...]
    agg_ref[...] = own_chip((adj_ref,), (value, there_ref[...]))
    direct_ref[...] = dot(value, self_ref[...]) + bias_ref[...].reshape(1, -1)
    grad_ref[...] = dot_nt(up_ref[...], weight_ref[...])


def mid_kernel(chips, hosts, count, *refs):
    adj_refs, refs = refs[:count], refs[count:]
    agg_ref, part_ref, sum_ref, pick_ref, recv_ref = refs[:5]
    came, (agg_out, grad_ref) = refs[5:-2], refs[-2:]
    rows = sum_ref.shape[0]
    chip, core = lax.axis_index("chip"), lax.axis_index("core")
    for i, adj_ref in enumerate(adj_refs):
        agg = agg_ref[i * rows : (i + 1) * rows, :]
        for k, ref in enumerate(came):
            x = lax.rem(chip - k - 1 + chips, chips)
            low = pl.multiple_of((x * CORES + core) * rows, rows)
            agg = agg + dot(adj_ref[pl.ds(low, rows), :], ref[rows:, :])
        agg_out[i * rows : (i + 1) * rows, :] = agg
    back = halo_part(recv_ref, hosts, chips, 1)
    grad = part_ref[:rows, :] + sum_ref[...]
    grad_ref[:rows, :] = grad + dot_tn(jnp.concatenate([pick_ref[...]] * chips, 0), back)
    if count > 1:
        grad_ref[rows:, :] = part_ref[rows:, :]


def full_aggregate(chips, far, rows, adj_refs, agg_ref, here_ref, shared_ref, halo):
    chip, core = lax.axis_index("chip"), lax.axis_index("core")
    at = (chips - 1) * rows
    for x in range(chips):
        for side, ref in ((core, here_ref), (1 - core, shared_ref)):
            low = pl.multiple_of((x * CORES + side) * far, far)
            halo[pl.ds(low, far), :] = ref[at + x * far : at + (x + 1) * far, :]
    parts = []
    for i, adj_ref in enumerate(adj_refs):
        agg = agg_ref[i * rows : (i + 1) * rows, :]
        for k in range(chips - 1):
            x = lax.rem(chip - k - 1 + chips, chips)
            low = pl.multiple_of((x * CORES + 1 - core) * rows, rows)
            agg = agg + dot(adj_ref[pl.ds(low, rows), :], shared_ref[k * rows : (k + 1) * rows, :])
        for j in range(halo.shape[0] // rows):
            low = chips * CORES * rows + j * rows
            agg = agg + dot(adj_ref[low : low + rows, :], halo[j * rows : (j + 1) * rows, :])
        parts.append(agg)
    return jnp.concatenate(parts, 0).astype(BF16)


def middle_kernel(
    chips,
    hosts,
    adj_ref,
    lent_ref,
    col_ref,
    agg_ref,
    direct_ref,
    grad_ref,
    pick_ref,
    here_ref,
    shared_ref,
    neigh_one_ref,
    hidden_ref,
    there_ref,
    grad_pre_ref,
    mine_ref,
    msg_ref,
    *rest,
):
    to_refs, halo, total = rest[:-2], rest[-2], rest[-1]
    far, rows = pick_ref.shape
    count = total.shape[0]
    agg = full_aggregate(
        chips, far, rows, (adj_ref, lent_ref), agg_ref, here_ref, shared_ref, halo
    )
    pre = direct_ref[...] + dot(agg, neigh_one_ref[...])
    sigmoid = jax.nn.sigmoid(pre)
    hidden = (pre * sigmoid).astype(BF16)
    hidden_ref[...] = hidden[:rows]
    there_ref[...] = hidden[rows:]
    low = (chips - 1) * rows + chips * far
    base = lent_ref.shape[0] - far - rows - count
    pick_two = lent_ref[base + count + rows :, :]
    add = shared_ref[low : low + rows, :].astype(F32)
    add = add + dot_tn(jnp.concatenate([pick_two] * chips, 0), shared_ref[low + rows :, :])
    grad = jnp.concatenate([grad_ref[:rows, :], grad_ref[rows:, :] + add], 0)
    grad_pre = (grad * sigmoid * (1.0 + pre * (1.0 - sigmoid))).astype(BF16)
    grad_pre_ref[...] = grad_pre[:rows]
    u = dot_nt(grad_pre, neigh_one_ref[...]).astype(BF16)
    total[...] = dot(col_ref[...], u[:rows]) + dot(
        lent_ref[base : base + count, :], u[rows:]
    )
    picked = dot(pick_ref[...], hidden[:rows])
    deal(chips, hosts, total, picked, hidden[:rows], mine_ref, msg_ref, to_refs)


def last_kernel(
    chips, far, adj_ref, agg_ref, direct_ref, here_ref, shared_ref, neigh_two_ref, output_ref, halo
):
    rows = agg_ref.shape[0]
    agg = full_aggregate(chips, far, rows, (adj_ref,), agg_ref, here_ref, shared_ref, halo)
    output_ref[...] = (direct_ref[...] + dot(agg, neigh_two_ref[...])).astype(BF16)


def call(kernel, name, out_shape, in_specs, args, scratch=(), limit=32, flops=0):
    return pl.pallas_call(
        kernel,
        out_shape=out_shape,
        in_specs=in_specs,
        out_specs=jax.tree.map(lambda _: VMEM, out_shape),
        scratch_shapes=scratch,
        compiler_params=pltpu.CompilerParams(vmem_limit_bytes=limit * MIB),
        cost_estimate=pl.CostEstimate(
            flops=flops, bytes_accessed=flops // 1024, transcendentals=0
        ),
        name=name,
    )(*args)


def shift(value, axis, k):
    size = lax.axis_size(axis)
    return lax.ppermute(value, axis, [(i, (i + k) % size) for i in range(size)])


def shape(rows, width, kind=BF16):
    return jax.ShapeDtypeStruct((rows, width), kind)


def body(
    features,
    send_list,
    tile_dst,
    tile_src,
    tile_rows,
    tile_val,
    self_one,
    neigh_one,
    bias_one,
    self_two,
    neigh_two,
    bias_two,
    cotangent,
):
    chips = lax.axis_size("chip")
    hosts = lax.axis_size("hst")
    rows, width = features.shape
    tiles, blk = tile_val.shape[:2]
    send = send_list.shape[3]
    far = hosts * send
    all_rows = chips * CORES * (rows + far)
    count = chips * (rows + far)
    rows_shape = shape(rows, width)
    sum_shape = shape(rows, width, F32)
    both_shape = shape(CORES * rows, width, F32)
    square = 2 * rows * width * width
    halo = pltpu.VMEM((chips * CORES * far, width), BF16)
    total = pltpu.VMEM((count, width), F32)
    halo_rows = (chips - 1) * rows + chips * far
    dealt = (
        sum_shape,
        jax.ShapeDtypeStruct((hosts * chips, 2 * send, width), BF16),
    ) + (shape(2 * rows, width),) * (chips - 1)

    def across(mine, msg, to, with_terms):
        terms = [shift(block, "chip", k + 1) for k, block in enumerate(to)]
        recv = lax.all_to_all(msg, ("hst", "chip"), split_axis=0, concat_axis=0, tiled=True)
        here, summed = call(
            functools.partial(merge_kernel, chips, hosts, with_terms),
            "merge",
            (shape(halo_rows + (rows + chips * far) * with_terms, width), sum_shape),
            [VMEM] * (1 + chips),
            (recv, mine, *terms),
        )
        return terms, recv, here, summed, shift(here, "core", 1)

    adj_t, give, up, picked, pick = call(
        functools.partial(prep_kernel, chips),
        "prep",
        (
            shape(all_rows, rows),
            shape(count + rows, width),
            rows_shape,
            shape(far, width),
            shape(far, rows),
        ),
        [HBM] * 8,
        [
            pltpu.with_memory_space_constraint(value, pltpu.HBM)
            for value in (
                tile_dst,
                tile_src,
                tile_rows,
                send_list,
                tile_val,
                features,
                cotangent,
                neigh_two,
            )
        ],
        [
            pltpu.SMEM(tile_dst.shape, jnp.int32),
            pltpu.SMEM(tile_src.shape, jnp.int32),
            pltpu.SMEM(tile_rows.shape, jnp.int32),
            pltpu.SMEM(send_list.shape, jnp.int32),
            pltpu.VMEM(tile_val.shape, BF16),
            pltpu.VMEM(features.shape, BF16),
            pltpu.VMEM(cotangent.shape, BF16),
            pltpu.VMEM(neigh_two.shape, BF16),
            pltpu.VMEM((count, rows), BF16),
            pltpu.SemaphoreType.DMA((7 + CHUNKS,)),
        ]
        + [pltpu.VMEM(((rows // blk) * (all_rows // blk), blk // PARTS, blk), F32)] * PARTS,
    )
    came = shift(give, "core", 1)
    adj, col, keep, lend = call(
        functools.partial(rest_kernel, chips),
        "rest",
        (
            shape(all_rows, rows),
            shape(count, rows),
            shape(count, width),
            shape(all_rows + count + rows + far, width),
        ),
        [VMEM] * 4,
        (adj_t, up, cotangent, pick),
        flops=3 * square,
    )
    came, lend = lax.optimization_barrier((came, lend))
    lent = shift(lend, "core", 1)
    mine, msg, *to = call(
        functools.partial(core_sum_kernel, chips, hosts),
        "core_sum",
        dealt,
        [VMEM] * 4,
        (keep, came, features, picked),
        [total],
    )
    terms, recv, here, summed, shared = across(mine, msg, to, 1)
    agg, direct, grad = call(
        functools.partial(early_one_kernel, chips),
        "early_one",
        (both_shape,) * 3,
        [VMEM] * 8,
        (adj, lent, features, came, self_one, bias_one, cotangent, self_two),
        flops=8 * square,
    )
    agg, grad = call(
        functools.partial(mid_kernel, chips, hosts, 2),
        "mid_one",
        (both_shape,) * 2,
        [VMEM] * (6 + chips),
        (adj, lent, agg, grad, summed, pick, recv, *terms),
        flops=3 * square,
    )
    hidden, there, grad_pre, mine, msg, *to = call(
        functools.partial(middle_kernel, chips, hosts),
        "middle",
        (rows_shape,) * 3 + dealt,
        [VMEM] * 10,
        (adj, lent, col, agg, direct, grad, pick, here, shared, neigh_one),
        [halo, total],
        flops=12 * square,
    )
    terms, recv, here, summed, shared = across(mine, msg, to, 0)
    agg, direct, grad = call(
        functools.partial(early_two_kernel, chips),
        "early_two",
        (sum_shape,) * 3,
        [VMEM] * 7,
        (adj, hidden, there, self_two, bias_two, grad_pre, self_one),
        flops=4 * square,
    )
    agg, grad = call(
        functools.partial(mid_kernel, chips, hosts, 1),
        "mid_two",
        (sum_shape,) * 2,
        [VMEM] * (5 + chips),
        (adj, agg, grad, summed, pick, recv, *terms),
        flops=2 * square,
    )
    output = call(
        functools.partial(last_kernel, chips, far),
        "last",
        rows_shape,
        [VMEM] * 6,
        (adj, agg, direct, here, shared, neigh_two),
        [halo],
        flops=3 * square,
    )
    return output, grad


def solution(mesh):
    hosts, devs = mesh.devices.shape
    mesh = Mesh(mesh.devices.reshape(hosts, devs // CORES, CORES), ("hst", "chip", "core"))
    dev = ("chip", "core")
    every = ("hst", "chip", "core")
    return jax.shard_map(
        body,
        mesh=mesh,
        in_specs=(
            P(every, None),
            P("hst", dev, None, None),
            P(every),
            P(every),
            P(every),
            P(every, None, None),
            P(),
            P(),
            P(),
            P(),
            P(),
            P(),
            P(every, None),
        ),
        out_specs=(P(every, None), P(every, None)),
        check_vma=False,
    )
```

```python
import functools

import jax
import jax.numpy as jnp
from jax import lax
from jax.experimental import pallas as pl
from jax.experimental.pallas import tpu as pltpu
from jax.sharding import Mesh, PartitionSpec as P

F32 = jnp.float32
BF16 = jnp.bfloat16
MIB = 1024 * 1024
CHUNKS = 8
PARTS = 4
CORES = 2

VMEM = pl.BlockSpec(memory_space=pltpu.VMEM)
HBM = pl.BlockSpec(memory_space=pltpu.HBM)


def dot(a, b):
    return jnp.dot(a, b, preferred_element_type=F32)


def dot_nt(a, b):
    return lax.dot_general(a, b, (((1,), (1,)), ((), ())), preferred_element_type=F32)


def dot_tn(a, b):
    return lax.dot_general(a, b, (((0,), (0,)), ((), ())), preferred_element_type=F32)


def pick_matrix(send_ref, rows):
    hosts, send = send_ref.shape[2], send_ref.shape[3]
    place = lax.broadcasted_iota(jnp.int32, (send, rows), 0)
    column = lax.broadcasted_iota(jnp.int32, (send, rows), 1)
    parts = []
    for g in range(hosts):
        index = jnp.zeros((send, rows), jnp.int32)
        for s in range(send):
            index = jnp.where(place == s, send_ref[0, 0, g, s], index)
        parts.append(jnp.where(index == column, 1.0, 0.0).astype(F32))
    return jnp.concatenate(parts, 0).astype(BF16)


def column(chips, far, rows, side, adj_ref, far_t, out_ref):
    each = rows + far
    own_rows = chips * CORES * rows
    for j in range(far_t.shape[0] // rows):
        low = own_rows + j * rows
        far_t[j * rows : (j + 1) * rows, :] = adj_ref[low : low + rows, :].T
    for x in range(chips):
        d = x * CORES + side
        at = x * each
        out_ref[at : at + rows, :] = adj_ref[pl.ds(pl.multiple_of(d * rows, rows), rows), :].T
        out_ref[at + rows : at + each, :] = far_t[pl.ds(pl.multiple_of(d * far, far), far), :]


def prep_kernel(
    chips,
    dst_hbm,
    src_hbm,
    rows_hbm,
    send_hbm,
    tile_hbm,
    features_hbm,
    cot_hbm,
    neigh_two_hbm,
    adj_ref,
    give_ref,
    up_ref,
    picked_ref,
    pick_ref,
    dst_ref,
    src_ref,
    rows_ref,
    send_ref,
    tile_buf,
    features_ref,
    cot_ref,
    neigh_two_ref,
    far_t,
    col,
    sems,
    *accs,
):
    tiles, blk = tile_buf.shape[0], tile_buf.shape[1]
    each = tiles // CHUNKS
    pairs = [
        (cot_hbm, cot_ref),
        (neigh_two_hbm, neigh_two_ref),
        (features_hbm, features_ref),
        (send_hbm, send_ref),
        (dst_hbm, dst_ref),
        (src_hbm, src_ref),
        (rows_hbm, rows_ref),
    ]
    pairs += [
        (tile_hbm.at[pl.ds(c * each, each)], tile_buf.at[pl.ds(c * each, each)])
        for c in range(CHUNKS)
    ]
    copies = [pltpu.make_async_copy(a, b, sems.at[i]) for i, (a, b) in enumerate(pairs)]
    for copy in copies:
        copy.start()
    rows = features_ref.shape[0]
    bpd = rows // blk
    sources = accs[0].shape[0] // bpd
    part = accs[0].shape[1]
    far = send_ref.shape[2] * send_ref.shape[3]
    for acc in accs:
        acc[...] = jnp.zeros_like(acc)
    copies[0].wait()
    copies[1].wait()
    u = dot_nt(cot_ref[...], neigh_two_ref[...]).astype(BF16)
    up_ref[...] = u
    copies[2].wait()
    copies[3].wait()
    pick_ref[...] = pick_matrix(send_ref, rows)
    picked_ref[...] = dot(pick_ref[...], features_ref[...]).astype(BF16)
    for copy in copies[4:7]:
        copy.wait()
    place = lax.broadcasted_iota(jnp.int32, (part, blk), 0)
    for c in range(CHUNKS):
        copies[7 + c].wait()

        def add(t, carry):
            slot = dst_ref[t] * sources + src_ref[t]
            for i, acc in enumerate(accs):
                value = tile_buf[t, i * part : (i + 1) * part, :].astype(F32)
                acc[slot] += jnp.where(place < rows_ref[t] - i * part, value, 0.0)
            return carry

        lax.fori_loop(c * each, (c + 1) * each, add, 0, unroll=True)
    for b in range(bpd):
        for j in range(sources):
            block = jnp.concatenate([acc[b * sources + j] for acc in accs], 0).astype(BF16)
            low = j // bpd * rows + b * blk
            left = j % bpd * blk
            adj_ref[low : low + blk, left : left + blk] = block
    column(chips, far, rows, 1 - lax.axis_index("core"), adj_ref, far_t, col)
    give_ref[...] = dot(col[...], u).astype(BF16)


def rest_kernel(
    chips, adj_ref, up_ref, cot_ref, value_ref, col_ref, keep_ref, lend_ref, far_t
):
    rows = up_ref.shape[0]
    far = col_ref.shape[0] // chips - rows
    column(chips, far, rows, lax.axis_index("core"), adj_ref, far_t, col_ref)
    keep_ref[...] = dot(col_ref[...], up_ref[...]).astype(BF16)
    low = adj_ref.shape[0]
    lend_ref[:low, :] = adj_ref[...]
    lend_ref[low : low + rows, :] = cot_ref[...]
    lend_ref[low + rows :, :] = value_ref[...]


def deal(chips, hosts, total, picked, value, mine_ref, msg_ref, to_refs):
    rows = value.shape[0]
    far = picked.shape[0]
    send = far // hosts
    each = rows + far
    chip = lax.axis_index("chip")
    mine_ref[...] = total[pl.ds(pl.multiple_of(chip * each, 8), rows), :]
    for k, ref in enumerate(to_refs):
        other = lax.rem(chip + k + 1, chips)
        ref[:rows, :] = total[pl.ds(pl.multiple_of(other * each, 8), rows), :].astype(BF16)
        ref[rows:, :] = value
    for g in range(hosts):
        for x in range(chips):
            low = x * each + rows + g * send
            both = jnp.concatenate(
                [picked[g * send : (g + 1) * send], total[low : low + send, :]], 0
            )
            msg_ref[g * chips + x] = both.astype(BF16)


def core_sum_kernel(
    chips, hosts, keep_ref, came_ref, value_ref, picked_ref, mine_ref, msg_ref, *rest
):
    total = rest[-1]
    total[...] = keep_ref[...].astype(F32) + came_ref[...].astype(F32)
    picked = picked_ref[...].astype(F32)
    deal(chips, hosts, total, picked, value_ref[...], mine_ref, msg_ref, rest[:-1])


def halo_part(recv_ref, hosts, chips, part):
    send = recv_ref.shape[1] // 2
    low = part * send
    blocks = [
        recv_ref[g * chips + x].astype(F32)[low : low + send]
        for x in range(chips)
        for g in range(hosts)
    ]
    return jnp.concatenate(blocks, 0).astype(BF16)


def merge_kernel(chips, hosts, with_terms, recv_ref, mine_ref, pick_ref, *refs):
    came, (out_ref, sum_ref) = refs[: chips - 1], refs[chips - 1 :]
    rows = mine_ref.shape[0]
    total = mine_ref[...]
    for k, ref in enumerate(came):
        total = total + ref[:rows, :].astype(F32)
        out_ref[k * rows : (k + 1) * rows, :] = ref[rows:, :]
    if with_terms:
        total = total + returned(pick_ref, recv_ref, hosts, chips)
    sum_ref[...] = total
    low = len(came) * rows
    halo = halo_part(recv_ref, hosts, chips, 0)
    high = low + halo.shape[0]
    out_ref[low:high, :] = halo
    if with_terms:
        out_ref[high:, :] = total.astype(BF16)


def returned(pick_ref, recv_ref, hosts, chips):
    back = halo_part(recv_ref, hosts, chips, 1)
    return dot_tn(jnp.concatenate([pick_ref[...]] * chips, 0), back)


def own_chip(adj_refs, blocks):
    chip, core = lax.axis_index("chip"), lax.axis_index("core")
    rows = blocks[0].shape[0]
    parts = []
    for adj_ref in adj_refs:
        total = 0.0
        for side, block in ((core, blocks[0]), (1 - core, blocks[1])):
            low = pl.multiple_of((chip * CORES + side) * rows, rows)
            total = total + dot(adj_ref[pl.ds(low, rows), :], block)
        parts.append(total)
    return jnp.concatenate(parts, 0)


def early_one_kernel(
    chips, adj_ref, lent_ref, value_ref, self_ref, bias_ref, up_ref, weight_ref,
    agg_ref, direct_ref, grad_ref, col_ref, far_t,
):
    value = value_ref[...]
    rows = value.shape[0]
    low = adj_ref.shape[0]
    there = lent_ref[low + rows :, :]
    agg_ref[...] = own_chip((adj_ref, lent_ref), (value, there))
    both = jnp.concatenate([value, there], 0)
    direct_ref[...] = dot(both, self_ref[...]) + bias_ref[...].reshape(1, -1)
    both = jnp.concatenate([up_ref[...], lent_ref[low : low + rows, :]], 0)
    grad_ref[...] = dot_nt(both, weight_ref[...])
    far = col_ref.shape[0] // chips - rows
    column(chips, far, rows, lax.axis_index("core"), lent_ref, far_t, col_ref)


def early_two_kernel(
    chips, adj_ref, value_ref, there_ref, self_ref, bias_ref, up_ref, weight_ref,
    agg_ref, direct_ref, grad_ref,
):
    value = value_ref[...]
    agg_ref[...] = own_chip((adj_ref,), (value, there_ref[...]))
    direct_ref[...] = dot(value, self_ref[...]) + bias_ref[...].reshape(1, -1)
    grad_ref[...] = dot_nt(up_ref[...], weight_ref[...])


def mid_kernel(chips, hosts, count, *refs):
    adj_refs, refs = refs[:count], refs[count:]
    agg_ref, part_ref, sum_ref, pick_ref, recv_ref = refs[:5]
    came, (agg_out, grad_ref) = refs[5:-2], refs[-2:]
    rows = sum_ref.shape[0]
    chip, core = lax.axis_index("chip"), lax.axis_index("core")
    for i, adj_ref in enumerate(adj_refs):
        agg = agg_ref[i * rows : (i + 1) * rows, :]
        for k, ref in enumerate(came):
            x = lax.rem(chip - k - 1 + chips, chips)
            low = pl.multiple_of((x * CORES + core) * rows, rows)
            agg = agg + dot(adj_ref[pl.ds(low, rows), :], ref[rows:, :])
        agg_out[i * rows : (i + 1) * rows, :] = agg
    if count > 1:
        grad_ref[:rows, :] = part_ref[:rows, :] + sum_ref[...]
        grad_ref[rows:, :] = part_ref[rows:, :]
    else:
        grad = part_ref[...] + sum_ref[...]
        grad_ref[...] = grad + returned(pick_ref, recv_ref, hosts, chips)


def full_aggregate(chips, far, rows, adj_refs, agg_ref, here_ref, shared_ref, halo):
    chip, core = lax.axis_index("chip"), lax.axis_index("core")
    at = (chips - 1) * rows
    for x in range(chips):
        for side, ref in ((core, here_ref), (1 - core, shared_ref)):
            low = pl.multiple_of((x * CORES + side) * far, far)
            halo[pl.ds(low, far), :] = ref[at + x * far : at + (x + 1) * far, :]
    parts = []
    for i, adj_ref in enumerate(adj_refs):
        agg = agg_ref[i * rows : (i + 1) * rows, :]
        for k in range(chips - 1):
            x = lax.rem(chip - k - 1 + chips, chips)
            low = pl.multiple_of((x * CORES + 1 - core) * rows, rows)
            agg = agg + dot(adj_ref[pl.ds(low, rows), :], shared_ref[k * rows : (k + 1) * rows, :])
        for j in range(halo.shape[0] // rows):
            low = chips * CORES * rows + j * rows
            agg = agg + dot(adj_ref[low : low + rows, :], halo[j * rows : (j + 1) * rows, :])
        parts.append(agg)
    return jnp.concatenate(parts, 0).astype(BF16)


def middle_kernel(
    chips,
    hosts,
    adj_ref,
    lent_ref,
    col_ref,
    col_two_ref,
    agg_ref,
    direct_ref,
    grad_ref,
    pick_ref,
    here_ref,
    shared_ref,
    neigh_one_ref,
    hidden_ref,
    there_ref,
    grad_pre_ref,
    mine_ref,
    msg_ref,
    *rest,
):
    to_refs, halo, total = rest[:-2], rest[-2], rest[-1]
    far, rows = pick_ref.shape
    agg = full_aggregate(
        chips, far, rows, (adj_ref, lent_ref), agg_ref, here_ref, shared_ref, halo
    )
    pre = direct_ref[...] + dot(agg, neigh_one_ref[...])
    sigmoid = jax.nn.sigmoid(pre)
    hidden = (pre * sigmoid).astype(BF16)
    hidden_ref[...] = hidden[:rows]
    there_ref[...] = hidden[rows:]
    low = (chips - 1) * rows + chips * far
    add = shared_ref[low:, :].astype(F32)
    grad = jnp.concatenate([grad_ref[:rows, :], grad_ref[rows:, :] + add], 0)
    grad_pre = (grad * sigmoid * (1.0 + pre * (1.0 - sigmoid))).astype(BF16)
    grad_pre_ref[...] = grad_pre[:rows]
    u = dot_nt(grad_pre, neigh_one_ref[...]).astype(BF16)
    total[...] = dot(col_ref[...], u[:rows]) + dot(col_two_ref[...], u[rows:])
    picked = dot(pick_ref[...], hidden[:rows])
    deal(chips, hosts, total, picked, hidden[:rows], mine_ref, msg_ref, to_refs)


def last_kernel(
    chips, far, adj_ref, agg_ref, direct_ref, here_ref, shared_ref, neigh_two_ref, output_ref, halo
):
    rows = agg_ref.shape[0]
    agg = full_aggregate(chips, far, rows, (adj_ref,), agg_ref, here_ref, shared_ref, halo)
    output_ref[...] = (direct_ref[...] + dot(agg, neigh_two_ref[...])).astype(BF16)


def call(kernel, name, out_shape, in_specs, args, scratch=(), limit=32, flops=0):
    return pl.pallas_call(
        kernel,
        out_shape=out_shape,
        in_specs=in_specs,
        out_specs=jax.tree.map(lambda _: VMEM, out_shape),
        scratch_shapes=scratch,
        compiler_params=pltpu.CompilerParams(vmem_limit_bytes=limit * MIB),
        cost_estimate=pl.CostEstimate(
            flops=flops, bytes_accessed=flops // 1024, transcendentals=0
        ),
        name=name,
    )(*args)


def shift(value, axis, k):
    size = lax.axis_size(axis)
    return lax.ppermute(value, axis, [(i, (i + k) % size) for i in range(size)])


def shape(rows, width, kind=BF16):
    return jax.ShapeDtypeStruct((rows, width), kind)


def body(
    features,
    send_list,
    tile_dst,
    tile_src,
    tile_rows,
    tile_val,
    self_one,
    neigh_one,
    bias_one,
    self_two,
    neigh_two,
    bias_two,
    cotangent,
):
    chips = lax.axis_size("chip")
    hosts = lax.axis_size("hst")
    rows, width = features.shape
    tiles, blk = tile_val.shape[:2]
    send = send_list.shape[3]
    far = hosts * send
    all_rows = chips * CORES * (rows + far)
    count = chips * (rows + far)
    rows_shape = shape(rows, width)
    sum_shape = shape(rows, width, F32)
    both_shape = shape(CORES * rows, width, F32)
    square = 2 * rows * width * width
    halo = pltpu.VMEM((chips * CORES * far, width), BF16)
    total = pltpu.VMEM((count, width), F32)
    halo_rows = (chips - 1) * rows + chips * far
    dealt = (
        sum_shape,
        jax.ShapeDtypeStruct((hosts * chips, 2 * send, width), BF16),
    ) + (shape(2 * rows, width),) * (chips - 1)

    def across(mine, msg, to, with_terms):
        terms = [shift(block, "chip", k + 1) for k, block in enumerate(to)]
        recv = lax.all_to_all(msg, ("hst", "chip"), split_axis=0, concat_axis=0, tiled=True)
        here, summed = call(
            functools.partial(merge_kernel, chips, hosts, with_terms),
            "merge",
            (shape(halo_rows + rows * with_terms, width), sum_shape),
            [VMEM] * (2 + chips),
            (recv, mine, pick, *terms),
        )
        return terms, recv, here, summed, shift(here, "core", 1)

    far_t = pltpu.VMEM((chips * CORES * far, rows), BF16)
    adj, give, up, picked, pick = call(
        functools.partial(prep_kernel, chips),
        "prep",
        (
            shape(all_rows, rows),
            shape(count, width),
            rows_shape,
            shape(far, width),
            shape(far, rows),
        ),
        [HBM] * 8,
        [
            pltpu.with_memory_space_constraint(value, pltpu.HBM)
            for value in (
                tile_dst,
                tile_src,
                tile_rows,
                send_list,
                tile_val,
                features,
                cotangent,
                neigh_two,
            )
        ],
        [
            pltpu.SMEM(tile_dst.shape, jnp.int32),
            pltpu.SMEM(tile_src.shape, jnp.int32),
            pltpu.SMEM(tile_rows.shape, jnp.int32),
            pltpu.SMEM(send_list.shape, jnp.int32),
            pltpu.VMEM(tile_val.shape, BF16),
            pltpu.VMEM(features.shape, BF16),
            pltpu.VMEM(cotangent.shape, BF16),
            pltpu.VMEM(neigh_two.shape, BF16),
            far_t,
            pltpu.VMEM((count, rows), BF16),
            pltpu.SemaphoreType.DMA((7 + CHUNKS,)),
        ]
        + [pltpu.VMEM(((rows // blk) * (all_rows // blk), blk // PARTS, blk), F32)] * PARTS,
    )
    came = shift(give, "core", 1)
    col, keep, lend = call(
        functools.partial(rest_kernel, chips),
        "rest",
        (shape(count, rows), shape(count, width), shape(all_rows + 2 * rows, width)),
        [VMEM] * 4,
        (adj, up, cotangent, features),
        [far_t],
        flops=3 * square,
    )
    lent = shift(lend, "core", 1)
    mine, msg, *to = call(
        functools.partial(core_sum_kernel, chips, hosts),
        "core_sum",
        dealt,
        [VMEM] * 4,
        (keep, came, features, picked),
        [total],
        flops=60 * square,
    )
    terms, recv, here, summed, shared = across(mine, msg, to, 1)
    agg, direct, grad, col_two = call(
        functools.partial(early_one_kernel, chips),
        "early_one",
        (both_shape,) * 3 + (shape(count, rows),),
        [VMEM] * 7,
        (adj, lent, features, self_one, bias_one, cotangent, self_two),
        [far_t],
        flops=8 * square,
    )
    agg, grad = call(
        functools.partial(mid_kernel, chips, hosts, 2),
        "mid_one",
        (both_shape,) * 2,
        [VMEM] * (6 + chips),
        (adj, lent, agg, grad, summed, pick, recv, *terms),
        flops=3 * square,
    )
    hidden, there, grad_pre, mine, msg, *to = call(
        functools.partial(middle_kernel, chips, hosts),
        "middle",
        (rows_shape,) * 3 + dealt,
        [VMEM] * 11,
        (adj, lent, col, col_two, agg, direct, grad, pick, here, shared, neigh_one),
        [halo, total],
        flops=12 * square,
    )
    terms, recv, here, summed, shared = across(mine, msg, to, 0)
    agg, direct, grad = call(
        functools.partial(early_two_kernel, chips),
        "early_two",
        (sum_shape,) * 3,
        [VMEM] * 7,
        (adj, hidden, there, self_two, bias_two, grad_pre, self_one),
        flops=4 * square,
    )
    agg, grad = call(
        functools.partial(mid_kernel, chips, hosts, 1),
        "mid_two",
        (sum_shape,) * 2,
        [VMEM] * (5 + chips),
        (adj, agg, grad, summed, pick, recv, *terms),
        flops=2 * square,
    )
    output = call(
        functools.partial(last_kernel, chips, far),
        "last",
        rows_shape,
        [VMEM] * 6,
        (adj, agg, direct, here, shared, neigh_two),
        [halo],
        flops=3 * square,
    )
    return output, grad


def solution(mesh):
    hosts, devs = mesh.devices.shape
    mesh = Mesh(mesh.devices.reshape(hosts, devs // CORES, CORES), ("hst", "chip", "core"))
    dev = ("chip", "core")
    every = ("hst", "chip", "core")
    return jax.shard_map(
        body,
        mesh=mesh,
        in_specs=(
            P(every, None),
            P("hst", dev, None, None),
            P(every),
            P(every),
            P(every),
            P(every, None, None),
            P(),
            P(),
            P(),
            P(),
            P(),
            P(),
            P(every, None),
        ),
        out_specs=(P(every, None), P(every, None)),
        check_vma=False,
    )
```

```python
import functools

import jax
import jax.numpy as jnp
from jax import lax
from jax.experimental import pallas as pl
from jax.experimental.pallas import tpu as pltpu
from jax.sharding import Mesh, PartitionSpec as P

F32 = jnp.float32
BF16 = jnp.bfloat16
MIB = 1024 * 1024
CHUNKS = 8
PARTS = 4
HALVES = 2
CORES = 2

VMEM = pl.BlockSpec(memory_space=pltpu.VMEM)
HBM = pl.BlockSpec(memory_space=pltpu.HBM)


def dot(a, b):
    return jnp.dot(a, b, preferred_element_type=F32)


def dot_nt(a, b):
    return lax.dot_general(a, b, (((1,), (1,)), ((), ())), preferred_element_type=F32)


def pick_matrix(send_ref, rows):
    hosts, send = send_ref.shape[2], send_ref.shape[3]
    place = lax.broadcasted_iota(jnp.int32, (send, rows), 0)
    column = lax.broadcasted_iota(jnp.int32, (send, rows), 1)
    parts = []
    for g in range(hosts):
        index = jnp.zeros((send, rows), jnp.int32)
        for s in range(send):
            index = jnp.where(place == s, send_ref[0, 0, g, s], index)
        parts.append(jnp.where(index == column, 1.0, 0.0).astype(F32))
    return jnp.concatenate(parts, 0).astype(BF16)


def column(chips, far, rows, side, adj_ref, far_t, out_ref):
    each = rows + far
    own_rows = chips * CORES * rows
    for j in range(far_t.shape[0] // rows):
        low = own_rows + j * rows
        far_t[j * rows : (j + 1) * rows, :] = adj_ref[low : low + rows, :].T
    for x in range(chips):
        d = x * CORES + side
        at = x * each
        out_ref[at : at + rows, :] = adj_ref[pl.ds(pl.multiple_of(d * rows, rows), rows), :].T
        out_ref[at + rows : at + each, :] = far_t[pl.ds(pl.multiple_of(d * far, far), far), :]


def prep_kernel(
    chips,
    dst_hbm,
    src_hbm,
    rows_hbm,
    send_hbm,
    tile_hbm,
    features_hbm,
    cot_hbm,
    neigh_two_hbm,
    adj_ref,
    give_ref,
    up_ref,
    picked_ref,
    pick_ref,
    dst_ref,
    src_ref,
    rows_ref,
    send_ref,
    tile_buf,
    features_ref,
    cot_ref,
    neigh_two_ref,
    far_t,
    col,
    sems,
    *accs,
):
    tiles, blk = tile_buf.shape[0], tile_buf.shape[1]
    each = tiles // CHUNKS
    first = CHUNKS * 3 // 4
    chunks = [
        (tile_hbm.at[pl.ds(c * each, each)], tile_buf.at[pl.ds(c * each, each)])
        for c in range(CHUNKS)
    ]
    pairs = [(dst_hbm, dst_ref), (src_hbm, src_ref), (rows_hbm, rows_ref)]
    pairs += chunks[:first]
    pairs += [
        (cot_hbm, cot_ref),
        (neigh_two_hbm, neigh_two_ref),
        (features_hbm, features_ref),
        (send_hbm, send_ref),
    ]
    pairs += chunks[first:]
    copies = [pltpu.make_async_copy(a, b, sems.at[i]) for i, (a, b) in enumerate(pairs)]
    for copy in copies:
        copy.start()
    rows = features_ref.shape[0]
    bpd = rows // blk
    sources = accs[0].shape[0] // bpd
    part = accs[0].shape[1]
    far = send_ref.shape[2] * send_ref.shape[3]
    for acc in accs:
        acc[...] = jnp.zeros_like(acc)
    place = lax.broadcasted_iota(jnp.int32, (part, blk), 0)

    def add(t, carry):
        slot = dst_ref[t] * sources + src_ref[t]
        for i, acc in enumerate(accs):
            value = tile_buf[t, i * part : (i + 1) * part, :].astype(F32)
            acc[slot] += jnp.where(place < rows_ref[t] - i * part, value, 0.0)
        return carry

    for copy in copies[:3]:
        copy.wait()
    for c in range(first):
        copies[3 + c].wait()
        lax.fori_loop(c * each, (c + 1) * each, add, 0, unroll=True)
    for copy in copies[3 + first : 7 + first]:
        copy.wait()
    u = dot_nt(cot_ref[...], neigh_two_ref[...]).astype(BF16)
    up_ref[...] = u
    pick_ref[...] = pick_matrix(send_ref, rows)
    picked_ref[...] = dot(pick_ref[...], features_ref[...]).astype(BF16)
    for c in range(first, CHUNKS):
        copies[7 + c].wait()
        lax.fori_loop(c * each, (c + 1) * each, add, 0, unroll=True)
    for b in range(bpd):
        for j in range(sources):
            block = jnp.concatenate([acc[b * sources + j] for acc in accs], 0).astype(BF16)
            low = j // bpd * rows + b * blk
            left = j % bpd * blk
            adj_ref[low : low + blk, left : left + blk] = block
    column(chips, far, rows, 1 - lax.axis_index("core"), adj_ref, far_t, col)
    give_ref[...] = dot(col[...], u).astype(BF16)


def rest_kernel(
    chips, adj_ref, up_ref, cot_ref, value_ref, pick_ref, col_ref, keep_ref, lend_ref, place_ref, far_t
):
    rows = up_ref.shape[0]
    far = col_ref.shape[0] // chips - rows
    column(chips, far, rows, lax.axis_index("core"), adj_ref, far_t, col_ref)
    keep_ref[...] = dot(col_ref[...], up_ref[...]).astype(BF16)
    low = adj_ref.shape[0]
    lend_ref[:low, :] = adj_ref[...]
    lend_ref[low : low + rows, :] = cot_ref[...]
    lend_ref[low + rows :, :] = value_ref[...]
    place_ref[...] = jnp.concatenate([pick_ref[...]] * chips, 0).T


def deal(chips, hosts, total, picked, value, mine_ref, msg_ref, to_refs):
    rows = value.shape[0]
    far = picked.shape[0]
    send = far // hosts
    each = rows + far
    chip = lax.axis_index("chip")
    mine_ref[...] = total[pl.ds(pl.multiple_of(chip * each, 8), rows), :]
    for k, ref in enumerate(to_refs):
        other = lax.rem(chip + k + 1, chips)
        ref[:rows, :] = total[pl.ds(pl.multiple_of(other * each, 8), rows), :].astype(BF16)
        ref[rows:, :] = value
    for g in range(hosts):
        for x in range(chips):
            low = x * each + rows + g * send
            both = jnp.concatenate(
                [picked[g * send : (g + 1) * send], total[low : low + send, :]], 0
            )
            msg_ref[g * chips + x] = both.astype(BF16)


def core_sum_kernel(
    chips, hosts, keep_ref, came_ref, value_ref, picked_ref, mine_ref, msg_ref, *rest
):
    total = rest[-1]
    total[...] = keep_ref[...].astype(F32) + came_ref[...].astype(F32)
    picked = picked_ref[...].astype(F32)
    deal(chips, hosts, total, picked, value_ref[...], mine_ref, msg_ref, rest[:-1])


def halo_part(recv_ref, hosts, chips, part):
    send = recv_ref.shape[1] // 2
    low = part * send
    blocks = [
        recv_ref[g * chips + x].astype(F32)[low : low + send]
        for x in range(chips)
        for g in range(hosts)
    ]
    return jnp.concatenate(blocks, 0).astype(BF16)


def merge_kernel(chips, hosts, with_terms, recv_ref, mine_ref, place_ref, *refs):
    came, (out_ref, sum_ref) = refs[: chips - 1], refs[chips - 1 :]
    rows = mine_ref.shape[0]
    total = mine_ref[...]
    for k, ref in enumerate(came):
        total = total + ref[:rows, :].astype(F32)
        out_ref[k * rows : (k + 1) * rows, :] = ref[rows:, :]
    if with_terms:
        total = total + returned(place_ref, recv_ref, hosts, chips)
    sum_ref[...] = total
    low = len(came) * rows
    halo = halo_part(recv_ref, hosts, chips, 0)
    high = low + halo.shape[0]
    out_ref[low:high, :] = halo
    if with_terms:
        out_ref[high:, :] = total.astype(BF16)


def returned(place_ref, recv_ref, hosts, chips):
    return dot(place_ref[...], halo_part(recv_ref, hosts, chips, 1))


def own_chip(adj_refs, blocks):
    chip, core = lax.axis_index("chip"), lax.axis_index("core")
    rows = blocks[0].shape[0]
    parts = []
    for adj_ref in adj_refs:
        total = 0.0
        for side, block in ((core, blocks[0]), (1 - core, blocks[1])):
            low = pl.multiple_of((chip * CORES + side) * rows, rows)
            total = total + dot(adj_ref[pl.ds(low, rows), :], block)
        parts.append(total)
    return jnp.concatenate(parts, 0)


def early_one_kernel(
    chips, adj_ref, lent_ref, value_ref, self_ref, bias_ref, up_ref, weight_ref,
    agg_ref, direct_ref, grad_ref, col_ref, far_t,
):
    value = value_ref[...]
    rows = value.shape[0]
    low = adj_ref.shape[0]
    there = lent_ref[low + rows :, :]
    agg_ref[...] = own_chip((adj_ref, lent_ref), (value, there))
    both = jnp.concatenate([value, there], 0)
    direct_ref[...] = dot(both, self_ref[...]) + bias_ref[...].reshape(1, -1)
    both = jnp.concatenate([up_ref[...], lent_ref[low : low + rows, :]], 0)
    grad_ref[...] = dot_nt(both, weight_ref[...])
    far = col_ref.shape[0] // chips - rows
    column(chips, far, rows, lax.axis_index("core"), lent_ref, far_t, col_ref)


def early_two_kernel(
    chips, adj_ref, value_ref, there_ref, self_ref, bias_ref, up_ref, weight_ref,
    agg_ref, direct_ref, grad_ref,
):
    value = value_ref[...]
    agg_ref[...] = own_chip((adj_ref,), (value, there_ref[...]))
    direct_ref[...] = dot(value, self_ref[...]) + bias_ref[...].reshape(1, -1)
    grad_ref[...] = dot_nt(up_ref[...], weight_ref[...])


def mid_kernel(chips, hosts, count, *refs):
    adj_refs, refs = refs[:count], refs[count:]
    agg_ref, part_ref, sum_ref, place_ref, recv_ref = refs[:5]
    came, (agg_out, grad_ref) = refs[5:-2], refs[-2:]
    rows = sum_ref.shape[0]
    chip, core = lax.axis_index("chip"), lax.axis_index("core")
    for i, adj_ref in enumerate(adj_refs):
        agg = agg_ref[i * rows : (i + 1) * rows, :]
        for k, ref in enumerate(came):
            x = lax.rem(chip - k - 1 + chips, chips)
            low = pl.multiple_of((x * CORES + core) * rows, rows)
            agg = agg + dot(adj_ref[pl.ds(low, rows), :], ref[rows:, :])
        agg_out[i * rows : (i + 1) * rows, :] = agg
    if count > 1:
        grad_ref[:rows, :] = part_ref[:rows, :] + sum_ref[...]
        grad_ref[rows:, :] = part_ref[rows:, :]
    else:
        grad = part_ref[...] + sum_ref[...]
        grad_ref[...] = grad + returned(place_ref, recv_ref, hosts, chips)


def put_halo(chips, far, rows, here_ref, shared_ref, halo):
    core = lax.axis_index("core")
    at = (chips - 1) * rows
    for x in range(chips):
        for side, ref in ((core, here_ref), (1 - core, shared_ref)):
            low = pl.multiple_of((x * CORES + side) * far, far)
            halo[pl.ds(low, far), :] = ref[at + x * far : at + (x + 1) * far, :]


def add_far(chips, rows, adj_ref, start, size, agg, shared_ref, halo):
    chip, core = lax.axis_index("chip"), lax.axis_index("core")
    for k in range(chips - 1):
        x = lax.rem(chip - k - 1 + chips, chips)
        low = pl.multiple_of((x * CORES + 1 - core) * rows + start, size)
        agg = agg + dot(adj_ref[pl.ds(low, size), :], shared_ref[k * rows : (k + 1) * rows, :])
    for j in range(halo.shape[0] // rows):
        low = chips * CORES * rows + j * rows + start
        agg = agg + dot(adj_ref[low : low + size, :], halo[j * rows : (j + 1) * rows, :])
    return agg


def middle_kernel(
    chips,
    hosts,
    adj_ref,
    lent_ref,
    col_ref,
    col_two_ref,
    agg_ref,
    direct_ref,
    grad_ref,
    pick_ref,
    here_ref,
    shared_ref,
    neigh_one_ref,
    hidden_ref,
    there_ref,
    grad_pre_ref,
    mine_ref,
    msg_ref,
    *rest,
):
    to_refs, halo, total = rest[:-2], rest[-2], rest[-1]
    far, rows = pick_ref.shape
    put_halo(chips, far, rows, here_ref, shared_ref, halo)
    parts = [
        add_far(
            chips, rows, ref, 0, rows, agg_ref[i * rows : (i + 1) * rows, :], shared_ref, halo
        )
        for i, ref in enumerate((adj_ref, lent_ref))
    ]
    agg = jnp.concatenate(parts, 0).astype(BF16)
    pre = direct_ref[...] + dot(agg, neigh_one_ref[...])
    sigmoid = jax.nn.sigmoid(pre)
    hidden = (pre * sigmoid).astype(BF16)
    hidden_ref[...] = hidden[:rows]
    there_ref[...] = hidden[rows:]
    low = (chips - 1) * rows + chips * far
    add = shared_ref[low:, :].astype(F32)
    grad = jnp.concatenate([grad_ref[:rows, :], grad_ref[rows:, :] + add], 0)
    grad_pre = (grad * sigmoid * (1.0 + pre * (1.0 - sigmoid))).astype(BF16)
    grad_pre_ref[...] = grad_pre[:rows]
    u = dot_nt(grad_pre, neigh_one_ref[...]).astype(BF16)
    total[...] = dot(col_ref[...], u[:rows]) + dot(col_two_ref[...], u[rows:])
    picked = dot(pick_ref[...], hidden[:rows])
    deal(chips, hosts, total, picked, hidden[:rows], mine_ref, msg_ref, to_refs)


def last_kernel(
    chips,
    far,
    adj_ref,
    agg_ref,
    direct_ref,
    here_ref,
    shared_ref,
    neigh_two_ref,
    output_hbm,
    halo,
    out,
    sems,
):
    rows = agg_ref.shape[0]
    halves = out.shape[0]
    each = rows // halves
    put_halo(chips, far, rows, here_ref, shared_ref, halo)
    copies = []
    for i in range(halves):
        part = pl.ds(i * each, each)
        agg = add_far(
            chips, rows, adj_ref, i * each, each, agg_ref[part, :], shared_ref, halo
        ).astype(BF16)
        out[i] = (direct_ref[part, :] + dot(agg, neigh_two_ref[...])).astype(BF16)
        copies.append(pltpu.make_async_copy(out.at[i], output_hbm.at[part], sems.at[i]))
        copies[-1].start()
    for copy in copies:
        copy.wait()


def call(kernel, name, out_shape, in_specs, args, scratch=(), limit=32, flops=0, out_space=pltpu.VMEM):
    return pl.pallas_call(
        kernel,
        out_shape=out_shape,
        in_specs=in_specs,
        out_specs=jax.tree.map(lambda _: pl.BlockSpec(memory_space=out_space), out_shape),
        scratch_shapes=scratch,
        compiler_params=pltpu.CompilerParams(vmem_limit_bytes=limit * MIB),
        cost_estimate=pl.CostEstimate(
            flops=flops, bytes_accessed=flops // 1024, transcendentals=0
        ),
        name=name,
    )(*args)


def shift(value, axis, k):
    size = lax.axis_size(axis)
    return lax.ppermute(value, axis, [(i, (i + k) % size) for i in range(size)])


def shape(rows, width, kind=BF16):
    return jax.ShapeDtypeStruct((rows, width), kind)


def body(
    features,
    send_list,
    tile_dst,
    tile_src,
    tile_rows,
    tile_val,
    self_one,
    neigh_one,
    bias_one,
    self_two,
    neigh_two,
    bias_two,
    cotangent,
):
    chips = lax.axis_size("chip")
    hosts = lax.axis_size("hst")
    rows, width = features.shape
    tiles, blk = tile_val.shape[:2]
    send = send_list.shape[3]
    far = hosts * send
    all_rows = chips * CORES * (rows + far)
    count = chips * (rows + far)
    rows_shape = shape(rows, width)
    sum_shape = shape(rows, width, F32)
    both_shape = shape(CORES * rows, width, F32)
    square = 2 * rows * width * width
    halo = pltpu.VMEM((chips * CORES * far, width), BF16)
    total = pltpu.VMEM((count, width), F32)
    halo_rows = (chips - 1) * rows + chips * far
    dealt = (
        sum_shape,
        jax.ShapeDtypeStruct((hosts * chips, 2 * send, width), BF16),
    ) + (shape(2 * rows, width),) * (chips - 1)

    def across(mine, msg, to, with_terms):
        terms = [shift(block, "chip", k + 1) for k, block in enumerate(to)]
        recv = lax.all_to_all(msg, ("hst", "chip"), split_axis=0, concat_axis=0, tiled=True)
        here, summed = call(
            functools.partial(merge_kernel, chips, hosts, with_terms),
            "merge",
            (shape(halo_rows + rows * with_terms, width), sum_shape),
            [VMEM] * (2 + chips),
            (recv, mine, place, *terms),
        )
        return terms, recv, here, summed, shift(here, "core", 1)

    far_t = pltpu.VMEM((chips * CORES * far, rows), BF16)
    adj, give, up, picked, pick = call(
        functools.partial(prep_kernel, chips),
        "prep",
        (
            shape(all_rows, rows),
            shape(count, width),
            rows_shape,
            shape(far, width),
            shape(far, rows),
        ),
        [HBM] * 8,
        [
            pltpu.with_memory_space_constraint(value, pltpu.HBM)
            for value in (
                tile_dst,
                tile_src,
                tile_rows,
                send_list,
                tile_val,
                features,
                cotangent,
                neigh_two,
            )
        ],
        [
            pltpu.SMEM(tile_dst.shape, jnp.int32),
            pltpu.SMEM(tile_src.shape, jnp.int32),
            pltpu.SMEM(tile_rows.shape, jnp.int32),
            pltpu.SMEM(send_list.shape, jnp.int32),
            pltpu.VMEM(tile_val.shape, BF16),
            pltpu.VMEM(features.shape, BF16),
            pltpu.VMEM(cotangent.shape, BF16),
            pltpu.VMEM(neigh_two.shape, BF16),
            far_t,
            pltpu.VMEM((count, rows), BF16),
            pltpu.SemaphoreType.DMA((7 + CHUNKS,)),
        ]
        + [pltpu.VMEM(((rows // blk) * (all_rows // blk), blk // PARTS, blk), F32)] * PARTS,
    )
    came = shift(give, "core", 1)
    col, keep, lend, place = call(
        functools.partial(rest_kernel, chips),
        "rest",
        (
            shape(count, rows),
            shape(count, width),
            shape(all_rows + 2 * rows, width),
            shape(rows, chips * far),
        ),
        [VMEM] * 5,
        (adj, up, cotangent, features, pick),
        [far_t],
        flops=3 * square,
    )
    lent = shift(lend, "core", 1)
    mine, msg, *to = call(
        functools.partial(core_sum_kernel, chips, hosts),
        "core_sum",
        dealt,
        [VMEM] * 4,
        (keep, came, features, picked),
        [total],
        flops=60 * square,
    )
    terms, recv, here, summed, shared = across(mine, msg, to, 1)
    agg, direct, grad, col_two = call(
        functools.partial(early_one_kernel, chips),
        "early_one",
        (both_shape,) * 3 + (shape(count, rows),),
        [VMEM] * 7,
        (adj, lent, features, self_one, bias_one, cotangent, self_two),
        [far_t],
        flops=8 * square,
    )
    agg, grad = call(
        functools.partial(mid_kernel, chips, hosts, 2),
        "mid_one",
        (both_shape,) * 2,
        [VMEM] * (6 + chips),
        (adj, lent, agg, grad, summed, place, recv, *terms),
        flops=3 * square,
    )
    hidden, there, grad_pre, mine, msg, *to = call(
        functools.partial(middle_kernel, chips, hosts),
        "middle",
        (rows_shape,) * 3 + dealt,
        [VMEM] * 11,
        (adj, lent, col, col_two, agg, direct, grad, pick, here, shared, neigh_one),
        [halo, total],
        flops=12 * square,
    )
    terms, recv, here, summed, shared = across(mine, msg, to, 0)
    agg, direct, grad = call(
        functools.partial(early_two_kernel, chips),
        "early_two",
        (sum_shape,) * 3,
        [VMEM] * 7,
        (adj, hidden, there, self_two, bias_two, grad_pre, self_one),
        flops=4 * square,
    )
    agg, grad = call(
        functools.partial(mid_kernel, chips, hosts, 1),
        "mid_two",
        (sum_shape,) * 2,
        [VMEM] * (5 + chips),
        (adj, agg, grad, summed, place, recv, *terms),
        flops=2 * square,
    )
    output = call(
        functools.partial(last_kernel, chips, far),
        "last",
        rows_shape,
        [VMEM] * 6,
        (adj, agg, direct, here, shared, neigh_two),
        [
            halo,
            pltpu.VMEM((HALVES, rows // HALVES, width), BF16),
            pltpu.SemaphoreType.DMA((HALVES,)),
        ],
        flops=3 * square,
        out_space=pl.ANY,
    )
    return output, grad


def solution(mesh):
    hosts, devs = mesh.devices.shape
    mesh = Mesh(mesh.devices.reshape(hosts, devs // CORES, CORES), ("hst", "chip", "core"))
    dev = ("chip", "core")
    every = ("hst", "chip", "core")
    return jax.shard_map(
        body,
        mesh=mesh,
        in_specs=(
            P(every, None),
            P("hst", dev, None, None),
            P(every),
            P(every),
            P(every),
            P(every, None, None),
            P(),
            P(),
            P(),
            P(),
            P(),
            P(),
            P(every, None),
        ),
        out_specs=(P(every, None), P(every, None)),
        check_vma=False,
    )
```

```python
import functools

import jax
import jax.numpy as jnp
from jax import lax
from jax.experimental import pallas as pl
from jax.experimental.pallas import tpu as pltpu
from jax.sharding import Mesh, PartitionSpec as P

F32 = jnp.float32
BF16 = jnp.bfloat16
MIB = 1024 * 1024
CHUNKS = 8
PARTS = 4
CORES = 2

VMEM = pl.BlockSpec(memory_space=pltpu.VMEM)
HBM = pl.BlockSpec(memory_space=pltpu.HBM)


def dot(a, b):
    return jnp.dot(a, b, preferred_element_type=F32)


def dot_nt(a, b):
    return lax.dot_general(a, b, (((1,), (1,)), ((), ())), preferred_element_type=F32)


def pick_matrix(send_ref, rows):
    hosts, send = send_ref.shape[2], send_ref.shape[3]
    place = lax.broadcasted_iota(jnp.int32, (send, rows), 0)
    column = lax.broadcasted_iota(jnp.int32, (send, rows), 1)
    parts = []
    for g in range(hosts):
        index = jnp.zeros((send, rows), jnp.int32)
        for s in range(send):
            index = jnp.where(place == s, send_ref[0, 0, g, s], index)
        parts.append(jnp.where(index == column, 1.0, 0.0).astype(F32))
    return jnp.concatenate(parts, 0).astype(BF16)


def column(chips, far, rows, side, adj_ref, far_t, out_ref):
    chip = lax.axis_index("chip")
    each = rows + far
    own_rows = chips * CORES * rows
    for j in range(far_t.shape[0] // rows):
        low = own_rows + j * rows
        far_t[j * rows : (j + 1) * rows, :] = adj_ref[low : low + rows, :].T
    for k in range(chips):
        d = lax.rem(chip + k, chips) * CORES + side
        at = k * each
        out_ref[at : at + rows, :] = adj_ref[pl.ds(pl.multiple_of(d * rows, rows), rows), :].T
        out_ref[at + rows : at + each, :] = far_t[pl.ds(pl.multiple_of(d * far, far), far), :]


def prep_kernel(
    chips,
    dst_hbm,
    src_hbm,
    rows_hbm,
    send_hbm,
    tile_hbm,
    features_hbm,
    cot_hbm,
    neigh_two_hbm,
    adj_ref,
    give_ref,
    up_ref,
    picked_ref,
    pick_ref,
    dst_ref,
    src_ref,
    rows_ref,
    send_ref,
    tile_buf,
    features_ref,
    cot_ref,
    neigh_two_ref,
    far_t,
    col,
    sems,
    *accs,
):
    tiles, blk = tile_buf.shape[0], tile_buf.shape[1]
    each = tiles // CHUNKS
    first = CHUNKS * 3 // 4
    chunks = [
        (tile_hbm.at[pl.ds(c * each, each)], tile_buf.at[pl.ds(c * each, each)])
        for c in range(CHUNKS)
    ]
    pairs = [(dst_hbm, dst_ref), (src_hbm, src_ref), (rows_hbm, rows_ref)]
    pairs += chunks[:first]
    pairs += [
        (cot_hbm, cot_ref),
        (neigh_two_hbm, neigh_two_ref),
        (features_hbm, features_ref),
        (send_hbm, send_ref),
    ]
    pairs += chunks[first:]
    copies = [pltpu.make_async_copy(a, b, sems.at[i]) for i, (a, b) in enumerate(pairs)]
    for copy in copies:
        copy.start()
    rows = features_ref.shape[0]
    bpd = rows // blk
    sources = accs[0].shape[0] // bpd
    part = accs[0].shape[1]
    far = send_ref.shape[2] * send_ref.shape[3]
    for acc in accs:
        acc[...] = jnp.zeros_like(acc)
    place = lax.broadcasted_iota(jnp.int32, (part, blk), 0)

    def add(t, carry):
        slot = dst_ref[t] * sources + src_ref[t]
        for i, acc in enumerate(accs):
            value = tile_buf[t, i * part : (i + 1) * part, :].astype(F32)
            acc[slot] += jnp.where(place < rows_ref[t] - i * part, value, 0.0)
        return carry

    for copy in copies[:3]:
        copy.wait()
    for c in range(first):
        copies[3 + c].wait()
        lax.fori_loop(c * each, (c + 1) * each, add, 0, unroll=True)
    for copy in copies[3 + first : 7 + first]:
        copy.wait()
    u = dot_nt(cot_ref[...], neigh_two_ref[...]).astype(BF16)
    up_ref[...] = u
    pick_ref[...] = pick_matrix(send_ref, rows)
    picked_ref[...] = dot(pick_ref[...], features_ref[...]).astype(BF16)
    for c in range(first, CHUNKS):
        copies[7 + c].wait()
        lax.fori_loop(c * each, (c + 1) * each, add, 0, unroll=True)
    for b in range(bpd):
        for j in range(sources):
            block = jnp.concatenate([acc[b * sources + j] for acc in accs], 0).astype(BF16)
            low = j // bpd * rows + b * blk
            left = j % bpd * blk
            adj_ref[low : low + blk, left : left + blk] = block
    column(chips, far, rows, 1 - lax.axis_index("core"), adj_ref, far_t, col)
    give_ref[...] = dot(col[...], u).astype(BF16)


def rest_kernel(
    chips, adj_ref, up_ref, cot_ref, value_ref, pick_ref, col_ref, keep_ref, lend_ref, place_ref, far_t
):
    rows = up_ref.shape[0]
    far = col_ref.shape[0] // chips - rows
    column(chips, far, rows, lax.axis_index("core"), adj_ref, far_t, col_ref)
    keep_ref[...] = dot(col_ref[...], up_ref[...]).astype(BF16)
    low = adj_ref.shape[0]
    lend_ref[:low, :] = adj_ref[...]
    lend_ref[low : low + rows, :] = cot_ref[...]
    lend_ref[low + rows :, :] = value_ref[...]
    place_ref[...] = jnp.concatenate([pick_ref[...]] * chips, 0).T


def deal(chips, hosts, total, picked, value, mine_ref, msg_ref, to_refs):
    rows = value.shape[0]
    far = picked.shape[0]
    send = far // hosts
    each = rows + far
    chip = lax.axis_index("chip")
    mine_ref[...] = total[:rows]
    for k in range(chips):
        low = k * each + rows
        if k > 0:
            to_refs[k - 1][:rows, :] = total[k * each : low].astype(BF16)
            to_refs[k - 1][rows:, :] = value
        x = lax.rem(chip + k, chips)
        for g in range(hosts):
            at = low + g * send
            both = [picked[g * send : (g + 1) * send], total[at : at + send]]
            msg_ref[g * chips + x] = jnp.concatenate(both, 0).astype(BF16)


def core_sum_kernel(
    chips, hosts, keep_ref, came_ref, value_ref, picked_ref, mine_ref, msg_ref, *rest
):
    total = keep_ref[...].astype(F32) + came_ref[...].astype(F32)
    picked = picked_ref[...].astype(F32)
    deal(chips, hosts, total, picked, value_ref[...], mine_ref, msg_ref, rest)


def halo_part(recv_ref, hosts, chips, part):
    send = recv_ref.shape[1] // 2
    low = part * send
    blocks = [
        recv_ref[g * chips + x].astype(F32)[low : low + send]
        for x in range(chips)
        for g in range(hosts)
    ]
    return jnp.concatenate(blocks, 0).astype(BF16)


def merge_kernel(chips, hosts, recv_ref, mine_ref, place_ref, *refs):
    came, (out_ref, sum_ref) = refs[: chips - 1], refs[chips - 1 :]
    rows = mine_ref.shape[0]
    total = mine_ref[...]
    for k, ref in enumerate(came):
        total = total + ref[:rows, :].astype(F32)
        out_ref[k * rows : (k + 1) * rows, :] = ref[rows:, :]
    total = total + returned(place_ref, recv_ref, hosts, chips)
    sum_ref[...] = total
    low = len(came) * rows
    halo = halo_part(recv_ref, hosts, chips, 0)
    high = low + halo.shape[0]
    out_ref[low:high, :] = halo
    out_ref[high:, :] = total.astype(BF16)


def returned(place_ref, recv_ref, hosts, chips):
    return dot(place_ref[...], halo_part(recv_ref, hosts, chips, 1))


def own_chip(adj_refs, blocks):
    chip, core = lax.axis_index("chip"), lax.axis_index("core")
    rows = blocks[0].shape[0]
    parts = []
    for adj_ref in adj_refs:
        total = 0.0
        for side, block in ((core, blocks[0]), (1 - core, blocks[1])):
            low = pl.multiple_of((chip * CORES + side) * rows, rows)
            total = total + dot(adj_ref[pl.ds(low, rows), :], block)
        parts.append(total)
    return jnp.concatenate(parts, 0)


def early_one_kernel(
    chips, adj_ref, lent_ref, value_ref, self_ref, bias_ref, up_ref, weight_ref,
    agg_ref, direct_ref, grad_ref, col_ref, far_t,
):
    value = value_ref[...]
    rows = value.shape[0]
    low = adj_ref.shape[0]
    there = lent_ref[low + rows :, :]
    agg_ref[...] = own_chip((adj_ref, lent_ref), (value, there))
    both = jnp.concatenate([value, there], 0)
    direct_ref[...] = dot(both, self_ref[...]) + bias_ref[...].reshape(1, -1)
    both = jnp.concatenate([up_ref[...], lent_ref[low : low + rows, :]], 0)
    grad_ref[...] = dot_nt(both, weight_ref[...])
    far = col_ref.shape[0] // chips - rows
    column(chips, far, rows, lax.axis_index("core"), lent_ref, far_t, col_ref)


def mid_kernel(chips, adj_ref, lent_ref, agg_ref, part_ref, sum_ref, *refs):
    came, (agg_out, grad_ref) = refs[:-2], refs[-2:]
    rows = sum_ref.shape[0]
    chip, core = lax.axis_index("chip"), lax.axis_index("core")
    for i, ref in enumerate((adj_ref, lent_ref)):
        agg = agg_ref[i * rows : (i + 1) * rows, :]
        for k, block in enumerate(came):
            x = lax.rem(chip - k - 1 + chips, chips)
            low = pl.multiple_of((x * CORES + core) * rows, rows)
            agg = agg + dot(ref[pl.ds(low, rows), :], block[rows:, :])
        agg_out[i * rows : (i + 1) * rows, :] = agg
    grad_ref[:rows, :] = part_ref[:rows, :] + sum_ref[...]
    grad_ref[rows:, :] = part_ref[rows:, :]


def column_product(chips, hosts, adj_ref, value_ref, came, recv_ref, neigh_ref, halo):
    rows = value_ref.shape[0]
    far = halo.shape[0] // (chips * CORES)
    chip, core = lax.axis_index("chip"), lax.axis_index("core")
    low = pl.multiple_of((chip * CORES + core) * rows, rows)
    agg = dot(adj_ref[pl.ds(low, rows), :], value_ref[...])
    for k, block in enumerate(came):
        x = lax.rem(chip - k - 1 + chips, chips)
        low = pl.multiple_of((x * CORES + core) * rows, rows)
        agg = agg + dot(adj_ref[pl.ds(low, rows), :], block[rows:, :])
    rows_here = halo_part(recv_ref, hosts, chips, 0)
    halo[...] = jnp.zeros_like(halo)
    for x in range(chips):
        low = pl.multiple_of((x * CORES + core) * far, far)
        halo[pl.ds(low, far), :] = rows_here[x * far : (x + 1) * far]
    for j in range(halo.shape[0] // rows):
        low = (chips * CORES + j) * rows
        agg = agg + dot(adj_ref[low : low + rows, :], halo[j * rows : (j + 1) * rows, :])
    return dot(agg.astype(BF16), neigh_ref[...])


def there_kernel(chips, hosts, lent_ref, value_ref, recv_ref, neigh_ref, *refs):
    came, out_ref, halo = refs[:-2], refs[-2], refs[-1]
    out_ref[...] = column_product(
        chips, hosts, lent_ref, value_ref, came, recv_ref, neigh_ref, halo
    ).astype(BF16)


def here_kernel(
    chips, hosts, adj_ref, value_ref, recv_ref, neigh_ref, self_ref, bias_ref, up_ref, weight_ref,
    mine_ref, place_ref, *refs
):
    came, out_ref, grad_ref, halo = refs[:-3], refs[-3], refs[-2], refs[-1]
    rows = mine_ref.shape[0]
    grad = dot_nt(up_ref[...], weight_ref[...]) + mine_ref[...]
    for block in came:
        grad = grad + block[:rows, :].astype(F32)
    grad_ref[...] = grad + returned(place_ref, recv_ref, hosts, chips)
    out = column_product(chips, hosts, adj_ref, value_ref, came, recv_ref, neigh_ref, halo)
    out_ref[...] = out + dot(value_ref[...], self_ref[...]) + bias_ref[...].reshape(1, -1)


def put_halo(chips, far, rows, here_ref, shared_ref, halo):
    core = lax.axis_index("core")
    at = (chips - 1) * rows
    for x in range(chips):
        for side, ref in ((core, here_ref), (1 - core, shared_ref)):
            low = pl.multiple_of((x * CORES + side) * far, far)
            halo[pl.ds(low, far), :] = ref[at + x * far : at + (x + 1) * far, :]


def add_far(chips, rows, adj_ref, start, size, agg, shared_ref, halo):
    chip, core = lax.axis_index("chip"), lax.axis_index("core")
    for k in range(chips - 1):
        x = lax.rem(chip - k - 1 + chips, chips)
        low = pl.multiple_of((x * CORES + 1 - core) * rows + start, size)
        agg = agg + dot(adj_ref[pl.ds(low, size), :], shared_ref[k * rows : (k + 1) * rows, :])
    for j in range(halo.shape[0] // rows):
        low = chips * CORES * rows + j * rows + start
        agg = agg + dot(adj_ref[low : low + size, :], halo[j * rows : (j + 1) * rows, :])
    return agg


def middle_kernel(
    chips,
    hosts,
    adj_ref,
    lent_ref,
    col_ref,
    col_two_ref,
    agg_ref,
    direct_ref,
    grad_ref,
    pick_ref,
    here_ref,
    shared_ref,
    neigh_one_ref,
    hidden_ref,
    grad_pre_ref,
    mine_ref,
    msg_ref,
    *rest,
):
    to_refs, halo = rest[:-1], rest[-1]
    far, rows = pick_ref.shape
    put_halo(chips, far, rows, here_ref, shared_ref, halo)
    parts = [
        add_far(
            chips, rows, ref, 0, rows, agg_ref[i * rows : (i + 1) * rows, :], shared_ref, halo
        )
        for i, ref in enumerate((adj_ref, lent_ref))
    ]
    agg = jnp.concatenate(parts, 0).astype(BF16)
    pre = direct_ref[...] + dot(agg, neigh_one_ref[...])
    sigmoid = jax.nn.sigmoid(pre)
    hidden = (pre * sigmoid).astype(BF16)
    hidden_ref[...] = hidden[:rows]
    low = (chips - 1) * rows + chips * far
    add = shared_ref[low:, :].astype(F32)
    grad = jnp.concatenate([grad_ref[:rows, :], grad_ref[rows:, :] + add], 0)
    grad_pre = (grad * sigmoid * (1.0 + pre * (1.0 - sigmoid))).astype(BF16)
    grad_pre_ref[...] = grad_pre[:rows]
    u = dot_nt(grad_pre, neigh_one_ref[...]).astype(BF16)
    total = dot(col_ref[...], u[:rows]) + dot(col_two_ref[...], u[rows:])
    picked = dot(pick_ref[...], hidden[:rows])
    deal(chips, hosts, total, picked, hidden[:rows], mine_ref, msg_ref, to_refs)


def last_kernel(here_ref, there_ref, output_ref):
    output_ref[...] = (here_ref[...] + there_ref[...].astype(F32)).astype(BF16)


def call(kernel, name, out_shape, in_specs, args, scratch=(), limit=32, flops=0):
    return pl.pallas_call(
        kernel,
        out_shape=out_shape,
        in_specs=in_specs,
        out_specs=jax.tree.map(lambda _: VMEM, out_shape),
        scratch_shapes=scratch,
        compiler_params=pltpu.CompilerParams(vmem_limit_bytes=limit * MIB),
        cost_estimate=pl.CostEstimate(
            flops=flops, bytes_accessed=flops // 1024, transcendentals=0
        ),
        name=name,
    )(*args)


def shift(value, axis, k):
    size = lax.axis_size(axis)
    return lax.ppermute(value, axis, [(i, (i + k) % size) for i in range(size)])


def shape(rows, width, kind=BF16):
    return jax.ShapeDtypeStruct((rows, width), kind)


def body(
    features,
    send_list,
    tile_dst,
    tile_src,
    tile_rows,
    tile_val,
    self_one,
    neigh_one,
    bias_one,
    self_two,
    neigh_two,
    bias_two,
    cotangent,
):
    chips = lax.axis_size("chip")
    hosts = lax.axis_size("hst")
    rows, width = features.shape
    tiles, blk = tile_val.shape[:2]
    send = send_list.shape[3]
    far = hosts * send
    all_rows = chips * CORES * (rows + far)
    count = chips * (rows + far)
    rows_shape = shape(rows, width)
    sum_shape = shape(rows, width, F32)
    both_shape = shape(CORES * rows, width, F32)
    square = 2 * rows * width * width
    halo = pltpu.VMEM((chips * CORES * far, width), BF16)
    halo_rows = (chips - 1) * rows + chips * far
    dealt = (
        sum_shape,
        jax.ShapeDtypeStruct((hosts * chips, 2 * send, width), BF16),
    ) + (shape(2 * rows, width),) * (chips - 1)

    def across(msg, to):
        terms = [shift(block, "chip", k + 1) for k, block in enumerate(to)]
        recv = lax.all_to_all(msg, ("hst", "chip"), split_axis=0, concat_axis=0, tiled=True)
        return terms, recv

    far_t = pltpu.VMEM((chips * CORES * far, rows), BF16)
    adj, give, up, picked, pick = call(
        functools.partial(prep_kernel, chips),
        "prep",
        (
            shape(all_rows, rows),
            shape(count, width),
            rows_shape,
            shape(far, width),
            shape(far, rows),
        ),
        [HBM] * 8,
        [
            pltpu.with_memory_space_constraint(value, pltpu.HBM)
            for value in (
                tile_dst,
                tile_src,
                tile_rows,
                send_list,
                tile_val,
                features,
                cotangent,
                neigh_two,
            )
        ],
        [
            pltpu.SMEM(tile_dst.shape, jnp.int32),
            pltpu.SMEM(tile_src.shape, jnp.int32),
            pltpu.SMEM(tile_rows.shape, jnp.int32),
            pltpu.SMEM(send_list.shape, jnp.int32),
            pltpu.VMEM(tile_val.shape, BF16),
            pltpu.VMEM(features.shape, BF16),
            pltpu.VMEM(cotangent.shape, BF16),
            pltpu.VMEM(neigh_two.shape, BF16),
            far_t,
            pltpu.VMEM((count, rows), BF16),
            pltpu.SemaphoreType.DMA((7 + CHUNKS,)),
        ]
        + [pltpu.VMEM(((rows // blk) * (all_rows // blk), blk // PARTS, blk), F32)] * PARTS,
    )
    came = shift(give, "core", 1)
    col, keep, lend, place = call(
        functools.partial(rest_kernel, chips),
        "rest",
        (
            shape(count, rows),
            shape(count, width),
            shape(all_rows + 2 * rows, width),
            shape(rows, chips * far),
        ),
        [VMEM] * 5,
        (adj, up, cotangent, features, pick),
        [far_t],
        flops=3 * square,
    )
    lent = shift(lend, "core", 1)
    mine, msg, *to = call(
        functools.partial(core_sum_kernel, chips, hosts),
        "core_sum",
        dealt,
        [VMEM] * 4,
        (keep, came, features, picked),
        flops=60 * square,
    )
    terms, recv = across(msg, to)
    here, summed = call(
        functools.partial(merge_kernel, chips, hosts),
        "merge",
        (shape(halo_rows + rows, width), sum_shape),
        [VMEM] * (2 + chips),
        (recv, mine, place, *terms),
    )
    shared = shift(here, "core", 1)
    agg, direct, grad, col_two = call(
        functools.partial(early_one_kernel, chips),
        "early_one",
        (both_shape,) * 3 + (shape(count, rows),),
        [VMEM] * 7,
        (adj, lent, features, self_one, bias_one, cotangent, self_two),
        [far_t],
        flops=8 * square,
    )
    agg, grad = call(
        functools.partial(mid_kernel, chips),
        "mid",
        (both_shape,) * 2,
        [VMEM] * (4 + chips),
        (adj, lent, agg, grad, summed, *terms),
        flops=3 * square,
    )
    hidden, grad_pre, mine, msg, *to = call(
        functools.partial(middle_kernel, chips, hosts),
        "middle",
        (rows_shape,) * 2 + dealt,
        [VMEM] * 11,
        (adj, lent, col, col_two, agg, direct, grad, pick, here, shared, neigh_one),
        [halo],
        flops=12 * square,
    )
    terms, recv = across(msg, to)
    there = call(
        functools.partial(there_kernel, chips, hosts),
        "there",
        rows_shape,
        [VMEM] * (3 + chips),
        (lent, hidden, recv, neigh_two, *terms),
        [halo],
    )
    shared = shift(there, "core", 1)
    here, grad = call(
        functools.partial(here_kernel, chips, hosts),
        "here",
        (sum_shape,) * 2,
        [VMEM] * (9 + chips),
        (
            adj,
            hidden,
            recv,
            neigh_two,
            self_two,
            bias_two,
            grad_pre,
            self_one,
            mine,
            place,
            *terms,
        ),
        [halo],
        flops=7 * square,
    )
    output = call(last_kernel, "last", rows_shape, [VMEM] * 2, (here, shared))
    return output, grad


def solution(mesh):
    hosts, devs = mesh.devices.shape
    mesh = Mesh(mesh.devices.reshape(hosts, devs // CORES, CORES), ("hst", "chip", "core"))
    dev = ("chip", "core")
    every = ("hst", "chip", "core")
    return jax.shard_map(
        body,
        mesh=mesh,
        in_specs=(
            P(every, None),
            P("hst", dev, None, None),
            P(every),
            P(every),
            P(every),
            P(every, None, None),
            P(),
            P(),
            P(),
            P(),
            P(),
            P(),
            P(every, None),
        ),
        out_specs=(P(every, None), P(every, None)),
        check_vma=False,
    )
```

```python
import functools

import jax
import jax.numpy as jnp
from jax import lax
from jax.experimental import pallas as pl
from jax.experimental.pallas import tpu as pltpu
from jax.sharding import Mesh, PartitionSpec as P

F32 = jnp.float32
BF16 = jnp.bfloat16
MIB = 1024 * 1024
CHUNKS = 8
PARTS = 4
CORES = 2

VMEM = pl.BlockSpec(memory_space=pltpu.VMEM)
HBM = pl.BlockSpec(memory_space=pltpu.HBM)


def dot(a, b):
    return jnp.dot(a, b, preferred_element_type=F32)


def dot_nt(a, b):
    return lax.dot_general(a, b, (((1,), (1,)), ((), ())), preferred_element_type=F32)


def pick_matrix(send_ref, rows):
    hosts, send = send_ref.shape[2], send_ref.shape[3]
    place = lax.broadcasted_iota(jnp.int32, (send, rows), 0)
    column = lax.broadcasted_iota(jnp.int32, (send, rows), 1)
    parts = []
    for g in range(hosts):
        index = jnp.zeros((send, rows), jnp.int32)
        for s in range(send):
            index = jnp.where(place == s, send_ref[0, 0, g, s], index)
        parts.append(jnp.where(index == column, 1.0, 0.0).astype(F32))
    return jnp.concatenate(parts, 0).astype(BF16)


def column(chips, far, rows, side, adj_ref, far_t, out_ref):
    chip = lax.axis_index("chip")
    each = rows + far
    own_rows = chips * CORES * rows
    for j in range(far_t.shape[0] // rows):
        low = own_rows + j * rows
        far_t[j * rows : (j + 1) * rows, :] = adj_ref[low : low + rows, :].T
    for k in range(chips):
        d = lax.rem(chip + k, chips) * CORES + side
        at = k * each
        out_ref[at : at + rows, :] = adj_ref[pl.ds(pl.multiple_of(d * rows, rows), rows), :].T
        out_ref[at + rows : at + each, :] = far_t[pl.ds(pl.multiple_of(d * far, far), far), :]


def prep_kernel(
    chips,
    dst_hbm,
    src_hbm,
    rows_hbm,
    send_hbm,
    tile_hbm,
    features_hbm,
    cot_hbm,
    neigh_two_hbm,
    adj_ref,
    give_ref,
    up_ref,
    picked_ref,
    pick_ref,
    dst_ref,
    src_ref,
    rows_ref,
    send_ref,
    tile_buf,
    features_ref,
    cot_ref,
    neigh_two_ref,
    far_t,
    col,
    sems,
    *accs,
):
    tiles, blk = tile_buf.shape[0], tile_buf.shape[1]
    each = tiles // CHUNKS
    first = CHUNKS * 3 // 4
    chunks = [
        (tile_hbm.at[pl.ds(c * each, each)], tile_buf.at[pl.ds(c * each, each)])
        for c in range(CHUNKS)
    ]
    pairs = [(dst_hbm, dst_ref), (src_hbm, src_ref), (rows_hbm, rows_ref)]
    pairs += chunks[:first]
    pairs += [
        (cot_hbm, cot_ref),
        (neigh_two_hbm, neigh_two_ref),
        (features_hbm, features_ref),
        (send_hbm, send_ref),
    ]
    pairs += chunks[first:]
    copies = [pltpu.make_async_copy(a, b, sems.at[i]) for i, (a, b) in enumerate(pairs)]
    for copy in copies:
        copy.start()
    rows = features_ref.shape[0]
    bpd = rows // blk
    sources = accs[0].shape[0] // bpd
    part = accs[0].shape[1]
    far = send_ref.shape[2] * send_ref.shape[3]
    for acc in accs:
        acc[...] = jnp.zeros_like(acc)
    place = lax.broadcasted_iota(jnp.int32, (part, blk), 0)

    def add(t, carry):
        slot = dst_ref[t] * sources + src_ref[t]
        for i, acc in enumerate(accs):
            value = tile_buf[t, i * part : (i + 1) * part, :].astype(F32)
            acc[slot] += jnp.where(place < rows_ref[t] - i * part, value, 0.0)
        return carry

    for copy in copies[:3]:
        copy.wait()
    for c in range(first):
        copies[3 + c].wait()
        lax.fori_loop(c * each, (c + 1) * each, add, 0, unroll=True)
    for copy in copies[3 + first : 7 + first]:
        copy.wait()
    u = dot_nt(cot_ref[...], neigh_two_ref[...]).astype(BF16)
    up_ref[...] = u
    pick_ref[...] = pick_matrix(send_ref, rows)
    picked_ref[...] = dot(pick_ref[...], features_ref[...]).astype(BF16)
    for c in range(first, CHUNKS):
        copies[7 + c].wait()
        lax.fori_loop(c * each, (c + 1) * each, add, 0, unroll=True)
    for b in range(bpd):
        for j in range(sources):
            block = jnp.concatenate([acc[b * sources + j] for acc in accs], 0).astype(BF16)
            low = j // bpd * rows + b * blk
            left = j % bpd * blk
            adj_ref[low : low + blk, left : left + blk] = block
    column(chips, far, rows, 1 - lax.axis_index("core"), adj_ref, far_t, col)
    give_ref[...] = dot(col[...], u).astype(BF16)


def rest_kernel(
    chips, adj_ref, up_ref, cot_ref, value_ref, pick_ref, col_ref, keep_ref, lend_ref, place_ref, far_t
):
    rows = up_ref.shape[0]
    far = col_ref.shape[0] // chips - rows
    column(chips, far, rows, lax.axis_index("core"), adj_ref, far_t, col_ref)
    keep_ref[...] = dot(col_ref[...], up_ref[...]).astype(BF16)
    low = adj_ref.shape[0]
    lend_ref[:low, :] = adj_ref[...]
    lend_ref[low : low + rows, :] = cot_ref[...]
    lend_ref[low + rows :, :] = value_ref[...]
    place_ref[...] = jnp.concatenate([pick_ref[...]] * chips, 0).T


def deal(chips, hosts, total, picked, value, mine_ref, msg_ref, to_refs):
    rows = value.shape[0]
    far = picked.shape[0]
    send = far // hosts
    each = rows + far
    chip = lax.axis_index("chip")
    mine_ref[...] = total[:rows]
    for k in range(chips):
        low = k * each + rows
        if k > 0:
            to_refs[k - 1][:rows, :] = total[k * each : low].astype(BF16)
            to_refs[k - 1][rows:, :] = value
        x = lax.rem(chip + k, chips)
        for g in range(hosts):
            at = low + g * send
            both = [picked[g * send : (g + 1) * send], total[at : at + send]]
            msg_ref[x * hosts + g] = jnp.concatenate(both, 0).astype(BF16)


def core_sum_kernel(
    chips, hosts, keep_ref, came_ref, value_ref, picked_ref, mine_ref, msg_ref, *rest
):
    total = keep_ref[...].astype(F32) + came_ref[...].astype(F32)
    picked = picked_ref[...].astype(F32)
    deal(chips, hosts, total, picked, value_ref[...], mine_ref, msg_ref, rest)


def halo_part(recv_ref, hosts, chips, part):
    send = recv_ref.shape[1] // 2
    low = part * send
    blocks = [
        recv_ref[x * hosts + g].astype(F32)[low : low + send]
        for x in range(chips)
        for g in range(hosts)
    ]
    return jnp.concatenate(blocks, 0).astype(BF16)


def merge_kernel(chips, hosts, recv_ref, mine_ref, place_ref, *refs):
    came, (out_ref, sum_ref) = refs[: chips - 1], refs[chips - 1 :]
    rows = mine_ref.shape[0]
    total = mine_ref[...]
    for k, ref in enumerate(came):
        total = total + ref[:rows, :].astype(F32)
        out_ref[k * rows : (k + 1) * rows, :] = ref[rows:, :]
    total = total + returned(place_ref, recv_ref, hosts, chips)
    sum_ref[...] = total
    low = len(came) * rows
    halo = halo_part(recv_ref, hosts, chips, 0)
    high = low + halo.shape[0]
    out_ref[low:high, :] = halo
    out_ref[high:, :] = total.astype(BF16)


def returned(place_ref, recv_ref, hosts, chips):
    return dot(place_ref[...], halo_part(recv_ref, hosts, chips, 1))


def joint(pairs):
    left = jnp.concatenate([a for a, _ in pairs], 1)
    return dot(left, jnp.concatenate([b for _, b in pairs], 0))


def square_of(adj_ref, x, side, rows):
    return adj_ref[pl.ds(pl.multiple_of((x * CORES + side) * rows, rows), rows), :]


def far_pairs(chips, rows, adj_ref, halo):
    base = chips * CORES * rows
    return [
        (adj_ref[base + low : base + low + rows, :], halo[low : low + rows, :])
        for low in range(0, halo.shape[0], rows)
    ]


def own_chip(adj_refs, blocks):
    chip, core = lax.axis_index("chip"), lax.axis_index("core")
    rows = blocks[0].shape[0]
    parts = [
        joint([(square_of(ref, chip, s, rows), b) for s, b in zip((core, 1 - core), blocks)])
        for ref in adj_refs
    ]
    return jnp.concatenate(parts, 0)


def early_one_kernel(
    chips, adj_ref, lent_ref, value_ref, self_ref, bias_ref, up_ref, weight_ref,
    agg_ref, direct_ref, grad_ref, col_ref, far_t,
):
    value = value_ref[...]
    rows = value.shape[0]
    low = adj_ref.shape[0]
    there = lent_ref[low + rows :, :]
    agg_ref[...] = own_chip((adj_ref, lent_ref), (value, there))
    both = jnp.concatenate([value, there], 0)
    direct_ref[...] = dot(both, self_ref[...]) + bias_ref[...].reshape(1, -1)
    both = jnp.concatenate([up_ref[...], lent_ref[low : low + rows, :]], 0)
    grad_ref[...] = dot_nt(both, weight_ref[...])
    far = col_ref.shape[0] // chips - rows
    column(chips, far, rows, lax.axis_index("core"), lent_ref, far_t, col_ref)


def mid_kernel(chips, adj_ref, lent_ref, agg_ref, part_ref, sum_ref, *refs):
    came, (agg_out, grad_ref) = refs[:-2], refs[-2:]
    rows = sum_ref.shape[0]
    chip, core = lax.axis_index("chip"), lax.axis_index("core")
    for i, ref in enumerate((adj_ref, lent_ref)):
        agg = agg_ref[i * rows : (i + 1) * rows, :]
        for k, block in enumerate(came):
            x = lax.rem(chip - k - 1 + chips, chips)
            low = pl.multiple_of((x * CORES + core) * rows, rows)
            agg = agg + dot(ref[pl.ds(low, rows), :], block[rows:, :])
        agg_out[i * rows : (i + 1) * rows, :] = agg
    grad_ref[:rows, :] = part_ref[:rows, :] + sum_ref[...]
    grad_ref[rows:, :] = part_ref[rows:, :]


def column_product(chips, hosts, adj_ref, value_ref, came, recv_ref, neigh_ref, halo):
    rows = value_ref.shape[0]
    far = halo.shape[0] // (chips * CORES)
    chip, core = lax.axis_index("chip"), lax.axis_index("core")
    pairs = [(square_of(adj_ref, chip, core, rows), value_ref[...])]
    for k, block in enumerate(came):
        x = lax.rem(chip - k - 1 + chips, chips)
        pairs.append((square_of(adj_ref, x, core, rows), block[rows:, :]))
    rows_here = halo_part(recv_ref, hosts, chips, 0)
    halo[...] = jnp.zeros_like(halo)
    for x in range(chips):
        low = pl.multiple_of((x * CORES + core) * far, far)
        halo[pl.ds(low, far), :] = rows_here[x * far : (x + 1) * far]
    agg = joint(pairs + far_pairs(chips, rows, adj_ref, halo))
    return dot(agg.astype(BF16), neigh_ref[...])


def there_kernel(chips, hosts, lent_ref, value_ref, recv_ref, neigh_ref, *refs):
    came, out_ref, halo = refs[:-2], refs[-2], refs[-1]
    out_ref[...] = column_product(
        chips, hosts, lent_ref, value_ref, came, recv_ref, neigh_ref, halo
    ).astype(BF16)


def here_kernel(
    chips, hosts, adj_ref, value_ref, recv_ref, neigh_ref, self_ref, bias_ref, up_ref, weight_ref,
    mine_ref, place_ref, *refs
):
    came, out_ref, grad_ref, halo = refs[:-3], refs[-3], refs[-2], refs[-1]
    rows = mine_ref.shape[0]
    grad = dot_nt(up_ref[...], weight_ref[...]) + mine_ref[...]
    for block in came:
        grad = grad + block[:rows, :].astype(F32)
    grad_ref[...] = grad + returned(place_ref, recv_ref, hosts, chips)
    out = column_product(chips, hosts, adj_ref, value_ref, came, recv_ref, neigh_ref, halo)
    out_ref[...] = out + dot(value_ref[...], self_ref[...]) + bias_ref[...].reshape(1, -1)


def put_halo(chips, far, rows, here_ref, shared_ref, halo):
    core = lax.axis_index("core")
    at = (chips - 1) * rows
    for x in range(chips):
        for side, ref in ((core, here_ref), (1 - core, shared_ref)):
            low = pl.multiple_of((x * CORES + side) * far, far)
            halo[pl.ds(low, far), :] = ref[at + x * far : at + (x + 1) * far, :]


def add_far(chips, rows, adj_ref, agg, shared_ref, halo):
    chip, core = lax.axis_index("chip"), lax.axis_index("core")
    pairs = []
    for k in range(chips - 1):
        x = lax.rem(chip - k - 1 + chips, chips)
        block = shared_ref[k * rows : (k + 1) * rows, :]
        pairs.append((square_of(adj_ref, x, 1 - core, rows), block))
    return agg + joint(pairs + far_pairs(chips, rows, adj_ref, halo))


def middle_kernel(
    chips,
    hosts,
    adj_ref,
    lent_ref,
    col_ref,
    col_two_ref,
    agg_ref,
    direct_ref,
    grad_ref,
    pick_ref,
    here_ref,
    shared_ref,
    neigh_one_ref,
    hidden_ref,
    grad_pre_ref,
    mine_ref,
    msg_ref,
    *rest,
):
    to_refs, halo = rest[:-1], rest[-1]
    far, rows = pick_ref.shape
    put_halo(chips, far, rows, here_ref, shared_ref, halo)
    parts = [
        add_far(chips, rows, ref, agg_ref[i * rows : (i + 1) * rows, :], shared_ref, halo)
        for i, ref in enumerate((adj_ref, lent_ref))
    ]
    agg = jnp.concatenate(parts, 0).astype(BF16)
    pre = direct_ref[...] + dot(agg, neigh_one_ref[...])
    sigmoid = jax.nn.sigmoid(pre)
    hidden = (pre * sigmoid).astype(BF16)
    hidden_ref[...] = hidden[:rows]
    low = (chips - 1) * rows + chips * far
    add = shared_ref[low:, :].astype(F32)
    grad = jnp.concatenate([grad_ref[:rows, :], grad_ref[rows:, :] + add], 0)
    grad_pre = (grad * sigmoid * (1.0 + pre * (1.0 - sigmoid))).astype(BF16)
    grad_pre_ref[...] = grad_pre[:rows]
    u = dot_nt(grad_pre, neigh_one_ref[...]).astype(BF16)
    total = joint([(col_ref[...], u[:rows]), (col_two_ref[...], u[rows:])])
    picked = dot(pick_ref[...], hidden[:rows])
    deal(chips, hosts, total, picked, hidden[:rows], mine_ref, msg_ref, to_refs)


def last_kernel(here_ref, there_ref, output_ref):
    output_ref[...] = (here_ref[...] + there_ref[...].astype(F32)).astype(BF16)


def call(kernel, name, out_shape, in_specs, args, scratch=(), limit=32, flops=0):
    return pl.pallas_call(
        kernel,
        out_shape=out_shape,
        in_specs=in_specs,
        out_specs=jax.tree.map(lambda _: VMEM, out_shape),
        scratch_shapes=scratch,
        compiler_params=pltpu.CompilerParams(vmem_limit_bytes=limit * MIB),
        cost_estimate=pl.CostEstimate(
            flops=flops, bytes_accessed=flops // 1024, transcendentals=0
        ),
        name=name,
    )(*args)


def shift(value, axis, k):
    size = lax.axis_size(axis)
    return lax.ppermute(value, axis, [(i, (i + k) % size) for i in range(size)])


def shape(rows, width, kind=BF16):
    return jax.ShapeDtypeStruct((rows, width), kind)


def body(
    features,
    send_list,
    tile_dst,
    tile_src,
    tile_rows,
    tile_val,
    self_one,
    neigh_one,
    bias_one,
    self_two,
    neigh_two,
    bias_two,
    cotangent,
):
    chips = lax.axis_size("chip")
    hosts = lax.axis_size("hst")
    rows, width = features.shape
    tiles, blk = tile_val.shape[:2]
    send = send_list.shape[3]
    far = hosts * send
    all_rows = chips * CORES * (rows + far)
    count = chips * (rows + far)
    rows_shape = shape(rows, width)
    sum_shape = shape(rows, width, F32)
    both_shape = shape(CORES * rows, width, F32)
    square = 2 * rows * width * width
    halo = pltpu.VMEM((chips * CORES * far, width), BF16)
    halo_rows = (chips - 1) * rows + chips * far
    dealt = (
        sum_shape,
        jax.ShapeDtypeStruct((hosts * chips, 2 * send, width), BF16),
    ) + (shape(2 * rows, width),) * (chips - 1)

    def across(msg, to):
        terms = [shift(block, "chip", k + 1) for k, block in enumerate(to)]
        recv = lax.all_to_all(msg, ("chip", "hst"), split_axis=0, concat_axis=0, tiled=True)
        return terms, recv

    far_t = pltpu.VMEM((chips * CORES * far, rows), BF16)
    adj, give, up, picked, pick = call(
        functools.partial(prep_kernel, chips),
        "prep",
        (
            shape(all_rows, rows),
            shape(count, width),
            rows_shape,
            shape(far, width),
            shape(far, rows),
        ),
        [HBM] * 8,
        [
            pltpu.with_memory_space_constraint(value, pltpu.HBM)
            for value in (
                tile_dst,
                tile_src,
                tile_rows,
                send_list,
                tile_val,
                features,
                cotangent,
                neigh_two,
            )
        ],
        [
            pltpu.SMEM(tile_dst.shape, jnp.int32),
            pltpu.SMEM(tile_src.shape, jnp.int32),
            pltpu.SMEM(tile_rows.shape, jnp.int32),
            pltpu.SMEM(send_list.shape, jnp.int32),
            pltpu.VMEM(tile_val.shape, BF16),
            pltpu.VMEM(features.shape, BF16),
            pltpu.VMEM(cotangent.shape, BF16),
            pltpu.VMEM(neigh_two.shape, BF16),
            far_t,
            pltpu.VMEM((count, rows), BF16),
            pltpu.SemaphoreType.DMA((7 + CHUNKS,)),
        ]
        + [pltpu.VMEM(((rows // blk) * (all_rows // blk), blk // PARTS, blk), F32)] * PARTS,
    )
    came = shift(give, "core", 1)
    col, keep, lend, place = call(
        functools.partial(rest_kernel, chips),
        "rest",
        (
            shape(count, rows),
            shape(count, width),
            shape(all_rows + 2 * rows, width),
            shape(rows, chips * far),
        ),
        [VMEM] * 5,
        (adj, up, cotangent, features, pick),
        [far_t],
        flops=3 * square,
    )
    lent = shift(lend, "core", 1)
    mine, msg, *to = call(
        functools.partial(core_sum_kernel, chips, hosts),
        "core_sum",
        dealt,
        [VMEM] * 4,
        (keep, came, features, picked),
        flops=60 * square,
    )
    terms, recv = across(msg, to)
    here, summed = call(
        functools.partial(merge_kernel, chips, hosts),
        "merge",
        (shape(halo_rows + rows, width), sum_shape),
        [VMEM] * (2 + chips),
        (recv, mine, place, *terms),
    )
    shared = shift(here, "core", 1)
    agg, direct, grad, col_two = call(
        functools.partial(early_one_kernel, chips),
        "early_one",
        (both_shape,) * 3 + (shape(count, rows),),
        [VMEM] * 7,
        (adj, lent, features, self_one, bias_one, cotangent, self_two),
        [far_t],
        flops=8 * square,
    )
    agg, grad = call(
        functools.partial(mid_kernel, chips),
        "mid",
        (both_shape,) * 2,
        [VMEM] * (4 + chips),
        (adj, lent, agg, grad, summed, *terms),
        flops=3 * square,
    )
    hidden, grad_pre, mine, msg, *to = call(
        functools.partial(middle_kernel, chips, hosts),
        "middle",
        (rows_shape,) * 2 + dealt,
        [VMEM] * 11,
        (adj, lent, col, col_two, agg, direct, grad, pick, here, shared, neigh_one),
        [halo],
        flops=12 * square,
    )
    terms, recv = across(msg, to)
    there = call(
        functools.partial(there_kernel, chips, hosts),
        "there",
        rows_shape,
        [VMEM] * (3 + chips),
        (lent, hidden, recv, neigh_two, *terms),
        [halo],
    )
    shared = shift(there, "core", 1)
    here, grad = call(
        functools.partial(here_kernel, chips, hosts),
        "here",
        (sum_shape,) * 2,
        [VMEM] * (9 + chips),
        (
            adj,
            hidden,
            recv,
            neigh_two,
            self_two,
            bias_two,
            grad_pre,
            self_one,
            mine,
            place,
            *terms,
        ),
        [halo],
        flops=7 * square,
    )
    output = call(last_kernel, "last", rows_shape, [VMEM] * 2, (here, shared))
    return output, grad


def solution(mesh):
    hosts, devs = mesh.devices.shape
    mesh = Mesh(mesh.devices.reshape(hosts, devs // CORES, CORES), ("hst", "chip", "core"))
    dev = ("chip", "core")
    every = ("hst", "chip", "core")
    return jax.shard_map(
        body,
        mesh=mesh,
        in_specs=(
            P(every, None),
            P("hst", dev, None, None),
            P(every),
            P(every),
            P(every),
            P(every, None, None),
            P(),
            P(),
            P(),
            P(),
            P(),
            P(),
            P(every, None),
        ),
        out_specs=(P(every, None), P(every, None)),
        check_vma=False,
    )
```

```python
import functools

import jax
import jax.numpy as jnp
from jax import lax
from jax.experimental import pallas as pl
from jax.experimental.pallas import tpu as pltpu
from jax.sharding import Mesh, PartitionSpec as P

F32 = jnp.float32
BF16 = jnp.bfloat16
MIB = 1024 * 1024
CHUNKS = 8
PARTS = 4
CORES = 2

VMEM = pl.BlockSpec(memory_space=pltpu.VMEM)
HBM = pl.BlockSpec(memory_space=pltpu.HBM)


def dot(a, b):
    return jnp.dot(a, b, preferred_element_type=F32)


def dot_nt(a, b):
    return lax.dot_general(a, b, (((1,), (1,)), ((), ())), preferred_element_type=F32)


def pick_matrix(send_ref, rows):
    hosts, send = send_ref.shape[2], send_ref.shape[3]
    place = lax.broadcasted_iota(jnp.int32, (send, rows), 0)
    column = lax.broadcasted_iota(jnp.int32, (send, rows), 1)
    parts = []
    for g in range(hosts):
        index = jnp.zeros((send, rows), jnp.int32)
        for s in range(send):
            index = jnp.where(place == s, send_ref[0, 0, g, s], index)
        parts.append(jnp.where(index == column, 1.0, 0.0).astype(F32))
    return jnp.concatenate(parts, 0).astype(BF16)


def column(chips, far, rows, side, adj_ref, far_t, out_ref):
    chip = lax.axis_index("chip")
    each = rows + far
    own_rows = chips * CORES * rows
    for j in range(far_t.shape[0] // rows):
        low = own_rows + j * rows
        far_t[j * rows : (j + 1) * rows, :] = adj_ref[low : low + rows, :].T
    for k in range(chips):
        d = lax.rem(chip + k, chips) * CORES + side
        at = k * each
        out_ref[at : at + rows, :] = adj_ref[pl.ds(pl.multiple_of(d * rows, rows), rows), :].T
        out_ref[at + rows : at + each, :] = far_t[pl.ds(pl.multiple_of(d * far, far), far), :]


def prep_kernel(
    chips,
    dst_hbm,
    src_hbm,
    rows_hbm,
    send_hbm,
    tile_hbm,
    features_hbm,
    cot_hbm,
    neigh_two_hbm,
    give_ref,
    up_ref,
    picked_ref,
    pick_ref,
    *rest,
):
    accs, rest = rest[:PARTS], rest[PARTS:]
    (
        dst_ref,
        src_ref,
        rows_ref,
        send_ref,
        tile_buf,
        features_ref,
        cot_ref,
        neigh_two_ref,
        square,
        far_t,
        col,
        sems,
    ) = rest
    tiles, blk = tile_buf.shape[0], tile_buf.shape[1]
    each = tiles // CHUNKS
    first = CHUNKS * 3 // 4
    chunks = [
        (tile_hbm.at[pl.ds(c * each, each)], tile_buf.at[pl.ds(c * each, each)])
        for c in range(CHUNKS)
    ]
    pairs = [(dst_hbm, dst_ref), (src_hbm, src_ref), (rows_hbm, rows_ref)]
    pairs += chunks[:first]
    pairs += [
        (cot_hbm, cot_ref),
        (neigh_two_hbm, neigh_two_ref),
        (features_hbm, features_ref),
        (send_hbm, send_ref),
    ]
    pairs += chunks[first:]
    copies = [pltpu.make_async_copy(a, b, sems.at[i]) for i, (a, b) in enumerate(pairs)]
    for copy in copies:
        copy.start()
    rows = features_ref.shape[0]
    bpd = rows // blk
    sources = accs[0].shape[0] // bpd
    part = accs[0].shape[1]
    far = send_ref.shape[2] * send_ref.shape[3]
    for acc in accs:
        acc[...] = jnp.zeros_like(acc)
    place = lax.broadcasted_iota(jnp.int32, (part, blk), 0)

    def add(t, carry):
        slot = dst_ref[t] * sources + src_ref[t]
        for i, acc in enumerate(accs):
            value = tile_buf[t, i * part : (i + 1) * part, :].astype(F32)
            acc[slot] += jnp.where(place < rows_ref[t] - i * part, value, 0.0)
        return carry

    for copy in copies[:3]:
        copy.wait()
    for c in range(first):
        copies[3 + c].wait()
        lax.fori_loop(c * each, (c + 1) * each, add, 0, unroll=True)
    for copy in copies[3 + first : 7 + first]:
        copy.wait()
    u = dot_nt(cot_ref[...], neigh_two_ref[...]).astype(BF16)
    up_ref[...] = u
    pick_ref[...] = pick_matrix(send_ref, rows)
    picked_ref[...] = dot(pick_ref[...], features_ref[...]).astype(BF16)
    for c in range(first, CHUNKS):
        copies[7 + c].wait()
        lax.fori_loop(c * each, (c + 1) * each, add, 0, unroll=True)
    chip, side = lax.axis_index("chip"), 1 - lax.axis_index("core")
    base = chips * CORES
    for j in range(far_t.shape[0] // rows):
        put_square(accs, bpd, base + j, square, 0)
        far_t[j * rows : (j + 1) * rows, :] = square[...].T
    for k in range(chips):
        d = lax.rem(chip + k, chips) * CORES + side
        at = k * (rows + far)
        put_square(accs, bpd, d, square, 0)
        col[at : at + rows, :] = square[...].T
        low = pl.multiple_of(d * far, far)
        col[at + rows : at + rows + far, :] = far_t[pl.ds(low, far), :]
    give_ref[...] = dot(col[...], u).astype(BF16)


def put_square(accs, bpd, d, out_ref, base):
    sources = accs[0].shape[0] // bpd
    part, blk = accs[0].shape[1:]
    for b in range(bpd):
        for j in range(bpd):
            for i, acc in enumerate(accs):
                low = base + b * blk + i * part
                value = acc[b * sources + d * bpd + j].astype(BF16)
                out_ref[low : low + part, j * blk : (j + 1) * blk] = value


def rest_kernel(chips, up_ref, cot_ref, value_ref, pick_ref, *refs):
    accs, (adj_ref, col_ref, keep_ref, lend_ref, place_ref, far_t) = refs[:PARTS], refs[PARTS:]
    rows = up_ref.shape[0]
    bpd = rows // accs[0].shape[2]
    for d in range(adj_ref.shape[0] // rows):
        put_square(accs, bpd, d, adj_ref, d * rows)
    far = col_ref.shape[0] // chips - rows
    column(chips, far, rows, lax.axis_index("core"), adj_ref, far_t, col_ref)
    keep_ref[...] = dot(col_ref[...], up_ref[...]).astype(BF16)
    low = adj_ref.shape[0]
    lend_ref[:low, :] = adj_ref[...]
    lend_ref[low : low + rows, :] = cot_ref[...]
    lend_ref[low + rows :, :] = value_ref[...]
    place_ref[...] = jnp.concatenate([pick_ref[...]] * chips, 0).T


def deal(chips, hosts, total, picked, value, mine_ref, msg_ref, to_refs):
    rows = value.shape[0]
    far = picked.shape[0]
    send = far // hosts
    each = rows + far
    chip = lax.axis_index("chip")
    mine_ref[...] = total[:rows]
    for k in range(chips):
        low = k * each + rows
        if k > 0:
            to_refs[k - 1][:rows, :] = total[k * each : low].astype(BF16)
            to_refs[k - 1][rows:, :] = value
        x = lax.rem(chip + k, chips)
        for g in range(hosts):
            at = low + g * send
            both = [picked[g * send : (g + 1) * send], total[at : at + send]]
            msg_ref[x * hosts + g] = jnp.concatenate(both, 0).astype(BF16)


def core_sum_kernel(
    chips, hosts, keep_ref, came_ref, value_ref, picked_ref, mine_ref, msg_ref, *rest
):
    total = keep_ref[...].astype(F32) + came_ref[...].astype(F32)
    picked = picked_ref[...].astype(F32)
    deal(chips, hosts, total, picked, value_ref[...], mine_ref, msg_ref, rest)


def halo_part(recv_ref, hosts, chips, part):
    send = recv_ref.shape[1] // 2
    low = part * send
    blocks = [
        recv_ref[x * hosts + g].astype(F32)[low : low + send]
        for x in range(chips)
        for g in range(hosts)
    ]
    return jnp.concatenate(blocks, 0).astype(BF16)


def merge_kernel(chips, hosts, recv_ref, mine_ref, place_ref, *refs):
    came, (out_ref, sum_ref) = refs[: chips - 1], refs[chips - 1 :]
    rows = mine_ref.shape[0]
    total = mine_ref[...]
    for k, ref in enumerate(came):
        total = total + ref[:rows, :].astype(F32)
        out_ref[k * rows : (k + 1) * rows, :] = ref[rows:, :]
    total = total + returned(place_ref, recv_ref, hosts, chips)
    sum_ref[...] = total
    low = len(came) * rows
    halo = halo_part(recv_ref, hosts, chips, 0)
    high = low + halo.shape[0]
    out_ref[low:high, :] = halo
    out_ref[high:, :] = total.astype(BF16)


def returned(place_ref, recv_ref, hosts, chips):
    return dot(place_ref[...], halo_part(recv_ref, hosts, chips, 1))


def joint(pairs):
    left = jnp.concatenate([a for a, _ in pairs], 1)
    return dot(left, jnp.concatenate([b for _, b in pairs], 0))


def square_of(adj_ref, x, side, rows):
    return adj_ref[pl.ds(pl.multiple_of((x * CORES + side) * rows, rows), rows), :]


def far_pairs(chips, rows, adj_ref, halo):
    base = chips * CORES * rows
    return [
        (adj_ref[base + low : base + low + rows, :], halo[low : low + rows, :])
        for low in range(0, halo.shape[0], rows)
    ]


def own_chip(adj_refs, blocks):
    chip, core = lax.axis_index("chip"), lax.axis_index("core")
    rows = blocks[0].shape[0]
    parts = [
        joint([(square_of(ref, chip, s, rows), b) for s, b in zip((core, 1 - core), blocks)])
        for ref in adj_refs
    ]
    return jnp.concatenate(parts, 0)


def early_one_kernel(
    chips, adj_ref, lent_ref, value_ref, self_ref, bias_ref, up_ref, weight_ref,
    agg_ref, direct_ref, grad_ref, col_ref, far_t,
):
    value = value_ref[...]
    rows = value.shape[0]
    low = adj_ref.shape[0]
    there = lent_ref[low + rows :, :]
    agg_ref[...] = own_chip((adj_ref, lent_ref), (value, there))
    both = jnp.concatenate([value, there], 0)
    direct_ref[...] = dot(both, self_ref[...]) + bias_ref[...].reshape(1, -1)
    both = jnp.concatenate([up_ref[...], lent_ref[low : low + rows, :]], 0)
    grad_ref[...] = dot_nt(both, weight_ref[...])
    far = col_ref.shape[0] // chips - rows
    column(chips, far, rows, lax.axis_index("core"), lent_ref, far_t, col_ref)


def mid_kernel(chips, adj_ref, lent_ref, agg_ref, part_ref, sum_ref, *refs):
    came, (agg_out, grad_ref) = refs[:-2], refs[-2:]
    rows = sum_ref.shape[0]
    chip, core = lax.axis_index("chip"), lax.axis_index("core")
    for i, ref in enumerate((adj_ref, lent_ref)):
        agg = agg_ref[i * rows : (i + 1) * rows, :]
        for k, block in enumerate(came):
            x = lax.rem(chip - k - 1 + chips, chips)
            low = pl.multiple_of((x * CORES + core) * rows, rows)
            agg = agg + dot(ref[pl.ds(low, rows), :], block[rows:, :])
        agg_out[i * rows : (i + 1) * rows, :] = agg
    grad_ref[:rows, :] = part_ref[:rows, :] + sum_ref[...]
    grad_ref[rows:, :] = part_ref[rows:, :]


def column_product(chips, hosts, adj_ref, value_ref, came, recv_ref, neigh_ref, halo):
    rows = value_ref.shape[0]
    far = halo.shape[0] // (chips * CORES)
    chip, core = lax.axis_index("chip"), lax.axis_index("core")
    pairs = [(square_of(adj_ref, chip, core, rows), value_ref[...])]
    for k, block in enumerate(came):
        x = lax.rem(chip - k - 1 + chips, chips)
        pairs.append((square_of(adj_ref, x, core, rows), block[rows:, :]))
    rows_here = halo_part(recv_ref, hosts, chips, 0)
    halo[...] = jnp.zeros_like(halo)
    for x in range(chips):
        low = pl.multiple_of((x * CORES + core) * far, far)
        halo[pl.ds(low, far), :] = rows_here[x * far : (x + 1) * far]
    agg = joint(pairs + far_pairs(chips, rows, adj_ref, halo))
    return dot(agg.astype(BF16), neigh_ref[...])


def there_kernel(chips, hosts, lent_ref, value_ref, recv_ref, neigh_ref, *refs):
    came, out_ref, halo = refs[:-2], refs[-2], refs[-1]
    out_ref[...] = column_product(
        chips, hosts, lent_ref, value_ref, came, recv_ref, neigh_ref, halo
    ).astype(BF16)


def here_kernel(
    chips, hosts, adj_ref, value_ref, recv_ref, neigh_ref, self_ref, bias_ref, up_ref, weight_ref,
    mine_ref, place_ref, *refs
):
    came, out_ref, grad_ref, halo = refs[:-3], refs[-3], refs[-2], refs[-1]
    rows = mine_ref.shape[0]
    grad = dot_nt(up_ref[...], weight_ref[...]) + mine_ref[...]
    for block in came:
        grad = grad + block[:rows, :].astype(F32)
    grad_ref[...] = grad + returned(place_ref, recv_ref, hosts, chips)
    out = column_product(chips, hosts, adj_ref, value_ref, came, recv_ref, neigh_ref, halo)
    out_ref[...] = out + dot(value_ref[...], self_ref[...]) + bias_ref[...].reshape(1, -1)


def put_halo(chips, far, rows, here_ref, shared_ref, halo):
    core = lax.axis_index("core")
    at = (chips - 1) * rows
    for x in range(chips):
        for side, ref in ((core, here_ref), (1 - core, shared_ref)):
            low = pl.multiple_of((x * CORES + side) * far, far)
            halo[pl.ds(low, far), :] = ref[at + x * far : at + (x + 1) * far, :]


def add_far(chips, rows, adj_ref, agg, shared_ref, halo):
    chip, core = lax.axis_index("chip"), lax.axis_index("core")
    pairs = []
    for k in range(chips - 1):
        x = lax.rem(chip - k - 1 + chips, chips)
        block = shared_ref[k * rows : (k + 1) * rows, :]
        pairs.append((square_of(adj_ref, x, 1 - core, rows), block))
    return agg + joint(pairs + far_pairs(chips, rows, adj_ref, halo))


def middle_kernel(
    chips,
    hosts,
    adj_ref,
    lent_ref,
    col_ref,
    col_two_ref,
    agg_ref,
    direct_ref,
    grad_ref,
    pick_ref,
    here_ref,
    shared_ref,
    neigh_one_ref,
    hidden_ref,
    grad_pre_ref,
    mine_ref,
    msg_ref,
    *rest,
):
    to_refs, halo = rest[:-1], rest[-1]
    far, rows = pick_ref.shape
    put_halo(chips, far, rows, here_ref, shared_ref, halo)
    parts = [
        add_far(chips, rows, ref, agg_ref[i * rows : (i + 1) * rows, :], shared_ref, halo)
        for i, ref in enumerate((adj_ref, lent_ref))
    ]
    agg = jnp.concatenate(parts, 0).astype(BF16)
    pre = direct_ref[...] + dot(agg, neigh_one_ref[...])
    sigmoid = jax.nn.sigmoid(pre)
    hidden = (pre[:rows] * sigmoid[:rows]).astype(BF16)
    hidden_ref[...] = hidden
    low = (chips - 1) * rows + chips * far
    add = shared_ref[low:, :].astype(F32)
    grad = jnp.concatenate([grad_ref[:rows, :], grad_ref[rows:, :] + add], 0)
    grad_pre = (grad * sigmoid * (1.0 + pre * (1.0 - sigmoid))).astype(BF16)
    grad_pre_ref[...] = grad_pre[:rows]
    u = dot_nt(grad_pre, neigh_one_ref[...]).astype(BF16)
    total = joint([(col_ref[...], u[:rows]), (col_two_ref[...], u[rows:])])
    picked = dot(pick_ref[...], hidden)
    deal(chips, hosts, total, picked, hidden, mine_ref, msg_ref, to_refs)


def last_kernel(here_ref, there_ref, output_ref):
    output_ref[...] = (here_ref[...] + there_ref[...].astype(F32)).astype(BF16)


def call(kernel, name, out_shape, in_specs, args, scratch=(), limit=32, flops=0):
    return pl.pallas_call(
        kernel,
        out_shape=out_shape,
        in_specs=in_specs,
        out_specs=jax.tree.map(lambda _: VMEM, out_shape),
        scratch_shapes=scratch,
        compiler_params=pltpu.CompilerParams(vmem_limit_bytes=limit * MIB),
        cost_estimate=pl.CostEstimate(
            flops=flops, bytes_accessed=flops // 1024, transcendentals=0
        ),
        name=name,
    )(*args)


def shift(value, axis, k):
    size = lax.axis_size(axis)
    return lax.ppermute(value, axis, [(i, (i + k) % size) for i in range(size)])


def shape(rows, width, kind=BF16):
    return jax.ShapeDtypeStruct((rows, width), kind)


def body(
    features,
    send_list,
    tile_dst,
    tile_src,
    tile_rows,
    tile_val,
    self_one,
    neigh_one,
    bias_one,
    self_two,
    neigh_two,
    bias_two,
    cotangent,
):
    chips = lax.axis_size("chip")
    hosts = lax.axis_size("hst")
    rows, width = features.shape
    tiles, blk = tile_val.shape[:2]
    send = send_list.shape[3]
    far = hosts * send
    all_rows = chips * CORES * (rows + far)
    count = chips * (rows + far)
    rows_shape = shape(rows, width)
    sum_shape = shape(rows, width, F32)
    both_shape = shape(CORES * rows, width, F32)
    square = 2 * rows * width * width
    halo = pltpu.VMEM((chips * CORES * far, width), BF16)
    halo_rows = (chips - 1) * rows + chips * far
    dealt = (
        sum_shape,
        jax.ShapeDtypeStruct((hosts * chips, 2 * send, width), BF16),
    ) + (shape(2 * rows, width),) * (chips - 1)

    def across(msg, to):
        terms = [shift(block, "chip", k + 1) for k, block in enumerate(to)]
        recv = lax.all_to_all(msg, ("chip", "hst"), split_axis=0, concat_axis=0, tiled=True)
        return terms, recv

    far_t = pltpu.VMEM((chips * CORES * far, rows), BF16)
    sums = jax.ShapeDtypeStruct(((rows // blk) * (all_rows // blk), blk // PARTS, blk), F32)
    give, up, picked, pick, *sums = call(
        functools.partial(prep_kernel, chips),
        "prep",
        (shape(count, width), rows_shape, shape(far, width), shape(far, rows)) + (sums,) * PARTS,
        [HBM] * 8,
        [
            pltpu.with_memory_space_constraint(value, pltpu.HBM)
            for value in (
                tile_dst,
                tile_src,
                tile_rows,
                send_list,
                tile_val,
                features,
                cotangent,
                neigh_two,
            )
        ],
        [
            pltpu.SMEM(tile_dst.shape, jnp.int32),
            pltpu.SMEM(tile_src.shape, jnp.int32),
            pltpu.SMEM(tile_rows.shape, jnp.int32),
            pltpu.SMEM(send_list.shape, jnp.int32),
            pltpu.VMEM(tile_val.shape, BF16),
            pltpu.VMEM(features.shape, BF16),
            pltpu.VMEM(cotangent.shape, BF16),
            pltpu.VMEM(neigh_two.shape, BF16),
            pltpu.VMEM((rows, rows), BF16),
            far_t,
            pltpu.VMEM((count, rows), BF16),
            pltpu.SemaphoreType.DMA((7 + CHUNKS,)),
        ],
    )
    came = shift(give, "core", 1)
    adj, col, keep, lend, place = call(
        functools.partial(rest_kernel, chips),
        "rest",
        (
            shape(all_rows, rows),
            shape(count, rows),
            shape(count, width),
            shape(all_rows + 2 * rows, width),
            shape(rows, chips * far),
        ),
        [VMEM] * (4 + PARTS),
        (up, cotangent, features, pick, *sums),
        [far_t],
        flops=3 * square,
    )
    lent = shift(lend, "core", 1)
    mine, msg, *to = call(
        functools.partial(core_sum_kernel, chips, hosts),
        "core_sum",
        dealt,
        [VMEM] * 4,
        (keep, came, features, picked),
        flops=60 * square,
    )
    terms, recv = across(msg, to)
    here, summed = call(
        functools.partial(merge_kernel, chips, hosts),
        "merge",
        (shape(halo_rows + rows, width), sum_shape),
        [VMEM] * (2 + chips),
        (recv, mine, place, *terms),
    )
    shared = shift(here, "core", 1)
    agg, direct, grad, col_two = call(
        functools.partial(early_one_kernel, chips),
        "early_one",
        (both_shape,) * 3 + (shape(count, rows),),
        [VMEM] * 7,
        (adj, lent, features, self_one, bias_one, cotangent, self_two),
        [far_t],
        flops=8 * square,
    )
    agg, grad = call(
        functools.partial(mid_kernel, chips),
        "mid",
        (both_shape,) * 2,
        [VMEM] * (4 + chips),
        (adj, lent, agg, grad, summed, *terms),
        flops=3 * square,
    )
    hidden, grad_pre, mine, msg, *to = call(
        functools.partial(middle_kernel, chips, hosts),
        "middle",
        (rows_shape,) * 2 + dealt,
        [VMEM] * 11,
        (adj, lent, col, col_two, agg, direct, grad, pick, here, shared, neigh_one),
        [halo],
        flops=12 * square,
    )
    terms, recv = across(msg, to)
    there = call(
        functools.partial(there_kernel, chips, hosts),
        "there",
        rows_shape,
        [VMEM] * (3 + chips),
        (lent, hidden, recv, neigh_two, *terms),
        [halo],
    )
    shared = shift(there, "core", 1)
    here, grad = call(
        functools.partial(here_kernel, chips, hosts),
        "here",
        (sum_shape,) * 2,
        [VMEM] * (9 + chips),
        (
            adj,
            hidden,
            recv,
            neigh_two,
            self_two,
            bias_two,
            grad_pre,
            self_one,
            mine,
            place,
            *terms,
        ),
        [halo],
        flops=7 * square,
    )
    output = call(last_kernel, "last", rows_shape, [VMEM] * 2, (here, shared))
    return output, grad


def solution(mesh):
    hosts, devs = mesh.devices.shape
    mesh = Mesh(mesh.devices.reshape(hosts, devs // CORES, CORES), ("hst", "chip", "core"))
    dev = ("chip", "core")
    every = ("hst", "chip", "core")
    return jax.shard_map(
        body,
        mesh=mesh,
        in_specs=(
            P(every, None),
            P("hst", dev, None, None),
            P(every),
            P(every),
            P(every),
            P(every, None, None),
            P(),
            P(),
            P(),
            P(),
            P(),
            P(),
            P(every, None),
        ),
        out_specs=(P(every, None), P(every, None)),
        check_vma=False,
    )
```

```python
import functools

import jax
import jax.numpy as jnp
from jax import lax
from jax.experimental import pallas as pl
from jax.experimental.pallas import tpu as pltpu
from jax.sharding import Mesh, PartitionSpec as P

F32 = jnp.float32
BF16 = jnp.bfloat16
MIB = 1024 * 1024
CHUNKS = 4
PARTS = 4
CORES = 2

VMEM = pl.BlockSpec(memory_space=pltpu.VMEM)
HBM = pl.BlockSpec(memory_space=pltpu.HBM)


def dot(a, b):
    return jnp.dot(a, b, preferred_element_type=F32)


def dot_nt(a, b):
    return lax.dot_general(a, b, (((1,), (1,)), ((), ())), preferred_element_type=F32)


def pick_matrix(send_ref, rows):
    hosts, send = send_ref.shape[2], send_ref.shape[3]
    place = lax.broadcasted_iota(jnp.int32, (send, rows), 0)
    column = lax.broadcasted_iota(jnp.int32, (send, rows), 1)
    parts = []
    for g in range(hosts):
        index = jnp.zeros((send, rows), jnp.int32)
        for s in range(send):
            index = jnp.where(place == s, send_ref[0, 0, g, s], index)
        parts.append(jnp.where(index == column, 1.0, 0.0).astype(F32))
    return jnp.concatenate(parts, 0).astype(BF16)


def column(chips, far, rows, side, adj_ref, far_t, out_ref):
    chip = lax.axis_index("chip")
    each = rows + far
    own_rows = chips * CORES * rows
    for j in range(far_t.shape[0] // rows):
        low = own_rows + j * rows
        far_t[j * rows : (j + 1) * rows, :] = adj_ref[low : low + rows, :].T
    for k in range(chips):
        d = lax.rem(chip + k, chips) * CORES + side
        at = k * each
        out_ref[at : at + rows, :] = adj_ref[pl.ds(pl.multiple_of(d * rows, rows), rows), :].T
        out_ref[at + rows : at + each, :] = far_t[pl.ds(pl.multiple_of(d * far, far), far), :]


def prep_kernel(
    chips,
    dst_hbm,
    src_hbm,
    rows_hbm,
    send_hbm,
    tile_hbm,
    features_hbm,
    cot_hbm,
    neigh_two_hbm,
    give_ref,
    up_ref,
    picked_ref,
    pick_ref,
    *rest,
):
    accs, rest = rest[:PARTS], rest[PARTS:]
    (
        dst_ref,
        src_ref,
        rows_ref,
        send_ref,
        tile_buf,
        features_ref,
        cot_ref,
        neigh_two_ref,
        square,
        far_t,
        col,
        sems,
    ) = rest
    tiles, blk = tile_buf.shape[0], tile_buf.shape[1]
    each = tiles // CHUNKS
    first = CHUNKS * 3 // 4
    chunks = [
        (tile_hbm.at[pl.ds(c * each, each)], tile_buf.at[pl.ds(c * each, each)])
        for c in range(CHUNKS)
    ]
    pairs = [(dst_hbm, dst_ref), (src_hbm, src_ref), (rows_hbm, rows_ref)]
    pairs += chunks[:first]
    pairs += [
        (cot_hbm, cot_ref),
        (neigh_two_hbm, neigh_two_ref),
        (features_hbm, features_ref),
        (send_hbm, send_ref),
    ]
    pairs += chunks[first:]
    copies = [pltpu.make_async_copy(a, b, sems.at[i]) for i, (a, b) in enumerate(pairs)]
    for copy in copies:
        copy.start()
    rows = features_ref.shape[0]
    bpd = rows // blk
    sources = accs[0].shape[0] // bpd
    part = accs[0].shape[1]
    far = send_ref.shape[2] * send_ref.shape[3]
    for acc in accs:
        acc[...] = jnp.zeros_like(acc)
    place = lax.broadcasted_iota(jnp.int32, (part, blk), 0)

    def add(t, carry):
        slot = dst_ref[t] * sources + src_ref[t]
        for i, acc in enumerate(accs):
            value = tile_buf[t, i * part : (i + 1) * part, :].astype(F32)
            acc[slot] += jnp.where(place < rows_ref[t] - i * part, value, 0.0)
        return carry

    for copy in copies[:3]:
        copy.wait()
    for c in range(first):
        copies[3 + c].wait()
        lax.fori_loop(c * each, (c + 1) * each, add, 0, unroll=True)
    for copy in copies[3 + first : 7 + first]:
        copy.wait()
    u = dot_nt(cot_ref[...], neigh_two_ref[...]).astype(BF16)
    up_ref[...] = u
    pick_ref[...] = pick_matrix(send_ref, rows)
    picked_ref[...] = dot(pick_ref[...], features_ref[...]).astype(BF16)
    for c in range(first, CHUNKS):
        copies[7 + c].wait()
        lax.fori_loop(c * each, (c + 1) * each, add, 0, unroll=True)
    chip, side = lax.axis_index("chip"), 1 - lax.axis_index("core")
    base = chips * CORES
    for j in range(far_t.shape[0] // rows):
        put_square(accs, bpd, base + j, square, 0)
        far_t[j * rows : (j + 1) * rows, :] = square[...].T
    for k in range(chips):
        d = lax.rem(chip + k, chips) * CORES + side
        at = k * (rows + far)
        put_square(accs, bpd, d, square, 0)
        col[at : at + rows, :] = square[...].T
        low = pl.multiple_of(d * far, far)
        col[at + rows : at + rows + far, :] = far_t[pl.ds(low, far), :]
    give_ref[...] = dot(col[...], u).astype(BF16)


def put_square(accs, bpd, d, out_ref, base):
    sources = accs[0].shape[0] // bpd
    part, blk = accs[0].shape[1:]
    for b in range(bpd):
        for j in range(bpd):
            for i, acc in enumerate(accs):
                low = base + b * blk + i * part
                value = acc[b * sources + d * bpd + j].astype(BF16)
                out_ref[low : low + part, j * blk : (j + 1) * blk] = value


def rest_kernel(chips, up_ref, cot_ref, value_ref, pick_ref, *refs):
    accs, (adj_ref, col_ref, keep_ref, lend_ref, place_ref, far_t) = refs[:PARTS], refs[PARTS:]
    rows = up_ref.shape[0]
    bpd = rows // accs[0].shape[2]
    for d in range(adj_ref.shape[0] // rows):
        put_square(accs, bpd, d, adj_ref, d * rows)
    far = col_ref.shape[0] // chips - rows
    column(chips, far, rows, lax.axis_index("core"), adj_ref, far_t, col_ref)
    keep_ref[...] = dot(col_ref[...], up_ref[...]).astype(BF16)
    low = adj_ref.shape[0]
    lend_ref[:low, :] = adj_ref[...]
    lend_ref[low : low + rows, :] = cot_ref[...]
    lend_ref[low + rows :, :] = value_ref[...]
    place_ref[...] = jnp.concatenate([pick_ref[...]] * chips, 0).T


def deal(chips, hosts, total, picked, value, mine_ref, msg_ref, to_refs):
    rows = value.shape[0]
    far = picked.shape[0]
    send = far // hosts
    each = rows + far
    chip = lax.axis_index("chip")
    mine_ref[...] = total[:rows]
    for k in range(chips):
        low = k * each + rows
        if k > 0:
            to_refs[k - 1][:rows, :] = total[k * each : low].astype(BF16)
            to_refs[k - 1][rows:, :] = value
        x = lax.rem(chip + k, chips)
        for g in range(hosts):
            at = low + g * send
            both = [picked[g * send : (g + 1) * send], total[at : at + send]]
            msg_ref[x * hosts + g] = jnp.concatenate(both, 0).astype(BF16)


def core_sum_kernel(
    chips, hosts, keep_ref, came_ref, value_ref, picked_ref, mine_ref, msg_ref, *rest
):
    total = keep_ref[...].astype(F32) + came_ref[...].astype(F32)
    picked = picked_ref[...].astype(F32)
    deal(chips, hosts, total, picked, value_ref[...], mine_ref, msg_ref, rest)


def halo_part(recv_ref, hosts, chips, part):
    send = recv_ref.shape[1] // 2
    low = part * send
    blocks = [
        recv_ref[x * hosts + g].astype(F32)[low : low + send]
        for x in range(chips)
        for g in range(hosts)
    ]
    return jnp.concatenate(blocks, 0).astype(BF16)


def merge_kernel(chips, hosts, recv_ref, mine_ref, place_ref, *refs):
    came, (out_ref, sum_ref) = refs[: chips - 1], refs[chips - 1 :]
    rows = mine_ref.shape[0]
    total = mine_ref[...]
    for k, ref in enumerate(came):
        total = total + ref[:rows, :].astype(F32)
        out_ref[k * rows : (k + 1) * rows, :] = ref[rows:, :]
    total = total + returned(place_ref, recv_ref, hosts, chips)
    sum_ref[...] = total
    low = len(came) * rows
    halo = halo_part(recv_ref, hosts, chips, 0)
    high = low + halo.shape[0]
    out_ref[low:high, :] = halo
    out_ref[high:, :] = total.astype(BF16)


def returned(place_ref, recv_ref, hosts, chips):
    return dot(place_ref[...], halo_part(recv_ref, hosts, chips, 1))


def joint(pairs):
    left = jnp.concatenate([a for a, _ in pairs], 1)
    return dot(left, jnp.concatenate([b for _, b in pairs], 0))


def square_of(adj_ref, x, side, rows):
    return adj_ref[pl.ds(pl.multiple_of((x * CORES + side) * rows, rows), rows), :]


def far_pairs(chips, rows, adj_ref, halo):
    base = chips * CORES * rows
    return [
        (adj_ref[base + low : base + low + rows, :], halo[low : low + rows, :])
        for low in range(0, halo.shape[0], rows)
    ]


def own_chip(adj_refs, blocks):
    chip, core = lax.axis_index("chip"), lax.axis_index("core")
    rows = blocks[0].shape[0]
    parts = [
        joint([(square_of(ref, chip, s, rows), b) for s, b in zip((core, 1 - core), blocks)])
        for ref in adj_refs
    ]
    return jnp.concatenate(parts, 0)


def early_one_kernel(
    chips, adj_ref, lent_ref, value_ref, self_ref, bias_ref, up_ref, weight_ref,
    agg_ref, direct_ref, grad_ref, col_ref, far_t,
):
    value = value_ref[...]
    rows = value.shape[0]
    low = adj_ref.shape[0]
    there = lent_ref[low + rows :, :]
    agg_ref[...] = own_chip((adj_ref, lent_ref), (value, there))
    both = jnp.concatenate([value, there], 0)
    direct_ref[...] = dot(both, self_ref[...]) + bias_ref[...].reshape(1, -1)
    both = jnp.concatenate([up_ref[...], lent_ref[low : low + rows, :]], 0)
    grad_ref[...] = dot_nt(both, weight_ref[...])
    far = col_ref.shape[0] // chips - rows
    column(chips, far, rows, lax.axis_index("core"), lent_ref, far_t, col_ref)


def mid_kernel(chips, adj_ref, lent_ref, agg_ref, part_ref, sum_ref, *refs):
    came, (agg_out, grad_ref) = refs[:-2], refs[-2:]
    rows = sum_ref.shape[0]
    chip, core = lax.axis_index("chip"), lax.axis_index("core")
    for i, ref in enumerate((adj_ref, lent_ref)):
        agg = agg_ref[i * rows : (i + 1) * rows, :]
        for k, block in enumerate(came):
            x = lax.rem(chip - k - 1 + chips, chips)
            low = pl.multiple_of((x * CORES + core) * rows, rows)
            agg = agg + dot(ref[pl.ds(low, rows), :], block[rows:, :])
        agg_out[i * rows : (i + 1) * rows, :] = agg
    grad_ref[:rows, :] = part_ref[:rows, :] + sum_ref[...]
    grad_ref[rows:, :] = part_ref[rows:, :]


def column_product(chips, hosts, adj_ref, value_ref, came, recv_ref, neigh_ref, halo):
    rows = value_ref.shape[0]
    far = halo.shape[0] // (chips * CORES)
    chip, core = lax.axis_index("chip"), lax.axis_index("core")
    pairs = [(square_of(adj_ref, chip, core, rows), value_ref[...])]
    for k, block in enumerate(came):
        x = lax.rem(chip - k - 1 + chips, chips)
        pairs.append((square_of(adj_ref, x, core, rows), block[rows:, :]))
    rows_here = halo_part(recv_ref, hosts, chips, 0)
    halo[...] = jnp.zeros_like(halo)
    for x in range(chips):
        low = pl.multiple_of((x * CORES + core) * far, far)
        halo[pl.ds(low, far), :] = rows_here[x * far : (x + 1) * far]
    agg = joint(pairs + far_pairs(chips, rows, adj_ref, halo))
    return dot(agg.astype(BF16), neigh_ref[...])


def there_kernel(chips, hosts, lent_ref, value_ref, recv_ref, neigh_ref, *refs):
    came, out_ref, halo = refs[:-2], refs[-2], refs[-1]
    out_ref[...] = column_product(
        chips, hosts, lent_ref, value_ref, came, recv_ref, neigh_ref, halo
    ).astype(BF16)


def here_kernel(
    chips, hosts, adj_ref, value_ref, recv_ref, neigh_ref, self_ref, bias_ref, up_ref, weight_ref,
    mine_ref, place_ref, *refs
):
    came, out_ref, grad_ref, halo = refs[:-3], refs[-3], refs[-2], refs[-1]
    rows = mine_ref.shape[0]
    grad = dot_nt(up_ref[...], weight_ref[...]) + mine_ref[...]
    for block in came:
        grad = grad + block[:rows, :].astype(F32)
    grad_ref[...] = grad + returned(place_ref, recv_ref, hosts, chips)
    out = column_product(chips, hosts, adj_ref, value_ref, came, recv_ref, neigh_ref, halo)
    out_ref[...] = out + dot(value_ref[...], self_ref[...]) + bias_ref[...].reshape(1, -1)


def put_halo(chips, far, rows, here_ref, shared_ref, halo):
    core = lax.axis_index("core")
    at = (chips - 1) * rows
    for x in range(chips):
        for side, ref in ((core, here_ref), (1 - core, shared_ref)):
            low = pl.multiple_of((x * CORES + side) * far, far)
            halo[pl.ds(low, far), :] = ref[at + x * far : at + (x + 1) * far, :]


def add_far(chips, rows, adj_ref, agg, shared_ref, halo):
    chip, core = lax.axis_index("chip"), lax.axis_index("core")
    pairs = []
    for k in range(chips - 1):
        x = lax.rem(chip - k - 1 + chips, chips)
        block = shared_ref[k * rows : (k + 1) * rows, :]
        pairs.append((square_of(adj_ref, x, 1 - core, rows), block))
    return agg + joint(pairs + far_pairs(chips, rows, adj_ref, halo))


def middle_kernel(
    chips,
    hosts,
    adj_ref,
    lent_ref,
    col_ref,
    col_two_ref,
    agg_ref,
    direct_ref,
    grad_ref,
    pick_ref,
    here_ref,
    shared_ref,
    neigh_one_ref,
    hidden_ref,
    grad_pre_ref,
    mine_ref,
    msg_ref,
    *rest,
):
    to_refs, halo = rest[:-1], rest[-1]
    far, rows = pick_ref.shape
    put_halo(chips, far, rows, here_ref, shared_ref, halo)
    parts = [
        add_far(chips, rows, ref, agg_ref[i * rows : (i + 1) * rows, :], shared_ref, halo)
        for i, ref in enumerate((adj_ref, lent_ref))
    ]
    agg = jnp.concatenate(parts, 0).astype(BF16)
    pre = direct_ref[...] + dot(agg, neigh_one_ref[...])
    sigmoid = jax.nn.sigmoid(pre)
    hidden = (pre[:rows] * sigmoid[:rows]).astype(BF16)
    hidden_ref[...] = hidden
    low = (chips - 1) * rows + chips * far
    add = shared_ref[low:, :].astype(F32)
    grad = jnp.concatenate([grad_ref[:rows, :], grad_ref[rows:, :] + add], 0)
    grad_pre = (grad * sigmoid * (1.0 + pre * (1.0 - sigmoid))).astype(BF16)
    grad_pre_ref[...] = grad_pre[:rows]
    u = dot_nt(grad_pre, neigh_one_ref[...]).astype(BF16)
    total = joint([(col_ref[...], u[:rows]), (col_two_ref[...], u[rows:])])
    picked = dot(pick_ref[...], hidden)
    deal(chips, hosts, total, picked, hidden, mine_ref, msg_ref, to_refs)


def last_kernel(here_ref, there_ref, output_ref):
    output_ref[...] = (here_ref[...] + there_ref[...].astype(F32)).astype(BF16)


def call(kernel, name, out_shape, in_specs, args, scratch=(), limit=32, flops=0):
    return pl.pallas_call(
        kernel,
        out_shape=out_shape,
        in_specs=in_specs,
        out_specs=jax.tree.map(lambda _: VMEM, out_shape),
        scratch_shapes=scratch,
        compiler_params=pltpu.CompilerParams(vmem_limit_bytes=limit * MIB),
        cost_estimate=pl.CostEstimate(
            flops=flops, bytes_accessed=flops // 1024, transcendentals=0
        ),
        name=name,
    )(*args)


def shift(value, axis, k):
    size = lax.axis_size(axis)
    return lax.ppermute(value, axis, [(i, (i + k) % size) for i in range(size)])


def shape(rows, width, kind=BF16):
    return jax.ShapeDtypeStruct((rows, width), kind)


def body(
    features,
    send_list,
    tile_dst,
    tile_src,
    tile_rows,
    tile_val,
    self_one,
    neigh_one,
    bias_one,
    self_two,
    neigh_two,
    bias_two,
    cotangent,
):
    chips = lax.axis_size("chip")
    hosts = lax.axis_size("hst")
    rows, width = features.shape
    tiles, blk = tile_val.shape[:2]
    send = send_list.shape[3]
    far = hosts * send
    all_rows = chips * CORES * (rows + far)
    count = chips * (rows + far)
    rows_shape = shape(rows, width)
    sum_shape = shape(rows, width, F32)
    both_shape = shape(CORES * rows, width, F32)
    square = 2 * rows * width * width
    halo = pltpu.VMEM((chips * CORES * far, width), BF16)
    halo_rows = (chips - 1) * rows + chips * far
    dealt = (
        sum_shape,
        jax.ShapeDtypeStruct((hosts * chips, 2 * send, width), BF16),
    ) + (shape(2 * rows, width),) * (chips - 1)

    def across(msg, to):
        terms = [shift(block, "chip", k + 1) for k, block in enumerate(to)]
        recv = lax.all_to_all(msg, ("chip", "hst"), split_axis=0, concat_axis=0, tiled=True)
        return terms, recv

    far_t = pltpu.VMEM((chips * CORES * far, rows), BF16)
    sums = jax.ShapeDtypeStruct(((rows // blk) * (all_rows // blk), blk // PARTS, blk), F32)
    give, up, picked, pick, *sums = call(
        functools.partial(prep_kernel, chips),
        "prep",
        (shape(count, width), rows_shape, shape(far, width), shape(far, rows)) + (sums,) * PARTS,
        [HBM] * 8,
        [
            pltpu.with_memory_space_constraint(value, pltpu.HBM)
            for value in (
                tile_dst,
                tile_src,
                tile_rows,
                send_list,
                tile_val,
                features,
                cotangent,
                neigh_two,
            )
        ],
        [
            pltpu.SMEM(tile_dst.shape, jnp.int32),
            pltpu.SMEM(tile_src.shape, jnp.int32),
            pltpu.SMEM(tile_rows.shape, jnp.int32),
            pltpu.SMEM(send_list.shape, jnp.int32),
            pltpu.VMEM(tile_val.shape, BF16),
            pltpu.VMEM(features.shape, BF16),
            pltpu.VMEM(cotangent.shape, BF16),
            pltpu.VMEM(neigh_two.shape, BF16),
            pltpu.VMEM((rows, rows), BF16),
            far_t,
            pltpu.VMEM((count, rows), BF16),
            pltpu.SemaphoreType.DMA((7 + CHUNKS,)),
        ],
    )
    came = shift(give, "core", 1)
    adj, col, keep, lend, place = call(
        functools.partial(rest_kernel, chips),
        "rest",
        (
            shape(all_rows, rows),
            shape(count, rows),
            shape(count, width),
            shape(all_rows + 2 * rows, width),
            shape(rows, chips * far),
        ),
        [VMEM] * (4 + PARTS),
        (up, cotangent, features, pick, *sums),
        [far_t],
        flops=3 * square,
    )
    lent = shift(lend, "core", 1)
    mine, msg, *to = call(
        functools.partial(core_sum_kernel, chips, hosts),
        "core_sum",
        dealt,
        [VMEM] * 4,
        (keep, came, features, picked),
        flops=60 * square,
    )
    terms, recv = across(msg, to)
    here, summed = call(
        functools.partial(merge_kernel, chips, hosts),
        "merge",
        (shape(halo_rows + rows, width), sum_shape),
        [VMEM] * (2 + chips),
        (recv, mine, place, *terms),
    )
    shared = shift(here, "core", 1)
    agg, direct, grad, col_two = call(
        functools.partial(early_one_kernel, chips),
        "early_one",
        (both_shape,) * 3 + (shape(count, rows),),
        [VMEM] * 7,
        (adj, lent, features, self_one, bias_one, cotangent, self_two),
        [far_t],
        flops=8 * square,
    )
    agg, grad = call(
        functools.partial(mid_kernel, chips),
        "mid",
        (both_shape,) * 2,
        [VMEM] * (4 + chips),
        (adj, lent, agg, grad, summed, *terms),
        flops=3 * square,
    )
    hidden, grad_pre, mine, msg, *to = call(
        functools.partial(middle_kernel, chips, hosts),
        "middle",
        (rows_shape,) * 2 + dealt,
        [VMEM] * 11,
        (adj, lent, col, col_two, agg, direct, grad, pick, here, shared, neigh_one),
        [halo],
        flops=12 * square,
    )
    terms, recv = across(msg, to)
    there = call(
        functools.partial(there_kernel, chips, hosts),
        "there",
        rows_shape,
        [VMEM] * (3 + chips),
        (lent, hidden, recv, neigh_two, *terms),
        [halo],
    )
    shared = shift(there, "core", 1)
    here, grad = call(
        functools.partial(here_kernel, chips, hosts),
        "here",
        (sum_shape,) * 2,
        [VMEM] * (9 + chips),
        (
            adj,
            hidden,
            recv,
            neigh_two,
            self_two,
            bias_two,
            grad_pre,
            self_one,
            mine,
            place,
            *terms,
        ),
        [halo],
        flops=7 * square,
    )
    output = call(last_kernel, "last", rows_shape, [VMEM] * 2, (here, shared))
    return output, grad


def solution(mesh):
    hosts, devs = mesh.devices.shape
    mesh = Mesh(mesh.devices.reshape(hosts, devs // CORES, CORES), ("hst", "chip", "core"))
    dev = ("chip", "core")
    every = ("hst", "chip", "core")
    return jax.shard_map(
        body,
        mesh=mesh,
        in_specs=(
            P(every, None),
            P("hst", dev, None, None),
            P(every),
            P(every),
            P(every),
            P(every, None, None),
            P(),
            P(),
            P(),
            P(),
            P(),
            P(),
            P(every, None),
        ),
        out_specs=(P(every, None), P(every, None)),
        check_vma=False,
    )
```

```python
import functools

import jax
import jax.numpy as jnp
from jax import lax
from jax.experimental import pallas as pl
from jax.experimental.pallas import tpu as pltpu
from jax.sharding import Mesh, PartitionSpec as P

F32 = jnp.float32
BF16 = jnp.bfloat16
MIB = 1024 * 1024
CHUNKS = 8
PARTS = 4
CORES = 2

VMEM = pl.BlockSpec(memory_space=pltpu.VMEM)
HBM = pl.BlockSpec(memory_space=pltpu.HBM)


def dot(a, b):
    return jnp.dot(a, b, preferred_element_type=F32)


def dot_nt(a, b):
    return lax.dot_general(a, b, (((1,), (1,)), ((), ())), preferred_element_type=F32)


def pick_matrix(send_ref, rows):
    hosts, send = send_ref.shape[2], send_ref.shape[3]
    place = lax.broadcasted_iota(jnp.int32, (send, rows), 0)
    column = lax.broadcasted_iota(jnp.int32, (send, rows), 1)
    parts = []
    for g in range(hosts):
        index = jnp.zeros((send, rows), jnp.int32)
        for s in range(send):
            index = jnp.where(place == s, send_ref[0, 0, g, s], index)
        parts.append(jnp.where(index == column, 1.0, 0.0).astype(F32))
    return jnp.concatenate(parts, 0).astype(BF16)


def column(chips, far, rows, side, adj_ref, far_t, out_ref):
    chip = lax.axis_index("chip")
    each = rows + far
    own_rows = chips * CORES * rows
    for j in range(far_t.shape[0] // rows):
        low = own_rows + j * rows
        far_t[j * rows : (j + 1) * rows, :] = adj_ref[low : low + rows, :].T
    for k in range(chips):
        d = lax.rem(chip + k, chips) * CORES + side
        at = k * each
        out_ref[at : at + rows, :] = adj_ref[pl.ds(pl.multiple_of(d * rows, rows), rows), :].T
        out_ref[at + rows : at + each, :] = far_t[pl.ds(pl.multiple_of(d * far, far), far), :]


def prep_kernel(
    chips,
    dst_hbm,
    src_hbm,
    rows_hbm,
    send_hbm,
    tile_hbm,
    features_hbm,
    cot_hbm,
    neigh_two_hbm,
    give_ref,
    up_ref,
    picked_ref,
    pick_ref,
    *rest,
):
    accs, rest = rest[:PARTS], rest[PARTS:]
    (
        dst_ref,
        src_ref,
        rows_ref,
        send_ref,
        tile_buf,
        features_ref,
        cot_ref,
        neigh_two_ref,
        square,
        far_t,
        col,
        sems,
    ) = rest
    tiles, blk = tile_buf.shape[0], tile_buf.shape[1]
    each = tiles // CHUNKS
    first = CHUNKS * 3 // 4
    chunks = [
        (tile_hbm.at[pl.ds(c * each, each)], tile_buf.at[pl.ds(c * each, each)])
        for c in range(CHUNKS)
    ]
    pairs = [(dst_hbm, dst_ref), (src_hbm, src_ref), (rows_hbm, rows_ref)]
    pairs += chunks[:first]
    pairs += [
        (cot_hbm, cot_ref),
        (neigh_two_hbm, neigh_two_ref),
        (features_hbm, features_ref),
        (send_hbm, send_ref),
    ]
    pairs += chunks[first:]
    copies = [pltpu.make_async_copy(a, b, sems.at[i]) for i, (a, b) in enumerate(pairs)]
    for copy in copies:
        copy.start()
    rows = features_ref.shape[0]
    bpd = rows // blk
    sources = accs[0].shape[0] // bpd
    part = accs[0].shape[1]
    far = send_ref.shape[2] * send_ref.shape[3]
    for acc in accs:
        acc[...] = jnp.zeros_like(acc)
    place = lax.broadcasted_iota(jnp.int32, (part, blk), 0)

    def add(t, carry):
        slot = dst_ref[t] * sources + src_ref[t]
        for i, acc in enumerate(accs):
            value = tile_buf[t, i * part : (i + 1) * part, :].astype(F32)
            acc[slot] += jnp.where(place < rows_ref[t] - i * part, value, 0.0)
        return carry

    for copy in copies[:3]:
        copy.wait()
    for c in range(first):
        copies[3 + c].wait()
        lax.fori_loop(c * each, (c + 1) * each, add, 0, unroll=True)
    for copy in copies[3 + first : 7 + first]:
        copy.wait()
    u = dot_nt(cot_ref[...], neigh_two_ref[...]).astype(BF16)
    up_ref[...] = u
    pick_ref[...] = pick_matrix(send_ref, rows)
    picked_ref[...] = dot(pick_ref[...], features_ref[...]).astype(BF16)
    for c in range(first, CHUNKS):
        copies[7 + c].wait()
        lax.fori_loop(c * each, (c + 1) * each, add, 0, unroll=True)
    chip, side = lax.axis_index("chip"), 1 - lax.axis_index("core")
    base = chips * CORES
    for j in range(far_t.shape[0] // rows):
        put_square(accs, bpd, base + j, square, 0)
        far_t[j * rows : (j + 1) * rows, :] = square[...].T
    for k in range(chips):
        d = lax.rem(chip + k, chips) * CORES + side
        at = k * (rows + far)
        put_square(accs, bpd, d, square, 0)
        col[at : at + rows, :] = square[...].T
        low = pl.multiple_of(d * far, far)
        col[at + rows : at + rows + far, :] = far_t[pl.ds(low, far), :]
    give_ref[...] = dot(col[...], u).astype(BF16)


def put_square(accs, bpd, d, out_ref, base):
    sources = accs[0].shape[0] // bpd
    part, blk = accs[0].shape[1:]
    for b in range(bpd):
        for j in range(bpd):
            for i, acc in enumerate(accs):
                low = base + b * blk + i * part
                value = acc[b * sources + d * bpd + j].astype(BF16)
                out_ref[low : low + part, j * blk : (j + 1) * blk] = value


def rest_kernel(chips, up_ref, cot_ref, value_ref, pick_ref, *refs):
    accs, (adj_ref, col_ref, keep_ref, lend_ref, place_ref, far_t) = refs[:PARTS], refs[PARTS:]
    rows = up_ref.shape[0]
    bpd = rows // accs[0].shape[2]
    for d in range(adj_ref.shape[0] // rows):
        put_square(accs, bpd, d, adj_ref, d * rows)
    far = col_ref.shape[0] // chips - rows
    column(chips, far, rows, lax.axis_index("core"), adj_ref, far_t, col_ref)
    keep_ref[...] = dot(col_ref[...], up_ref[...]).astype(BF16)
    low = adj_ref.shape[0]
    lend_ref[:low, :] = adj_ref[...]
    lend_ref[low : low + rows, :] = cot_ref[...]
    lend_ref[low + rows :, :] = value_ref[...]
    place_ref[...] = jnp.concatenate([pick_ref[...]] * chips, 0).T


def deal(chips, hosts, total, picked, value, mine_ref, msg_ref, to_refs):
    rows = value.shape[0]
    far = picked.shape[0]
    send = far // hosts
    each = rows + far
    chip, core = lax.axis_index("chip"), lax.axis_index("core")
    mine_ref[...] = total[:rows]
    for k in range(chips):
        low = k * each + rows
        if k > 0:
            to_refs[k - 1][:rows, :] = total[k * each : low].astype(BF16)
            to_refs[k - 1][rows:, :] = value
        x = lax.rem(chip + k, chips)
        for g in range(hosts):
            at = low + g * send
            to = (x * hosts + g) * CORES
            msg_ref[to + core] = total[at : at + send].astype(BF16)
            msg_ref[to + 1 - core] = picked[g * send : (g + 1) * send].astype(BF16)


def core_sum_kernel(
    chips, hosts, keep_ref, came_ref, value_ref, picked_ref, mine_ref, msg_ref, *rest
):
    total = keep_ref[...].astype(F32) + came_ref[...].astype(F32)
    picked = picked_ref[...].astype(F32)
    deal(chips, hosts, total, picked, value_ref[...], mine_ref, msg_ref, rest)


def received(recv_ref, hosts, chips, side):
    blocks = [
        recv_ref[(x * hosts + g) * CORES + side].astype(F32)
        for x in range(chips)
        for g in range(hosts)
    ]
    return jnp.concatenate(blocks, 0).astype(BF16)


def merge_kernel(chips, hosts, recv_ref, mine_ref, place_ref, *refs):
    came, (out_ref, sum_ref) = refs[: chips - 1], refs[chips - 1 :]
    rows = mine_ref.shape[0]
    total = mine_ref[...]
    for k, ref in enumerate(came):
        total = total + ref[:rows, :].astype(F32)
        out_ref[k * rows : (k + 1) * rows, :] = ref[rows:, :]
    total = total + returned(place_ref, recv_ref, hosts, chips)
    sum_ref[...] = total
    low = len(came) * rows
    halo = received(recv_ref, hosts, chips, 1 - lax.axis_index("core"))
    high = low + halo.shape[0]
    out_ref[low:high, :] = halo
    out_ref[high:, :] = total.astype(BF16)


def returned(place_ref, recv_ref, hosts, chips):
    return dot(place_ref[...], received(recv_ref, hosts, chips, lax.axis_index("core")))


def joint(pairs):
    left = jnp.concatenate([a for a, _ in pairs], 1)
    return dot(left, jnp.concatenate([b for _, b in pairs], 0))


def square_of(adj_ref, x, side, rows):
    return adj_ref[pl.ds(pl.multiple_of((x * CORES + side) * rows, rows), rows), :]


def far_pairs(chips, rows, adj_ref, halo):
    base = chips * CORES * rows
    return [
        (adj_ref[base + low : base + low + rows, :], halo[low : low + rows, :])
        for low in range(0, halo.shape[0], rows)
    ]


def own_chip(adj_refs, blocks):
    chip, core = lax.axis_index("chip"), lax.axis_index("core")
    rows = blocks[0].shape[0]
    parts = [
        joint([(square_of(ref, chip, s, rows), b) for s, b in zip((core, 1 - core), blocks)])
        for ref in adj_refs
    ]
    return jnp.concatenate(parts, 0)


def early_one_kernel(
    chips, adj_ref, lent_ref, value_ref, self_ref, bias_ref, up_ref, weight_ref,
    agg_ref, direct_ref, grad_ref, col_ref, far_t,
):
    value = value_ref[...]
    rows = value.shape[0]
    low = adj_ref.shape[0]
    there = lent_ref[low + rows :, :]
    agg_ref[...] = own_chip((adj_ref, lent_ref), (value, there))
    both = jnp.concatenate([value, there], 0)
    direct_ref[...] = dot(both, self_ref[...]) + bias_ref[...].reshape(1, -1)
    both = jnp.concatenate([up_ref[...], lent_ref[low : low + rows, :]], 0)
    grad_ref[...] = dot_nt(both, weight_ref[...])
    far = col_ref.shape[0] // chips - rows
    column(chips, far, rows, lax.axis_index("core"), lent_ref, far_t, col_ref)


def mid_kernel(chips, adj_ref, lent_ref, agg_ref, part_ref, sum_ref, *refs):
    came, (agg_out, grad_ref) = refs[:-2], refs[-2:]
    rows = sum_ref.shape[0]
    chip, core = lax.axis_index("chip"), lax.axis_index("core")
    for i, ref in enumerate((adj_ref, lent_ref)):
        agg = agg_ref[i * rows : (i + 1) * rows, :]
        for k, block in enumerate(came):
            x = lax.rem(chip - k - 1 + chips, chips)
            low = pl.multiple_of((x * CORES + core) * rows, rows)
            agg = agg + dot(ref[pl.ds(low, rows), :], block[rows:, :])
        agg_out[i * rows : (i + 1) * rows, :] = agg
    grad_ref[:rows, :] = part_ref[:rows, :] + sum_ref[...]
    grad_ref[rows:, :] = part_ref[rows:, :]


def column_product(chips, hosts, adj_ref, value_ref, came, recv_ref, neigh_ref, halo):
    rows = value_ref.shape[0]
    far = halo.shape[0] // (chips * CORES)
    chip, core = lax.axis_index("chip"), lax.axis_index("core")
    pairs = [(square_of(adj_ref, chip, core, rows), value_ref[...])]
    for k, block in enumerate(came):
        x = lax.rem(chip - k - 1 + chips, chips)
        pairs.append((square_of(adj_ref, x, core, rows), block[rows:, :]))
    rows_here = received(recv_ref, hosts, chips, 1 - core)
    halo[...] = jnp.zeros_like(halo)
    for x in range(chips):
        low = pl.multiple_of((x * CORES + 1 - core) * far, far)
        halo[pl.ds(low, far), :] = rows_here[x * far : (x + 1) * far]
    agg = joint(pairs + far_pairs(chips, rows, adj_ref, halo))
    return dot(agg.astype(BF16), neigh_ref[...])


def there_kernel(chips, hosts, lent_ref, value_ref, recv_ref, neigh_ref, *refs):
    came, out_ref, halo = refs[:-2], refs[-2], refs[-1]
    out_ref[...] = column_product(
        chips, hosts, lent_ref, value_ref, came, recv_ref, neigh_ref, halo
    ).astype(BF16)


def here_kernel(
    chips, hosts, adj_ref, value_ref, recv_ref, neigh_ref, self_ref, bias_ref, up_ref, weight_ref,
    mine_ref, place_ref, *refs
):
    came, out_ref, grad_ref, halo = refs[:-3], refs[-3], refs[-2], refs[-1]
    rows = mine_ref.shape[0]
    grad = dot_nt(up_ref[...], weight_ref[...]) + mine_ref[...]
    for block in came:
        grad = grad + block[:rows, :].astype(F32)
    grad_ref[...] = grad + returned(place_ref, recv_ref, hosts, chips)
    out = column_product(chips, hosts, adj_ref, value_ref, came, recv_ref, neigh_ref, halo)
    out_ref[...] = out + dot(value_ref[...], self_ref[...]) + bias_ref[...].reshape(1, -1)


def put_halo(chips, far, rows, here_ref, shared_ref, halo):
    core = lax.axis_index("core")
    at = (chips - 1) * rows
    for x in range(chips):
        for side, ref in ((1 - core, here_ref), (core, shared_ref)):
            low = pl.multiple_of((x * CORES + side) * far, far)
            halo[pl.ds(low, far), :] = ref[at + x * far : at + (x + 1) * far, :]


def add_far(chips, rows, adj_ref, agg, shared_ref, halo):
    chip, core = lax.axis_index("chip"), lax.axis_index("core")
    pairs = []
    for k in range(chips - 1):
        x = lax.rem(chip - k - 1 + chips, chips)
        block = shared_ref[k * rows : (k + 1) * rows, :]
        pairs.append((square_of(adj_ref, x, 1 - core, rows), block))
    return agg + joint(pairs + far_pairs(chips, rows, adj_ref, halo))


def middle_kernel(
    chips,
    hosts,
    adj_ref,
    lent_ref,
    col_ref,
    col_two_ref,
    agg_ref,
    direct_ref,
    grad_ref,
    pick_ref,
    here_ref,
    shared_ref,
    neigh_one_ref,
    hidden_ref,
    grad_pre_ref,
    mine_ref,
    msg_ref,
    *rest,
):
    to_refs, halo = rest[:-1], rest[-1]
    far, rows = pick_ref.shape
    put_halo(chips, far, rows, here_ref, shared_ref, halo)
    parts = [
        add_far(chips, rows, ref, agg_ref[i * rows : (i + 1) * rows, :], shared_ref, halo)
        for i, ref in enumerate((adj_ref, lent_ref))
    ]
    agg = jnp.concatenate(parts, 0).astype(BF16)
    pre = direct_ref[...] + dot(agg, neigh_one_ref[...])
    sigmoid = jax.nn.sigmoid(pre)
    hidden = (pre[:rows] * sigmoid[:rows]).astype(BF16)
    hidden_ref[...] = hidden
    low = (chips - 1) * rows + chips * far
    add = shared_ref[low:, :].astype(F32)
    grad = jnp.concatenate([grad_ref[:rows, :], grad_ref[rows:, :] + add], 0)
    grad_pre = (grad * sigmoid * (1.0 + pre * (1.0 - sigmoid))).astype(BF16)
    grad_pre_ref[...] = grad_pre[:rows]
    u = dot_nt(grad_pre, neigh_one_ref[...]).astype(BF16)
    total = joint([(col_ref[...], u[:rows]), (col_two_ref[...], u[rows:])])
    picked = dot(pick_ref[...], hidden)
    deal(chips, hosts, total, picked, hidden, mine_ref, msg_ref, to_refs)


def last_kernel(here_ref, there_ref, output_ref):
    output_ref[...] = (here_ref[...] + there_ref[...].astype(F32)).astype(BF16)


def call(kernel, name, out_shape, in_specs, args, scratch=(), limit=32, flops=0):
    return pl.pallas_call(
        kernel,
        out_shape=out_shape,
        in_specs=in_specs,
        out_specs=jax.tree.map(lambda _: VMEM, out_shape),
        scratch_shapes=scratch,
        compiler_params=pltpu.CompilerParams(vmem_limit_bytes=limit * MIB),
        cost_estimate=pl.CostEstimate(
            flops=flops, bytes_accessed=flops // 1024, transcendentals=0
        ),
        name=name,
    )(*args)


def shift(value, axis, k):
    size = lax.axis_size(axis)
    return lax.ppermute(value, axis, [(i, (i + k) % size) for i in range(size)])


def shape(rows, width, kind=BF16):
    return jax.ShapeDtypeStruct((rows, width), kind)


def body(
    features,
    send_list,
    tile_dst,
    tile_src,
    tile_rows,
    tile_val,
    self_one,
    neigh_one,
    bias_one,
    self_two,
    neigh_two,
    bias_two,
    cotangent,
):
    chips = lax.axis_size("chip")
    hosts = lax.axis_size("hst")
    rows, width = features.shape
    tiles, blk = tile_val.shape[:2]
    send = send_list.shape[3]
    far = hosts * send
    all_rows = chips * CORES * (rows + far)
    count = chips * (rows + far)
    rows_shape = shape(rows, width)
    sum_shape = shape(rows, width, F32)
    both_shape = shape(CORES * rows, width, F32)
    square = 2 * rows * width * width
    halo = pltpu.VMEM((chips * CORES * far, width), BF16)
    halo_rows = (chips - 1) * rows + chips * far
    dealt = (
        sum_shape,
        jax.ShapeDtypeStruct((chips * hosts * CORES, send, width), BF16),
    ) + (shape(2 * rows, width),) * (chips - 1)

    def across(msg, to):
        terms = [shift(block, "chip", k + 1) for k, block in enumerate(to)]
        recv = lax.all_to_all(msg, ("chip", "hst", "core"), split_axis=0, concat_axis=0, tiled=True)
        return terms, recv

    far_t = pltpu.VMEM((chips * CORES * far, rows), BF16)
    sums = jax.ShapeDtypeStruct(((rows // blk) * (all_rows // blk), blk // PARTS, blk), F32)
    give, up, picked, pick, *sums = call(
        functools.partial(prep_kernel, chips),
        "prep",
        (shape(count, width), rows_shape, shape(far, width), shape(far, rows)) + (sums,) * PARTS,
        [HBM] * 8,
        [
            pltpu.with_memory_space_constraint(value, pltpu.HBM)
            for value in (
                tile_dst,
                tile_src,
                tile_rows,
                send_list,
                tile_val,
                features,
                cotangent,
                neigh_two,
            )
        ],
        [
            pltpu.SMEM(tile_dst.shape, jnp.int32),
            pltpu.SMEM(tile_src.shape, jnp.int32),
            pltpu.SMEM(tile_rows.shape, jnp.int32),
            pltpu.SMEM(send_list.shape, jnp.int32),
            pltpu.VMEM(tile_val.shape, BF16),
            pltpu.VMEM(features.shape, BF16),
            pltpu.VMEM(cotangent.shape, BF16),
            pltpu.VMEM(neigh_two.shape, BF16),
            pltpu.VMEM((rows, rows), BF16),
            far_t,
            pltpu.VMEM((count, rows), BF16),
            pltpu.SemaphoreType.DMA((7 + CHUNKS,)),
        ],
    )
    came = shift(give, "core", 1)
    adj, col, keep, lend, place = call(
        functools.partial(rest_kernel, chips),
        "rest",
        (
            shape(all_rows, rows),
            shape(count, rows),
            shape(count, width),
            shape(all_rows + 2 * rows, width),
            shape(rows, chips * far),
        ),
        [VMEM] * (4 + PARTS),
        (up, cotangent, features, pick, *sums),
        [far_t],
        flops=3 * square,
    )
    lent = shift(lend, "core", 1)
    mine, msg, *to = call(
        functools.partial(core_sum_kernel, chips, hosts),
        "core_sum",
        dealt,
        [VMEM] * 4,
        (keep, came, features, picked),
        flops=60 * square,
    )
    terms, recv = across(msg, to)
    here, summed = call(
        functools.partial(merge_kernel, chips, hosts),
        "merge",
        (shape(halo_rows + rows, width), sum_shape),
        [VMEM] * (2 + chips),
        (recv, mine, place, *terms),
    )
    shared = shift(here, "core", 1)
    agg, direct, grad, col_two = call(
        functools.partial(early_one_kernel, chips),
        "early_one",
        (both_shape,) * 3 + (shape(count, rows),),
        [VMEM] * 7,
        (adj, lent, features, self_one, bias_one, cotangent, self_two),
        [far_t],
        flops=8 * square,
    )
    agg, grad = call(
        functools.partial(mid_kernel, chips),
        "mid",
        (both_shape,) * 2,
        [VMEM] * (4 + chips),
        (adj, lent, agg, grad, summed, *terms),
        flops=3 * square,
    )
    hidden, grad_pre, mine, msg, *to = call(
        functools.partial(middle_kernel, chips, hosts),
        "middle",
        (rows_shape,) * 2 + dealt,
        [VMEM] * 11,
        (adj, lent, col, col_two, agg, direct, grad, pick, here, shared, neigh_one),
        [halo],
        flops=12 * square,
    )
    terms, recv = across(msg, to)
    there = call(
        functools.partial(there_kernel, chips, hosts),
        "there",
        rows_shape,
        [VMEM] * (3 + chips),
        (lent, hidden, recv, neigh_two, *terms),
        [halo],
    )
    shared = shift(there, "core", 1)
    here, grad = call(
        functools.partial(here_kernel, chips, hosts),
        "here",
        (sum_shape,) * 2,
        [VMEM] * (9 + chips),
        (
            adj,
            hidden,
            recv,
            neigh_two,
            self_two,
            bias_two,
            grad_pre,
            self_one,
            mine,
            place,
            *terms,
        ),
        [halo],
        flops=7 * square,
    )
    output = call(last_kernel, "last", rows_shape, [VMEM] * 2, (here, shared))
    return output, grad


def solution(mesh):
    hosts, devs = mesh.devices.shape
    mesh = Mesh(mesh.devices.reshape(hosts, devs // CORES, CORES), ("hst", "chip", "core"))
    dev = ("chip", "core")
    every = ("hst", "chip", "core")
    return jax.shard_map(
        body,
        mesh=mesh,
        in_specs=(
            P(every, None),
            P("hst", dev, None, None),
            P(every),
            P(every),
            P(every),
            P(every, None, None),
            P(),
            P(),
            P(),
            P(),
            P(),
            P(),
            P(every, None),
        ),
        out_specs=(P(every, None), P(every, None)),
        check_vma=False,
    )
```

```python
import functools

import jax
import jax.numpy as jnp
from jax import lax
from jax.experimental import pallas as pl
from jax.experimental.pallas import tpu as pltpu
from jax.sharding import Mesh, PartitionSpec as P

F32 = jnp.float32
BF16 = jnp.bfloat16
MIB = 1024 * 1024
CHUNKS = 8
PARTS = 4
CORES = 2

VMEM = pl.BlockSpec(memory_space=pltpu.VMEM)
HBM = pl.BlockSpec(memory_space=pltpu.HBM)


def dot(a, b):
    return jnp.dot(a, b, preferred_element_type=F32)


def dot_nt(a, b):
    return lax.dot_general(a, b, (((1,), (1,)), ((), ())), preferred_element_type=F32)


def pick_matrix(send_ref, rows):
    hosts, send = send_ref.shape[2], send_ref.shape[3]
    place = lax.broadcasted_iota(jnp.int32, (send, rows), 0)
    column = lax.broadcasted_iota(jnp.int32, (send, rows), 1)
    parts = []
    for g in range(hosts):
        index = jnp.zeros((send, rows), jnp.int32)
        for s in range(send):
            index = jnp.where(place == s, send_ref[0, 0, g, s], index)
        parts.append(jnp.where(index == column, 1.0, 0.0).astype(F32))
    return jnp.concatenate(parts, 0).astype(BF16)


def column(chips, far, rows, side, adj_ref, far_t, out_ref):
    chip = lax.axis_index("chip")
    each = rows + far
    own_rows = chips * CORES * rows
    for j in range(far_t.shape[0] // rows):
        low = own_rows + j * rows
        far_t[j * rows : (j + 1) * rows, :] = adj_ref[low : low + rows, :].T
    for k in range(chips):
        d = lax.rem(chip + k, chips) * CORES + side
        at = k * each
        out_ref[at : at + rows, :] = adj_ref[pl.ds(pl.multiple_of(d * rows, rows), rows), :].T
        out_ref[at + rows : at + each, :] = far_t[pl.ds(pl.multiple_of(d * far, far), far), :]


def far_columns(chips, far_t, out_ref):
    far = far_t.shape[0] // (chips * CORES)
    core = lax.axis_index("core")
    parts = [
        far_t[pl.ds(pl.multiple_of((x * CORES + side) * far, far), far), :]
        for side in (1 - core, core)
        for x in range(chips)
    ]
    out_ref[...] = jnp.concatenate(parts, 0).T


def prep_kernel(
    chips,
    dst_hbm,
    src_hbm,
    rows_hbm,
    send_hbm,
    tile_hbm,
    features_hbm,
    cot_hbm,
    neigh_two_hbm,
    give_ref,
    up_ref,
    picked_ref,
    pick_ref,
    *rest,
):
    accs, rest = rest[:PARTS], rest[PARTS:]
    (
        dst_ref,
        src_ref,
        rows_ref,
        send_ref,
        tile_buf,
        features_ref,
        cot_ref,
        neigh_two_ref,
        square,
        far_t,
        col,
        sems,
    ) = rest
    tiles, blk = tile_buf.shape[0], tile_buf.shape[1]
    each = tiles // CHUNKS
    first = CHUNKS * 3 // 4
    chunks = [
        (tile_hbm.at[pl.ds(c * each, each)], tile_buf.at[pl.ds(c * each, each)])
        for c in range(CHUNKS)
    ]
    pairs = [(dst_hbm, dst_ref), (src_hbm, src_ref), (rows_hbm, rows_ref)]
    pairs += chunks[:first]
    pairs += [
        (cot_hbm, cot_ref),
        (neigh_two_hbm, neigh_two_ref),
        (features_hbm, features_ref),
        (send_hbm, send_ref),
    ]
    pairs += chunks[first:]
    copies = [pltpu.make_async_copy(a, b, sems.at[i]) for i, (a, b) in enumerate(pairs)]
    for copy in copies:
        copy.start()
    rows = features_ref.shape[0]
    bpd = rows // blk
    sources = accs[0].shape[0] // bpd
    part = accs[0].shape[1]
    far = send_ref.shape[2] * send_ref.shape[3]
    for acc in accs:
        acc[...] = jnp.zeros_like(acc)
    place = lax.broadcasted_iota(jnp.int32, (part, blk), 0)

    def add(t, carry):
        slot = dst_ref[t] * sources + src_ref[t]
        for i, acc in enumerate(accs):
            value = tile_buf[t, i * part : (i + 1) * part, :].astype(F32)
            acc[slot] += jnp.where(place < rows_ref[t] - i * part, value, 0.0)
        return carry

    for copy in copies[:3]:
        copy.wait()
    for c in range(first):
        copies[3 + c].wait()
        lax.fori_loop(c * each, (c + 1) * each, add, 0, unroll=True)
    for copy in copies[3 + first : 7 + first]:
        copy.wait()
    u = dot_nt(cot_ref[...], neigh_two_ref[...]).astype(BF16)
    up_ref[...] = u
    pick_ref[...] = pick_matrix(send_ref, rows)
    picked_ref[...] = dot(pick_ref[...], features_ref[...]).astype(BF16)
    for c in range(first, CHUNKS):
        copies[7 + c].wait()
        lax.fori_loop(c * each, (c + 1) * each, add, 0, unroll=True)
    chip, side = lax.axis_index("chip"), 1 - lax.axis_index("core")
    base = chips * CORES
    for j in range(far_t.shape[0] // rows):
        put_square(accs, bpd, base + j, square, 0)
        far_t[j * rows : (j + 1) * rows, :] = square[...].T
    for k in range(chips):
        d = lax.rem(chip + k, chips) * CORES + side
        at = k * (rows + far)
        put_square(accs, bpd, d, square, 0)
        col[at : at + rows, :] = square[...].T
        low = pl.multiple_of(d * far, far)
        col[at + rows : at + rows + far, :] = far_t[pl.ds(low, far), :]
    give_ref[...] = dot(col[...], u).astype(BF16)


def put_square(accs, bpd, d, out_ref, base):
    sources = accs[0].shape[0] // bpd
    part, blk = accs[0].shape[1:]
    for b in range(bpd):
        for j in range(bpd):
            for i, acc in enumerate(accs):
                low = base + b * blk + i * part
                value = acc[b * sources + d * bpd + j].astype(BF16)
                out_ref[low : low + part, j * blk : (j + 1) * blk] = value


def rest_kernel(chips, up_ref, cot_ref, value_ref, pick_ref, *refs):
    accs = refs[:PARTS]
    adj_ref, col_ref, keep_ref, lend_ref, place_ref, far_ref, far_t = refs[PARTS:]
    rows = up_ref.shape[0]
    bpd = rows // accs[0].shape[2]
    for d in range(adj_ref.shape[0] // rows):
        put_square(accs, bpd, d, adj_ref, d * rows)
    far = col_ref.shape[0] // chips - rows
    column(chips, far, rows, lax.axis_index("core"), adj_ref, far_t, col_ref)
    far_columns(chips, far_t, far_ref)
    keep_ref[...] = dot(col_ref[...], up_ref[...]).astype(BF16)
    low = adj_ref.shape[0]
    lend_ref[:low, :] = adj_ref[...]
    lend_ref[low : low + rows, :] = cot_ref[...]
    lend_ref[low + rows :, :] = value_ref[...]
    place_ref[...] = jnp.concatenate([pick_ref[...]] * chips, 0).T


def deal(chips, hosts, total, picked, value, mine_ref, msg_ref, to_refs):
    rows = value.shape[0]
    far = picked.shape[0]
    send = far // hosts
    each = rows + far
    chip, core = lax.axis_index("chip"), lax.axis_index("core")
    mine_ref[...] = total[:rows]
    for k in range(chips):
        low = k * each + rows
        if k > 0:
            to_refs[k - 1][:rows, :] = total[k * each : low].astype(BF16)
            to_refs[k - 1][rows:, :] = value
        x = lax.rem(chip + k, chips)
        for g in range(hosts):
            at = low + g * send
            to = (g * chips + x) * CORES
            msg_ref[to + core] = total[at : at + send].astype(BF16)
            msg_ref[to + 1 - core] = picked[g * send : (g + 1) * send].astype(BF16)


def core_sum_kernel(
    chips, hosts, keep_ref, came_ref, value_ref, picked_ref, mine_ref, msg_ref, *rest
):
    total = keep_ref[...].astype(F32) + came_ref[...].astype(F32)
    picked = picked_ref[...].astype(F32)
    deal(chips, hosts, total, picked, value_ref[...], mine_ref, msg_ref, rest)


def received(recv_ref, hosts, chips, side):
    blocks = [
        recv_ref[(g * chips + x) * CORES + side].astype(F32)
        for x in range(chips)
        for g in range(hosts)
    ]
    return jnp.concatenate(blocks, 0).astype(BF16)


def merge_kernel(chips, hosts, recv_ref, mine_ref, place_ref, *refs):
    came, (out_ref, sum_ref) = refs[: chips - 1], refs[chips - 1 :]
    rows = mine_ref.shape[0]
    total = mine_ref[...]
    for k, ref in enumerate(came):
        total = total + ref[:rows, :].astype(F32)
        out_ref[k * rows : (k + 1) * rows, :] = ref[rows:, :]
    total = total + returned(place_ref, recv_ref, hosts, chips)
    sum_ref[...] = total
    low = len(came) * rows
    halo = received(recv_ref, hosts, chips, 1 - lax.axis_index("core"))
    high = low + halo.shape[0]
    out_ref[low:high, :] = halo
    out_ref[high:, :] = total.astype(BF16)


def returned(place_ref, recv_ref, hosts, chips):
    return dot(place_ref[...], received(recv_ref, hosts, chips, lax.axis_index("core")))


def joint(pairs):
    left = jnp.concatenate([a for a, _ in pairs], 1)
    return dot(left, jnp.concatenate([b for _, b in pairs], 0))


def square_of(adj_ref, x, side, rows):
    return adj_ref[pl.ds(pl.multiple_of((x * CORES + side) * rows, rows), rows), :]


def own_chip(adj_refs, blocks):
    chip, core = lax.axis_index("chip"), lax.axis_index("core")
    rows = blocks[0].shape[0]
    parts = [
        joint([(square_of(ref, chip, s, rows), b) for s, b in zip((core, 1 - core), blocks)])
        for ref in adj_refs
    ]
    return jnp.concatenate(parts, 0)


def early_one_kernel(
    chips, adj_ref, lent_ref, value_ref, self_ref, bias_ref, up_ref, weight_ref, unused_ref,
    agg_ref, direct_ref, grad_ref, col_ref, far_ref, far_t,
):
    value = value_ref[...]
    rows = value.shape[0]
    low = adj_ref.shape[0]
    there = lent_ref[low + rows :, :]
    agg_ref[...] = own_chip((adj_ref, lent_ref), (value, there))
    both = jnp.concatenate([value, there], 0)
    direct_ref[...] = dot(both, self_ref[...]) + bias_ref[...].reshape(1, -1)
    both = jnp.concatenate([up_ref[...], lent_ref[low : low + rows, :]], 0)
    grad_ref[...] = dot_nt(both, weight_ref[...])
    far = col_ref.shape[0] // chips - rows
    column(chips, far, rows, lax.axis_index("core"), lent_ref, far_t, col_ref)
    far_columns(chips, far_t, far_ref)


def mid_kernel(
    chips, adj_ref, lent_ref, far_ref, far_two_ref, agg_ref, part_ref, sum_ref, here_ref, *refs
):
    came, (agg_out, grad_ref) = refs[:-2], refs[-2:]
    rows = sum_ref.shape[0]
    halo = here_ref[(chips - 1) * rows : here_ref.shape[0] - rows, :]
    for i, (ref, columns) in enumerate(((adj_ref, far_ref), (lent_ref, far_two_ref))):
        pairs = other_chips(chips, ref, came) + [(columns[:, : halo.shape[0]], halo)]
        part = slice(i * rows, (i + 1) * rows)
        agg_out[part, :] = agg_ref[part, :] + joint(pairs)
    grad_ref[:rows, :] = part_ref[:rows, :] + sum_ref[...]
    grad_ref[rows:, :] = part_ref[rows:, :]


def other_chips(chips, adj_ref, came):
    chip, core = lax.axis_index("chip"), lax.axis_index("core")
    pairs = []
    for k, block in enumerate(came):
        rows = block.shape[0] // 2
        x = lax.rem(chip - k - 1 + chips, chips)
        pairs.append((square_of(adj_ref, x, core, rows), block[rows:, :]))
    return pairs


def column_product(chips, hosts, adj_ref, far_ref, value_ref, came, recv_ref, neigh_ref):
    rows = value_ref.shape[0]
    chip, core = lax.axis_index("chip"), lax.axis_index("core")
    halo = received(recv_ref, hosts, chips, 1 - core)
    pairs = [(square_of(adj_ref, chip, core, rows), value_ref[...])]
    pairs += other_chips(chips, adj_ref, came) + [(far_ref[:, : halo.shape[0]], halo)]
    return dot(joint(pairs).astype(BF16), neigh_ref[...])


def there_kernel(chips, hosts, lent_ref, far_ref, value_ref, recv_ref, neigh_ref, *refs):
    came, out_ref = refs[:-1], refs[-1]
    out_ref[...] = column_product(
        chips, hosts, lent_ref, far_ref, value_ref, came, recv_ref, neigh_ref
    ).astype(BF16)


def here_kernel(
    chips, hosts, adj_ref, far_ref, value_ref, recv_ref, neigh_ref, self_ref, bias_ref, up_ref,
    weight_ref, mine_ref, place_ref, *refs
):
    came, (out_ref, grad_ref) = refs[:-2], refs[-2:]
    rows = mine_ref.shape[0]
    grad = dot_nt(up_ref[...], weight_ref[...]) + mine_ref[...]
    for block in came:
        grad = grad + block[:rows, :].astype(F32)
    grad_ref[...] = grad + returned(place_ref, recv_ref, hosts, chips)
    out = column_product(chips, hosts, adj_ref, far_ref, value_ref, came, recv_ref, neigh_ref)
    out_ref[...] = out + dot(value_ref[...], self_ref[...]) + bias_ref[...].reshape(1, -1)


def add_rest(chips, rows, adj_ref, far_ref, agg, shared_ref):
    chip, core = lax.axis_index("chip"), lax.axis_index("core")
    pairs = []
    for k in range(chips - 1):
        x = lax.rem(chip - k - 1 + chips, chips)
        block = shared_ref[k * rows : (k + 1) * rows, :]
        pairs.append((square_of(adj_ref, x, 1 - core, rows), block))
    half = far_ref.shape[1] // 2
    low = (chips - 1) * rows
    pairs.append((far_ref[:, half:], shared_ref[low : low + half, :]))
    return agg + joint(pairs)


def middle_kernel(
    chips,
    hosts,
    adj_ref,
    lent_ref,
    far_ref,
    far_two_ref,
    col_ref,
    col_two_ref,
    agg_ref,
    direct_ref,
    grad_ref,
    pick_ref,
    shared_ref,
    neigh_one_ref,
    hidden_ref,
    grad_pre_ref,
    mine_ref,
    msg_ref,
    *rest,
):
    to_refs = rest
    far, rows = pick_ref.shape
    parts = [
        add_rest(chips, rows, ref, columns, agg_ref[i * rows : (i + 1) * rows, :], shared_ref)
        for i, (ref, columns) in enumerate(((adj_ref, far_ref), (lent_ref, far_two_ref)))
    ]
    agg = jnp.concatenate(parts, 0).astype(BF16)
    pre = direct_ref[...] + dot(agg, neigh_one_ref[...])
    sigmoid = jax.nn.sigmoid(pre)
    hidden = (pre[:rows] * sigmoid[:rows]).astype(BF16)
    hidden_ref[...] = hidden
    low = (chips - 1) * rows + chips * far
    add = shared_ref[low:, :].astype(F32)
    grad = jnp.concatenate([grad_ref[:rows, :], grad_ref[rows:, :] + add], 0)
    grad_pre = (grad * sigmoid * (1.0 + pre * (1.0 - sigmoid))).astype(BF16)
    grad_pre_ref[...] = grad_pre[:rows]
    u = dot_nt(grad_pre, neigh_one_ref[...]).astype(BF16)
    total = joint([(col_ref[...], u[:rows]), (col_two_ref[...], u[rows:])])
    picked = dot(pick_ref[...], hidden)
    deal(chips, hosts, total, picked, hidden, mine_ref, msg_ref, to_refs)


def last_kernel(here_ref, there_ref, output_ref):
    output_ref[...] = (here_ref[...] + there_ref[...].astype(F32)).astype(BF16)


def call(kernel, name, out_shape, in_specs, args, scratch=(), limit=32, flops=0):
    return pl.pallas_call(
        kernel,
        out_shape=out_shape,
        in_specs=in_specs,
        out_specs=jax.tree.map(lambda _: VMEM, out_shape),
        scratch_shapes=scratch,
        compiler_params=pltpu.CompilerParams(vmem_limit_bytes=limit * MIB),
        cost_estimate=pl.CostEstimate(
            flops=flops, bytes_accessed=flops // 1024, transcendentals=0
        ),
        name=name,
    )(*args)


def shift(value, axis, k):
    size = lax.axis_size(axis)
    return lax.ppermute(value, axis, [(i, (i + k) % size) for i in range(size)])


def shape(rows, width, kind=BF16):
    return jax.ShapeDtypeStruct((rows, width), kind)


def body(
    features,
    send_list,
    tile_dst,
    tile_src,
    tile_rows,
    tile_val,
    self_one,
    neigh_one,
    bias_one,
    self_two,
    neigh_two,
    bias_two,
    cotangent,
):
    chips = lax.axis_size("chip")
    hosts = lax.axis_size("hst")
    rows, width = features.shape
    tiles, blk = tile_val.shape[:2]
    send = send_list.shape[3]
    far = hosts * send
    all_rows = chips * CORES * (rows + far)
    count = chips * (rows + far)
    rows_shape = shape(rows, width)
    sum_shape = shape(rows, width, F32)
    both_shape = shape(CORES * rows, width, F32)
    square = 2 * rows * width * width
    far_shape = shape(rows, chips * CORES * far)
    halo_rows = (chips - 1) * rows + chips * far
    dealt = (
        sum_shape,
        jax.ShapeDtypeStruct((chips * hosts * CORES, send, width), BF16),
    ) + (shape(2 * rows, width),) * (chips - 1)

    def across(msg, to):
        terms = [shift(block, "chip", k + 1) for k, block in enumerate(to)]
        recv = lax.all_to_all(msg, ("hst", "chip", "core"), split_axis=0, concat_axis=0, tiled=True)
        return terms, recv

    far_t = pltpu.VMEM((chips * CORES * far, rows), BF16)
    sums = jax.ShapeDtypeStruct(((rows // blk) * (all_rows // blk), blk // PARTS, blk), F32)
    give, up, picked, pick, *sums = call(
        functools.partial(prep_kernel, chips),
        "prep",
        (shape(count, width), rows_shape, shape(far, width), shape(far, rows)) + (sums,) * PARTS,
        [HBM] * 8,
        [
            pltpu.with_memory_space_constraint(value, pltpu.HBM)
            for value in (
                tile_dst,
                tile_src,
                tile_rows,
                send_list,
                tile_val,
                features,
                cotangent,
                neigh_two,
            )
        ],
        [
            pltpu.SMEM(tile_dst.shape, jnp.int32),
            pltpu.SMEM(tile_src.shape, jnp.int32),
            pltpu.SMEM(tile_rows.shape, jnp.int32),
            pltpu.SMEM(send_list.shape, jnp.int32),
            pltpu.VMEM(tile_val.shape, BF16),
            pltpu.VMEM(features.shape, BF16),
            pltpu.VMEM(cotangent.shape, BF16),
            pltpu.VMEM(neigh_two.shape, BF16),
            pltpu.VMEM((rows, rows), BF16),
            far_t,
            pltpu.VMEM((count, rows), BF16),
            pltpu.SemaphoreType.DMA((7 + CHUNKS,)),
        ],
    )
    came = shift(give, "core", 1)
    adj, col, keep, lend, place, columns = call(
        functools.partial(rest_kernel, chips),
        "rest",
        (
            shape(all_rows, rows),
            shape(count, rows),
            shape(count, width),
            shape(all_rows + 2 * rows, width),
            shape(rows, chips * far),
            far_shape,
        ),
        [VMEM] * (4 + PARTS),
        (up, cotangent, features, pick, *sums),
        [far_t],
        flops=3 * square,
    )
    lent = shift(lend, "core", 1)
    mine, msg, *to = call(
        functools.partial(core_sum_kernel, chips, hosts),
        "core_sum",
        dealt,
        [VMEM] * 4,
        (keep, came, features, picked),
        flops=60 * square,
    )
    terms, recv = across(msg, to)
    here, summed = call(
        functools.partial(merge_kernel, chips, hosts),
        "merge",
        (shape(halo_rows + rows, width), sum_shape),
        [VMEM] * (2 + chips),
        (recv, mine, place, *terms),
    )
    shared = shift(here, "core", 1)
    agg, direct, grad, col_two, columns_two = call(
        functools.partial(early_one_kernel, chips),
        "early_one",
        (both_shape,) * 3 + (shape(count, rows), far_shape),
        [VMEM] * 8,
        (adj, lent, features, self_one, bias_one, cotangent, self_two, neigh_one),
        [far_t],
        flops=8 * square,
    )
    agg, grad = call(
        functools.partial(mid_kernel, chips),
        "mid",
        (both_shape,) * 2,
        [VMEM] * (7 + chips),
        (adj, lent, columns, columns_two, agg, grad, summed, here, *terms),
        flops=3 * square,
    )
    hidden, grad_pre, mine, msg, *to = call(
        functools.partial(middle_kernel, chips, hosts),
        "middle",
        (rows_shape,) * 2 + dealt,
        [VMEM] * 12,
        (
            adj,
            lent,
            columns,
            columns_two,
            col,
            col_two,
            agg,
            direct,
            grad,
            pick,
            shared,
            neigh_one,
        ),
        flops=12 * square,
    )
    terms, recv = across(msg, to)
    there = call(
        functools.partial(there_kernel, chips, hosts),
        "there",
        rows_shape,
        [VMEM] * (4 + chips),
        (lent, columns_two, hidden, recv, neigh_two, *terms),
    )
    shared = shift(there, "core", 1)
    here, grad = call(
        functools.partial(here_kernel, chips, hosts),
        "here",
        (sum_shape,) * 2,
        [VMEM] * (10 + chips),
        (
            adj,
            columns,
            hidden,
            recv,
            neigh_two,
            self_two,
            bias_two,
            grad_pre,
            self_one,
            mine,
            place,
            *terms,
        ),
        flops=7 * square,
    )
    output = call(last_kernel, "last", rows_shape, [VMEM] * 2, (here, shared))
    return output, grad


def solution(mesh):
    hosts, devs = mesh.devices.shape
    mesh = Mesh(mesh.devices.reshape(hosts, devs // CORES, CORES), ("hst", "chip", "core"))
    dev = ("chip", "core")
    every = ("hst", "chip", "core")
    return jax.shard_map(
        body,
        mesh=mesh,
        in_specs=(
            P(every, None),
            P("hst", dev, None, None),
            P(every),
            P(every),
            P(every),
            P(every, None, None),
            P(),
            P(),
            P(),
            P(),
            P(),
            P(),
            P(every, None),
        ),
        out_specs=(P(every, None), P(every, None)),
        check_vma=False,
    )
```

```python
import functools

import jax
import jax.numpy as jnp
from jax import lax
from jax.experimental import pallas as pl
from jax.experimental.pallas import tpu as pltpu
from jax.sharding import Mesh, PartitionSpec as P

F32 = jnp.float32
BF16 = jnp.bfloat16
MIB = 1024 * 1024
CHUNKS = 8
PARTS = 4
CORES = 2

VMEM = pl.BlockSpec(memory_space=pltpu.VMEM)
HBM = pl.BlockSpec(memory_space=pltpu.HBM)


def dot(a, b):
    return jnp.dot(a, b, preferred_element_type=F32)


def dot_nt(a, b):
    return lax.dot_general(a, b, (((1,), (1,)), ((), ())), preferred_element_type=F32)


def pick_matrix(send_ref, rows):
    hosts, send = send_ref.shape[2], send_ref.shape[3]
    place = lax.broadcasted_iota(jnp.int32, (send, rows), 0)
    column = lax.broadcasted_iota(jnp.int32, (send, rows), 1)
    parts = []
    for g in range(hosts):
        index = jnp.zeros((send, rows), jnp.int32)
        for s in range(send):
            index = jnp.where(place == s, send_ref[0, 0, g, s], index)
        parts.append(jnp.where(index == column, 1.0, 0.0).astype(F32))
    return jnp.concatenate(parts, 0).astype(BF16)


def column(chips, far, rows, side, adj_ref, far_t, out_ref):
    chip = lax.axis_index("chip")
    each = rows + far
    own_rows = chips * CORES * rows
    for j in range(far_t.shape[0] // rows):
        low = own_rows + j * rows
        far_t[j * rows : (j + 1) * rows, :] = adj_ref[low : low + rows, :].T
    for k in range(chips):
        d = lax.rem(chip + k, chips) * CORES + side
        at = k * each
        out_ref[at : at + rows, :] = adj_ref[pl.ds(pl.multiple_of(d * rows, rows), rows), :].T
        out_ref[at + rows : at + each, :] = far_t[pl.ds(pl.multiple_of(d * far, far), far), :]


def far_columns(chips, far_t, out_ref):
    far = far_t.shape[0] // (chips * CORES)
    core = lax.axis_index("core")
    parts = [
        far_t[pl.ds(pl.multiple_of((x * CORES + side) * far, far), far), :]
        for side in (1 - core, core)
        for x in range(chips)
    ]
    out_ref[...] = jnp.concatenate(parts, 0).T


def prep_kernel(
    chips,
    dst_hbm,
    src_hbm,
    rows_hbm,
    send_hbm,
    tile_hbm,
    features_hbm,
    cot_hbm,
    neigh_two_hbm,
    give_ref,
    up_ref,
    picked_ref,
    pick_ref,
    *rest,
):
    accs, rest = rest[:PARTS], rest[PARTS:]
    (
        dst_ref,
        src_ref,
        rows_ref,
        send_ref,
        tile_buf,
        features_ref,
        cot_ref,
        neigh_two_ref,
        square,
        far_t,
        col,
        sems,
    ) = rest
    tiles, blk = tile_buf.shape[0], tile_buf.shape[1]
    each = tiles // CHUNKS
    first = CHUNKS * 3 // 4
    chunks = [
        (tile_hbm.at[pl.ds(c * each, each)], tile_buf.at[pl.ds(c * each, each)])
        for c in range(CHUNKS)
    ]
    pairs = [(dst_hbm, dst_ref), (src_hbm, src_ref), (rows_hbm, rows_ref)]
    pairs += chunks[:first]
    pairs += [
        (cot_hbm, cot_ref),
        (neigh_two_hbm, neigh_two_ref),
        (features_hbm, features_ref),
        (send_hbm, send_ref),
    ]
    pairs += chunks[first:]
    copies = [pltpu.make_async_copy(a, b, sems.at[i]) for i, (a, b) in enumerate(pairs)]
    for copy in copies:
        copy.start()
    rows = features_ref.shape[0]
    bpd = rows // blk
    sources = accs[0].shape[0] // bpd
    part = accs[0].shape[1]
    far = send_ref.shape[2] * send_ref.shape[3]
    for acc in accs:
        acc[...] = jnp.zeros_like(acc)
    place = lax.broadcasted_iota(jnp.int32, (part, blk), 0)

    def add(t, carry):
        slot = dst_ref[t] * sources + src_ref[t]
        for i, acc in enumerate(accs):
            value = tile_buf[t, i * part : (i + 1) * part, :].astype(F32)
            acc[slot] += jnp.where(place < rows_ref[t] - i * part, value, 0.0)
        return carry

    for copy in copies[:3]:
        copy.wait()
    for c in range(first):
        copies[3 + c].wait()
        lax.fori_loop(c * each, (c + 1) * each, add, 0, unroll=True)
    for copy in copies[3 + first : 7 + first]:
        copy.wait()
    u = dot_nt(cot_ref[...], neigh_two_ref[...]).astype(BF16)
    up_ref[...] = u
    pick_ref[...] = pick_matrix(send_ref, rows)
    picked_ref[...] = dot(pick_ref[...], features_ref[...]).astype(BF16)
    for c in range(first, CHUNKS):
        copies[7 + c].wait()
        lax.fori_loop(c * each, (c + 1) * each, add, 0, unroll=True)
    chip, side = lax.axis_index("chip"), 1 - lax.axis_index("core")
    base = chips * CORES
    for j in range(far_t.shape[0] // rows):
        put_square(accs, bpd, base + j, square, 0)
        far_t[j * rows : (j + 1) * rows, :] = square[...].T
    for k in range(chips):
        d = lax.rem(chip + k, chips) * CORES + side
        at = k * (rows + far)
        put_square(accs, bpd, d, square, 0)
        col[at : at + rows, :] = square[...].T
        low = pl.multiple_of(d * far, far)
        col[at + rows : at + rows + far, :] = far_t[pl.ds(low, far), :]
    give_ref[...] = dot(col[...], u).astype(BF16)


def put_square(accs, bpd, d, out_ref, base):
    sources = accs[0].shape[0] // bpd
    part, blk = accs[0].shape[1:]
    for b in range(bpd):
        for j in range(bpd):
            for i, acc in enumerate(accs):
                low = base + b * blk + i * part
                value = acc[b * sources + d * bpd + j].astype(BF16)
                out_ref[low : low + part, j * blk : (j + 1) * blk] = value


def rest_kernel(chips, up_ref, cot_ref, value_ref, pick_ref, *refs):
    accs = refs[:PARTS]
    adj_ref, col_ref, keep_ref, lend_ref, place_ref, far_ref, far_t = refs[PARTS:]
    rows = up_ref.shape[0]
    bpd = rows // accs[0].shape[2]
    for d in range(adj_ref.shape[0] // rows):
        put_square(accs, bpd, d, adj_ref, d * rows)
    far = col_ref.shape[0] // chips - rows
    column(chips, far, rows, lax.axis_index("core"), adj_ref, far_t, col_ref)
    far_columns(chips, far_t, far_ref)
    keep_ref[...] = dot(col_ref[...], up_ref[...]).astype(BF16)
    low = adj_ref.shape[0]
    lend_ref[:low, :] = adj_ref[...]
    lend_ref[low : low + rows, :] = cot_ref[...]
    lend_ref[low + rows :, :] = value_ref[...]
    place_ref[...] = jnp.concatenate([pick_ref[...]] * chips, 0).T


def node_part(rows, far, value):
    each = rows + far
    return [value[low : low + rows, :] for low in range(each, value.shape[0], each)]


def far_part(rows, far, value):
    each = rows + far
    return [value[low + rows : low + each, :] for low in range(0, value.shape[0], each)]


def send_to_chips(blocks, value, to_refs):
    rows = value.shape[0]
    for block, ref in zip(blocks, to_refs):
        ref[:rows, :] = block.astype(BF16)
        ref[rows:, :] = value


def send_to_hosts(chips, hosts, terms, picked, msg_ref):
    send = picked.shape[0] // hosts
    chip, core = lax.axis_index("chip"), lax.axis_index("core")
    for k, block in enumerate(terms):
        x = lax.rem(chip + k, chips)
        for g in range(hosts):
            part = slice(g * send, (g + 1) * send)
            to = (g * chips + x) * CORES
            msg_ref[to + core] = block[part].astype(BF16)
            msg_ref[to + 1 - core] = picked[part].astype(BF16)


def core_sum_kernel(
    chips, hosts, keep_ref, came_ref, value_ref, picked_ref, mine_ref, msg_ref, *rest
):
    total = keep_ref[...].astype(F32) + came_ref[...].astype(F32)
    picked = picked_ref[...].astype(F32)
    rows = value_ref.shape[0]
    far = picked.shape[0]
    mine_ref[...] = total[:rows]
    send_to_chips(node_part(rows, far, total), value_ref[...], rest)
    send_to_hosts(chips, hosts, far_part(rows, far, total), picked, msg_ref)


def received(recv_ref, hosts, chips, side):
    blocks = [
        recv_ref[(g * chips + x) * CORES + side].astype(F32)
        for x in range(chips)
        for g in range(hosts)
    ]
    return jnp.concatenate(blocks, 0).astype(BF16)


def merge_kernel(chips, hosts, recv_ref, mine_ref, place_ref, *refs):
    came, (out_ref, sum_ref) = refs[: chips - 1], refs[chips - 1 :]
    rows = mine_ref.shape[0]
    total = mine_ref[...]
    for k, ref in enumerate(came):
        total = total + ref[:rows, :].astype(F32)
        out_ref[k * rows : (k + 1) * rows, :] = ref[rows:, :]
    total = total + returned(place_ref, recv_ref, hosts, chips)
    sum_ref[...] = total
    low = len(came) * rows
    halo = received(recv_ref, hosts, chips, 1 - lax.axis_index("core"))
    high = low + halo.shape[0]
    out_ref[low:high, :] = halo
    out_ref[high:, :] = total.astype(BF16)


def returned(place_ref, recv_ref, hosts, chips):
    return dot(place_ref[...], received(recv_ref, hosts, chips, lax.axis_index("core")))


def joint(pairs):
    left = jnp.concatenate([a for a, _ in pairs], 1)
    return dot(left, jnp.concatenate([b for _, b in pairs], 0))


def square_of(adj_ref, x, side, rows):
    return adj_ref[pl.ds(pl.multiple_of((x * CORES + side) * rows, rows), rows), :]


def own_chip(adj_refs, blocks):
    chip, core = lax.axis_index("chip"), lax.axis_index("core")
    rows = blocks[0].shape[0]
    parts = [
        joint([(square_of(ref, chip, s, rows), b) for s, b in zip((core, 1 - core), blocks)])
        for ref in adj_refs
    ]
    return jnp.concatenate(parts, 0)


def early_one_kernel(
    chips, adj_ref, lent_ref, value_ref, self_ref, bias_ref, up_ref, weight_ref, unused_ref,
    agg_ref, direct_ref, grad_ref, col_ref, far_ref, far_t,
):
    value = value_ref[...]
    rows = value.shape[0]
    low = adj_ref.shape[0]
    there = lent_ref[low + rows :, :]
    agg_ref[...] = own_chip((adj_ref, lent_ref), (value, there))
    both = jnp.concatenate([value, there], 0)
    direct_ref[...] = dot(both, self_ref[...]) + bias_ref[...].reshape(1, -1)
    both = jnp.concatenate([up_ref[...], lent_ref[low : low + rows, :]], 0)
    grad_ref[...] = dot_nt(both, weight_ref[...])
    far = col_ref.shape[0] // chips - rows
    column(chips, far, rows, lax.axis_index("core"), lent_ref, far_t, col_ref)
    far_columns(chips, far_t, far_ref)


def mid_kernel(
    chips, adj_ref, lent_ref, far_ref, far_two_ref, agg_ref, part_ref, sum_ref, here_ref, *refs
):
    came, (agg_out, grad_ref) = refs[:-2], refs[-2:]
    rows = sum_ref.shape[0]
    halo = here_ref[(chips - 1) * rows : here_ref.shape[0] - rows, :]
    for i, (ref, columns) in enumerate(((adj_ref, far_ref), (lent_ref, far_two_ref))):
        pairs = other_chips(chips, ref, came) + [(columns[:, : halo.shape[0]], halo)]
        part = slice(i * rows, (i + 1) * rows)
        agg_out[part, :] = agg_ref[part, :] + joint(pairs)
    grad_ref[:rows, :] = part_ref[:rows, :] + sum_ref[...]
    grad_ref[rows:, :] = part_ref[rows:, :]


def other_chips(chips, adj_ref, came):
    chip, core = lax.axis_index("chip"), lax.axis_index("core")
    pairs = []
    for k, block in enumerate(came):
        rows = block.shape[0] // 2
        x = lax.rem(chip - k - 1 + chips, chips)
        pairs.append((square_of(adj_ref, x, core, rows), block[rows:, :]))
    return pairs


def column_product(chips, hosts, adj_ref, far_ref, value_ref, came, recv_ref, neigh_ref):
    rows = value_ref.shape[0]
    chip, core = lax.axis_index("chip"), lax.axis_index("core")
    halo = received(recv_ref, hosts, chips, 1 - core)
    pairs = [(square_of(adj_ref, chip, core, rows), value_ref[...])]
    pairs += other_chips(chips, adj_ref, came) + [(far_ref[:, : halo.shape[0]], halo)]
    return dot(joint(pairs).astype(BF16), neigh_ref[...])


def there_kernel(chips, hosts, lent_ref, far_ref, value_ref, recv_ref, neigh_ref, *refs):
    came, out_ref = refs[:-1], refs[-1]
    out_ref[...] = column_product(
        chips, hosts, lent_ref, far_ref, value_ref, came, recv_ref, neigh_ref
    ).astype(BF16)


def here_kernel(
    chips, hosts, adj_ref, far_ref, value_ref, recv_ref, neigh_ref, self_ref, bias_ref, up_ref,
    weight_ref, mine_ref, place_ref, *refs
):
    came, (out_ref, grad_ref) = refs[:-2], refs[-2:]
    rows = mine_ref.shape[0]
    grad = dot_nt(up_ref[...], weight_ref[...]) + mine_ref[...]
    for block in came:
        grad = grad + block[:rows, :].astype(F32)
    grad_ref[...] = grad + returned(place_ref, recv_ref, hosts, chips)
    out = column_product(chips, hosts, adj_ref, far_ref, value_ref, came, recv_ref, neigh_ref)
    out_ref[...] = out + dot(value_ref[...], self_ref[...]) + bias_ref[...].reshape(1, -1)


def add_rest(chips, rows, adj_ref, far_ref, agg, shared_ref):
    chip, core = lax.axis_index("chip"), lax.axis_index("core")
    pairs = []
    for k in range(chips - 1):
        x = lax.rem(chip - k - 1 + chips, chips)
        block = shared_ref[k * rows : (k + 1) * rows, :]
        pairs.append((square_of(adj_ref, x, 1 - core, rows), block))
    half = far_ref.shape[1] // 2
    low = (chips - 1) * rows
    pairs.append((far_ref[:, half:], shared_ref[low : low + half, :]))
    return agg + joint(pairs)


def middle_kernel(
    chips,
    adj_ref,
    lent_ref,
    far_ref,
    far_two_ref,
    col_ref,
    col_two_ref,
    agg_ref,
    direct_ref,
    grad_ref,
    pick_ref,
    shared_ref,
    neigh_one_ref,
    hidden_ref,
    grad_pre_ref,
    up_ref,
    *to_refs,
):
    far, rows = pick_ref.shape
    parts = [
        add_rest(chips, rows, ref, columns, agg_ref[i * rows : (i + 1) * rows, :], shared_ref)
        for i, (ref, columns) in enumerate(((adj_ref, far_ref), (lent_ref, far_two_ref)))
    ]
    agg = jnp.concatenate(parts, 0).astype(BF16)
    pre = direct_ref[...] + dot(agg, neigh_one_ref[...])
    sigmoid = jax.nn.sigmoid(pre)
    hidden = (pre[:rows] * sigmoid[:rows]).astype(BF16)
    hidden_ref[...] = hidden
    low = (chips - 1) * rows + chips * far
    add = shared_ref[low:, :].astype(F32)
    grad = jnp.concatenate([grad_ref[:rows, :], grad_ref[rows:, :] + add], 0)
    grad_pre = (grad * sigmoid * (1.0 + pre * (1.0 - sigmoid))).astype(BF16)
    grad_pre_ref[...] = grad_pre[:rows]
    u = dot_nt(grad_pre, neigh_one_ref[...]).astype(BF16)
    up_ref[...] = u
    columns = [node_part(rows, far, ref) for ref in (col_ref, col_two_ref)]
    blocks = [joint([(one, u[:rows]), (two, u[rows:])]) for one, two in zip(*columns)]
    send_to_chips(blocks, hidden, to_refs)


def messages_kernel(
    chips, hosts, col_ref, col_two_ref, up_ref, hidden_ref, pick_ref, mine_ref, msg_ref
):
    far, rows = pick_ref.shape
    u = up_ref[...]
    columns = [
        jnp.concatenate([ref[:rows, :]] + far_part(rows, far, ref), 0)
        for ref in (col_ref, col_two_ref)
    ]
    total = joint([(columns[0], u[:rows]), (columns[1], u[rows:])])
    mine_ref[...] = total[:rows]
    terms = [total[low : low + far] for low in range(rows, total.shape[0], far)]
    send_to_hosts(chips, hosts, terms, dot(pick_ref[...], hidden_ref[...]), msg_ref)


def last_kernel(here_ref, there_ref, output_ref):
    output_ref[...] = (here_ref[...] + there_ref[...].astype(F32)).astype(BF16)


def call(kernel, name, out_shape, in_specs, args, scratch=(), limit=32, flops=0):
    return pl.pallas_call(
        kernel,
        out_shape=out_shape,
        in_specs=in_specs,
        out_specs=jax.tree.map(lambda _: VMEM, out_shape),
        scratch_shapes=scratch,
        compiler_params=pltpu.CompilerParams(vmem_limit_bytes=limit * MIB),
        cost_estimate=pl.CostEstimate(
            flops=flops, bytes_accessed=flops // 1024, transcendentals=0
        ),
        name=name,
    )(*args)


def shift(value, axis, k):
    size = lax.axis_size(axis)
    return lax.ppermute(value, axis, [(i, (i + k) % size) for i in range(size)])


def shape(rows, width, kind=BF16):
    return jax.ShapeDtypeStruct((rows, width), kind)


def body(
    features,
    send_list,
    tile_dst,
    tile_src,
    tile_rows,
    tile_val,
    self_one,
    neigh_one,
    bias_one,
    self_two,
    neigh_two,
    bias_two,
    cotangent,
):
    chips = lax.axis_size("chip")
    hosts = lax.axis_size("hst")
    rows, width = features.shape
    tiles, blk = tile_val.shape[:2]
    send = send_list.shape[3]
    far = hosts * send
    all_rows = chips * CORES * (rows + far)
    count = chips * (rows + far)
    rows_shape = shape(rows, width)
    sum_shape = shape(rows, width, F32)
    both_shape = shape(CORES * rows, width, F32)
    square = 2 * rows * width * width
    far_shape = shape(rows, chips * CORES * far)
    halo_rows = (chips - 1) * rows + chips * far
    dealt = (sum_shape, jax.ShapeDtypeStruct((chips * hosts * CORES, send, width), BF16))
    to_shapes = (shape(2 * rows, width),) * (chips - 1)

    def to_chips(blocks):
        return [shift(block, "chip", k + 1) for k, block in enumerate(blocks)]

    def to_hosts(msg):
        return lax.all_to_all(msg, ("hst", "chip", "core"), split_axis=0, concat_axis=0, tiled=True)

    far_t = pltpu.VMEM((chips * CORES * far, rows), BF16)
    sums = jax.ShapeDtypeStruct(((rows // blk) * (all_rows // blk), blk // PARTS, blk), F32)
    give, up, picked, pick, *sums = call(
        functools.partial(prep_kernel, chips),
        "prep",
        (shape(count, width), rows_shape, shape(far, width), shape(far, rows)) + (sums,) * PARTS,
        [HBM] * 8,
        [
            pltpu.with_memory_space_constraint(value, pltpu.HBM)
            for value in (
                tile_dst,
                tile_src,
                tile_rows,
                send_list,
                tile_val,
                features,
                cotangent,
                neigh_two,
            )
        ],
        [
            pltpu.SMEM(tile_dst.shape, jnp.int32),
            pltpu.SMEM(tile_src.shape, jnp.int32),
            pltpu.SMEM(tile_rows.shape, jnp.int32),
            pltpu.SMEM(send_list.shape, jnp.int32),
            pltpu.VMEM(tile_val.shape, BF16),
            pltpu.VMEM(features.shape, BF16),
            pltpu.VMEM(cotangent.shape, BF16),
            pltpu.VMEM(neigh_two.shape, BF16),
            pltpu.VMEM((rows, rows), BF16),
            far_t,
            pltpu.VMEM((count, rows), BF16),
            pltpu.SemaphoreType.DMA((7 + CHUNKS,)),
        ],
    )
    came = shift(give, "core", 1)
    adj, col, keep, lend, place, columns = call(
        functools.partial(rest_kernel, chips),
        "rest",
        (
            shape(all_rows, rows),
            shape(count, rows),
            shape(count, width),
            shape(all_rows + 2 * rows, width),
            shape(rows, chips * far),
            far_shape,
        ),
        [VMEM] * (4 + PARTS),
        (up, cotangent, features, pick, *sums),
        [far_t],
        flops=3 * square,
    )
    lent = shift(lend, "core", 1)
    mine, msg, *to = call(
        functools.partial(core_sum_kernel, chips, hosts),
        "core_sum",
        dealt + to_shapes,
        [VMEM] * 4,
        (keep, came, features, picked),
        flops=60 * square,
    )
    terms = to_chips(to)
    recv = to_hosts(msg)
    here, summed = call(
        functools.partial(merge_kernel, chips, hosts),
        "merge",
        (shape(halo_rows + rows, width), sum_shape),
        [VMEM] * (2 + chips),
        (recv, mine, place, *terms),
    )
    shared = shift(here, "core", 1)
    agg, direct, grad, col_two, columns_two = call(
        functools.partial(early_one_kernel, chips),
        "early_one",
        (both_shape,) * 3 + (shape(count, rows), far_shape),
        [VMEM] * 8,
        (adj, lent, features, self_one, bias_one, cotangent, self_two, neigh_one),
        [far_t],
        flops=8 * square,
    )
    agg, grad = call(
        functools.partial(mid_kernel, chips),
        "mid",
        (both_shape,) * 2,
        [VMEM] * (7 + chips),
        (adj, lent, columns, columns_two, agg, grad, summed, here, *terms),
        flops=3 * square,
    )
    hidden, grad_pre, up, *to = call(
        functools.partial(middle_kernel, chips),
        "middle",
        (rows_shape,) * 2 + (shape(CORES * rows, width),) + to_shapes,
        [VMEM] * 12,
        (
            adj,
            lent,
            columns,
            columns_two,
            col,
            col_two,
            agg,
            direct,
            grad,
            pick,
            shared,
            neigh_one,
        ),
        flops=12 * square,
    )
    terms = to_chips(to)
    mine, msg = call(
        functools.partial(messages_kernel, chips, hosts),
        "messages",
        dealt,
        [VMEM] * 5,
        (col, col_two, up, hidden, pick),
        flops=5 * square,
    )
    recv = to_hosts(msg)
    there = call(
        functools.partial(there_kernel, chips, hosts),
        "there",
        rows_shape,
        [VMEM] * (4 + chips),
        (lent, columns_two, hidden, recv, neigh_two, *terms),
    )
    shared = shift(there, "core", 1)
    here, grad = call(
        functools.partial(here_kernel, chips, hosts),
        "here",
        (sum_shape,) * 2,
        [VMEM] * (10 + chips),
        (
            adj,
            columns,
            hidden,
            recv,
            neigh_two,
            self_two,
            bias_two,
            grad_pre,
            self_one,
            mine,
            place,
            *terms,
        ),
        flops=7 * square,
    )
    output = call(last_kernel, "last", rows_shape, [VMEM] * 2, (here, shared))
    return output, grad


def solution(mesh):
    hosts, devs = mesh.devices.shape
    mesh = Mesh(mesh.devices.reshape(hosts, devs // CORES, CORES), ("hst", "chip", "core"))
    dev = ("chip", "core")
    every = ("hst", "chip", "core")
    return jax.shard_map(
        body,
        mesh=mesh,
        in_specs=(
            P(every, None),
            P("hst", dev, None, None),
            P(every),
            P(every),
            P(every),
            P(every, None, None),
            P(),
            P(),
            P(),
            P(),
            P(),
            P(),
            P(every, None),
        ),
        out_specs=(P(every, None), P(every, None)),
        check_vma=False,
    )
```

```python
import functools

import jax
import jax.numpy as jnp
from jax import lax
from jax.experimental import pallas as pl
from jax.experimental.pallas import tpu as pltpu
from jax.sharding import Mesh, PartitionSpec as P

F32 = jnp.float32
BF16 = jnp.bfloat16
MIB = 1024 * 1024
CHUNKS = 8
PARTS = 4
CORES = 2

VMEM = pl.BlockSpec(memory_space=pltpu.VMEM)
HBM = pl.BlockSpec(memory_space=pltpu.HBM)


def dot(a, b):
    return jnp.dot(a, b, preferred_element_type=F32)


def dot_nt(a, b):
    return lax.dot_general(a, b, (((1,), (1,)), ((), ())), preferred_element_type=F32)


def pick_matrix(send_ref, rows):
    hosts, send = send_ref.shape[2], send_ref.shape[3]
    place = lax.broadcasted_iota(jnp.int32, (send, rows), 0)
    column = lax.broadcasted_iota(jnp.int32, (send, rows), 1)
    parts = []
    for g in range(hosts):
        index = jnp.zeros((send, rows), jnp.int32)
        for s in range(send):
            index = jnp.where(place == s, send_ref[0, 0, g, s], index)
        parts.append(jnp.where(index == column, 1.0, 0.0).astype(F32))
    return jnp.concatenate(parts, 0).astype(BF16)


def column(chips, far, rows, side, adj_ref, far_t, out_ref):
    chip = lax.axis_index("chip")
    each = rows + far
    own_rows = chips * CORES * rows
    for j in range(far_t.shape[0] // rows):
        low = own_rows + j * rows
        far_t[j * rows : (j + 1) * rows, :] = adj_ref[low : low + rows, :].T
    for k in range(chips):
        d = lax.rem(chip + k, chips) * CORES + side
        at = k * each
        out_ref[at : at + rows, :] = adj_ref[pl.ds(pl.multiple_of(d * rows, rows), rows), :].T
        out_ref[at + rows : at + each, :] = far_t[pl.ds(pl.multiple_of(d * far, far), far), :]


def far_columns(chips, far_t, out_ref):
    far = far_t.shape[0] // (chips * CORES)
    core = lax.axis_index("core")
    parts = [
        far_t[pl.ds(pl.multiple_of((x * CORES + side) * far, far), far), :]
        for side in (1 - core, core)
        for x in range(chips)
    ]
    out_ref[...] = jnp.concatenate(parts, 0).T


def prep_kernel(
    chips,
    dst_hbm,
    src_hbm,
    rows_hbm,
    send_hbm,
    tile_hbm,
    features_hbm,
    cot_hbm,
    neigh_two_hbm,
    neigh_one_hbm,
    give_ref,
    up_ref,
    sent_ref,
    picked_ref,
    pick_ref,
    *rest,
):
    accs, rest = rest[:PARTS], rest[PARTS:]
    (
        dst_ref,
        src_ref,
        rows_ref,
        send_ref,
        tile_buf,
        features_ref,
        cot_ref,
        neigh_two_ref,
        neigh_one_ref,
        square,
        far_t,
        col,
        sems,
    ) = rest
    tiles, blk = tile_buf.shape[0], tile_buf.shape[1]
    each = tiles // CHUNKS
    first = CHUNKS * 3 // 4
    chunks = [
        (tile_hbm.at[pl.ds(c * each, each)], tile_buf.at[pl.ds(c * each, each)])
        for c in range(CHUNKS)
    ]
    pairs = [(dst_hbm, dst_ref), (src_hbm, src_ref), (rows_hbm, rows_ref)]
    pairs += chunks[:first]
    pairs += [
        (cot_hbm, cot_ref),
        (neigh_two_hbm, neigh_two_ref),
        (neigh_one_hbm, neigh_one_ref),
        (features_hbm, features_ref),
        (send_hbm, send_ref),
    ]
    pairs += chunks[first:]
    copies = [pltpu.make_async_copy(a, b, sems.at[i]) for i, (a, b) in enumerate(pairs)]
    for copy in copies:
        copy.start()
    rows = features_ref.shape[0]
    bpd = rows // blk
    sources = accs[0].shape[0] // bpd
    part = accs[0].shape[1]
    far = send_ref.shape[2] * send_ref.shape[3]
    for acc in accs:
        acc[...] = jnp.zeros_like(acc)
    place = lax.broadcasted_iota(jnp.int32, (part, blk), 0)

    def add(t, carry):
        slot = dst_ref[t] * sources + src_ref[t]
        for i, acc in enumerate(accs):
            value = tile_buf[t, i * part : (i + 1) * part, :].astype(F32)
            acc[slot] += jnp.where(place < rows_ref[t] - i * part, value, 0.0)
        return carry

    for copy in copies[:3]:
        copy.wait()
    for c in range(first):
        copies[3 + c].wait()
        lax.fori_loop(c * each, (c + 1) * each, add, 0, unroll=True)
    for copy in copies[3 + first : 8 + first]:
        copy.wait()
    u = dot_nt(cot_ref[...], neigh_two_ref[...]).astype(BF16)
    up_ref[...] = u
    pick_ref[...] = pick_matrix(send_ref, rows)
    sent_ref[...] = dot(features_ref[...], neigh_one_ref[...]).astype(BF16)
    picked_ref[...] = dot(pick_ref[...], sent_ref[...]).astype(BF16)
    for c in range(first, CHUNKS):
        copies[8 + c].wait()
        lax.fori_loop(c * each, (c + 1) * each, add, 0, unroll=True)
    chip, side = lax.axis_index("chip"), 1 - lax.axis_index("core")
    base = chips * CORES
    for j in range(far_t.shape[0] // rows):
        put_square(accs, bpd, base + j, square, 0)
        far_t[j * rows : (j + 1) * rows, :] = square[...].T
    for k in range(chips):
        d = lax.rem(chip + k, chips) * CORES + side
        at = k * (rows + far)
        put_square(accs, bpd, d, square, 0)
        col[at : at + rows, :] = square[...].T
        low = pl.multiple_of(d * far, far)
        col[at + rows : at + rows + far, :] = far_t[pl.ds(low, far), :]
    give_ref[...] = dot(col[...], u).astype(BF16)


def put_square(accs, bpd, d, out_ref, base):
    sources = accs[0].shape[0] // bpd
    part, blk = accs[0].shape[1:]
    for b in range(bpd):
        for j in range(bpd):
            for i, acc in enumerate(accs):
                low = base + b * blk + i * part
                value = acc[b * sources + d * bpd + j].astype(BF16)
                out_ref[low : low + part, j * blk : (j + 1) * blk] = value


def rest_kernel(chips, up_ref, cot_ref, value_ref, pick_ref, *refs):
    accs = refs[:PARTS]
    adj_ref, col_ref, keep_ref, lend_ref, place_ref, far_ref, far_t = refs[PARTS:]
    rows = up_ref.shape[0]
    bpd = rows // accs[0].shape[2]
    for d in range(adj_ref.shape[0] // rows):
        put_square(accs, bpd, d, adj_ref, d * rows)
    far = col_ref.shape[0] // chips - rows
    column(chips, far, rows, lax.axis_index("core"), adj_ref, far_t, col_ref)
    far_columns(chips, far_t, far_ref)
    keep_ref[...] = dot(col_ref[...], up_ref[...]).astype(BF16)
    low = adj_ref.shape[0]
    lend_ref[:low, :] = adj_ref[...]
    lend_ref[low : low + rows, :] = cot_ref[...]
    lend_ref[low + rows :, :] = value_ref[...]
    place_ref[...] = jnp.concatenate([pick_ref[...]] * chips, 0).T


def deal(chips, hosts, total, picked, value, mine_ref, msg_ref, to_refs):
    rows = value.shape[0]
    far = picked.shape[0]
    send = far // hosts
    each = rows + far
    chip, core = lax.axis_index("chip"), lax.axis_index("core")
    mine_ref[...] = total[:rows]
    for k in range(chips):
        low = k * each + rows
        if k > 0:
            to_refs[k - 1][:rows, :] = total[k * each : low].astype(BF16)
            to_refs[k - 1][rows:, :] = value
        x = lax.rem(chip + k, chips)
        for g in range(hosts):
            at = low + g * send
            to = (g * chips + x) * CORES
            msg_ref[to + core] = total[at : at + send].astype(BF16)
            msg_ref[to + 1 - core] = picked[g * send : (g + 1) * send].astype(BF16)


def core_sum_kernel(
    chips, hosts, keep_ref, came_ref, value_ref, picked_ref, mine_ref, msg_ref, *rest
):
    total = keep_ref[...].astype(F32) + came_ref[...].astype(F32)
    picked = picked_ref[...].astype(F32)
    deal(chips, hosts, total, picked, value_ref[...], mine_ref, msg_ref, rest)


def received(recv_ref, hosts, chips, side):
    blocks = [
        recv_ref[(g * chips + x) * CORES + side].astype(F32)
        for x in range(chips)
        for g in range(hosts)
    ]
    return jnp.concatenate(blocks, 0).astype(BF16)


def merge_kernel(chips, hosts, recv_ref, mine_ref, place_ref, *refs):
    came, (out_ref, sum_ref) = refs[: chips - 1], refs[chips - 1 :]
    rows = mine_ref.shape[0]
    total = mine_ref[...]
    for k, ref in enumerate(came):
        total = total + ref[:rows, :].astype(F32)
        out_ref[k * rows : (k + 1) * rows, :] = ref[rows:, :]
    total = total + returned(place_ref, recv_ref, hosts, chips)
    sum_ref[...] = total
    low = len(came) * rows
    halo = received(recv_ref, hosts, chips, 1 - lax.axis_index("core"))
    high = low + halo.shape[0]
    out_ref[low:high, :] = halo
    out_ref[high:, :] = total.astype(BF16)


def returned(place_ref, recv_ref, hosts, chips):
    return dot(place_ref[...], received(recv_ref, hosts, chips, lax.axis_index("core")))


def joint(pairs):
    left = jnp.concatenate([a for a, _ in pairs], 1)
    return dot(left, jnp.concatenate([b for _, b in pairs], 0))


def square_of(adj_ref, x, side, rows):
    return adj_ref[pl.ds(pl.multiple_of((x * CORES + side) * rows, rows), rows), :]


def own_chip(adj_refs, blocks):
    chip, core = lax.axis_index("chip"), lax.axis_index("core")
    rows = blocks[0].shape[0]
    parts = [
        joint([(square_of(ref, chip, s, rows), b) for s, b in zip((core, 1 - core), blocks)])
        for ref in adj_refs
    ]
    return jnp.concatenate(parts, 0)


def early_one_kernel(
    chips, adj_ref, lent_ref, value_ref, self_ref, bias_ref, up_ref, weight_ref, neigh_ref, sent_ref,
    agg_ref, direct_ref, grad_ref, col_ref, far_ref, far_t,
):
    value = value_ref[...]
    rows = value.shape[0]
    low = adj_ref.shape[0]
    there = lent_ref[low + rows :, :]
    sent = dot(there, neigh_ref[...]).astype(BF16)
    agg_ref[...] = own_chip((adj_ref, lent_ref), (sent_ref[...], sent))
    both = jnp.concatenate([value, there], 0)
    direct_ref[...] = dot(both, self_ref[...]) + bias_ref[...].reshape(1, -1)
    both = jnp.concatenate([up_ref[...], lent_ref[low : low + rows, :]], 0)
    grad_ref[...] = dot_nt(both, weight_ref[...])
    far = col_ref.shape[0] // chips - rows
    column(chips, far, rows, lax.axis_index("core"), lent_ref, far_t, col_ref)
    far_columns(chips, far_t, far_ref)


def mid_kernel(
    chips, adj_ref, lent_ref, far_ref, far_two_ref, agg_ref, part_ref, sum_ref, here_ref, *refs
):
    came, (agg_out, grad_ref) = refs[:-2], refs[-2:]
    rows = sum_ref.shape[0]
    halo = here_ref[(chips - 1) * rows : here_ref.shape[0] - rows, :]
    for i, (ref, columns) in enumerate(((adj_ref, far_ref), (lent_ref, far_two_ref))):
        pairs = other_chips(chips, ref, came) + [(columns[:, : halo.shape[0]], halo)]
        part = slice(i * rows, (i + 1) * rows)
        agg_out[part, :] = agg_ref[part, :] + joint(pairs)
    grad_ref[:rows, :] = part_ref[:rows, :] + sum_ref[...]
    grad_ref[rows:, :] = part_ref[rows:, :]


def other_chips(chips, adj_ref, came):
    chip, core = lax.axis_index("chip"), lax.axis_index("core")
    pairs = []
    for k, block in enumerate(came):
        rows = block.shape[0] // 2
        x = lax.rem(chip - k - 1 + chips, chips)
        pairs.append((square_of(adj_ref, x, core, rows), block[rows:, :]))
    return pairs


def column_product(chips, hosts, adj_ref, far_ref, value_ref, came, recv_ref):
    rows = value_ref.shape[0]
    chip, core = lax.axis_index("chip"), lax.axis_index("core")
    halo = received(recv_ref, hosts, chips, 1 - core)
    pairs = [(square_of(adj_ref, chip, core, rows), value_ref[...])]
    pairs += other_chips(chips, adj_ref, came) + [(far_ref[:, : halo.shape[0]], halo)]
    return joint(pairs)


def there_kernel(chips, hosts, lent_ref, far_ref, value_ref, recv_ref, *refs):
    came, out_ref = refs[:-1], refs[-1]
    out_ref[...] = column_product(
        chips, hosts, lent_ref, far_ref, value_ref, came, recv_ref
    ).astype(BF16)


def here_kernel(
    chips, hosts, adj_ref, far_ref, sent_ref, recv_ref, value_ref, self_ref, bias_ref, up_ref,
    weight_ref, mine_ref, place_ref, *refs
):
    came, (out_ref, grad_ref) = refs[:-2], refs[-2:]
    rows = mine_ref.shape[0]
    grad = dot_nt(up_ref[...], weight_ref[...]) + mine_ref[...]
    for block in came:
        grad = grad + block[:rows, :].astype(F32)
    grad_ref[...] = grad + returned(place_ref, recv_ref, hosts, chips)
    out = column_product(chips, hosts, adj_ref, far_ref, sent_ref, came, recv_ref)
    out_ref[...] = out + dot(value_ref[...], self_ref[...]) + bias_ref[...].reshape(1, -1)


def add_rest(chips, rows, adj_ref, far_ref, agg, shared_ref):
    chip, core = lax.axis_index("chip"), lax.axis_index("core")
    pairs = []
    for k in range(chips - 1):
        x = lax.rem(chip - k - 1 + chips, chips)
        block = shared_ref[k * rows : (k + 1) * rows, :]
        pairs.append((square_of(adj_ref, x, 1 - core, rows), block))
    half = far_ref.shape[1] // 2
    low = (chips - 1) * rows
    pairs.append((far_ref[:, half:], shared_ref[low : low + half, :]))
    return agg + joint(pairs)


def middle_kernel(
    chips,
    hosts,
    adj_ref,
    lent_ref,
    far_ref,
    far_two_ref,
    col_ref,
    col_two_ref,
    agg_ref,
    direct_ref,
    grad_ref,
    pick_ref,
    shared_ref,
    neigh_one_ref,
    neigh_two_ref,
    hidden_ref,
    sent_ref,
    grad_pre_ref,
    mine_ref,
    msg_ref,
    *rest,
):
    to_refs = rest
    far, rows = pick_ref.shape
    parts = [
        add_rest(chips, rows, ref, columns, agg_ref[i * rows : (i + 1) * rows, :], shared_ref)
        for i, (ref, columns) in enumerate(((adj_ref, far_ref), (lent_ref, far_two_ref)))
    ]
    pre = direct_ref[...] + jnp.concatenate(parts, 0)
    sigmoid = jax.nn.sigmoid(pre)
    hidden = (pre[:rows] * sigmoid[:rows]).astype(BF16)
    hidden_ref[...] = hidden
    sent = dot(hidden, neigh_two_ref[...]).astype(BF16)
    sent_ref[...] = sent
    low = (chips - 1) * rows + chips * far
    add = shared_ref[low:, :].astype(F32)
    grad = jnp.concatenate([grad_ref[:rows, :], grad_ref[rows:, :] + add], 0)
    grad_pre = (grad * sigmoid * (1.0 + pre * (1.0 - sigmoid))).astype(BF16)
    grad_pre_ref[...] = grad_pre[:rows]
    u = dot_nt(grad_pre, neigh_one_ref[...]).astype(BF16)
    total = joint([(col_ref[...], u[:rows]), (col_two_ref[...], u[rows:])])
    picked = dot(pick_ref[...], sent)
    deal(chips, hosts, total, picked, sent, mine_ref, msg_ref, to_refs)


def last_kernel(here_ref, there_ref, output_ref):
    output_ref[...] = (here_ref[...] + there_ref[...].astype(F32)).astype(BF16)


def call(kernel, name, out_shape, in_specs, args, scratch=(), limit=32, flops=0):
    return pl.pallas_call(
        kernel,
        out_shape=out_shape,
        in_specs=in_specs,
        out_specs=jax.tree.map(lambda _: VMEM, out_shape),
        scratch_shapes=scratch,
        compiler_params=pltpu.CompilerParams(vmem_limit_bytes=limit * MIB),
        cost_estimate=pl.CostEstimate(
            flops=flops, bytes_accessed=flops // 1024, transcendentals=0
        ),
        name=name,
    )(*args)


def shift(value, axis, k):
    size = lax.axis_size(axis)
    return lax.ppermute(value, axis, [(i, (i + k) % size) for i in range(size)])


def shape(rows, width, kind=BF16):
    return jax.ShapeDtypeStruct((rows, width), kind)


def body(
    features,
    send_list,
    tile_dst,
    tile_src,
    tile_rows,
    tile_val,
    self_one,
    neigh_one,
    bias_one,
    self_two,
    neigh_two,
    bias_two,
    cotangent,
):
    chips = lax.axis_size("chip")
    hosts = lax.axis_size("hst")
    rows, width = features.shape
    tiles, blk = tile_val.shape[:2]
    send = send_list.shape[3]
    far = hosts * send
    all_rows = chips * CORES * (rows + far)
    count = chips * (rows + far)
    rows_shape = shape(rows, width)
    sum_shape = shape(rows, width, F32)
    both_shape = shape(CORES * rows, width, F32)
    square = 2 * rows * width * width
    far_shape = shape(rows, chips * CORES * far)
    halo_rows = (chips - 1) * rows + chips * far
    dealt = (
        sum_shape,
        jax.ShapeDtypeStruct((chips * hosts * CORES, send, width), BF16),
    ) + (shape(2 * rows, width),) * (chips - 1)

    def across(msg, to):
        terms = [shift(block, "chip", k + 1) for k, block in enumerate(to)]
        recv = lax.all_to_all(msg, ("hst", "chip", "core"), split_axis=0, concat_axis=0, tiled=True)
        return terms, recv

    far_t = pltpu.VMEM((chips * CORES * far, rows), BF16)
    sums = jax.ShapeDtypeStruct(((rows // blk) * (all_rows // blk), blk // PARTS, blk), F32)
    give, up, sent, picked, pick, *sums = call(
        functools.partial(prep_kernel, chips),
        "prep",
        (shape(count, width), rows_shape, rows_shape, shape(far, width), shape(far, rows))
        + (sums,) * PARTS,
        [HBM] * 9,
        [
            pltpu.with_memory_space_constraint(value, pltpu.HBM)
            for value in (
                tile_dst,
                tile_src,
                tile_rows,
                send_list,
                tile_val,
                features,
                cotangent,
                neigh_two,
                neigh_one,
            )
        ],
        [
            pltpu.SMEM(tile_dst.shape, jnp.int32),
            pltpu.SMEM(tile_src.shape, jnp.int32),
            pltpu.SMEM(tile_rows.shape, jnp.int32),
            pltpu.SMEM(send_list.shape, jnp.int32),
            pltpu.VMEM(tile_val.shape, BF16),
            pltpu.VMEM(features.shape, BF16),
            pltpu.VMEM(cotangent.shape, BF16),
            pltpu.VMEM(neigh_two.shape, BF16),
            pltpu.VMEM(neigh_one.shape, BF16),
            pltpu.VMEM((rows, rows), BF16),
            far_t,
            pltpu.VMEM((count, rows), BF16),
            pltpu.SemaphoreType.DMA((8 + CHUNKS,)),
        ],
    )
    came = shift(give, "core", 1)
    adj, col, keep, lend, place, columns = call(
        functools.partial(rest_kernel, chips),
        "rest",
        (
            shape(all_rows, rows),
            shape(count, rows),
            shape(count, width),
            shape(all_rows + 2 * rows, width),
            shape(rows, chips * far),
            far_shape,
        ),
        [VMEM] * (4 + PARTS),
        (up, cotangent, features, pick, *sums),
        [far_t],
        flops=3 * square,
    )
    lent = shift(lend, "core", 1)
    mine, msg, *to = call(
        functools.partial(core_sum_kernel, chips, hosts),
        "core_sum",
        dealt,
        [VMEM] * 4,
        (keep, came, sent, picked),
        flops=60 * square,
    )
    terms, recv = across(msg, to)
    here, summed = call(
        functools.partial(merge_kernel, chips, hosts),
        "merge",
        (shape(halo_rows + rows, width), sum_shape),
        [VMEM] * (2 + chips),
        (recv, mine, place, *terms),
    )
    shared = shift(here, "core", 1)
    agg, direct, grad, col_two, columns_two = call(
        functools.partial(early_one_kernel, chips),
        "early_one",
        (both_shape,) * 3 + (shape(count, rows), far_shape),
        [VMEM] * 9,
        (adj, lent, features, self_one, bias_one, cotangent, self_two, neigh_one, sent),
        [far_t],
        flops=8 * square,
    )
    agg, grad = call(
        functools.partial(mid_kernel, chips),
        "mid",
        (both_shape,) * 2,
        [VMEM] * (7 + chips),
        (adj, lent, columns, columns_two, agg, grad, summed, here, *terms),
        flops=3 * square,
    )
    hidden, sent, grad_pre, mine, msg, *to = call(
        functools.partial(middle_kernel, chips, hosts),
        "middle",
        (rows_shape,) * 3 + dealt,
        [VMEM] * 13,
        (
            adj,
            lent,
            columns,
            columns_two,
            col,
            col_two,
            agg,
            direct,
            grad,
            pick,
            shared,
            neigh_one,
            neigh_two,
        ),
        flops=12 * square,
    )
    terms, recv = across(msg, to)
    there = call(
        functools.partial(there_kernel, chips, hosts),
        "there",
        rows_shape,
        [VMEM] * (3 + chips),
        (lent, columns_two, sent, recv, *terms),
    )
    shared = shift(there, "core", 1)
    here, grad = call(
        functools.partial(here_kernel, chips, hosts),
        "here",
        (sum_shape,) * 2,
        [VMEM] * (10 + chips),
        (
            adj,
            columns,
            sent,
            recv,
            hidden,
            self_two,
            bias_two,
            grad_pre,
            self_one,
            mine,
            place,
            *terms,
        ),
        flops=7 * square,
    )
    output = call(last_kernel, "last", rows_shape, [VMEM] * 2, (here, shared))
    return output, grad


def solution(mesh):
    hosts, devs = mesh.devices.shape
    mesh = Mesh(mesh.devices.reshape(hosts, devs // CORES, CORES), ("hst", "chip", "core"))
    dev = ("chip", "core")
    every = ("hst", "chip", "core")
    return jax.shard_map(
        body,
        mesh=mesh,
        in_specs=(
            P(every, None),
            P("hst", dev, None, None),
            P(every),
            P(every),
            P(every),
            P(every, None, None),
            P(),
            P(),
            P(),
            P(),
            P(),
            P(),
            P(every, None),
        ),
        out_specs=(P(every, None), P(every, None)),
        check_vma=False,
    )
```

```python
import functools

import jax
import jax.numpy as jnp
from jax import lax
from jax.experimental import pallas as pl
from jax.experimental.pallas import tpu as pltpu
from jax.sharding import Mesh, PartitionSpec as P

F32 = jnp.float32
BF16 = jnp.bfloat16
MIB = 1024 * 1024
CHUNKS = 8
PARTS = 4
CORES = 2

VMEM = pl.BlockSpec(memory_space=pltpu.VMEM)
HBM = pl.BlockSpec(memory_space=pltpu.HBM)


def dot(a, b):
    return jnp.dot(a, b, preferred_element_type=F32)


def dot_nt(a, b):
    return lax.dot_general(a, b, (((1,), (1,)), ((), ())), preferred_element_type=F32)


def pick_matrix(send_ref, rows):
    hosts, send = send_ref.shape[2], send_ref.shape[3]
    place = lax.broadcasted_iota(jnp.int32, (send, rows), 0)
    column = lax.broadcasted_iota(jnp.int32, (send, rows), 1)
    parts = []
    for g in range(hosts):
        index = jnp.zeros((send, rows), jnp.int32)
        for s in range(send):
            index = jnp.where(place == s, send_ref[0, 0, g, s], index)
        parts.append(jnp.where(index == column, 1.0, 0.0).astype(F32))
    return jnp.concatenate(parts, 0).astype(BF16)


def column(chips, far, rows, side, adj_ref, far_t, out_ref):
    chip = lax.axis_index("chip")
    each = rows + far
    own_rows = chips * CORES * rows
    for j in range(far_t.shape[0] // rows):
        low = own_rows + j * rows
        far_t[j * rows : (j + 1) * rows, :] = adj_ref[low : low + rows, :].T
    for k in range(chips):
        d = lax.rem(chip + k, chips) * CORES + side
        at = k * each
        out_ref[at : at + rows, :] = adj_ref[pl.ds(pl.multiple_of(d * rows, rows), rows), :].T
        out_ref[at + rows : at + each, :] = far_t[pl.ds(pl.multiple_of(d * far, far), far), :]


def far_columns(chips, far_t, out_ref):
    far = far_t.shape[0] // (chips * CORES)
    core = lax.axis_index("core")
    parts = [
        far_t[pl.ds(pl.multiple_of((x * CORES + side) * far, far), far), :]
        for side in (1 - core, core)
        for x in range(chips)
    ]
    out_ref[...] = jnp.concatenate(parts, 0).T


def prep_kernel(
    chips,
    dst_hbm,
    src_hbm,
    rows_hbm,
    send_hbm,
    tile_hbm,
    cot_hbm,
    neigh_two_hbm,
    give_ref,
    up_ref,
    pick_ref,
    *rest,
):
    accs, rest = rest[:PARTS], rest[PARTS:]
    (
        dst_ref,
        src_ref,
        rows_ref,
        send_ref,
        tile_buf,
        cot_ref,
        neigh_two_ref,
        square,
        far_t,
        col,
        sems,
    ) = rest
    tiles, blk = tile_buf.shape[0], tile_buf.shape[1]
    each = tiles // CHUNKS
    first = CHUNKS * 3 // 4
    chunks = [
        (tile_hbm.at[pl.ds(c * each, each)], tile_buf.at[pl.ds(c * each, each)])
        for c in range(CHUNKS)
    ]
    pairs = [(dst_hbm, dst_ref), (src_hbm, src_ref), (rows_hbm, rows_ref)]
    pairs += chunks[:first]
    pairs += [
        (cot_hbm, cot_ref),
        (neigh_two_hbm, neigh_two_ref),
        (send_hbm, send_ref),
    ]
    pairs += chunks[first:]
    copies = [pltpu.make_async_copy(a, b, sems.at[i]) for i, (a, b) in enumerate(pairs)]
    for copy in copies:
        copy.start()
    rows = cot_ref.shape[0]
    bpd = rows // blk
    sources = accs[0].shape[0] // bpd
    part = accs[0].shape[1]
    far = send_ref.shape[2] * send_ref.shape[3]
    for acc in accs:
        acc[...] = jnp.zeros_like(acc)
    place = lax.broadcasted_iota(jnp.int32, (part, blk), 0)

    def add(t, carry):
        slot = dst_ref[t] * sources + src_ref[t]
        for i, acc in enumerate(accs):
            value = tile_buf[t, i * part : (i + 1) * part, :].astype(F32)
            acc[slot] += jnp.where(place < rows_ref[t] - i * part, value, 0.0)
        return carry

    for copy in copies[:3]:
        copy.wait()
    for c in range(first):
        copies[3 + c].wait()
        lax.fori_loop(c * each, (c + 1) * each, add, 0, unroll=True)
    for copy in copies[3 + first : 6 + first]:
        copy.wait()
    u = dot_nt(cot_ref[...], neigh_two_ref[...]).astype(BF16)
    up_ref[...] = u
    pick_ref[...] = pick_matrix(send_ref, rows)
    for c in range(first, CHUNKS):
        copies[6 + c].wait()
        lax.fori_loop(c * each, (c + 1) * each, add, 0, unroll=True)
    chip, side = lax.axis_index("chip"), 1 - lax.axis_index("core")
    base = chips * CORES
    for j in range(far_t.shape[0] // rows):
        put_square(accs, bpd, base + j, square, 0)
        far_t[j * rows : (j + 1) * rows, :] = square[...].T
    for k in range(chips):
        d = lax.rem(chip + k, chips) * CORES + side
        at = k * (rows + far)
        put_square(accs, bpd, d, square, 0)
        col[at : at + rows, :] = square[...].T
        low = pl.multiple_of(d * far, far)
        col[at + rows : at + rows + far, :] = far_t[pl.ds(low, far), :]
    give_ref[...] = dot(col[...], u).astype(BF16)


def put_square(accs, bpd, d, out_ref, base):
    sources = accs[0].shape[0] // bpd
    part, blk = accs[0].shape[1:]
    for b in range(bpd):
        for j in range(bpd):
            for i, acc in enumerate(accs):
                low = base + b * blk + i * part
                value = acc[b * sources + d * bpd + j].astype(BF16)
                out_ref[low : low + part, j * blk : (j + 1) * blk] = value


def rest_kernel(chips, up_ref, cot_ref, value_ref, pick_ref, neigh_ref, *refs):
    accs = refs[:PARTS]
    sent_ref, picked_ref, adj_ref, col_ref, keep_ref, lend_ref, place_ref, far_ref, far_t = refs[PARTS:]
    sent = dot(value_ref[...], neigh_ref[...]).astype(BF16)
    sent_ref[...] = sent
    picked_ref[...] = dot(pick_ref[...], sent).astype(BF16)
    rows = up_ref.shape[0]
    bpd = rows // accs[0].shape[2]
    for d in range(adj_ref.shape[0] // rows):
        put_square(accs, bpd, d, adj_ref, d * rows)
    far = col_ref.shape[0] // chips - rows
    column(chips, far, rows, lax.axis_index("core"), adj_ref, far_t, col_ref)
    far_columns(chips, far_t, far_ref)
    keep_ref[...] = dot(col_ref[...], up_ref[...]).astype(BF16)
    low = adj_ref.shape[0]
    lend_ref[:low, :] = adj_ref[...]
    lend_ref[low : low + rows, :] = cot_ref[...]
    lend_ref[low + rows :, :] = value_ref[...]
    place_ref[...] = jnp.concatenate([pick_ref[...]] * chips, 0).T


def deal(chips, hosts, total, picked, value, mine_ref, msg_ref, to_refs):
    rows = value.shape[0]
    far = picked.shape[0]
    send = far // hosts
    each = rows + far
    chip, core = lax.axis_index("chip"), lax.axis_index("core")
    mine_ref[...] = total[:rows]
    for k in range(chips):
        low = k * each + rows
        if k > 0:
            to_refs[k - 1][:rows, :] = total[k * each : low].astype(BF16)
            to_refs[k - 1][rows:, :] = value
        x = lax.rem(chip + k, chips)
        for g in range(hosts):
            at = low + g * send
            to = (g * chips + x) * CORES
            msg_ref[to + core] = total[at : at + send].astype(BF16)
            msg_ref[to + 1 - core] = picked[g * send : (g + 1) * send].astype(BF16)


def core_sum_kernel(
    chips, hosts, keep_ref, came_ref, value_ref, picked_ref, mine_ref, msg_ref, *rest
):
    total = keep_ref[...].astype(F32) + came_ref[...].astype(F32)
    picked = picked_ref[...].astype(F32)
    deal(chips, hosts, total, picked, value_ref[...], mine_ref, msg_ref, rest)


def received(recv_ref, hosts, chips, side):
    blocks = [
        recv_ref[(g * chips + x) * CORES + side].astype(F32)
        for x in range(chips)
        for g in range(hosts)
    ]
    return jnp.concatenate(blocks, 0).astype(BF16)


def merge_kernel(chips, hosts, recv_ref, mine_ref, place_ref, *refs):
    came, (out_ref, sum_ref) = refs[: chips - 1], refs[chips - 1 :]
    rows = mine_ref.shape[0]
    total = mine_ref[...]
    for k, ref in enumerate(came):
        total = total + ref[:rows, :].astype(F32)
        out_ref[k * rows : (k + 1) * rows, :] = ref[rows:, :]
    total = total + returned(place_ref, recv_ref, hosts, chips)
    sum_ref[...] = total
    low = len(came) * rows
    halo = received(recv_ref, hosts, chips, 1 - lax.axis_index("core"))
    high = low + halo.shape[0]
    out_ref[low:high, :] = halo
    out_ref[high:, :] = total.astype(BF16)


def returned(place_ref, recv_ref, hosts, chips):
    return dot(place_ref[...], received(recv_ref, hosts, chips, lax.axis_index("core")))


def joint(pairs):
    left = jnp.concatenate([a for a, _ in pairs], 1)
    return dot(left, jnp.concatenate([b for _, b in pairs], 0))


def square_of(adj_ref, x, side, rows):
    return adj_ref[pl.ds(pl.multiple_of((x * CORES + side) * rows, rows), rows), :]


def own_chip(adj_refs, blocks):
    chip, core = lax.axis_index("chip"), lax.axis_index("core")
    rows = blocks[0].shape[0]
    parts = [
        joint([(square_of(ref, chip, s, rows), b) for s, b in zip((core, 1 - core), blocks)])
        for ref in adj_refs
    ]
    return jnp.concatenate(parts, 0)


def early_one_kernel(
    chips, adj_ref, lent_ref, value_ref, self_ref, bias_ref, up_ref, weight_ref, neigh_ref, sent_ref, unused_ref,
    agg_ref, direct_ref, grad_ref, col_ref, far_ref, far_t,
):
    value = value_ref[...]
    rows = value.shape[0]
    low = adj_ref.shape[0]
    there = lent_ref[low + rows :, :]
    sent = dot(there, neigh_ref[...]).astype(BF16)
    agg_ref[...] = own_chip((adj_ref, lent_ref), (sent_ref[...], sent))
    both = jnp.concatenate([value, there], 0)
    direct_ref[...] = dot(both, self_ref[...]) + bias_ref[...].reshape(1, -1)
    both = jnp.concatenate([up_ref[...], lent_ref[low : low + rows, :]], 0)
    grad_ref[...] = dot_nt(both, weight_ref[...])
    far = col_ref.shape[0] // chips - rows
    column(chips, far, rows, lax.axis_index("core"), lent_ref, far_t, col_ref)
    far_columns(chips, far_t, far_ref)


def mid_kernel(
    chips, adj_ref, lent_ref, far_ref, far_two_ref, agg_ref, part_ref, sum_ref, here_ref, *refs
):
    came, (agg_out, grad_ref) = refs[:-2], refs[-2:]
    rows = sum_ref.shape[0]
    halo = here_ref[(chips - 1) * rows : here_ref.shape[0] - rows, :]
    for i, (ref, columns) in enumerate(((adj_ref, far_ref), (lent_ref, far_two_ref))):
        pairs = other_chips(chips, ref, came) + [(columns[:, : halo.shape[0]], halo)]
        part = slice(i * rows, (i + 1) * rows)
        agg_out[part, :] = agg_ref[part, :] + joint(pairs)
    grad_ref[:rows, :] = part_ref[:rows, :] + sum_ref[...]
    grad_ref[rows:, :] = part_ref[rows:, :]


def other_chips(chips, adj_ref, came):
    chip, core = lax.axis_index("chip"), lax.axis_index("core")
    pairs = []
    for k, block in enumerate(came):
        rows = block.shape[0] // 2
        x = lax.rem(chip - k - 1 + chips, chips)
        pairs.append((square_of(adj_ref, x, core, rows), block[rows:, :]))
    return pairs


def column_product(chips, hosts, adj_ref, far_ref, value_ref, came, recv_ref):
    rows = value_ref.shape[0]
    chip, core = lax.axis_index("chip"), lax.axis_index("core")
    halo = received(recv_ref, hosts, chips, 1 - core)
    pairs = [(square_of(adj_ref, chip, core, rows), value_ref[...])]
    pairs += other_chips(chips, adj_ref, came) + [(far_ref[:, : halo.shape[0]], halo)]
    return joint(pairs)


def there_kernel(chips, hosts, lent_ref, far_ref, value_ref, recv_ref, *refs):
    came, out_ref = refs[:-1], refs[-1]
    out_ref[...] = column_product(
        chips, hosts, lent_ref, far_ref, value_ref, came, recv_ref
    ).astype(BF16)


def here_kernel(
    chips, hosts, adj_ref, far_ref, sent_ref, recv_ref, value_ref, self_ref, bias_ref, up_ref,
    weight_ref, mine_ref, place_ref, *refs
):
    came, (out_ref, grad_ref) = refs[:-2], refs[-2:]
    rows = mine_ref.shape[0]
    grad = dot_nt(up_ref[...], weight_ref[...]) + mine_ref[...]
    for block in came:
        grad = grad + block[:rows, :].astype(F32)
    grad_ref[...] = grad + returned(place_ref, recv_ref, hosts, chips)
    out = column_product(chips, hosts, adj_ref, far_ref, sent_ref, came, recv_ref)
    out_ref[...] = out + dot(value_ref[...], self_ref[...]) + bias_ref[...].reshape(1, -1)


def add_rest(chips, rows, adj_ref, far_ref, agg, shared_ref):
    chip, core = lax.axis_index("chip"), lax.axis_index("core")
    pairs = []
    for k in range(chips - 1):
        x = lax.rem(chip - k - 1 + chips, chips)
        block = shared_ref[k * rows : (k + 1) * rows, :]
        pairs.append((square_of(adj_ref, x, 1 - core, rows), block))
    half = far_ref.shape[1] // 2
    low = (chips - 1) * rows
    pairs.append((far_ref[:, half:], shared_ref[low : low + half, :]))
    return agg + joint(pairs)


def middle_kernel(
    chips,
    hosts,
    adj_ref,
    lent_ref,
    far_ref,
    far_two_ref,
    col_ref,
    col_two_ref,
    agg_ref,
    direct_ref,
    grad_ref,
    pick_ref,
    shared_ref,
    neigh_one_ref,
    neigh_two_ref,
    hidden_ref,
    sent_ref,
    grad_pre_ref,
    mine_ref,
    msg_ref,
    *rest,
):
    to_refs = rest
    far, rows = pick_ref.shape
    parts = [
        add_rest(chips, rows, ref, columns, agg_ref[i * rows : (i + 1) * rows, :], shared_ref)
        for i, (ref, columns) in enumerate(((adj_ref, far_ref), (lent_ref, far_two_ref)))
    ]
    pre = direct_ref[...] + jnp.concatenate(parts, 0)
    sigmoid = jax.nn.sigmoid(pre)
    hidden = (pre[:rows] * sigmoid[:rows]).astype(BF16)
    hidden_ref[...] = hidden
    sent = dot(hidden, neigh_two_ref[...]).astype(BF16)
    sent_ref[...] = sent
    low = (chips - 1) * rows + chips * far
    add = shared_ref[low:, :].astype(F32)
    grad = jnp.concatenate([grad_ref[:rows, :], grad_ref[rows:, :] + add], 0)
    grad_pre = (grad * sigmoid * (1.0 + pre * (1.0 - sigmoid))).astype(BF16)
    grad_pre_ref[...] = grad_pre[:rows]
    u = dot_nt(grad_pre, neigh_one_ref[...]).astype(BF16)
    total = joint([(col_ref[...], u[:rows]), (col_two_ref[...], u[rows:])])
    picked = dot(pick_ref[...], sent)
    deal(chips, hosts, total, picked, sent, mine_ref, msg_ref, to_refs)


def last_kernel(here_ref, there_ref, output_ref):
    output_ref[...] = (here_ref[...] + there_ref[...].astype(F32)).astype(BF16)


def call(kernel, name, out_shape, in_specs, args, scratch=(), limit=32, flops=0):
    return pl.pallas_call(
        kernel,
        out_shape=out_shape,
        in_specs=in_specs,
        out_specs=jax.tree.map(lambda _: VMEM, out_shape),
        scratch_shapes=scratch,
        compiler_params=pltpu.CompilerParams(vmem_limit_bytes=limit * MIB),
        cost_estimate=pl.CostEstimate(
            flops=flops, bytes_accessed=flops // 1024, transcendentals=0
        ),
        name=name,
    )(*args)


def shift(value, axis, k):
    size = lax.axis_size(axis)
    return lax.ppermute(value, axis, [(i, (i + k) % size) for i in range(size)])


def shape(rows, width, kind=BF16):
    return jax.ShapeDtypeStruct((rows, width), kind)


def body(
    features,
    send_list,
    tile_dst,
    tile_src,
    tile_rows,
    tile_val,
    self_one,
    neigh_one,
    bias_one,
    self_two,
    neigh_two,
    bias_two,
    cotangent,
):
    chips = lax.axis_size("chip")
    hosts = lax.axis_size("hst")
    rows, width = features.shape
    tiles, blk = tile_val.shape[:2]
    send = send_list.shape[3]
    far = hosts * send
    all_rows = chips * CORES * (rows + far)
    count = chips * (rows + far)
    rows_shape = shape(rows, width)
    sum_shape = shape(rows, width, F32)
    both_shape = shape(CORES * rows, width, F32)
    square = 2 * rows * width * width
    far_shape = shape(rows, chips * CORES * far)
    halo_rows = (chips - 1) * rows + chips * far
    dealt = (
        sum_shape,
        jax.ShapeDtypeStruct((chips * hosts * CORES, send, width), BF16),
    ) + (shape(2 * rows, width),) * (chips - 1)

    def across(msg, to):
        terms = [shift(block, "chip", k + 1) for k, block in enumerate(to)]
        recv = lax.all_to_all(msg, ("hst", "chip", "core"), split_axis=0, concat_axis=0, tiled=True)
        return terms, recv

    far_t = pltpu.VMEM((chips * CORES * far, rows), BF16)
    sums = jax.ShapeDtypeStruct(((rows // blk) * (all_rows // blk), blk // PARTS, blk), F32)
    give, up, pick, *sums = call(
        functools.partial(prep_kernel, chips),
        "prep",
        (shape(count, width), rows_shape, shape(far, rows)) + (sums,) * PARTS,
        [HBM] * 7,
        [
            pltpu.with_memory_space_constraint(value, pltpu.HBM)
            for value in (
                tile_dst,
                tile_src,
                tile_rows,
                send_list,
                tile_val,
                cotangent,
                neigh_two,
            )
        ],
        [
            pltpu.SMEM(tile_dst.shape, jnp.int32),
            pltpu.SMEM(tile_src.shape, jnp.int32),
            pltpu.SMEM(tile_rows.shape, jnp.int32),
            pltpu.SMEM(send_list.shape, jnp.int32),
            pltpu.VMEM(tile_val.shape, BF16),
            pltpu.VMEM(cotangent.shape, BF16),
            pltpu.VMEM(neigh_two.shape, BF16),
            pltpu.VMEM((rows, rows), BF16),
            far_t,
            pltpu.VMEM((count, rows), BF16),
            pltpu.SemaphoreType.DMA((6 + CHUNKS,)),
        ],
    )
    came = shift(give, "core", 1)
    sent, picked, adj, col, keep, lend, place, columns = call(
        functools.partial(rest_kernel, chips),
        "rest",
        (
            rows_shape,
            shape(far, width),
            shape(all_rows, rows),
            shape(count, rows),
            shape(count, width),
            shape(all_rows + 2 * rows, width),
            shape(rows, chips * far),
            far_shape,
        ),
        [VMEM] * (5 + PARTS),
        (up, cotangent, features, pick, neigh_one, *sums),
        [far_t],
        flops=3 * square,
    )
    lent = shift(lend, "core", 1)
    mine, msg, *to = call(
        functools.partial(core_sum_kernel, chips, hosts),
        "core_sum",
        dealt,
        [VMEM] * 4,
        (keep, came, sent, picked),
        flops=60 * square,
    )
    terms, recv = across(msg, to)
    here, summed = call(
        functools.partial(merge_kernel, chips, hosts),
        "merge",
        (shape(halo_rows + rows, width), sum_shape),
        [VMEM] * (2 + chips),
        (recv, mine, place, *terms),
    )
    shared = shift(here, "core", 1)
    agg, direct, grad, col_two, columns_two = call(
        functools.partial(early_one_kernel, chips),
        "early_one",
        (both_shape,) * 3 + (shape(count, rows), far_shape),
        [VMEM] * 10,
        (
            adj,
            lent,
            features,
            self_one,
            bias_one,
            cotangent,
            self_two,
            neigh_one,
            sent,
            neigh_two,
        ),
        [far_t],
        flops=8 * square,
    )
    agg, grad = call(
        functools.partial(mid_kernel, chips),
        "mid",
        (both_shape,) * 2,
        [VMEM] * (7 + chips),
        (adj, lent, columns, columns_two, agg, grad, summed, here, *terms),
        flops=3 * square,
    )
    hidden, sent, grad_pre, mine, msg, *to = call(
        functools.partial(middle_kernel, chips, hosts),
        "middle",
        (rows_shape,) * 3 + dealt,
        [VMEM] * 13,
        (
            adj,
            lent,
            columns,
            columns_two,
            col,
            col_two,
            agg,
            direct,
            grad,
            pick,
            shared,
            neigh_one,
            neigh_two,
        ),
        flops=12 * square,
    )
    terms, recv = across(msg, to)
    there = call(
        functools.partial(there_kernel, chips, hosts),
        "there",
        rows_shape,
        [VMEM] * (3 + chips),
        (lent, columns_two, sent, recv, *terms),
    )
    shared = shift(there, "core", 1)
    here, grad = call(
        functools.partial(here_kernel, chips, hosts),
        "here",
        (sum_shape,) * 2,
        [VMEM] * (10 + chips),
        (
            adj,
            columns,
            sent,
            recv,
            hidden,
            self_two,
            bias_two,
            grad_pre,
            self_one,
            mine,
            place,
            *terms,
        ),
        flops=7 * square,
    )
    output = call(last_kernel, "last", rows_shape, [VMEM] * 2, (here, shared))
    return output, grad


def solution(mesh):
    hosts, devs = mesh.devices.shape
    mesh = Mesh(mesh.devices.reshape(hosts, devs // CORES, CORES), ("hst", "chip", "core"))
    dev = ("chip", "core")
    every = ("hst", "chip", "core")
    return jax.shard_map(
        body,
        mesh=mesh,
        in_specs=(
            P(every, None),
            P("hst", dev, None, None),
            P(every),
            P(every),
            P(every),
            P(every, None, None),
            P(),
            P(),
            P(),
            P(),
            P(),
            P(),
            P(every, None),
        ),
        out_specs=(P(every, None), P(every, None)),
        check_vma=False,
    )
```

```python
import functools

import jax
import jax.numpy as jnp
from jax import lax
from jax.experimental import pallas as pl
from jax.experimental.pallas import tpu as pltpu
from jax.sharding import Mesh, PartitionSpec as P

F32 = jnp.float32
BF16 = jnp.bfloat16
MIB = 1024 * 1024
CHUNKS = 8
PARTS = 4
CORES = 2

VMEM = pl.BlockSpec(memory_space=pltpu.VMEM)
HBM = pl.BlockSpec(memory_space=pltpu.HBM)


def dot(a, b):
    return jnp.dot(a, b, preferred_element_type=F32)


def dot_nt(a, b):
    return lax.dot_general(a, b, (((1,), (1,)), ((), ())), preferred_element_type=F32)


def pick_matrix(send_ref, rows):
    hosts, send = send_ref.shape[2], send_ref.shape[3]
    place = lax.broadcasted_iota(jnp.int32, (send, rows), 0)
    column = lax.broadcasted_iota(jnp.int32, (send, rows), 1)
    parts = []
    for g in range(hosts):
        index = jnp.zeros((send, rows), jnp.int32)
        for s in range(send):
            index = jnp.where(place == s, send_ref[0, 0, g, s], index)
        parts.append(jnp.where(index == column, 1.0, 0.0).astype(F32))
    return jnp.concatenate(parts, 0).astype(BF16)


def column(chips, far, rows, side, adj_ref, far_t, out_ref):
    chip = lax.axis_index("chip")
    each = rows + far
    own_rows = chips * CORES * rows
    for j in range(far_t.shape[0] // rows):
        low = own_rows + j * rows
        far_t[j * rows : (j + 1) * rows, :] = adj_ref[low : low + rows, :].T
    for k in range(chips):
        d = lax.rem(chip + k, chips) * CORES + side
        at = k * each
        out_ref[at : at + rows, :] = adj_ref[pl.ds(pl.multiple_of(d * rows, rows), rows), :].T
        out_ref[at + rows : at + each, :] = far_t[pl.ds(pl.multiple_of(d * far, far), far), :]


def far_columns(chips, far_t, out_ref):
    far = far_t.shape[0] // (chips * CORES)
    core = lax.axis_index("core")
    parts = [
        far_t[pl.ds(pl.multiple_of((x * CORES + side) * far, far), far), :]
        for side in (1 - core, core)
        for x in range(chips)
    ]
    out_ref[...] = jnp.concatenate(parts, 0).T


def prep_kernel(
    chips,
    dst_hbm,
    src_hbm,
    rows_hbm,
    send_hbm,
    tile_hbm,
    cot_hbm,
    neigh_two_hbm,
    give_ref,
    up_ref,
    pick_ref,
    *rest,
):
    accs, rest = rest[:PARTS], rest[PARTS:]
    (
        dst_ref,
        src_ref,
        rows_ref,
        send_ref,
        tile_buf,
        cot_ref,
        neigh_two_ref,
        square,
        far_t,
        col,
        sems,
    ) = rest
    tiles, blk = tile_buf.shape[0], tile_buf.shape[1]
    each = tiles // CHUNKS
    first = CHUNKS * 3 // 4
    chunks = [
        (tile_hbm.at[pl.ds(c * each, each)], tile_buf.at[pl.ds(c * each, each)])
        for c in range(CHUNKS)
    ]
    pairs = [(dst_hbm, dst_ref), (src_hbm, src_ref), (rows_hbm, rows_ref)]
    pairs += chunks[:first]
    pairs += [
        (cot_hbm, cot_ref),
        (neigh_two_hbm, neigh_two_ref),
        (send_hbm, send_ref),
    ]
    pairs += chunks[first:]
    copies = [pltpu.make_async_copy(a, b, sems.at[i]) for i, (a, b) in enumerate(pairs)]
    for copy in copies:
        copy.start()
    rows = cot_ref.shape[0]
    bpd = rows // blk
    sources = accs[0].shape[0] // bpd
    part = accs[0].shape[1]
    far = send_ref.shape[2] * send_ref.shape[3]
    for acc in accs:
        acc[...] = jnp.zeros_like(acc)
    place = lax.broadcasted_iota(jnp.int32, (part, blk), 0)

    def add(t, carry):
        slot = dst_ref[t] * sources + src_ref[t]
        for i, acc in enumerate(accs):
            value = tile_buf[t, i * part : (i + 1) * part, :].astype(F32)
            acc[slot] += jnp.where(place < rows_ref[t] - i * part, value, 0.0)
        return carry

    for copy in copies[:3]:
        copy.wait()
    for c in range(first):
        copies[3 + c].wait()
        lax.fori_loop(c * each, (c + 1) * each, add, 0, unroll=True)
    for copy in copies[3 + first : 6 + first]:
        copy.wait()
    u = dot_nt(cot_ref[...], neigh_two_ref[...]).astype(BF16)
    up_ref[...] = u
    pick_ref[...] = pick_matrix(send_ref, rows)
    for c in range(first, CHUNKS):
        copies[6 + c].wait()
        lax.fori_loop(c * each, (c + 1) * each, add, 0, unroll=True)
    chip, side = lax.axis_index("chip"), 1 - lax.axis_index("core")
    base = chips * CORES
    for j in range(far_t.shape[0] // rows):
        put_square(accs, bpd, base + j, square, 0)
        far_t[j * rows : (j + 1) * rows, :] = square[...].T
    for k in range(chips):
        d = lax.rem(chip + k, chips) * CORES + side
        at = k * (rows + far)
        put_square(accs, bpd, d, square, 0)
        col[at : at + rows, :] = square[...].T
        low = pl.multiple_of(d * far, far)
        col[at + rows : at + rows + far, :] = far_t[pl.ds(low, far), :]
    give_ref[...] = dot(col[...], u).astype(BF16)


def put_square(accs, bpd, d, out_ref, base):
    sources = accs[0].shape[0] // bpd
    part, blk = accs[0].shape[1:]
    for b in range(bpd):
        for j in range(bpd):
            for i, acc in enumerate(accs):
                low = base + b * blk + i * part
                value = acc[b * sources + d * bpd + j].astype(BF16)
                out_ref[low : low + part, j * blk : (j + 1) * blk] = value


def rest_kernel(chips, up_ref, cot_ref, value_ref, pick_ref, neigh_ref, *refs):
    accs = refs[:PARTS]
    sent_ref, picked_ref, adj_ref, col_ref, keep_ref, lend_ref, place_ref, far_ref, far_t = refs[PARTS:]
    sent = dot(value_ref[...], neigh_ref[...]).astype(BF16)
    sent_ref[...] = sent
    picked_ref[...] = dot(pick_ref[...], sent).astype(BF16)
    rows = up_ref.shape[0]
    bpd = rows // accs[0].shape[2]
    for d in range(adj_ref.shape[0] // rows):
        put_square(accs, bpd, d, adj_ref, d * rows)
    far = col_ref.shape[0] // chips - rows
    column(chips, far, rows, lax.axis_index("core"), adj_ref, far_t, col_ref)
    far_columns(chips, far_t, far_ref)
    keep_ref[...] = dot(col_ref[...], up_ref[...]).astype(BF16)
    low = adj_ref.shape[0]
    lend_ref[:low, :] = adj_ref[...]
    lend_ref[low : low + rows, :] = cot_ref[...]
    lend_ref[low + rows :, :] = value_ref[...]
    place_ref[...] = jnp.concatenate([pick_ref[...]] * chips, 0).T


def deal(chips, hosts, total, picked, value, mine_ref, msg_ref, to_refs):
    rows = value.shape[0]
    far = picked.shape[0]
    send = far // hosts
    each = rows + far
    chip, core = lax.axis_index("chip"), lax.axis_index("core")
    mine_ref[...] = total[:rows]
    for k in range(chips):
        low = k * each + rows
        if k > 0:
            to_refs[k - 1][:rows, :] = total[k * each : low].astype(BF16)
            to_refs[k - 1][rows:, :] = value
        x = lax.rem(chip + k, chips)
        for g in range(hosts):
            at = low + g * send
            to = (g * chips + x) * CORES
            msg_ref[to + core] = total[at : at + send].astype(BF16)
            msg_ref[to + 1 - core] = picked[g * send : (g + 1) * send].astype(BF16)


def core_sum_kernel(
    chips, hosts, keep_ref, came_ref, value_ref, picked_ref, mine_ref, msg_ref, *rest
):
    total = keep_ref[...].astype(F32) + came_ref[...].astype(F32)
    picked = picked_ref[...].astype(F32)
    deal(chips, hosts, total, picked, value_ref[...], mine_ref, msg_ref, rest)


def received(recv_ref, hosts, chips, side):
    blocks = [
        recv_ref[(g * chips + x) * CORES + side].astype(F32)
        for x in range(chips)
        for g in range(hosts)
    ]
    return jnp.concatenate(blocks, 0).astype(BF16)


def merge_kernel(chips, hosts, recv_ref, mine_ref, place_ref, *refs):
    came, (out_ref, sum_ref) = refs[: chips - 1], refs[chips - 1 :]
    rows = mine_ref.shape[0]
    total = mine_ref[...]
    for k, ref in enumerate(came):
        total = total + ref[:rows, :].astype(F32)
        out_ref[k * rows : (k + 1) * rows, :] = ref[rows:, :]
    total = total + returned(place_ref, recv_ref, hosts, chips)
    sum_ref[...] = total
    low = len(came) * rows
    halo = received(recv_ref, hosts, chips, 1 - lax.axis_index("core"))
    high = low + halo.shape[0]
    out_ref[low:high, :] = halo
    out_ref[high:, :] = total.astype(BF16)


def returned(place_ref, recv_ref, hosts, chips):
    return dot(place_ref[...], received(recv_ref, hosts, chips, lax.axis_index("core")))


def joint(pairs):
    left = jnp.concatenate([a for a, _ in pairs], 1)
    return dot(left, jnp.concatenate([b for _, b in pairs], 0))


def square_of(adj_ref, x, side, rows):
    return adj_ref[pl.ds(pl.multiple_of((x * CORES + side) * rows, rows), rows), :]


def own_chip(adj_refs, blocks):
    chip, core = lax.axis_index("chip"), lax.axis_index("core")
    rows = blocks[0].shape[0]
    parts = [
        joint([(square_of(ref, chip, s, rows), b) for s, b in zip((core, 1 - core), blocks)])
        for ref in adj_refs
    ]
    return jnp.concatenate(parts, 0)


def early_one_kernel(
    chips, adj_ref, lent_ref, value_ref, self_ref, bias_ref, up_ref, weight_ref, neigh_ref, sent_ref, unused_ref,
    agg_ref, direct_ref, grad_ref, col_ref, far_ref, far_t,
):
    value = value_ref[...]
    rows = value.shape[0]
    low = adj_ref.shape[0]
    there = lent_ref[low + rows :, :]
    sent = dot(there, neigh_ref[...]).astype(BF16)
    agg_ref[...] = own_chip((adj_ref, lent_ref), (sent_ref[...], sent))
    both = jnp.concatenate([value, there], 0)
    direct_ref[...] = dot(both, self_ref[...]) + bias_ref[...].reshape(1, -1)
    both = jnp.concatenate([up_ref[...], lent_ref[low : low + rows, :]], 0)
    grad_ref[...] = dot_nt(both, weight_ref[...])
    far = col_ref.shape[0] // chips - rows
    column(chips, far, rows, lax.axis_index("core"), lent_ref, far_t, col_ref)
    far_columns(chips, far_t, far_ref)


def mid_kernel(
    chips, adj_ref, lent_ref, far_ref, far_two_ref, agg_ref, part_ref, sum_ref, here_ref, *refs
):
    came, (agg_out, grad_ref) = refs[:-2], refs[-2:]
    rows = sum_ref.shape[0]
    halo = here_ref[(chips - 1) * rows : here_ref.shape[0] - rows, :]
    for i, (ref, columns) in enumerate(((adj_ref, far_ref), (lent_ref, far_two_ref))):
        pairs = other_chips(chips, ref, came) + [(columns[:, : halo.shape[0]], halo)]
        part = slice(i * rows, (i + 1) * rows)
        agg_out[part, :] = agg_ref[part, :] + joint(pairs)
    grad_ref[:rows, :] = part_ref[:rows, :] + sum_ref[...]
    grad_ref[rows:, :] = part_ref[rows:, :]


def other_chips(chips, adj_ref, came):
    chip, core = lax.axis_index("chip"), lax.axis_index("core")
    pairs = []
    for k, block in enumerate(came):
        rows = block.shape[0] // 2
        x = lax.rem(chip - k - 1 + chips, chips)
        pairs.append((square_of(adj_ref, x, core, rows), block[rows:, :]))
    return pairs


def column_product(chips, hosts, adj_ref, far_ref, value_ref, came, recv_ref):
    rows = value_ref.shape[0]
    chip, core = lax.axis_index("chip"), lax.axis_index("core")
    halo = received(recv_ref, hosts, chips, 1 - core)
    pairs = [(square_of(adj_ref, chip, core, rows), value_ref[...])]
    pairs += other_chips(chips, adj_ref, came) + [(far_ref[:, : halo.shape[0]], halo)]
    return joint(pairs)


def there_kernel(chips, hosts, lent_ref, far_ref, value_ref, recv_ref, *refs):
    came, out_ref = refs[:-1], refs[-1]
    out_ref[...] = column_product(
        chips, hosts, lent_ref, far_ref, value_ref, came, recv_ref
    ).astype(BF16)


def here_kernel(
    chips, hosts, adj_ref, far_ref, sent_ref, recv_ref, value_ref, self_ref, bias_ref, up_ref,
    weight_ref, neigh_ref, mine_ref, place_ref, *refs
):
    came, (out_ref, grad_ref) = refs[:-2], refs[-2:]
    rows = mine_ref.shape[0]
    total = mine_ref[...] + returned(place_ref, recv_ref, hosts, chips)
    for block in came:
        total = total + block[:rows, :].astype(F32)
    grad = dot_nt(total.astype(BF16), neigh_ref[...])
    grad_ref[...] = grad + dot_nt(up_ref[...], weight_ref[...])
    out = column_product(chips, hosts, adj_ref, far_ref, sent_ref, came, recv_ref)
    out_ref[...] = out + dot(value_ref[...], self_ref[...]) + bias_ref[...].reshape(1, -1)


def add_rest(chips, rows, adj_ref, far_ref, agg, shared_ref):
    chip, core = lax.axis_index("chip"), lax.axis_index("core")
    pairs = []
    for k in range(chips - 1):
        x = lax.rem(chip - k - 1 + chips, chips)
        block = shared_ref[k * rows : (k + 1) * rows, :]
        pairs.append((square_of(adj_ref, x, 1 - core, rows), block))
    half = far_ref.shape[1] // 2
    low = (chips - 1) * rows
    pairs.append((far_ref[:, half:], shared_ref[low : low + half, :]))
    return agg + joint(pairs)


def middle_kernel(
    chips,
    hosts,
    adj_ref,
    lent_ref,
    far_ref,
    far_two_ref,
    col_ref,
    col_two_ref,
    agg_ref,
    direct_ref,
    grad_ref,
    pick_ref,
    shared_ref,
    neigh_two_ref,
    hidden_ref,
    sent_ref,
    grad_pre_ref,
    mine_ref,
    msg_ref,
    *rest,
):
    to_refs = rest
    far, rows = pick_ref.shape
    parts = [
        add_rest(chips, rows, ref, columns, agg_ref[i * rows : (i + 1) * rows, :], shared_ref)
        for i, (ref, columns) in enumerate(((adj_ref, far_ref), (lent_ref, far_two_ref)))
    ]
    pre = direct_ref[...] + jnp.concatenate(parts, 0)
    sigmoid = jax.nn.sigmoid(pre)
    hidden = (pre[:rows] * sigmoid[:rows]).astype(BF16)
    hidden_ref[...] = hidden
    sent = dot(hidden, neigh_two_ref[...]).astype(BF16)
    sent_ref[...] = sent
    low = (chips - 1) * rows + chips * far
    add = shared_ref[low:, :].astype(F32)
    grad = jnp.concatenate([grad_ref[:rows, :], grad_ref[rows:, :] + add], 0)
    grad_pre = (grad * sigmoid * (1.0 + pre * (1.0 - sigmoid))).astype(BF16)
    grad_pre_ref[...] = grad_pre[:rows]
    total = joint([(col_ref[...], grad_pre[:rows]), (col_two_ref[...], grad_pre[rows:])])
    picked = dot(pick_ref[...], sent)
    deal(chips, hosts, total, picked, sent, mine_ref, msg_ref, to_refs)


def last_kernel(here_ref, there_ref, output_ref):
    output_ref[...] = (here_ref[...] + there_ref[...].astype(F32)).astype(BF16)


def call(kernel, name, out_shape, in_specs, args, scratch=(), limit=32, flops=0):
    return pl.pallas_call(
        kernel,
        out_shape=out_shape,
        in_specs=in_specs,
        out_specs=jax.tree.map(lambda _: VMEM, out_shape),
        scratch_shapes=scratch,
        compiler_params=pltpu.CompilerParams(vmem_limit_bytes=limit * MIB),
        cost_estimate=pl.CostEstimate(
            flops=flops, bytes_accessed=flops // 1024, transcendentals=0
        ),
        name=name,
    )(*args)


def shift(value, axis, k):
    size = lax.axis_size(axis)
    return lax.ppermute(value, axis, [(i, (i + k) % size) for i in range(size)])


def shape(rows, width, kind=BF16):
    return jax.ShapeDtypeStruct((rows, width), kind)


def body(
    features,
    send_list,
    tile_dst,
    tile_src,
    tile_rows,
    tile_val,
    self_one,
    neigh_one,
    bias_one,
    self_two,
    neigh_two,
    bias_two,
    cotangent,
):
    chips = lax.axis_size("chip")
    hosts = lax.axis_size("hst")
    rows, width = features.shape
    tiles, blk = tile_val.shape[:2]
    send = send_list.shape[3]
    far = hosts * send
    all_rows = chips * CORES * (rows + far)
    count = chips * (rows + far)
    rows_shape = shape(rows, width)
    sum_shape = shape(rows, width, F32)
    both_shape = shape(CORES * rows, width, F32)
    square = 2 * rows * width * width
    far_shape = shape(rows, chips * CORES * far)
    halo_rows = (chips - 1) * rows + chips * far
    dealt = (
        sum_shape,
        jax.ShapeDtypeStruct((chips * hosts * CORES, send, width), BF16),
    ) + (shape(2 * rows, width),) * (chips - 1)

    def across(msg, to):
        terms = [shift(block, "chip", k + 1) for k, block in enumerate(to)]
        recv = lax.all_to_all(msg, ("hst", "chip", "core"), split_axis=0, concat_axis=0, tiled=True)
        return terms, recv

    far_t = pltpu.VMEM((chips * CORES * far, rows), BF16)
    sums = jax.ShapeDtypeStruct(((rows // blk) * (all_rows // blk), blk // PARTS, blk), F32)
    give, up, pick, *sums = call(
        functools.partial(prep_kernel, chips),
        "prep",
        (shape(count, width), rows_shape, shape(far, rows)) + (sums,) * PARTS,
        [HBM] * 7,
        [
            pltpu.with_memory_space_constraint(value, pltpu.HBM)
            for value in (
                tile_dst,
                tile_src,
                tile_rows,
                send_list,
                tile_val,
                cotangent,
                neigh_two,
            )
        ],
        [
            pltpu.SMEM(tile_dst.shape, jnp.int32),
            pltpu.SMEM(tile_src.shape, jnp.int32),
            pltpu.SMEM(tile_rows.shape, jnp.int32),
            pltpu.SMEM(send_list.shape, jnp.int32),
            pltpu.VMEM(tile_val.shape, BF16),
            pltpu.VMEM(cotangent.shape, BF16),
            pltpu.VMEM(neigh_two.shape, BF16),
            pltpu.VMEM((rows, rows), BF16),
            far_t,
            pltpu.VMEM((count, rows), BF16),
            pltpu.SemaphoreType.DMA((6 + CHUNKS,)),
        ],
    )
    came = shift(give, "core", 1)
    sent, picked, adj, col, keep, lend, place, columns = call(
        functools.partial(rest_kernel, chips),
        "rest",
        (
            rows_shape,
            shape(far, width),
            shape(all_rows, rows),
            shape(count, rows),
            shape(count, width),
            shape(all_rows + 2 * rows, width),
            shape(rows, chips * far),
            far_shape,
        ),
        [VMEM] * (5 + PARTS),
        (up, cotangent, features, pick, neigh_one, *sums),
        [far_t],
        flops=3 * square,
    )
    lent = shift(lend, "core", 1)
    mine, msg, *to = call(
        functools.partial(core_sum_kernel, chips, hosts),
        "core_sum",
        dealt,
        [VMEM] * 4,
        (keep, came, sent, picked),
        flops=60 * square,
    )
    terms, recv = across(msg, to)
    here, summed = call(
        functools.partial(merge_kernel, chips, hosts),
        "merge",
        (shape(halo_rows + rows, width), sum_shape),
        [VMEM] * (2 + chips),
        (recv, mine, place, *terms),
    )
    shared = shift(here, "core", 1)
    agg, direct, grad, col_two, columns_two = call(
        functools.partial(early_one_kernel, chips),
        "early_one",
        (both_shape,) * 3 + (shape(count, rows), far_shape),
        [VMEM] * 10,
        (
            adj,
            lent,
            features,
            self_one,
            bias_one,
            cotangent,
            self_two,
            neigh_one,
            sent,
            neigh_two,
        ),
        [far_t],
        flops=8 * square,
    )
    agg, grad = call(
        functools.partial(mid_kernel, chips),
        "mid",
        (both_shape,) * 2,
        [VMEM] * (7 + chips),
        (adj, lent, columns, columns_two, agg, grad, summed, here, *terms),
        flops=3 * square,
    )
    hidden, sent, grad_pre, mine, msg, *to = call(
        functools.partial(middle_kernel, chips, hosts),
        "middle",
        (rows_shape,) * 3 + dealt,
        [VMEM] * 12,
        (
            adj,
            lent,
            columns,
            columns_two,
            col,
            col_two,
            agg,
            direct,
            grad,
            pick,
            shared,
            neigh_two,
        ),
        flops=12 * square,
    )
    terms, recv = across(msg, to)
    there = call(
        functools.partial(there_kernel, chips, hosts),
        "there",
        rows_shape,
        [VMEM] * (3 + chips),
        (lent, columns_two, sent, recv, *terms),
    )
    shared = shift(there, "core", 1)
    here, grad = call(
        functools.partial(here_kernel, chips, hosts),
        "here",
        (sum_shape,) * 2,
        [VMEM] * (11 + chips),
        (
            adj,
            columns,
            sent,
            recv,
            hidden,
            self_two,
            bias_two,
            grad_pre,
            self_one,
            neigh_one,
            mine,
            place,
            *terms,
        ),
        flops=7 * square,
    )
    output = call(last_kernel, "last", rows_shape, [VMEM] * 2, (here, shared))
    return output, grad


def solution(mesh):
    hosts, devs = mesh.devices.shape
    mesh = Mesh(mesh.devices.reshape(hosts, devs // CORES, CORES), ("hst", "chip", "core"))
    dev = ("chip", "core")
    every = ("hst", "chip", "core")
    return jax.shard_map(
        body,
        mesh=mesh,
        in_specs=(
            P(every, None),
            P("hst", dev, None, None),
            P(every),
            P(every),
            P(every),
            P(every, None, None),
            P(),
            P(),
            P(),
            P(),
            P(),
            P(),
            P(every, None),
        ),
        out_specs=(P(every, None), P(every, None)),
        check_vma=False,
    )
```

```python
import functools

import jax
import jax.numpy as jnp
from jax import lax
from jax.experimental import pallas as pl
from jax.experimental.pallas import tpu as pltpu
from jax.sharding import Mesh, PartitionSpec as P

F32 = jnp.float32
BF16 = jnp.bfloat16
MIB = 1024 * 1024
CHUNKS = 8
PARTS = 4
CORES = 2

VMEM = pl.BlockSpec(memory_space=pltpu.VMEM)
HBM = pl.BlockSpec(memory_space=pltpu.HBM)


def dot(a, b):
    return jnp.dot(a, b, preferred_element_type=F32)


def dot_nt(a, b):
    return lax.dot_general(a, b, (((1,), (1,)), ((), ())), preferred_element_type=F32)


def pick_matrix(send_ref, rows):
    hosts, send = send_ref.shape[2], send_ref.shape[3]
    place = lax.broadcasted_iota(jnp.int32, (send, rows), 0)
    column = lax.broadcasted_iota(jnp.int32, (send, rows), 1)
    parts = []
    for g in range(hosts):
        index = jnp.zeros((send, rows), jnp.int32)
        for s in range(send):
            index = jnp.where(place == s, send_ref[0, 0, g, s], index)
        parts.append(jnp.where(index == column, 1.0, 0.0).astype(F32))
    return jnp.concatenate(parts, 0).astype(BF16)


def column(chips, far, rows, side, adj_ref, far_t, out_ref):
    chip = lax.axis_index("chip")
    each = rows + far
    own_rows = chips * CORES * rows
    for j in range(far_t.shape[0] // rows):
        low = own_rows + j * rows
        far_t[j * rows : (j + 1) * rows, :] = adj_ref[low : low + rows, :].T
    for k in range(chips):
        d = lax.rem(chip + k, chips) * CORES + side
        at = k * each
        out_ref[at : at + rows, :] = adj_ref[pl.ds(pl.multiple_of(d * rows, rows), rows), :].T
        out_ref[at + rows : at + each, :] = far_t[pl.ds(pl.multiple_of(d * far, far), far), :]


def far_columns(chips, far_t, out_ref):
    far = far_t.shape[0] // (chips * CORES)
    core = lax.axis_index("core")
    parts = [
        far_t[pl.ds(pl.multiple_of((x * CORES + side) * far, far), far), :]
        for side in (1 - core, core)
        for x in range(chips)
    ]
    out_ref[...] = jnp.concatenate(parts, 0).T


def prep_kernel(
    chips,
    dst_hbm,
    src_hbm,
    rows_hbm,
    send_hbm,
    tile_hbm,
    cot_hbm,
    give_ref,
    pick_ref,
    *rest,
):
    accs, rest = rest[:PARTS], rest[PARTS:]
    (
        dst_ref,
        src_ref,
        rows_ref,
        send_ref,
        tile_buf,
        cot_ref,
        square,
        far_t,
        col,
        sems,
    ) = rest
    tiles, blk = tile_buf.shape[0], tile_buf.shape[1]
    each = tiles // CHUNKS
    first = CHUNKS * 3 // 4
    chunks = [
        (tile_hbm.at[pl.ds(c * each, each)], tile_buf.at[pl.ds(c * each, each)])
        for c in range(CHUNKS)
    ]
    pairs = [(dst_hbm, dst_ref), (src_hbm, src_ref), (rows_hbm, rows_ref)]
    pairs += chunks[:first]
    pairs += [
        (cot_hbm, cot_ref),
        (send_hbm, send_ref),
    ]
    pairs += chunks[first:]
    copies = [pltpu.make_async_copy(a, b, sems.at[i]) for i, (a, b) in enumerate(pairs)]
    for copy in copies:
        copy.start()
    rows = cot_ref.shape[0]
    bpd = rows // blk
    sources = accs[0].shape[0] // bpd
    part = accs[0].shape[1]
    far = send_ref.shape[2] * send_ref.shape[3]
    for acc in accs:
        acc[...] = jnp.zeros_like(acc)
    place = lax.broadcasted_iota(jnp.int32, (part, blk), 0)

    def add(t, carry):
        slot = dst_ref[t] * sources + src_ref[t]
        for i, acc in enumerate(accs):
            value = tile_buf[t, i * part : (i + 1) * part, :].astype(F32)
            acc[slot] += jnp.where(place < rows_ref[t] - i * part, value, 0.0)
        return carry

    for copy in copies[:3]:
        copy.wait()
    for c in range(first):
        copies[3 + c].wait()
        lax.fori_loop(c * each, (c + 1) * each, add, 0, unroll=True)
    for copy in copies[3 + first : 5 + first]:
        copy.wait()
    pick_ref[...] = pick_matrix(send_ref, rows)
    for c in range(first, CHUNKS):
        copies[5 + c].wait()
        lax.fori_loop(c * each, (c + 1) * each, add, 0, unroll=True)
    chip, side = lax.axis_index("chip"), 1 - lax.axis_index("core")
    base = chips * CORES
    for j in range(far_t.shape[0] // rows):
        put_square(accs, bpd, base + j, square, 0)
        far_t[j * rows : (j + 1) * rows, :] = square[...].T
    for k in range(chips):
        d = lax.rem(chip + k, chips) * CORES + side
        at = k * (rows + far)
        put_square(accs, bpd, d, square, 0)
        col[at : at + rows, :] = square[...].T
        low = pl.multiple_of(d * far, far)
        col[at + rows : at + rows + far, :] = far_t[pl.ds(low, far), :]
    give_ref[...] = dot(col[...], cot_ref[...]).astype(BF16)


def put_square(accs, bpd, d, out_ref, base):
    sources = accs[0].shape[0] // bpd
    part, blk = accs[0].shape[1:]
    for b in range(bpd):
        for j in range(bpd):
            for i, acc in enumerate(accs):
                low = base + b * blk + i * part
                value = acc[b * sources + d * bpd + j].astype(BF16)
                out_ref[low : low + part, j * blk : (j + 1) * blk] = value


def rest_kernel(chips, cot_ref, value_ref, pick_ref, neigh_ref, *refs):
    accs = refs[:PARTS]
    sent_ref, picked_ref, adj_ref, col_ref, keep_ref, lend_ref, place_ref, far_ref, far_t = refs[PARTS:]
    sent = dot(value_ref[...], neigh_ref[...]).astype(BF16)
    sent_ref[...] = sent
    picked_ref[...] = dot(pick_ref[...], sent).astype(BF16)
    rows = cot_ref.shape[0]
    bpd = rows // accs[0].shape[2]
    for d in range(adj_ref.shape[0] // rows):
        put_square(accs, bpd, d, adj_ref, d * rows)
    far = col_ref.shape[0] // chips - rows
    column(chips, far, rows, lax.axis_index("core"), adj_ref, far_t, col_ref)
    far_columns(chips, far_t, far_ref)
    keep_ref[...] = dot(col_ref[...], cot_ref[...]).astype(BF16)
    low = adj_ref.shape[0]
    lend_ref[:low, :] = adj_ref[...]
    lend_ref[low : low + rows, :] = cot_ref[...]
    lend_ref[low + rows :, :] = value_ref[...]
    place_ref[...] = jnp.concatenate([pick_ref[...]] * chips, 0).T


def deal(chips, hosts, total, picked, value, mine_ref, msg_ref, to_refs):
    rows = value.shape[0]
    far = picked.shape[0]
    send = far // hosts
    each = rows + far
    chip, core = lax.axis_index("chip"), lax.axis_index("core")
    mine_ref[...] = total[:rows]
    for k in range(chips):
        low = k * each + rows
        if k > 0:
            to_refs[k - 1][:rows, :] = total[k * each : low].astype(BF16)
            to_refs[k - 1][rows:, :] = value
        x = lax.rem(chip + k, chips)
        for g in range(hosts):
            at = low + g * send
            to = (g * chips + x) * CORES
            msg_ref[to + core] = total[at : at + send].astype(BF16)
            msg_ref[to + 1 - core] = picked[g * send : (g + 1) * send].astype(BF16)


def core_sum_kernel(
    chips, hosts, keep_ref, came_ref, value_ref, picked_ref, mine_ref, msg_ref, *rest
):
    total = keep_ref[...].astype(F32) + came_ref[...].astype(F32)
    picked = picked_ref[...].astype(F32)
    deal(chips, hosts, total, picked, value_ref[...], mine_ref, msg_ref, rest)


def received(recv_ref, hosts, chips, side):
    blocks = [
        recv_ref[(g * chips + x) * CORES + side].astype(F32)
        for x in range(chips)
        for g in range(hosts)
    ]
    return jnp.concatenate(blocks, 0).astype(BF16)


def merge_kernel(chips, hosts, recv_ref, mine_ref, place_ref, *refs):
    came, (out_ref, sum_ref) = refs[: chips - 1], refs[chips - 1 :]
    rows = mine_ref.shape[0]
    total = mine_ref[...]
    for k, ref in enumerate(came):
        total = total + ref[:rows, :].astype(F32)
        out_ref[k * rows : (k + 1) * rows, :] = ref[rows:, :]
    total = total + returned(place_ref, recv_ref, hosts, chips)
    sum_ref[...] = total
    low = len(came) * rows
    halo = received(recv_ref, hosts, chips, 1 - lax.axis_index("core"))
    high = low + halo.shape[0]
    out_ref[low:high, :] = halo
    out_ref[high:, :] = total.astype(BF16)


def returned(place_ref, recv_ref, hosts, chips):
    return dot(place_ref[...], received(recv_ref, hosts, chips, lax.axis_index("core")))


def joint(pairs):
    left = jnp.concatenate([a for a, _ in pairs], 1)
    return dot(left, jnp.concatenate([b for _, b in pairs], 0))


def square_of(adj_ref, x, side, rows):
    return adj_ref[pl.ds(pl.multiple_of((x * CORES + side) * rows, rows), rows), :]


def own_chip(adj_refs, blocks):
    chip, core = lax.axis_index("chip"), lax.axis_index("core")
    rows = blocks[0].shape[0]
    parts = [
        joint([(square_of(ref, chip, s, rows), b) for s, b in zip((core, 1 - core), blocks)])
        for ref in adj_refs
    ]
    return jnp.concatenate(parts, 0)


def early_one_kernel(
    chips, adj_ref, lent_ref, value_ref, self_ref, bias_ref, up_ref, weight_ref, neigh_ref, sent_ref,
    agg_ref, direct_ref, grad_ref, col_ref, far_ref, far_t,
):
    value = value_ref[...]
    rows = value.shape[0]
    low = adj_ref.shape[0]
    there = lent_ref[low + rows :, :]
    sent = dot(there, neigh_ref[...]).astype(BF16)
    agg_ref[...] = own_chip((adj_ref, lent_ref), (sent_ref[...], sent))
    both = jnp.concatenate([value, there], 0)
    direct_ref[...] = dot(both, self_ref[...]) + bias_ref[...].reshape(1, -1)
    both = jnp.concatenate([up_ref[...], lent_ref[low : low + rows, :]], 0)
    grad_ref[...] = dot_nt(both, weight_ref[...])
    far = col_ref.shape[0] // chips - rows
    column(chips, far, rows, lax.axis_index("core"), lent_ref, far_t, col_ref)
    far_columns(chips, far_t, far_ref)


def mid_kernel(
    chips, adj_ref, lent_ref, far_ref, far_two_ref, agg_ref, part_ref, sum_ref, neigh_ref, here_ref, *refs
):
    came, (agg_out, grad_ref) = refs[:-2], refs[-2:]
    rows = sum_ref.shape[0]
    halo = here_ref[(chips - 1) * rows : here_ref.shape[0] - rows, :]
    for i, (ref, columns) in enumerate(((adj_ref, far_ref), (lent_ref, far_two_ref))):
        pairs = other_chips(chips, ref, came) + [(columns[:, : halo.shape[0]], halo)]
        part = slice(i * rows, (i + 1) * rows)
        agg_out[part, :] = agg_ref[part, :] + joint(pairs)
    total = sum_ref[...].astype(BF16)
    grad_ref[:rows, :] = part_ref[:rows, :] + dot_nt(total, neigh_ref[...])
    grad_ref[rows:, :] = part_ref[rows:, :]


def other_chips(chips, adj_ref, came):
    chip, core = lax.axis_index("chip"), lax.axis_index("core")
    pairs = []
    for k, block in enumerate(came):
        rows = block.shape[0] // 2
        x = lax.rem(chip - k - 1 + chips, chips)
        pairs.append((square_of(adj_ref, x, core, rows), block[rows:, :]))
    return pairs


def column_product(chips, hosts, adj_ref, far_ref, value_ref, came, recv_ref):
    rows = value_ref.shape[0]
    chip, core = lax.axis_index("chip"), lax.axis_index("core")
    halo = received(recv_ref, hosts, chips, 1 - core)
    pairs = [(square_of(adj_ref, chip, core, rows), value_ref[...])]
    pairs += other_chips(chips, adj_ref, came) + [(far_ref[:, : halo.shape[0]], halo)]
    return joint(pairs)


def there_kernel(chips, hosts, lent_ref, far_ref, value_ref, recv_ref, *refs):
    came, out_ref = refs[:-1], refs[-1]
    out_ref[...] = column_product(
        chips, hosts, lent_ref, far_ref, value_ref, came, recv_ref
    ).astype(BF16)


def here_kernel(
    chips, hosts, adj_ref, far_ref, sent_ref, recv_ref, value_ref, self_ref, bias_ref, up_ref,
    weight_ref, neigh_ref, mine_ref, place_ref, *refs
):
    came, (out_ref, grad_ref) = refs[:-2], refs[-2:]
    rows = mine_ref.shape[0]
    total = mine_ref[...] + returned(place_ref, recv_ref, hosts, chips)
    for block in came:
        total = total + block[:rows, :].astype(F32)
    grad = dot_nt(total.astype(BF16), neigh_ref[...])
    grad_ref[...] = grad + dot_nt(up_ref[...], weight_ref[...])
    out = column_product(chips, hosts, adj_ref, far_ref, sent_ref, came, recv_ref)
    out_ref[...] = out + dot(value_ref[...], self_ref[...]) + bias_ref[...].reshape(1, -1)


def add_rest(chips, rows, adj_ref, far_ref, agg, shared_ref):
    chip, core = lax.axis_index("chip"), lax.axis_index("core")
    pairs = []
    for k in range(chips - 1):
        x = lax.rem(chip - k - 1 + chips, chips)
        block = shared_ref[k * rows : (k + 1) * rows, :]
        pairs.append((square_of(adj_ref, x, 1 - core, rows), block))
    half = far_ref.shape[1] // 2
    low = (chips - 1) * rows
    pairs.append((far_ref[:, half:], shared_ref[low : low + half, :]))
    return agg + joint(pairs)


def middle_kernel(
    chips,
    hosts,
    adj_ref,
    lent_ref,
    far_ref,
    far_two_ref,
    col_ref,
    col_two_ref,
    agg_ref,
    direct_ref,
    grad_ref,
    pick_ref,
    shared_ref,
    neigh_two_ref,
    hidden_ref,
    sent_ref,
    grad_pre_ref,
    mine_ref,
    msg_ref,
    *rest,
):
    to_refs = rest
    far, rows = pick_ref.shape
    parts = [
        add_rest(chips, rows, ref, columns, agg_ref[i * rows : (i + 1) * rows, :], shared_ref)
        for i, (ref, columns) in enumerate(((adj_ref, far_ref), (lent_ref, far_two_ref)))
    ]
    pre = direct_ref[...] + jnp.concatenate(parts, 0)
    sigmoid = jax.nn.sigmoid(pre)
    hidden = (pre[:rows] * sigmoid[:rows]).astype(BF16)
    hidden_ref[...] = hidden
    sent = dot(hidden, neigh_two_ref[...]).astype(BF16)
    sent_ref[...] = sent
    low = (chips - 1) * rows + chips * far
    add = dot_nt(shared_ref[low:, :], neigh_two_ref[...])
    grad = jnp.concatenate([grad_ref[:rows, :], grad_ref[rows:, :] + add], 0)
    grad_pre = (grad * sigmoid * (1.0 + pre * (1.0 - sigmoid))).astype(BF16)
    grad_pre_ref[...] = grad_pre[:rows]
    total = joint([(col_ref[...], grad_pre[:rows]), (col_two_ref[...], grad_pre[rows:])])
    picked = dot(pick_ref[...], sent)
    deal(chips, hosts, total, picked, sent, mine_ref, msg_ref, to_refs)


def last_kernel(here_ref, there_ref, output_ref):
    output_ref[...] = (here_ref[...] + there_ref[...].astype(F32)).astype(BF16)


def call(kernel, name, out_shape, in_specs, args, scratch=(), limit=32, flops=0):
    return pl.pallas_call(
        kernel,
        out_shape=out_shape,
        in_specs=in_specs,
        out_specs=jax.tree.map(lambda _: VMEM, out_shape),
        scratch_shapes=scratch,
        compiler_params=pltpu.CompilerParams(vmem_limit_bytes=limit * MIB),
        cost_estimate=pl.CostEstimate(
            flops=flops, bytes_accessed=flops // 1024, transcendentals=0
        ),
        name=name,
    )(*args)


def shift(value, axis, k):
    size = lax.axis_size(axis)
    return lax.ppermute(value, axis, [(i, (i + k) % size) for i in range(size)])


def shape(rows, width, kind=BF16):
    return jax.ShapeDtypeStruct((rows, width), kind)


def body(
    features,
    send_list,
    tile_dst,
    tile_src,
    tile_rows,
    tile_val,
    self_one,
    neigh_one,
    bias_one,
    self_two,
    neigh_two,
    bias_two,
    cotangent,
):
    chips = lax.axis_size("chip")
    hosts = lax.axis_size("hst")
    rows, width = features.shape
    tiles, blk = tile_val.shape[:2]
    send = send_list.shape[3]
    far = hosts * send
    all_rows = chips * CORES * (rows + far)
    count = chips * (rows + far)
    rows_shape = shape(rows, width)
    sum_shape = shape(rows, width, F32)
    both_shape = shape(CORES * rows, width, F32)
    square = 2 * rows * width * width
    far_shape = shape(rows, chips * CORES * far)
    halo_rows = (chips - 1) * rows + chips * far
    dealt = (
        sum_shape,
        jax.ShapeDtypeStruct((chips * hosts * CORES, send, width), BF16),
    ) + (shape(2 * rows, width),) * (chips - 1)

    def across(msg, to):
        terms = [shift(block, "chip", k + 1) for k, block in enumerate(to)]
        recv = lax.all_to_all(msg, ("hst", "chip", "core"), split_axis=0, concat_axis=0, tiled=True)
        return terms, recv

    far_t = pltpu.VMEM((chips * CORES * far, rows), BF16)
    sums = jax.ShapeDtypeStruct(((rows // blk) * (all_rows // blk), blk // PARTS, blk), F32)
    give, pick, *sums = call(
        functools.partial(prep_kernel, chips),
        "prep",
        (shape(count, width), shape(far, rows)) + (sums,) * PARTS,
        [HBM] * 6,
        [
            pltpu.with_memory_space_constraint(value, pltpu.HBM)
            for value in (
                tile_dst,
                tile_src,
                tile_rows,
                send_list,
                tile_val,
                cotangent,
            )
        ],
        [
            pltpu.SMEM(tile_dst.shape, jnp.int32),
            pltpu.SMEM(tile_src.shape, jnp.int32),
            pltpu.SMEM(tile_rows.shape, jnp.int32),
            pltpu.SMEM(send_list.shape, jnp.int32),
            pltpu.VMEM(tile_val.shape, BF16),
            pltpu.VMEM(cotangent.shape, BF16),
            pltpu.VMEM((rows, rows), BF16),
            far_t,
            pltpu.VMEM((count, rows), BF16),
            pltpu.SemaphoreType.DMA((5 + CHUNKS,)),
        ],
    )
    came = shift(give, "core", 1)
    sent, picked, adj, col, keep, lend, place, columns = call(
        functools.partial(rest_kernel, chips),
        "rest",
        (
            rows_shape,
            shape(far, width),
            shape(all_rows, rows),
            shape(count, rows),
            shape(count, width),
            shape(all_rows + 2 * rows, width),
            shape(rows, chips * far),
            far_shape,
        ),
        [VMEM] * (4 + PARTS),
        (cotangent, features, pick, neigh_one, *sums),
        [far_t],
        flops=3 * square,
    )
    lent = shift(lend, "core", 1)
    mine, msg, *to = call(
        functools.partial(core_sum_kernel, chips, hosts),
        "core_sum",
        dealt,
        [VMEM] * 4,
        (keep, came, sent, picked),
        flops=60 * square,
    )
    terms, recv = across(msg, to)
    here, summed = call(
        functools.partial(merge_kernel, chips, hosts),
        "merge",
        (shape(halo_rows + rows, width), sum_shape),
        [VMEM] * (2 + chips),
        (recv, mine, place, *terms),
    )
    shared = shift(here, "core", 1)
    agg, direct, grad, col_two, columns_two = call(
        functools.partial(early_one_kernel, chips),
        "early_one",
        (both_shape,) * 3 + (shape(count, rows), far_shape),
        [VMEM] * 9,
        (
            adj,
            lent,
            features,
            self_one,
            bias_one,
            cotangent,
            self_two,
            neigh_one,
            sent,
        ),
        [far_t],
        flops=8 * square,
    )
    agg, grad = call(
        functools.partial(mid_kernel, chips),
        "mid",
        (both_shape,) * 2,
        [VMEM] * (8 + chips),
        (adj, lent, columns, columns_two, agg, grad, summed, neigh_two, here, *terms),
        flops=3 * square,
    )
    hidden, sent, grad_pre, mine, msg, *to = call(
        functools.partial(middle_kernel, chips, hosts),
        "middle",
        (rows_shape,) * 3 + dealt,
        [VMEM] * 12,
        (
            adj,
            lent,
            columns,
            columns_two,
            col,
            col_two,
            agg,
            direct,
            grad,
            pick,
            shared,
            neigh_two,
        ),
        flops=12 * square,
    )
    terms, recv = across(msg, to)
    there = call(
        functools.partial(there_kernel, chips, hosts),
        "there",
        rows_shape,
        [VMEM] * (3 + chips),
        (lent, columns_two, sent, recv, *terms),
    )
    shared = shift(there, "core", 1)
    here, grad = call(
        functools.partial(here_kernel, chips, hosts),
        "here",
        (sum_shape,) * 2,
        [VMEM] * (11 + chips),
        (
            adj,
            columns,
            sent,
            recv,
            hidden,
            self_two,
            bias_two,
            grad_pre,
            self_one,
            neigh_one,
            mine,
            place,
            *terms,
        ),
        flops=7 * square,
    )
    output = call(last_kernel, "last", rows_shape, [VMEM] * 2, (here, shared))
    return output, grad


def solution(mesh):
    hosts, devs = mesh.devices.shape
    mesh = Mesh(mesh.devices.reshape(hosts, devs // CORES, CORES), ("hst", "chip", "core"))
    dev = ("chip", "core")
    every = ("hst", "chip", "core")
    return jax.shard_map(
        body,
        mesh=mesh,
        in_specs=(
            P(every, None),
            P("hst", dev, None, None),
            P(every),
            P(every),
            P(every),
            P(every, None, None),
            P(),
            P(),
            P(),
            P(),
            P(),
            P(),
            P(every, None),
        ),
        out_specs=(P(every, None), P(every, None)),
        check_vma=False,
    )
```

```python
import functools

import jax
import jax.numpy as jnp
from jax import lax
from jax.experimental import pallas as pl
from jax.experimental.pallas import tpu as pltpu
from jax.sharding import Mesh, PartitionSpec as P

F32 = jnp.float32
BF16 = jnp.bfloat16
MIB = 1024 * 1024
CHUNKS = 8
PARTS = 4
CORES = 2

VMEM = pl.BlockSpec(memory_space=pltpu.VMEM)
HBM = pl.BlockSpec(memory_space=pltpu.HBM)


def dot(a, b):
    return jnp.dot(a, b, preferred_element_type=F32)


def dot_nt(a, b):
    return lax.dot_general(a, b, (((1,), (1,)), ((), ())), preferred_element_type=F32)


def precise_nt(a, b):
    high = a.astype(BF16)
    low = (a - high.astype(F32)).astype(BF16)
    return dot_nt(high, b) + dot_nt(low, b)


def pick_matrix(send_ref, rows):
    hosts, send = send_ref.shape[2], send_ref.shape[3]
    place = lax.broadcasted_iota(jnp.int32, (send, rows), 0)
    column = lax.broadcasted_iota(jnp.int32, (send, rows), 1)
    parts = []
    for g in range(hosts):
        index = jnp.zeros((send, rows), jnp.int32)
        for s in range(send):
            index = jnp.where(place == s, send_ref[0, 0, g, s], index)
        parts.append(jnp.where(index == column, 1.0, 0.0).astype(F32))
    return jnp.concatenate(parts, 0).astype(BF16)


def column(chips, far, rows, side, adj_ref, far_t, out_ref):
    chip = lax.axis_index("chip")
    each = rows + far
    own_rows = chips * CORES * rows
    for j in range(far_t.shape[0] // rows):
        low = own_rows + j * rows
        far_t[j * rows : (j + 1) * rows, :] = adj_ref[low : low + rows, :].T
    for k in range(chips):
        d = lax.rem(chip + k, chips) * CORES + side
        at = k * each
        out_ref[at : at + rows, :] = adj_ref[pl.ds(pl.multiple_of(d * rows, rows), rows), :].T
        out_ref[at + rows : at + each, :] = far_t[pl.ds(pl.multiple_of(d * far, far), far), :]


def far_columns(chips, far_t, out_ref):
    far = far_t.shape[0] // (chips * CORES)
    core = lax.axis_index("core")
    parts = [
        far_t[pl.ds(pl.multiple_of((x * CORES + side) * far, far), far), :]
        for side in (1 - core, core)
        for x in range(chips)
    ]
    out_ref[...] = jnp.concatenate(parts, 0).T


def prep_kernel(
    chips,
    dst_hbm,
    src_hbm,
    rows_hbm,
    send_hbm,
    tile_hbm,
    cot_hbm,
    give_ref,
    pick_ref,
    *rest,
):
    accs, rest = rest[:PARTS], rest[PARTS:]
    (
        dst_ref,
        src_ref,
        rows_ref,
        send_ref,
        tile_buf,
        cot_ref,
        square,
        far_t,
        col,
        sems,
    ) = rest
    tiles, blk = tile_buf.shape[0], tile_buf.shape[1]
    each = tiles // CHUNKS
    chunks = [
        (tile_hbm.at[pl.ds(c * each, each)], tile_buf.at[pl.ds(c * each, each)])
        for c in range(CHUNKS)
    ]
    pairs = [(send_hbm, send_ref), (dst_hbm, dst_ref), (src_hbm, src_ref), (rows_hbm, rows_ref)]
    pairs += chunks + [(cot_hbm, cot_ref)]
    copies = [pltpu.make_async_copy(a, b, sems.at[i]) for i, (a, b) in enumerate(pairs)]
    for copy in copies:
        copy.start()
    rows = cot_ref.shape[0]
    bpd = rows // blk
    sources = accs[0].shape[0] // bpd
    part = accs[0].shape[1]
    far = send_ref.shape[2] * send_ref.shape[3]
    for acc in accs:
        acc[...] = jnp.zeros_like(acc)
    place = lax.broadcasted_iota(jnp.int32, (part, blk), 0)

    def add(t, carry):
        slot = dst_ref[t] * sources + src_ref[t]
        for i, acc in enumerate(accs):
            value = tile_buf[t, i * part : (i + 1) * part, :].astype(F32)
            acc[slot] += jnp.where(place < rows_ref[t] - i * part, value, 0.0)
        return carry

    copies[0].wait()
    pick_ref[...] = pick_matrix(send_ref, rows)
    for copy in copies[1:4]:
        copy.wait()
    for c in range(CHUNKS):
        copies[4 + c].wait()
        lax.fori_loop(c * each, (c + 1) * each, add, 0, unroll=True)
    copies[4 + CHUNKS].wait()
    chip, side = lax.axis_index("chip"), 1 - lax.axis_index("core")
    base = chips * CORES
    for j in range(far_t.shape[0] // rows):
        put_square(accs, bpd, base + j, square, 0)
        far_t[j * rows : (j + 1) * rows, :] = square[...].T
    for k in range(chips):
        d = lax.rem(chip + k, chips) * CORES + side
        at = k * (rows + far)
        put_square(accs, bpd, d, square, 0)
        col[at : at + rows, :] = square[...].T
        low = pl.multiple_of(d * far, far)
        col[at + rows : at + rows + far, :] = far_t[pl.ds(low, far), :]
    give_ref[...] = dot(col[...], cot_ref[...]).astype(BF16)


def put_square(accs, bpd, d, out_ref, base):
    sources = accs[0].shape[0] // bpd
    part, blk = accs[0].shape[1:]
    for b in range(bpd):
        for j in range(bpd):
            for i, acc in enumerate(accs):
                low = base + b * blk + i * part
                value = acc[b * sources + d * bpd + j].astype(BF16)
                out_ref[low : low + part, j * blk : (j + 1) * blk] = value


def rest_kernel(chips, cot_ref, value_ref, pick_ref, neigh_ref, *refs):
    accs = refs[:PARTS]
    sent_ref, picked_ref, adj_ref, col_ref, keep_ref, lend_ref, place_ref, far_ref, far_t = refs[PARTS:]
    sent = dot(value_ref[...], neigh_ref[...]).astype(BF16)
    sent_ref[...] = sent
    picked_ref[...] = dot(pick_ref[...], sent).astype(BF16)
    rows = cot_ref.shape[0]
    bpd = rows // accs[0].shape[2]
    for d in range(adj_ref.shape[0] // rows):
        put_square(accs, bpd, d, adj_ref, d * rows)
    far = col_ref.shape[0] // chips - rows
    column(chips, far, rows, lax.axis_index("core"), adj_ref, far_t, col_ref)
    far_columns(chips, far_t, far_ref)
    keep_ref[...] = dot(col_ref[...], cot_ref[...]).astype(BF16)
    low = adj_ref.shape[0]
    lend_ref[:low, :] = adj_ref[...]
    lend_ref[low : low + rows, :] = cot_ref[...]
    lend_ref[low + rows :, :] = value_ref[...]
    place_ref[...] = jnp.concatenate([pick_ref[...]] * chips, 0).T


def deal(chips, hosts, total, picked, value, mine_ref, msg_ref, to_refs):
    rows = value.shape[0]
    far = picked.shape[0]
    send = far // hosts
    each = rows + far
    chip, core = lax.axis_index("chip"), lax.axis_index("core")
    mine_ref[...] = total[:rows]
    for k in range(chips):
        low = k * each + rows
        if k > 0:
            to_refs[k - 1][:rows, :] = total[k * each : low].astype(BF16)
            to_refs[k - 1][rows:, :] = value
        x = lax.rem(chip + k, chips)
        for g in range(hosts):
            at = low + g * send
            to = (g * chips + x) * CORES
            msg_ref[to + core] = total[at : at + send].astype(BF16)
            msg_ref[to + 1 - core] = picked[g * send : (g + 1) * send].astype(BF16)


def core_sum_kernel(
    chips, hosts, keep_ref, came_ref, value_ref, picked_ref, mine_ref, msg_ref, *rest
):
    total = keep_ref[...].astype(F32) + came_ref[...].astype(F32)
    picked = picked_ref[...].astype(F32)
    deal(chips, hosts, total, picked, value_ref[...], mine_ref, msg_ref, rest)


def received(recv_ref, hosts, chips, side):
    blocks = [
        recv_ref[(g * chips + x) * CORES + side].astype(F32)
        for x in range(chips)
        for g in range(hosts)
    ]
    return jnp.concatenate(blocks, 0).astype(BF16)


def merge_kernel(chips, hosts, recv_ref, mine_ref, place_ref, *refs):
    came, (out_ref, sum_ref) = refs[: chips - 1], refs[chips - 1 :]
    rows = mine_ref.shape[0]
    total = mine_ref[...]
    for k, ref in enumerate(came):
        total = total + ref[:rows, :].astype(F32)
        out_ref[k * rows : (k + 1) * rows, :] = ref[rows:, :]
    total = total + returned(place_ref, recv_ref, hosts, chips)
    sum_ref[...] = total
    low = len(came) * rows
    halo = received(recv_ref, hosts, chips, 1 - lax.axis_index("core"))
    high = low + halo.shape[0]
    out_ref[low:high, :] = halo
    out_ref[high:, :] = total.astype(BF16)


def returned(place_ref, recv_ref, hosts, chips):
    return dot(place_ref[...], received(recv_ref, hosts, chips, lax.axis_index("core")))


def joint(pairs):
    left = jnp.concatenate([a for a, _ in pairs], 1)
    return dot(left, jnp.concatenate([b for _, b in pairs], 0))


def square_of(adj_ref, x, side, rows):
    return adj_ref[pl.ds(pl.multiple_of((x * CORES + side) * rows, rows), rows), :]


def own_chip(adj_refs, blocks):
    chip, core = lax.axis_index("chip"), lax.axis_index("core")
    rows = blocks[0].shape[0]
    parts = [
        joint([(square_of(ref, chip, s, rows), b) for s, b in zip((core, 1 - core), blocks)])
        for ref in adj_refs
    ]
    return jnp.concatenate(parts, 0)


def early_one_kernel(
    chips, adj_ref, lent_ref, value_ref, self_ref, bias_ref, up_ref, weight_ref, neigh_ref, sent_ref,
    agg_ref, direct_ref, grad_ref, col_ref, far_ref, far_t,
):
    value = value_ref[...]
    rows = value.shape[0]
    low = adj_ref.shape[0]
    there = lent_ref[low + rows :, :]
    sent = dot(there, neigh_ref[...]).astype(BF16)
    agg_ref[...] = own_chip((adj_ref, lent_ref), (sent_ref[...], sent))
    both = jnp.concatenate([value, there], 0)
    direct_ref[...] = dot(both, self_ref[...]) + bias_ref[...].reshape(1, -1)
    both = jnp.concatenate([up_ref[...], lent_ref[low : low + rows, :]], 0)
    grad_ref[...] = dot_nt(both, weight_ref[...])
    far = col_ref.shape[0] // chips - rows
    column(chips, far, rows, lax.axis_index("core"), lent_ref, far_t, col_ref)
    far_columns(chips, far_t, far_ref)


def mid_kernel(
    chips, adj_ref, lent_ref, far_ref, far_two_ref, agg_ref, part_ref, sum_ref, neigh_ref, here_ref, *refs
):
    came, (agg_out, grad_ref) = refs[:-2], refs[-2:]
    rows = sum_ref.shape[0]
    halo = here_ref[(chips - 1) * rows : here_ref.shape[0] - rows, :]
    for i, (ref, columns) in enumerate(((adj_ref, far_ref), (lent_ref, far_two_ref))):
        pairs = other_chips(chips, ref, came) + [(columns[:, : halo.shape[0]], halo)]
        part = slice(i * rows, (i + 1) * rows)
        agg_out[part, :] = agg_ref[part, :] + joint(pairs)
    grad_ref[:rows, :] = part_ref[:rows, :] + precise_nt(sum_ref[...], neigh_ref[...])
    grad_ref[rows:, :] = part_ref[rows:, :]


def other_chips(chips, adj_ref, came):
    chip, core = lax.axis_index("chip"), lax.axis_index("core")
    pairs = []
    for k, block in enumerate(came):
        rows = block.shape[0] // 2
        x = lax.rem(chip - k - 1 + chips, chips)
        pairs.append((square_of(adj_ref, x, core, rows), block[rows:, :]))
    return pairs


def column_product(chips, hosts, adj_ref, far_ref, value_ref, came, recv_ref):
    rows = value_ref.shape[0]
    chip, core = lax.axis_index("chip"), lax.axis_index("core")
    halo = received(recv_ref, hosts, chips, 1 - core)
    pairs = [(square_of(adj_ref, chip, core, rows), value_ref[...])]
    pairs += other_chips(chips, adj_ref, came) + [(far_ref[:, : halo.shape[0]], halo)]
    return joint(pairs)


def there_kernel(chips, hosts, lent_ref, far_ref, value_ref, recv_ref, *refs):
    came, out_ref = refs[:-1], refs[-1]
    out_ref[...] = column_product(
        chips, hosts, lent_ref, far_ref, value_ref, came, recv_ref
    ).astype(BF16)


def here_kernel(
    chips, hosts, adj_ref, far_ref, sent_ref, recv_ref, value_ref, self_ref, bias_ref, up_ref,
    weight_ref, neigh_ref, mine_ref, place_ref, *refs
):
    came, (out_ref, grad_ref) = refs[:-2], refs[-2:]
    rows = mine_ref.shape[0]
    total = mine_ref[...] + returned(place_ref, recv_ref, hosts, chips)
    for block in came:
        total = total + block[:rows, :].astype(F32)
    grad = precise_nt(total, neigh_ref[...])
    grad_ref[...] = grad + dot_nt(up_ref[...], weight_ref[...])
    out = column_product(chips, hosts, adj_ref, far_ref, sent_ref, came, recv_ref)
    out_ref[...] = out + dot(value_ref[...], self_ref[...]) + bias_ref[...].reshape(1, -1)


def add_rest(chips, rows, adj_ref, far_ref, agg, shared_ref):
    chip, core = lax.axis_index("chip"), lax.axis_index("core")
    pairs = []
    for k in range(chips - 1):
        x = lax.rem(chip - k - 1 + chips, chips)
        block = shared_ref[k * rows : (k + 1) * rows, :]
        pairs.append((square_of(adj_ref, x, 1 - core, rows), block))
    half = far_ref.shape[1] // 2
    low = (chips - 1) * rows
    pairs.append((far_ref[:, half:], shared_ref[low : low + half, :]))
    return agg + joint(pairs)


def middle_kernel(
    chips,
    hosts,
    adj_ref,
    lent_ref,
    far_ref,
    far_two_ref,
    col_ref,
    col_two_ref,
    agg_ref,
    direct_ref,
    grad_ref,
    pick_ref,
    shared_ref,
    neigh_two_ref,
    hidden_ref,
    sent_ref,
    grad_pre_ref,
    mine_ref,
    msg_ref,
    *rest,
):
    to_refs = rest
    far, rows = pick_ref.shape
    parts = [
        add_rest(chips, rows, ref, columns, agg_ref[i * rows : (i + 1) * rows, :], shared_ref)
        for i, (ref, columns) in enumerate(((adj_ref, far_ref), (lent_ref, far_two_ref)))
    ]
    pre = direct_ref[...] + jnp.concatenate(parts, 0)
    sigmoid = jax.nn.sigmoid(pre)
    hidden = (pre[:rows] * sigmoid[:rows]).astype(BF16)
    hidden_ref[...] = hidden
    sent = dot(hidden, neigh_two_ref[...]).astype(BF16)
    sent_ref[...] = sent
    low = (chips - 1) * rows + chips * far
    add = dot_nt(shared_ref[low:, :], neigh_two_ref[...])
    grad = jnp.concatenate([grad_ref[:rows, :], grad_ref[rows:, :] + add], 0)
    grad_pre = (grad * sigmoid * (1.0 + pre * (1.0 - sigmoid))).astype(BF16)
    grad_pre_ref[...] = grad_pre[:rows]
    total = joint([(col_ref[...], grad_pre[:rows]), (col_two_ref[...], grad_pre[rows:])])
    picked = dot(pick_ref[...], sent)
    deal(chips, hosts, total, picked, sent, mine_ref, msg_ref, to_refs)


def last_kernel(here_ref, there_ref, output_ref):
    output_ref[...] = (here_ref[...] + there_ref[...].astype(F32)).astype(BF16)


def call(kernel, name, out_shape, in_specs, args, scratch=(), limit=32, flops=0):
    return pl.pallas_call(
        kernel,
        out_shape=out_shape,
        in_specs=in_specs,
        out_specs=jax.tree.map(lambda _: VMEM, out_shape),
        scratch_shapes=scratch,
        compiler_params=pltpu.CompilerParams(vmem_limit_bytes=limit * MIB),
        cost_estimate=pl.CostEstimate(
            flops=flops, bytes_accessed=flops // 1024, transcendentals=0
        ),
        name=name,
    )(*args)


def shift(value, axis, k):
    size = lax.axis_size(axis)
    return lax.ppermute(value, axis, [(i, (i + k) % size) for i in range(size)])


def shape(rows, width, kind=BF16):
    return jax.ShapeDtypeStruct((rows, width), kind)


def body(
    features,
    send_list,
    tile_dst,
    tile_src,
    tile_rows,
    tile_val,
    self_one,
    neigh_one,
    bias_one,
    self_two,
    neigh_two,
    bias_two,
    cotangent,
):
    chips = lax.axis_size("chip")
    hosts = lax.axis_size("hst")
    rows, width = features.shape
    tiles, blk = tile_val.shape[:2]
    send = send_list.shape[3]
    far = hosts * send
    all_rows = chips * CORES * (rows + far)
    count = chips * (rows + far)
    rows_shape = shape(rows, width)
    sum_shape = shape(rows, width, F32)
    both_shape = shape(CORES * rows, width, F32)
    square = 2 * rows * width * width
    far_shape = shape(rows, chips * CORES * far)
    halo_rows = (chips - 1) * rows + chips * far
    dealt = (
        sum_shape,
        jax.ShapeDtypeStruct((chips * hosts * CORES, send, width), BF16),
    ) + (shape(2 * rows, width),) * (chips - 1)

    def across(msg, to):
        terms = [shift(block, "chip", k + 1) for k, block in enumerate(to)]
        recv = lax.all_to_all(msg, ("hst", "chip", "core"), split_axis=0, concat_axis=0, tiled=True)
        return terms, recv

    far_t = pltpu.VMEM((chips * CORES * far, rows), BF16)
    sums = jax.ShapeDtypeStruct(((rows // blk) * (all_rows // blk), blk // PARTS, blk), F32)
    give, pick, *sums = call(
        functools.partial(prep_kernel, chips),
        "prep",
        (shape(count, width), shape(far, rows)) + (sums,) * PARTS,
        [HBM] * 6,
        [
            pltpu.with_memory_space_constraint(value, pltpu.HBM)
            for value in (
                tile_dst,
                tile_src,
                tile_rows,
                send_list,
                tile_val,
                cotangent,
            )
        ],
        [
            pltpu.SMEM(tile_dst.shape, jnp.int32),
            pltpu.SMEM(tile_src.shape, jnp.int32),
            pltpu.SMEM(tile_rows.shape, jnp.int32),
            pltpu.SMEM(send_list.shape, jnp.int32),
            pltpu.VMEM(tile_val.shape, BF16),
            pltpu.VMEM(cotangent.shape, BF16),
            pltpu.VMEM((rows, rows), BF16),
            far_t,
            pltpu.VMEM((count, rows), BF16),
            pltpu.SemaphoreType.DMA((5 + CHUNKS,)),
        ],
    )
    came = shift(give, "core", 1)
    sent, picked, adj, col, keep, lend, place, columns = call(
        functools.partial(rest_kernel, chips),
        "rest",
        (
            rows_shape,
            shape(far, width),
            shape(all_rows, rows),
            shape(count, rows),
            shape(count, width),
            shape(all_rows + 2 * rows, width),
            shape(rows, chips * far),
            far_shape,
        ),
        [VMEM] * (4 + PARTS),
        (cotangent, features, pick, neigh_one, *sums),
        [far_t],
        flops=3 * square,
    )
    lent = shift(lend, "core", 1)
    mine, msg, *to = call(
        functools.partial(core_sum_kernel, chips, hosts),
        "core_sum",
        dealt,
        [VMEM] * 4,
        (keep, came, sent, picked),
        flops=60 * square,
    )
    terms, recv = across(msg, to)
    here, summed = call(
        functools.partial(merge_kernel, chips, hosts),
        "merge",
        (shape(halo_rows + rows, width), sum_shape),
        [VMEM] * (2 + chips),
        (recv, mine, place, *terms),
    )
    shared = shift(here, "core", 1)
    agg, direct, grad, col_two, columns_two = call(
        functools.partial(early_one_kernel, chips),
        "early_one",
        (both_shape,) * 3 + (shape(count, rows), far_shape),
        [VMEM] * 9,
        (
            adj,
            lent,
            features,
            self_one,
            bias_one,
            cotangent,
            self_two,
            neigh_one,
            sent,
        ),
        [far_t],
        flops=8 * square,
    )
    agg, grad = call(
        functools.partial(mid_kernel, chips),
        "mid",
        (both_shape,) * 2,
        [VMEM] * (8 + chips),
        (adj, lent, columns, columns_two, agg, grad, summed, neigh_two, here, *terms),
        flops=3 * square,
    )
    hidden, sent, grad_pre, mine, msg, *to = call(
        functools.partial(middle_kernel, chips, hosts),
        "middle",
        (rows_shape,) * 3 + dealt,
        [VMEM] * 12,
        (
            adj,
            lent,
            columns,
            columns_two,
            col,
            col_two,
            agg,
            direct,
            grad,
            pick,
            shared,
            neigh_two,
        ),
        flops=12 * square,
    )
    terms, recv = across(msg, to)
    there = call(
        functools.partial(there_kernel, chips, hosts),
        "there",
        rows_shape,
        [VMEM] * (3 + chips),
        (lent, columns_two, sent, recv, *terms),
    )
    shared = shift(there, "core", 1)
    here, grad = call(
        functools.partial(here_kernel, chips, hosts),
        "here",
        (sum_shape,) * 2,
        [VMEM] * (11 + chips),
        (
            adj,
            columns,
            sent,
            recv,
            hidden,
            self_two,
            bias_two,
            grad_pre,
            self_one,
            neigh_one,
            mine,
            place,
            *terms,
        ),
        flops=7 * square,
    )
    output = call(last_kernel, "last", rows_shape, [VMEM] * 2, (here, shared))
    return output, grad


def solution(mesh):
    hosts, devs = mesh.devices.shape
    mesh = Mesh(mesh.devices.reshape(hosts, devs // CORES, CORES), ("hst", "chip", "core"))
    dev = ("chip", "core")
    every = ("hst", "chip", "core")
    return jax.shard_map(
        body,
        mesh=mesh,
        in_specs=(
            P(every, None),
            P("hst", dev, None, None),
            P(every),
            P(every),
            P(every),
            P(every, None, None),
            P(),
            P(),
            P(),
            P(),
            P(),
            P(),
            P(every, None),
        ),
        out_specs=(P(every, None), P(every, None)),
        check_vma=False,
    )
```

```python
import functools

import jax
import jax.numpy as jnp
from jax import lax
from jax.experimental import pallas as pl
from jax.experimental.pallas import tpu as pltpu
from jax.sharding import Mesh, PartitionSpec as P

F32 = jnp.float32
BF16 = jnp.bfloat16
MIB = 1024 * 1024
CHUNKS = 16
PARTS = 4
CORES = 2

VMEM = pl.BlockSpec(memory_space=pltpu.VMEM)
HBM = pl.BlockSpec(memory_space=pltpu.HBM)


def dot(a, b):
    return jnp.dot(a, b, preferred_element_type=F32)


def dot_nt(a, b):
    return lax.dot_general(a, b, (((1,), (1,)), ((), ())), preferred_element_type=F32)


def precise_nt(a, b):
    high = a.astype(BF16)
    low = (a - high.astype(F32)).astype(BF16)
    return dot_nt(high, b) + dot_nt(low, b)


def pick_matrix(send_ref, rows):
    hosts, send = send_ref.shape[2], send_ref.shape[3]
    place = lax.broadcasted_iota(jnp.int32, (send, rows), 0)
    column = lax.broadcasted_iota(jnp.int32, (send, rows), 1)
    parts = []
    for g in range(hosts):
        index = jnp.zeros((send, rows), jnp.int32)
        for s in range(send):
            index = jnp.where(place == s, send_ref[0, 0, g, s], index)
        parts.append(jnp.where(index == column, 1.0, 0.0).astype(F32))
    return jnp.concatenate(parts, 0).astype(BF16)


def column(chips, far, rows, side, adj_ref, far_t, out_ref):
    chip = lax.axis_index("chip")
    each = rows + far
    own_rows = chips * CORES * rows
    for j in range(far_t.shape[0] // rows):
        low = own_rows + j * rows
        far_t[j * rows : (j + 1) * rows, :] = adj_ref[low : low + rows, :].T
    for k in range(chips):
        d = lax.rem(chip + k, chips) * CORES + side
        at = k * each
        out_ref[at : at + rows, :] = adj_ref[pl.ds(pl.multiple_of(d * rows, rows), rows), :].T
        out_ref[at + rows : at + each, :] = far_t[pl.ds(pl.multiple_of(d * far, far), far), :]


def far_columns(chips, far_t, out_ref):
    far = far_t.shape[0] // (chips * CORES)
    core = lax.axis_index("core")
    parts = [
        far_t[pl.ds(pl.multiple_of((x * CORES + side) * far, far), far), :]
        for side in (1 - core, core)
        for x in range(chips)
    ]
    out_ref[...] = jnp.concatenate(parts, 0).T


def prep_kernel(
    chips,
    dst_hbm,
    src_hbm,
    rows_hbm,
    send_hbm,
    tile_hbm,
    cot_hbm,
    give_ref,
    pick_ref,
    *rest,
):
    accs, rest = rest[:PARTS], rest[PARTS:]
    (
        dst_ref,
        src_ref,
        rows_ref,
        send_ref,
        tile_buf,
        cot_ref,
        square,
        far_t,
        col,
        sems,
    ) = rest
    tiles, blk = tile_buf.shape[0], tile_buf.shape[1]
    each = tiles // CHUNKS
    chunks = [
        (tile_hbm.at[pl.ds(c * each, each)], tile_buf.at[pl.ds(c * each, each)])
        for c in range(CHUNKS)
    ]
    pairs = [(send_hbm, send_ref), (dst_hbm, dst_ref), (src_hbm, src_ref), (rows_hbm, rows_ref)]
    pairs += chunks + [(cot_hbm, cot_ref)]
    copies = [pltpu.make_async_copy(a, b, sems.at[i]) for i, (a, b) in enumerate(pairs)]
    for copy in copies:
        copy.start()
    rows = cot_ref.shape[0]
    bpd = rows // blk
    sources = accs[0].shape[0] // bpd
    part = accs[0].shape[1]
    far = send_ref.shape[2] * send_ref.shape[3]
    for acc in accs:
        acc[...] = jnp.zeros_like(acc)
    place = lax.broadcasted_iota(jnp.int32, (part, blk), 0)

    def add(t, carry):
        slot = dst_ref[t] * sources + src_ref[t]
        for i, acc in enumerate(accs):
            value = tile_buf[t, i * part : (i + 1) * part, :].astype(F32)
            acc[slot] += jnp.where(place < rows_ref[t] - i * part, value, 0.0)
        return carry

    copies[0].wait()
    pick_ref[...] = pick_matrix(send_ref, rows)
    for copy in copies[1:4]:
        copy.wait()
    for c in range(CHUNKS):
        copies[4 + c].wait()
        lax.fori_loop(c * each, (c + 1) * each, add, 0, unroll=True)
    copies[4 + CHUNKS].wait()
    chip, side = lax.axis_index("chip"), 1 - lax.axis_index("core")
    base = chips * CORES
    for j in range(far_t.shape[0] // rows):
        put_square(accs, bpd, base + j, square, 0)
        far_t[j * rows : (j + 1) * rows, :] = square[...].T
    for k in range(chips):
        d = lax.rem(chip + k, chips) * CORES + side
        at = k * (rows + far)
        put_square(accs, bpd, d, square, 0)
        col[at : at + rows, :] = square[...].T
        low = pl.multiple_of(d * far, far)
        col[at + rows : at + rows + far, :] = far_t[pl.ds(low, far), :]
    give_ref[...] = dot(col[...], cot_ref[...]).astype(BF16)


def put_square(accs, bpd, d, out_ref, base):
    sources = accs[0].shape[0] // bpd
    part, blk = accs[0].shape[1:]
    for b in range(bpd):
        for j in range(bpd):
            for i, acc in enumerate(accs):
                low = base + b * blk + i * part
                value = acc[b * sources + d * bpd + j].astype(BF16)
                out_ref[low : low + part, j * blk : (j + 1) * blk] = value


def rest_kernel(chips, cot_ref, value_ref, pick_ref, neigh_ref, *refs):
    accs = refs[:PARTS]
    sent_ref, picked_ref, adj_ref, col_ref, keep_ref, lend_ref, place_ref, far_ref, far_t = refs[PARTS:]
    sent = dot(value_ref[...], neigh_ref[...]).astype(BF16)
    sent_ref[...] = sent
    picked_ref[...] = dot(pick_ref[...], sent).astype(BF16)
    rows = cot_ref.shape[0]
    bpd = rows // accs[0].shape[2]
    for d in range(adj_ref.shape[0] // rows):
        put_square(accs, bpd, d, adj_ref, d * rows)
    far = col_ref.shape[0] // chips - rows
    column(chips, far, rows, lax.axis_index("core"), adj_ref, far_t, col_ref)
    far_columns(chips, far_t, far_ref)
    keep_ref[...] = dot(col_ref[...], cot_ref[...]).astype(BF16)
    low = adj_ref.shape[0]
    lend_ref[:low, :] = adj_ref[...]
    lend_ref[low : low + rows, :] = cot_ref[...]
    lend_ref[low + rows :, :] = value_ref[...]
    place_ref[...] = jnp.concatenate([pick_ref[...]] * chips, 0).T


def deal(chips, hosts, total, picked, value, mine_ref, msg_ref, to_refs):
    rows = value.shape[0]
    far = picked.shape[0]
    send = far // hosts
    each = rows + far
    chip, core = lax.axis_index("chip"), lax.axis_index("core")
    mine_ref[...] = total[:rows]
    for k in range(chips):
        low = k * each + rows
        if k > 0:
            to_refs[k - 1][:rows, :] = total[k * each : low].astype(BF16)
            to_refs[k - 1][rows:, :] = value
        x = lax.rem(chip + k, chips)
        for g in range(hosts):
            at = low + g * send
            to = (g * chips + x) * CORES
            msg_ref[to + core] = total[at : at + send].astype(BF16)
            msg_ref[to + 1 - core] = picked[g * send : (g + 1) * send].astype(BF16)


def core_sum_kernel(
    chips, hosts, keep_ref, came_ref, value_ref, picked_ref, mine_ref, msg_ref, *rest
):
    total = keep_ref[...].astype(F32) + came_ref[...].astype(F32)
    picked = picked_ref[...].astype(F32)
    deal(chips, hosts, total, picked, value_ref[...], mine_ref, msg_ref, rest)


def received(recv_ref, hosts, chips, side):
    blocks = [
        recv_ref[(g * chips + x) * CORES + side].astype(F32)
        for x in range(chips)
        for g in range(hosts)
    ]
    return jnp.concatenate(blocks, 0).astype(BF16)


def merge_kernel(chips, hosts, recv_ref, mine_ref, place_ref, *refs):
    came, (out_ref, sum_ref) = refs[: chips - 1], refs[chips - 1 :]
    rows = mine_ref.shape[0]
    total = mine_ref[...]
    for k, ref in enumerate(came):
        total = total + ref[:rows, :].astype(F32)
        out_ref[k * rows : (k + 1) * rows, :] = ref[rows:, :]
    total = total + returned(place_ref, recv_ref, hosts, chips)
    sum_ref[...] = total
    low = len(came) * rows
    halo = received(recv_ref, hosts, chips, 1 - lax.axis_index("core"))
    high = low + halo.shape[0]
    out_ref[low:high, :] = halo
    out_ref[high:, :] = total.astype(BF16)


def returned(place_ref, recv_ref, hosts, chips):
    return dot(place_ref[...], received(recv_ref, hosts, chips, lax.axis_index("core")))


def joint(pairs):
    left = jnp.concatenate([a for a, _ in pairs], 1)
    return dot(left, jnp.concatenate([b for _, b in pairs], 0))


def square_of(adj_ref, x, side, rows):
    return adj_ref[pl.ds(pl.multiple_of((x * CORES + side) * rows, rows), rows), :]


def own_chip(adj_refs, blocks):
    chip, core = lax.axis_index("chip"), lax.axis_index("core")
    rows = blocks[0].shape[0]
    parts = [
        joint([(square_of(ref, chip, s, rows), b) for s, b in zip((core, 1 - core), blocks)])
        for ref in adj_refs
    ]
    return jnp.concatenate(parts, 0)


def early_one_kernel(
    chips, adj_ref, lent_ref, value_ref, self_ref, bias_ref, up_ref, weight_ref, neigh_ref, sent_ref,
    agg_ref, direct_ref, grad_ref, col_ref, far_ref, far_t,
):
    value = value_ref[...]
    rows = value.shape[0]
    low = adj_ref.shape[0]
    there = lent_ref[low + rows :, :]
    sent = dot(there, neigh_ref[...]).astype(BF16)
    agg_ref[...] = own_chip((adj_ref, lent_ref), (sent_ref[...], sent))
    both = jnp.concatenate([value, there], 0)
    direct_ref[...] = dot(both, self_ref[...]) + bias_ref[...].reshape(1, -1)
    both = jnp.concatenate([up_ref[...], lent_ref[low : low + rows, :]], 0)
    grad_ref[...] = dot_nt(both, weight_ref[...])
    far = col_ref.shape[0] // chips - rows
    column(chips, far, rows, lax.axis_index("core"), lent_ref, far_t, col_ref)
    far_columns(chips, far_t, far_ref)


def mid_kernel(
    chips, adj_ref, lent_ref, far_ref, far_two_ref, agg_ref, part_ref, sum_ref, neigh_ref, here_ref, *refs
):
    came, (agg_out, grad_ref) = refs[:-2], refs[-2:]
    rows = sum_ref.shape[0]
    halo = here_ref[(chips - 1) * rows : here_ref.shape[0] - rows, :]
    for i, (ref, columns) in enumerate(((adj_ref, far_ref), (lent_ref, far_two_ref))):
        pairs = other_chips(chips, ref, came) + [(columns[:, : halo.shape[0]], halo)]
        part = slice(i * rows, (i + 1) * rows)
        agg_out[part, :] = agg_ref[part, :] + joint(pairs)
    grad_ref[:rows, :] = part_ref[:rows, :] + precise_nt(sum_ref[...], neigh_ref[...])
    grad_ref[rows:, :] = part_ref[rows:, :]


def other_chips(chips, adj_ref, came):
    chip, core = lax.axis_index("chip"), lax.axis_index("core")
    pairs = []
    for k, block in enumerate(came):
        rows = block.shape[0] // 2
        x = lax.rem(chip - k - 1 + chips, chips)
        pairs.append((square_of(adj_ref, x, core, rows), block[rows:, :]))
    return pairs


def column_product(chips, hosts, adj_ref, far_ref, value_ref, came, recv_ref):
    rows = value_ref.shape[0]
    chip, core = lax.axis_index("chip"), lax.axis_index("core")
    halo = received(recv_ref, hosts, chips, 1 - core)
    pairs = [(square_of(adj_ref, chip, core, rows), value_ref[...])]
    pairs += other_chips(chips, adj_ref, came) + [(far_ref[:, : halo.shape[0]], halo)]
    return joint(pairs)


def there_kernel(chips, hosts, lent_ref, far_ref, value_ref, recv_ref, *refs):
    came, out_ref = refs[:-1], refs[-1]
    out_ref[...] = column_product(
        chips, hosts, lent_ref, far_ref, value_ref, came, recv_ref
    ).astype(BF16)


def here_kernel(
    chips, hosts, adj_ref, far_ref, sent_ref, recv_ref, value_ref, self_ref, bias_ref, up_ref,
    weight_ref, neigh_ref, mine_ref, place_ref, *refs
):
    came, (out_ref, grad_ref) = refs[:-2], refs[-2:]
    rows = mine_ref.shape[0]
    total = mine_ref[...] + returned(place_ref, recv_ref, hosts, chips)
    for block in came:
        total = total + block[:rows, :].astype(F32)
    grad = dot_nt(total.astype(BF16), neigh_ref[...])
    grad_ref[...] = grad + dot_nt(up_ref[...], weight_ref[...])
    out = column_product(chips, hosts, adj_ref, far_ref, sent_ref, came, recv_ref)
    out_ref[...] = out + dot(value_ref[...], self_ref[...]) + bias_ref[...].reshape(1, -1)


def add_rest(chips, rows, adj_ref, far_ref, agg, shared_ref):
    chip, core = lax.axis_index("chip"), lax.axis_index("core")
    pairs = []
    for k in range(chips - 1):
        x = lax.rem(chip - k - 1 + chips, chips)
        block = shared_ref[k * rows : (k + 1) * rows, :]
        pairs.append((square_of(adj_ref, x, 1 - core, rows), block))
    half = far_ref.shape[1] // 2
    low = (chips - 1) * rows
    pairs.append((far_ref[:, half:], shared_ref[low : low + half, :]))
    return agg + joint(pairs)


def middle_kernel(
    chips,
    hosts,
    adj_ref,
    lent_ref,
    far_ref,
    far_two_ref,
    col_ref,
    col_two_ref,
    agg_ref,
    direct_ref,
    grad_ref,
    pick_ref,
    shared_ref,
    neigh_two_ref,
    hidden_ref,
    sent_ref,
    grad_pre_ref,
    mine_ref,
    msg_ref,
    *rest,
):
    to_refs = rest
    far, rows = pick_ref.shape
    parts = [
        add_rest(chips, rows, ref, columns, agg_ref[i * rows : (i + 1) * rows, :], shared_ref)
        for i, (ref, columns) in enumerate(((adj_ref, far_ref), (lent_ref, far_two_ref)))
    ]
    pre = direct_ref[...] + jnp.concatenate(parts, 0)
    sigmoid = jax.nn.sigmoid(pre)
    hidden = (pre[:rows] * sigmoid[:rows]).astype(BF16)
    hidden_ref[...] = hidden
    sent = dot(hidden, neigh_two_ref[...]).astype(BF16)
    sent_ref[...] = sent
    low = (chips - 1) * rows + chips * far
    add = dot_nt(shared_ref[low:, :], neigh_two_ref[...])
    grad = jnp.concatenate([grad_ref[:rows, :], grad_ref[rows:, :] + add], 0)
    grad_pre = (grad * sigmoid * (1.0 + pre * (1.0 - sigmoid))).astype(BF16)
    grad_pre_ref[...] = grad_pre[:rows]
    total = joint([(col_ref[...], grad_pre[:rows]), (col_two_ref[...], grad_pre[rows:])])
    picked = dot(pick_ref[...], sent)
    deal(chips, hosts, total, picked, sent, mine_ref, msg_ref, to_refs)


def last_kernel(here_ref, there_ref, output_ref):
    output_ref[...] = (here_ref[...] + there_ref[...].astype(F32)).astype(BF16)


def call(kernel, name, out_shape, in_specs, args, scratch=(), limit=32, flops=0):
    return pl.pallas_call(
        kernel,
        out_shape=out_shape,
        in_specs=in_specs,
        out_specs=jax.tree.map(lambda _: VMEM, out_shape),
        scratch_shapes=scratch,
        compiler_params=pltpu.CompilerParams(vmem_limit_bytes=limit * MIB),
        cost_estimate=pl.CostEstimate(
            flops=flops, bytes_accessed=flops // 1024, transcendentals=0
        ),
        name=name,
    )(*args)


def shift(value, axis, k):
    size = lax.axis_size(axis)
    return lax.ppermute(value, axis, [(i, (i + k) % size) for i in range(size)])


def shape(rows, width, kind=BF16):
    return jax.ShapeDtypeStruct((rows, width), kind)


def body(
    features,
    send_list,
    tile_dst,
    tile_src,
    tile_rows,
    tile_val,
    self_one,
    neigh_one,
    bias_one,
    self_two,
    neigh_two,
    bias_two,
    cotangent,
):
    chips = lax.axis_size("chip")
    hosts = lax.axis_size("hst")
    rows, width = features.shape
    tiles, blk = tile_val.shape[:2]
    send = send_list.shape[3]
    far = hosts * send
    all_rows = chips * CORES * (rows + far)
    count = chips * (rows + far)
    rows_shape = shape(rows, width)
    sum_shape = shape(rows, width, F32)
    both_shape = shape(CORES * rows, width, F32)
    square = 2 * rows * width * width
    far_shape = shape(rows, chips * CORES * far)
    halo_rows = (chips - 1) * rows + chips * far
    dealt = (
        sum_shape,
        jax.ShapeDtypeStruct((chips * hosts * CORES, send, width), BF16),
    ) + (shape(2 * rows, width),) * (chips - 1)

    def across(msg, to):
        terms = [shift(block, "chip", k + 1) for k, block in enumerate(to)]
        recv = lax.all_to_all(msg, ("hst", "chip", "core"), split_axis=0, concat_axis=0, tiled=True)
        return terms, recv

    far_t = pltpu.VMEM((chips * CORES * far, rows), BF16)
    sums = jax.ShapeDtypeStruct(((rows // blk) * (all_rows // blk), blk // PARTS, blk), F32)
    give, pick, *sums = call(
        functools.partial(prep_kernel, chips),
        "prep",
        (shape(count, width), shape(far, rows)) + (sums,) * PARTS,
        [HBM] * 6,
        [
            pltpu.with_memory_space_constraint(value, pltpu.HBM)
            for value in (
                tile_dst,
                tile_src,
                tile_rows,
                send_list,
                tile_val,
                cotangent,
            )
        ],
        [
            pltpu.SMEM(tile_dst.shape, jnp.int32),
            pltpu.SMEM(tile_src.shape, jnp.int32),
            pltpu.SMEM(tile_rows.shape, jnp.int32),
            pltpu.SMEM(send_list.shape, jnp.int32),
            pltpu.VMEM(tile_val.shape, BF16),
            pltpu.VMEM(cotangent.shape, BF16),
            pltpu.VMEM((rows, rows), BF16),
            far_t,
            pltpu.VMEM((count, rows), BF16),
            pltpu.SemaphoreType.DMA((5 + CHUNKS,)),
        ],
    )
    came = shift(give, "core", 1)
    sent, picked, adj, col, keep, lend, place, columns = call(
        functools.partial(rest_kernel, chips),
        "rest",
        (
            rows_shape,
            shape(far, width),
            shape(all_rows, rows),
            shape(count, rows),
            shape(count, width),
            shape(all_rows + 2 * rows, width),
            shape(rows, chips * far),
            far_shape,
        ),
        [VMEM] * (4 + PARTS),
        (cotangent, features, pick, neigh_one, *sums),
        [far_t],
        flops=3 * square,
    )
    lent = shift(lend, "core", 1)
    mine, msg, *to = call(
        functools.partial(core_sum_kernel, chips, hosts),
        "core_sum",
        dealt,
        [VMEM] * 4,
        (keep, came, sent, picked),
        flops=60 * square,
    )
    terms, recv = across(msg, to)
    here, summed = call(
        functools.partial(merge_kernel, chips, hosts),
        "merge",
        (shape(halo_rows + rows, width), sum_shape),
        [VMEM] * (2 + chips),
        (recv, mine, place, *terms),
    )
    shared = shift(here, "core", 1)
    agg, direct, grad, col_two, columns_two = call(
        functools.partial(early_one_kernel, chips),
        "early_one",
        (both_shape,) * 3 + (shape(count, rows), far_shape),
        [VMEM] * 9,
        (
            adj,
            lent,
            features,
            self_one,
            bias_one,
            cotangent,
            self_two,
            neigh_one,
            sent,
        ),
        [far_t],
        flops=8 * square,
    )
    agg, grad = call(
        functools.partial(mid_kernel, chips),
        "mid",
        (both_shape,) * 2,
        [VMEM] * (8 + chips),
        (adj, lent, columns, columns_two, agg, grad, summed, neigh_two, here, *terms),
        flops=3 * square,
    )
    hidden, sent, grad_pre, mine, msg, *to = call(
        functools.partial(middle_kernel, chips, hosts),
        "middle",
        (rows_shape,) * 3 + dealt,
        [VMEM] * 12,
        (
            adj,
            lent,
            columns,
            columns_two,
            col,
            col_two,
            agg,
            direct,
            grad,
            pick,
            shared,
            neigh_two,
        ),
        flops=12 * square,
    )
    terms, recv = across(msg, to)
    there = call(
        functools.partial(there_kernel, chips, hosts),
        "there",
        rows_shape,
        [VMEM] * (3 + chips),
        (lent, columns_two, sent, recv, *terms),
    )
    shared = shift(there, "core", 1)
    here, grad = call(
        functools.partial(here_kernel, chips, hosts),
        "here",
        (sum_shape,) * 2,
        [VMEM] * (11 + chips),
        (
            adj,
            columns,
            sent,
            recv,
            hidden,
            self_two,
            bias_two,
            grad_pre,
            self_one,
            neigh_one,
            mine,
            place,
            *terms,
        ),
        flops=7 * square,
    )
    output = call(last_kernel, "last", rows_shape, [VMEM] * 2, (here, shared))
    return output, grad


def solution(mesh):
    hosts, devs = mesh.devices.shape
    mesh = Mesh(mesh.devices.reshape(hosts, devs // CORES, CORES), ("hst", "chip", "core"))
    dev = ("chip", "core")
    every = ("hst", "chip", "core")
    return jax.shard_map(
        body,
        mesh=mesh,
        in_specs=(
            P(every, None),
            P("hst", dev, None, None),
            P(every),
            P(every),
            P(every),
            P(every, None, None),
            P(),
            P(),
            P(),
            P(),
            P(),
            P(),
            P(every, None),
        ),
        out_specs=(P(every, None), P(every, None)),
        check_vma=False,
    )
```

```python
import functools

import jax
import jax.numpy as jnp
from jax import lax
from jax.experimental import pallas as pl
from jax.experimental.pallas import tpu as pltpu
from jax.sharding import Mesh, PartitionSpec as P

F32 = jnp.float32
BF16 = jnp.bfloat16
MIB = 1024 * 1024
CHUNKS = 8
PARTS = 4
CORES = 2

VMEM = pl.BlockSpec(memory_space=pltpu.VMEM)
HBM = pl.BlockSpec(memory_space=pltpu.HBM)


def dot(a, b):
    return jnp.dot(a, b, preferred_element_type=F32)


def dot_nt(a, b):
    return lax.dot_general(a, b, (((1,), (1,)), ((), ())), preferred_element_type=F32)


def precise_nt(a, b):
    high = a.astype(BF16)
    low = (a - high.astype(F32)).astype(BF16)
    return dot_nt(high, b) + dot_nt(low, b)


def pick_matrix(send_ref, rows):
    hosts, send = send_ref.shape[2], send_ref.shape[3]
    place = lax.broadcasted_iota(jnp.int32, (send, rows), 0)
    column = lax.broadcasted_iota(jnp.int32, (send, rows), 1)
    parts = []
    for g in range(hosts):
        index = jnp.zeros((send, rows), jnp.int32)
        for s in range(send):
            index = jnp.where(place == s, send_ref[0, 0, g, s], index)
        parts.append(jnp.where(index == column, 1.0, 0.0).astype(F32))
    return jnp.concatenate(parts, 0).astype(BF16)


def column(chips, far, rows, side, adj_ref, far_t, out_ref):
    chip = lax.axis_index("chip")
    each = rows + far
    own_rows = chips * CORES * rows
    for j in range(far_t.shape[0] // rows):
        low = own_rows + j * rows
        far_t[j * rows : (j + 1) * rows, :] = adj_ref[low : low + rows, :].T
    for k in range(chips):
        d = lax.rem(chip + k, chips) * CORES + side
        at = k * each
        out_ref[at : at + rows, :] = adj_ref[pl.ds(pl.multiple_of(d * rows, rows), rows), :].T
        out_ref[at + rows : at + each, :] = far_t[pl.ds(pl.multiple_of(d * far, far), far), :]


def far_columns(chips, far_t, out_ref):
    far = far_t.shape[0] // (chips * CORES)
    core = lax.axis_index("core")
    parts = [
        far_t[pl.ds(pl.multiple_of((x * CORES + side) * far, far), far), :]
        for side in (1 - core, core)
        for x in range(chips)
    ]
    out_ref[...] = jnp.concatenate(parts, 0).T


def prep_kernel(
    chips,
    dst_hbm,
    src_hbm,
    rows_hbm,
    send_hbm,
    tile_hbm,
    cot_hbm,
    give_ref,
    pick_ref,
    *rest,
):
    accs, rest = rest[:PARTS], rest[PARTS:]
    (
        dst_ref,
        src_ref,
        rows_ref,
        send_ref,
        tile_buf,
        cot_ref,
        square,
        far_t,
        col,
        sems,
    ) = rest
    tiles, blk = tile_buf.shape[0], tile_buf.shape[1]
    each = tiles // CHUNKS
    cuts = [c * each for c in range(CHUNKS)] + [tiles - each // 2, tiles]
    chunks = [
        (tile_hbm.at[pl.ds(low, high - low)], tile_buf.at[pl.ds(low, high - low)])
        for low, high in zip(cuts, cuts[1:])
    ]
    pairs = [(send_hbm, send_ref), (dst_hbm, dst_ref), (src_hbm, src_ref), (rows_hbm, rows_ref)]
    pairs += chunks + [(cot_hbm, cot_ref)]
    copies = [pltpu.make_async_copy(a, b, sems.at[i]) for i, (a, b) in enumerate(pairs)]
    for copy in copies:
        copy.start()
    rows = cot_ref.shape[0]
    bpd = rows // blk
    sources = accs[0].shape[0] // bpd
    part = accs[0].shape[1]
    far = send_ref.shape[2] * send_ref.shape[3]
    for acc in accs:
        acc[...] = jnp.zeros_like(acc)
    place = lax.broadcasted_iota(jnp.int32, (part, blk), 0)

    def add(t, carry):
        slot = dst_ref[t] * sources + src_ref[t]
        for i, acc in enumerate(accs):
            value = tile_buf[t, i * part : (i + 1) * part, :].astype(F32)
            acc[slot] += jnp.where(place < rows_ref[t] - i * part, value, 0.0)
        return carry

    copies[0].wait()
    pick_ref[...] = pick_matrix(send_ref, rows)
    for copy in copies[1:4]:
        copy.wait()
    for copy, low, high in zip(copies[4:], cuts, cuts[1:]):
        copy.wait()
        lax.fori_loop(low, high, add, 0, unroll=True)
    copies[-1].wait()
    chip, side = lax.axis_index("chip"), 1 - lax.axis_index("core")
    base = chips * CORES
    for j in range(far_t.shape[0] // rows):
        put_square(accs, bpd, base + j, square, 0)
        far_t[j * rows : (j + 1) * rows, :] = square[...].T
    for k in range(chips):
        d = lax.rem(chip + k, chips) * CORES + side
        at = k * (rows + far)
        put_square(accs, bpd, d, square, 0)
        col[at : at + rows, :] = square[...].T
        low = pl.multiple_of(d * far, far)
        col[at + rows : at + rows + far, :] = far_t[pl.ds(low, far), :]
    give_ref[...] = dot(col[...], cot_ref[...]).astype(BF16)


def put_square(accs, bpd, d, out_ref, base):
    sources = accs[0].shape[0] // bpd
    part, blk = accs[0].shape[1:]
    for b in range(bpd):
        for j in range(bpd):
            for i, acc in enumerate(accs):
                low = base + b * blk + i * part
                value = acc[b * sources + d * bpd + j].astype(BF16)
                out_ref[low : low + part, j * blk : (j + 1) * blk] = value


def rest_kernel(chips, cot_ref, value_ref, pick_ref, neigh_ref, *refs):
    accs = refs[:PARTS]
    sent_ref, picked_ref, adj_ref, col_ref, keep_ref, lend_ref, place_ref, far_ref, far_t = refs[PARTS:]
    sent = dot(value_ref[...], neigh_ref[...]).astype(BF16)
    sent_ref[...] = sent
    picked_ref[...] = dot(pick_ref[...], sent).astype(BF16)
    rows = cot_ref.shape[0]
    bpd = rows // accs[0].shape[2]
    for d in range(adj_ref.shape[0] // rows):
        put_square(accs, bpd, d, adj_ref, d * rows)
    far = col_ref.shape[0] // chips - rows
    column(chips, far, rows, lax.axis_index("core"), adj_ref, far_t, col_ref)
    far_columns(chips, far_t, far_ref)
    keep_ref[...] = dot(col_ref[...], cot_ref[...]).astype(BF16)
    low = adj_ref.shape[0]
    lend_ref[:low, :] = adj_ref[...]
    lend_ref[low : low + rows, :] = cot_ref[...]
    lend_ref[low + rows :, :] = value_ref[...]
    place_ref[...] = jnp.concatenate([pick_ref[...]] * chips, 0).T


def deal(chips, hosts, total, picked, value, mine_ref, msg_ref, to_refs):
    rows = value.shape[0]
    far = picked.shape[0]
    send = far // hosts
    each = rows + far
    chip, core = lax.axis_index("chip"), lax.axis_index("core")
    mine_ref[...] = total[:rows]
    for k in range(chips):
        low = k * each + rows
        if k > 0:
            to_refs[k - 1][:rows, :] = total[k * each : low].astype(BF16)
            to_refs[k - 1][rows:, :] = value
        x = lax.rem(chip + k, chips)
        for g in range(hosts):
            at = low + g * send
            to = (g * chips + x) * CORES
            msg_ref[to + core] = total[at : at + send].astype(BF16)
            msg_ref[to + 1 - core] = picked[g * send : (g + 1) * send].astype(BF16)


def core_sum_kernel(
    chips, hosts, keep_ref, came_ref, value_ref, picked_ref, mine_ref, msg_ref, *rest
):
    total = keep_ref[...].astype(F32) + came_ref[...].astype(F32)
    picked = picked_ref[...].astype(F32)
    deal(chips, hosts, total, picked, value_ref[...], mine_ref, msg_ref, rest)


def received(recv_ref, hosts, chips, side):
    blocks = [
        recv_ref[(g * chips + x) * CORES + side].astype(F32)
        for x in range(chips)
        for g in range(hosts)
    ]
    return jnp.concatenate(blocks, 0).astype(BF16)


def merge_kernel(chips, hosts, recv_ref, mine_ref, place_ref, *refs):
    came, (out_ref, sum_ref) = refs[: chips - 1], refs[chips - 1 :]
    rows = mine_ref.shape[0]
    total = mine_ref[...]
    for k, ref in enumerate(came):
        total = total + ref[:rows, :].astype(F32)
        out_ref[k * rows : (k + 1) * rows, :] = ref[rows:, :]
    total = total + returned(place_ref, recv_ref, hosts, chips)
    sum_ref[...] = total
    low = len(came) * rows
    halo = received(recv_ref, hosts, chips, 1 - lax.axis_index("core"))
    high = low + halo.shape[0]
    out_ref[low:high, :] = halo
    out_ref[high:, :] = total.astype(BF16)


def returned(place_ref, recv_ref, hosts, chips):
    return dot(place_ref[...], received(recv_ref, hosts, chips, lax.axis_index("core")))


def joint(pairs):
    left = jnp.concatenate([a for a, _ in pairs], 1)
    return dot(left, jnp.concatenate([b for _, b in pairs], 0))


def square_of(adj_ref, x, side, rows):
    return adj_ref[pl.ds(pl.multiple_of((x * CORES + side) * rows, rows), rows), :]


def own_chip(adj_refs, blocks):
    chip, core = lax.axis_index("chip"), lax.axis_index("core")
    rows = blocks[0].shape[0]
    parts = [
        joint([(square_of(ref, chip, s, rows), b) for s, b in zip((core, 1 - core), blocks)])
        for ref in adj_refs
    ]
    return jnp.concatenate(parts, 0)


def early_one_kernel(
    chips, adj_ref, lent_ref, value_ref, self_ref, bias_ref, up_ref, weight_ref, neigh_ref, sent_ref,
    agg_ref, direct_ref, grad_ref, col_ref, far_ref, far_t,
):
    value = value_ref[...]
    rows = value.shape[0]
    low = adj_ref.shape[0]
    there = lent_ref[low + rows :, :]
    sent = dot(there, neigh_ref[...]).astype(BF16)
    agg_ref[...] = own_chip((adj_ref, lent_ref), (sent_ref[...], sent))
    both = jnp.concatenate([value, there], 0)
    direct_ref[...] = dot(both, self_ref[...]) + bias_ref[...].reshape(1, -1)
    both = jnp.concatenate([up_ref[...], lent_ref[low : low + rows, :]], 0)
    grad_ref[...] = dot_nt(both, weight_ref[...])
    far = col_ref.shape[0] // chips - rows
    column(chips, far, rows, lax.axis_index("core"), lent_ref, far_t, col_ref)
    far_columns(chips, far_t, far_ref)


def mid_kernel(
    chips, adj_ref, lent_ref, far_ref, far_two_ref, agg_ref, part_ref, sum_ref, neigh_ref, here_ref, *refs
):
    came, (agg_out, grad_ref) = refs[:-2], refs[-2:]
    rows = sum_ref.shape[0]
    halo = here_ref[(chips - 1) * rows : here_ref.shape[0] - rows, :]
    for i, (ref, columns) in enumerate(((adj_ref, far_ref), (lent_ref, far_two_ref))):
        pairs = other_chips(chips, ref, came) + [(columns[:, : halo.shape[0]], halo)]
        part = slice(i * rows, (i + 1) * rows)
        agg_out[part, :] = agg_ref[part, :] + joint(pairs)
    grad_ref[:rows, :] = part_ref[:rows, :] + precise_nt(sum_ref[...], neigh_ref[...])
    grad_ref[rows:, :] = part_ref[rows:, :]


def other_chips(chips, adj_ref, came):
    chip, core = lax.axis_index("chip"), lax.axis_index("core")
    pairs = []
    for k, block in enumerate(came):
        rows = block.shape[0] // 2
        x = lax.rem(chip - k - 1 + chips, chips)
        pairs.append((square_of(adj_ref, x, core, rows), block[rows:, :]))
    return pairs


def column_product(chips, hosts, adj_ref, far_ref, value_ref, came, recv_ref):
    rows = value_ref.shape[0]
    chip, core = lax.axis_index("chip"), lax.axis_index("core")
    halo = received(recv_ref, hosts, chips, 1 - core)
    pairs = [(square_of(adj_ref, chip, core, rows), value_ref[...])]
    pairs += other_chips(chips, adj_ref, came) + [(far_ref[:, : halo.shape[0]], halo)]
    return joint(pairs)


def there_kernel(chips, hosts, lent_ref, far_ref, value_ref, recv_ref, *refs):
    came, out_ref = refs[:-1], refs[-1]
    out_ref[...] = column_product(
        chips, hosts, lent_ref, far_ref, value_ref, came, recv_ref
    ).astype(BF16)


def here_kernel(
    chips, hosts, adj_ref, far_ref, sent_ref, recv_ref, value_ref, self_ref, bias_ref, up_ref,
    weight_ref, neigh_ref, mine_ref, place_ref, *refs
):
    came, (out_ref, grad_ref) = refs[:-2], refs[-2:]
    rows = mine_ref.shape[0]
    total = mine_ref[...] + returned(place_ref, recv_ref, hosts, chips)
    for block in came:
        total = total + block[:rows, :].astype(F32)
    grad = dot_nt(total.astype(BF16), neigh_ref[...])
    grad_ref[...] = grad + dot_nt(up_ref[...], weight_ref[...])
    out = column_product(chips, hosts, adj_ref, far_ref, sent_ref, came, recv_ref)
    out_ref[...] = out + dot(value_ref[...], self_ref[...]) + bias_ref[...].reshape(1, -1)


def add_rest(chips, rows, adj_ref, far_ref, agg, shared_ref):
    chip, core = lax.axis_index("chip"), lax.axis_index("core")
    pairs = []
    for k in range(chips - 1):
        x = lax.rem(chip - k - 1 + chips, chips)
        block = shared_ref[k * rows : (k + 1) * rows, :]
        pairs.append((square_of(adj_ref, x, 1 - core, rows), block))
    half = far_ref.shape[1] // 2
    low = (chips - 1) * rows
    pairs.append((far_ref[:, half:], shared_ref[low : low + half, :]))
    return agg + joint(pairs)


def middle_kernel(
    chips,
    hosts,
    adj_ref,
    lent_ref,
    far_ref,
    far_two_ref,
    col_ref,
    col_two_ref,
    agg_ref,
    direct_ref,
    grad_ref,
    pick_ref,
    shared_ref,
    neigh_two_ref,
    hidden_ref,
    sent_ref,
    grad_pre_ref,
    mine_ref,
    msg_ref,
    *rest,
):
    to_refs = rest
    far, rows = pick_ref.shape
    parts = [
        add_rest(chips, rows, ref, columns, agg_ref[i * rows : (i + 1) * rows, :], shared_ref)
        for i, (ref, columns) in enumerate(((adj_ref, far_ref), (lent_ref, far_two_ref)))
    ]
    pre = direct_ref[...] + jnp.concatenate(parts, 0)
    sigmoid = jax.nn.sigmoid(pre)
    hidden = (pre[:rows] * sigmoid[:rows]).astype(BF16)
    hidden_ref[...] = hidden
    sent = dot(hidden, neigh_two_ref[...]).astype(BF16)
    sent_ref[...] = sent
    low = (chips - 1) * rows + chips * far
    add = dot_nt(shared_ref[low:, :], neigh_two_ref[...])
    grad = jnp.concatenate([grad_ref[:rows, :], grad_ref[rows:, :] + add], 0)
    grad_pre = (grad * sigmoid * (1.0 + pre * (1.0 - sigmoid))).astype(BF16)
    grad_pre_ref[...] = grad_pre[:rows]
    total = joint([(col_ref[...], grad_pre[:rows]), (col_two_ref[...], grad_pre[rows:])])
    picked = dot(pick_ref[...], sent)
    deal(chips, hosts, total, picked, sent, mine_ref, msg_ref, to_refs)


def last_kernel(here_ref, there_ref, output_ref):
    output_ref[...] = (here_ref[...] + there_ref[...].astype(F32)).astype(BF16)


def call(kernel, name, out_shape, in_specs, args, scratch=(), limit=32, flops=0):
    return pl.pallas_call(
        kernel,
        out_shape=out_shape,
        in_specs=in_specs,
        out_specs=jax.tree.map(lambda _: VMEM, out_shape),
        scratch_shapes=scratch,
        compiler_params=pltpu.CompilerParams(vmem_limit_bytes=limit * MIB),
        cost_estimate=pl.CostEstimate(
            flops=flops, bytes_accessed=flops // 1024, transcendentals=0
        ),
        name=name,
    )(*args)


def shift(value, axis, k):
    size = lax.axis_size(axis)
    return lax.ppermute(value, axis, [(i, (i + k) % size) for i in range(size)])


def shape(rows, width, kind=BF16):
    return jax.ShapeDtypeStruct((rows, width), kind)


def body(
    features,
    send_list,
    tile_dst,
    tile_src,
    tile_rows,
    tile_val,
    self_one,
    neigh_one,
    bias_one,
    self_two,
    neigh_two,
    bias_two,
    cotangent,
):
    chips = lax.axis_size("chip")
    hosts = lax.axis_size("hst")
    rows, width = features.shape
    tiles, blk = tile_val.shape[:2]
    send = send_list.shape[3]
    far = hosts * send
    all_rows = chips * CORES * (rows + far)
    count = chips * (rows + far)
    rows_shape = shape(rows, width)
    sum_shape = shape(rows, width, F32)
    both_shape = shape(CORES * rows, width, F32)
    square = 2 * rows * width * width
    far_shape = shape(rows, chips * CORES * far)
    halo_rows = (chips - 1) * rows + chips * far
    dealt = (
        sum_shape,
        jax.ShapeDtypeStruct((chips * hosts * CORES, send, width), BF16),
    ) + (shape(2 * rows, width),) * (chips - 1)

    def across(msg, to):
        terms = [shift(block, "chip", k + 1) for k, block in enumerate(to)]
        recv = lax.all_to_all(msg, ("hst", "chip", "core"), split_axis=0, concat_axis=0, tiled=True)
        return terms, recv

    far_t = pltpu.VMEM((chips * CORES * far, rows), BF16)
    sums = jax.ShapeDtypeStruct(((rows // blk) * (all_rows // blk), blk // PARTS, blk), F32)
    give, pick, *sums = call(
        functools.partial(prep_kernel, chips),
        "prep",
        (shape(count, width), shape(far, rows)) + (sums,) * PARTS,
        [HBM] * 6,
        [
            pltpu.with_memory_space_constraint(value, pltpu.HBM)
            for value in (
                tile_dst,
                tile_src,
                tile_rows,
                send_list,
                tile_val,
                cotangent,
            )
        ],
        [
            pltpu.SMEM(tile_dst.shape, jnp.int32),
            pltpu.SMEM(tile_src.shape, jnp.int32),
            pltpu.SMEM(tile_rows.shape, jnp.int32),
            pltpu.SMEM(send_list.shape, jnp.int32),
            pltpu.VMEM(tile_val.shape, BF16),
            pltpu.VMEM(cotangent.shape, BF16),
            pltpu.VMEM((rows, rows), BF16),
            far_t,
            pltpu.VMEM((count, rows), BF16),
            pltpu.SemaphoreType.DMA((6 + CHUNKS,)),
        ],
    )
    came = shift(give, "core", 1)
    sent, picked, adj, col, keep, lend, place, columns = call(
        functools.partial(rest_kernel, chips),
        "rest",
        (
            rows_shape,
            shape(far, width),
            shape(all_rows, rows),
            shape(count, rows),
            shape(count, width),
            shape(all_rows + 2 * rows, width),
            shape(rows, chips * far),
            far_shape,
        ),
        [VMEM] * (4 + PARTS),
        (cotangent, features, pick, neigh_one, *sums),
        [far_t],
        flops=3 * square,
    )
    lent = shift(lend, "core", 1)
    mine, msg, *to = call(
        functools.partial(core_sum_kernel, chips, hosts),
        "core_sum",
        dealt,
        [VMEM] * 4,
        (keep, came, sent, picked),
        flops=60 * square,
    )
    terms, recv = across(msg, to)
    here, summed = call(
        functools.partial(merge_kernel, chips, hosts),
        "merge",
        (shape(halo_rows + rows, width), sum_shape),
        [VMEM] * (2 + chips),
        (recv, mine, place, *terms),
    )
    shared = shift(here, "core", 1)
    agg, direct, grad, col_two, columns_two = call(
        functools.partial(early_one_kernel, chips),
        "early_one",
        (both_shape,) * 3 + (shape(count, rows), far_shape),
        [VMEM] * 9,
        (
            adj,
            lent,
            features,
            self_one,
            bias_one,
            cotangent,
            self_two,
            neigh_one,
            sent,
        ),
        [far_t],
        flops=8 * square,
    )
    agg, grad = call(
        functools.partial(mid_kernel, chips),
        "mid",
        (both_shape,) * 2,
        [VMEM] * (8 + chips),
        (adj, lent, columns, columns_two, agg, grad, summed, neigh_two, here, *terms),
        flops=3 * square,
    )
    hidden, sent, grad_pre, mine, msg, *to = call(
        functools.partial(middle_kernel, chips, hosts),
        "middle",
        (rows_shape,) * 3 + dealt,
        [VMEM] * 12,
        (
            adj,
            lent,
            columns,
            columns_two,
            col,
            col_two,
            agg,
            direct,
            grad,
            pick,
            shared,
            neigh_two,
        ),
        flops=12 * square,
    )
    terms, recv = across(msg, to)
    there = call(
        functools.partial(there_kernel, chips, hosts),
        "there",
        rows_shape,
        [VMEM] * (3 + chips),
        (lent, columns_two, sent, recv, *terms),
    )
    shared = shift(there, "core", 1)
    here, grad = call(
        functools.partial(here_kernel, chips, hosts),
        "here",
        (sum_shape,) * 2,
        [VMEM] * (11 + chips),
        (
            adj,
            columns,
            sent,
            recv,
            hidden,
            self_two,
            bias_two,
            grad_pre,
            self_one,
            neigh_one,
            mine,
            place,
            *terms,
        ),
        flops=7 * square,
    )
    output = call(last_kernel, "last", rows_shape, [VMEM] * 2, (here, shared))
    return output, grad


def solution(mesh):
    hosts, devs = mesh.devices.shape
    mesh = Mesh(mesh.devices.reshape(hosts, devs // CORES, CORES), ("hst", "chip", "core"))
    dev = ("chip", "core")
    every = ("hst", "chip", "core")
    return jax.shard_map(
        body,
        mesh=mesh,
        in_specs=(
            P(every, None),
            P("hst", dev, None, None),
            P(every),
            P(every),
            P(every),
            P(every, None, None),
            P(),
            P(),
            P(),
            P(),
            P(),
            P(),
            P(every, None),
        ),
        out_specs=(P(every, None), P(every, None)),
        check_vma=False,
    )
```

```python
import functools

import jax
import jax.numpy as jnp
from jax import lax
from jax.experimental import pallas as pl
from jax.experimental.pallas import tpu as pltpu
from jax.sharding import Mesh, PartitionSpec as P

F32 = jnp.float32
BF16 = jnp.bfloat16
MIB = 1024 * 1024
CHUNKS = 8
PARTS = 4
CORES = 2

VMEM = pl.BlockSpec(memory_space=pltpu.VMEM)
HBM = pl.BlockSpec(memory_space=pltpu.HBM)


def dot(a, b):
    return jnp.dot(a, b, preferred_element_type=F32)


def dot_nt(a, b):
    return lax.dot_general(a, b, (((1,), (1,)), ((), ())), preferred_element_type=F32)


def precise_nt(a, b):
    high = a.astype(BF16)
    low = (a - high.astype(F32)).astype(BF16)
    return dot_nt(high, b) + dot_nt(low, b)


def pick_matrix(send_ref, rows):
    hosts, send = send_ref.shape[2], send_ref.shape[3]
    place = lax.broadcasted_iota(jnp.int32, (send, rows), 0)
    column = lax.broadcasted_iota(jnp.int32, (send, rows), 1)
    parts = []
    for g in range(hosts):
        index = jnp.zeros((send, rows), jnp.int32)
        for s in range(send):
            index = jnp.where(place == s, send_ref[0, 0, g, s], index)
        parts.append(jnp.where(index == column, 1.0, 0.0).astype(F32))
    return jnp.concatenate(parts, 0).astype(BF16)


def column(chips, far, rows, side, adj_ref, far_t, out_ref):
    chip = lax.axis_index("chip")
    each = rows + far
    own_rows = chips * CORES * rows
    for j in range(far_t.shape[0] // rows):
        low = own_rows + j * rows
        far_t[j * rows : (j + 1) * rows, :] = adj_ref[low : low + rows, :].T
    for k in range(chips):
        d = lax.rem(chip + k, chips) * CORES + side
        at = k * each
        out_ref[at : at + rows, :] = adj_ref[pl.ds(pl.multiple_of(d * rows, rows), rows), :].T
        out_ref[at + rows : at + each, :] = far_t[pl.ds(pl.multiple_of(d * far, far), far), :]


def far_columns(chips, far_t, out_ref):
    far = far_t.shape[0] // (chips * CORES)
    core = lax.axis_index("core")
    parts = [
        far_t[pl.ds(pl.multiple_of((x * CORES + side) * far, far), far), :]
        for side in (1 - core, core)
        for x in range(chips)
    ]
    out_ref[...] = jnp.concatenate(parts, 0).T


def prep_kernel(
    chips,
    dst_hbm,
    src_hbm,
    rows_hbm,
    send_hbm,
    tile_hbm,
    cot_hbm,
    give_ref,
    pick_ref,
    *rest,
):
    accs, rest = rest[:PARTS], rest[PARTS:]
    (
        dst_ref,
        src_ref,
        rows_ref,
        send_ref,
        tile_buf,
        cot_ref,
        square,
        far_t,
        col,
        sems,
    ) = rest
    tiles, blk = tile_buf.shape[0], tile_buf.shape[1]
    each = tiles // CHUNKS
    cuts = [c * each for c in range(CHUNKS)] + [tiles - each // 2, tiles]
    chunks = [
        (tile_hbm.at[pl.ds(low, high - low)], tile_buf.at[pl.ds(low, high - low)])
        for low, high in zip(cuts, cuts[1:])
    ]
    pairs = [(send_hbm, send_ref), (dst_hbm, dst_ref), (src_hbm, src_ref), (rows_hbm, rows_ref)]
    pairs += chunks + [(cot_hbm, cot_ref)]
    copies = [pltpu.make_async_copy(a, b, sems.at[i]) for i, (a, b) in enumerate(pairs)]
    for copy in copies:
        copy.start()
    rows = cot_ref.shape[0]
    bpd = rows // blk
    sources = accs[0].shape[0] // bpd
    part = accs[0].shape[1]
    far = send_ref.shape[2] * send_ref.shape[3]
    for acc in accs:
        acc[...] = jnp.zeros_like(acc)
    place = lax.broadcasted_iota(jnp.int32, (part, blk), 0)

    def add(t, carry):
        slot = dst_ref[t] * sources + src_ref[t]
        for i, acc in enumerate(accs):
            value = tile_buf[t, i * part : (i + 1) * part, :].astype(F32)
            acc[slot] += jnp.where(place < rows_ref[t] - i * part, value, 0.0)
        return carry

    copies[0].wait()
    pick_ref[...] = pick_matrix(send_ref, rows)
    for copy in copies[1:4]:
        copy.wait()
    for copy, low, high in zip(copies[4:], cuts, cuts[1:]):
        copy.wait()
        lax.fori_loop(low, high, add, 0, unroll=True)
    copies[-1].wait()
    chip, side = lax.axis_index("chip"), 1 - lax.axis_index("core")
    base = chips * CORES
    for j in range(far_t.shape[0] // rows):
        put_square(accs, bpd, base + j, square, 0)
        far_t[j * rows : (j + 1) * rows, :] = square[...].T
    for k in range(chips):
        d = lax.rem(chip + k, chips) * CORES + side
        at = k * (rows + far)
        put_square(accs, bpd, d, square, 0)
        col[at : at + rows, :] = square[...].T
        low = pl.multiple_of(d * far, far)
        col[at + rows : at + rows + far, :] = far_t[pl.ds(low, far), :]
    give_ref[...] = dot(col[...], cot_ref[...]).astype(BF16)


def put_square(accs, bpd, d, out_ref, base):
    sources = accs[0].shape[0] // bpd
    part, blk = accs[0].shape[1:]
    for b in range(bpd):
        for j in range(bpd):
            for i, acc in enumerate(accs):
                low = base + b * blk + i * part
                value = acc[b * sources + d * bpd + j].astype(BF16)
                out_ref[low : low + part, j * blk : (j + 1) * blk] = value


def rest_kernel(chips, cot_ref, value_ref, pick_ref, neigh_ref, *refs):
    accs = refs[:PARTS]
    sent_ref, picked_ref, adj_ref, col_ref, keep_ref, lend_ref, place_ref, far_ref, far_t = refs[PARTS:]
    sent = dot(value_ref[...], neigh_ref[...]).astype(BF16)
    sent_ref[...] = sent
    picked_ref[...] = dot(pick_ref[...], sent).astype(BF16)
    rows = cot_ref.shape[0]
    bpd = rows // accs[0].shape[2]
    for d in range(adj_ref.shape[0] // rows):
        put_square(accs, bpd, d, adj_ref, d * rows)
    far = col_ref.shape[0] // chips - rows
    column(chips, far, rows, lax.axis_index("core"), adj_ref, far_t, col_ref)
    far_columns(chips, far_t, far_ref)
    keep_ref[...] = dot(col_ref[...], cot_ref[...]).astype(BF16)
    low = adj_ref.shape[0]
    lend_ref[:low, :] = adj_ref[...]
    lend_ref[low : low + rows, :] = cot_ref[...]
    lend_ref[low + rows :, :] = value_ref[...]
    place_ref[...] = jnp.concatenate([pick_ref[...]] * chips, 0).T


def deal(chips, hosts, total, picked, value, mine_ref, msg_ref, to_refs):
    rows = value.shape[0]
    far = picked.shape[0]
    send = far // hosts
    each = rows + far
    chip, core = lax.axis_index("chip"), lax.axis_index("core")
    mine_ref[...] = total[:rows]
    for k in range(chips):
        low = k * each + rows
        if k > 0:
            to_refs[k - 1][:rows, :] = total[k * each : low].astype(BF16)
            to_refs[k - 1][rows:, :] = value
        x = lax.rem(chip + k, chips)
        for g in range(hosts):
            at = low + g * send
            to = (g * chips + x) * CORES
            msg_ref[to + core] = total[at : at + send].astype(BF16)
            msg_ref[to + 1 - core] = picked[g * send : (g + 1) * send].astype(BF16)


def core_sum_kernel(
    chips, hosts, keep_ref, came_ref, value_ref, picked_ref, mine_ref, msg_ref, *rest
):
    total = keep_ref[...].astype(F32) + came_ref[...].astype(F32)
    picked = picked_ref[...].astype(F32)
    deal(chips, hosts, total, picked, value_ref[...], mine_ref, msg_ref, rest)


def received(recv_ref, hosts, chips, side):
    blocks = [
        recv_ref[(g * chips + x) * CORES + side].astype(F32)
        for x in range(chips)
        for g in range(hosts)
    ]
    return jnp.concatenate(blocks, 0).astype(BF16)


def merge_kernel(chips, hosts, recv_ref, mine_ref, place_ref, *refs):
    came, (nodes_ref, out_ref, sum_ref) = refs[: chips - 1], refs[chips - 1 :]
    rows = mine_ref.shape[0]
    total = mine_ref[...]
    for k, ref in enumerate(came):
        total = total + ref[:rows, :].astype(F32)
        nodes_ref[k * rows : (k + 1) * rows, :] = ref[rows:, :]
    total = total + returned(place_ref, recv_ref, hosts, chips)
    sum_ref[...] = total
    halo = received(recv_ref, hosts, chips, 1 - lax.axis_index("core"))
    out_ref[: halo.shape[0], :] = halo
    out_ref[halo.shape[0] :, :] = total.astype(BF16)


def returned(place_ref, recv_ref, hosts, chips):
    return dot(place_ref[...], received(recv_ref, hosts, chips, lax.axis_index("core")))


def joint(pairs):
    left = jnp.concatenate([a for a, _ in pairs], 1)
    return dot(left, jnp.concatenate([b for _, b in pairs], 0))


def square_of(adj_ref, x, side, rows):
    return adj_ref[pl.ds(pl.multiple_of((x * CORES + side) * rows, rows), rows), :]


def own_chip(adj_refs, blocks):
    chip, core = lax.axis_index("chip"), lax.axis_index("core")
    rows = blocks[0].shape[0]
    parts = [
        joint([(square_of(ref, chip, s, rows), b) for s, b in zip((core, 1 - core), blocks)])
        for ref in adj_refs
    ]
    return jnp.concatenate(parts, 0)


def early_one_kernel(
    chips, adj_ref, lent_ref, value_ref, self_ref, bias_ref, up_ref, weight_ref, neigh_ref, sent_ref,
    agg_ref, direct_ref, grad_ref, col_ref, far_ref, far_t,
):
    value = value_ref[...]
    rows = value.shape[0]
    low = adj_ref.shape[0]
    there = lent_ref[low + rows :, :]
    sent = dot(there, neigh_ref[...]).astype(BF16)
    agg_ref[...] = own_chip((adj_ref, lent_ref), (sent_ref[...], sent))
    both = jnp.concatenate([value, there], 0)
    direct_ref[...] = dot(both, self_ref[...]) + bias_ref[...].reshape(1, -1)
    both = jnp.concatenate([up_ref[...], lent_ref[low : low + rows, :]], 0)
    grad_ref[...] = dot_nt(both, weight_ref[...])
    far = col_ref.shape[0] // chips - rows
    column(chips, far, rows, lax.axis_index("core"), lent_ref, far_t, col_ref)
    far_columns(chips, far_t, far_ref)


def mid_kernel(
    chips, adj_ref, lent_ref, far_ref, far_two_ref, agg_ref, part_ref, sum_ref, neigh_ref, here_ref, *refs
):
    came, (agg_out, grad_ref) = refs[:-2], refs[-2:]
    rows = sum_ref.shape[0]
    halo = here_ref[: here_ref.shape[0] - rows, :]
    for i, (ref, columns) in enumerate(((adj_ref, far_ref), (lent_ref, far_two_ref))):
        pairs = other_chips(chips, ref, came) + [(columns[:, : halo.shape[0]], halo)]
        part = slice(i * rows, (i + 1) * rows)
        agg_out[part, :] = agg_ref[part, :] + joint(pairs)
    grad_ref[:rows, :] = part_ref[:rows, :] + precise_nt(sum_ref[...], neigh_ref[...])
    grad_ref[rows:, :] = part_ref[rows:, :]


def other_chips(chips, adj_ref, came):
    chip, core = lax.axis_index("chip"), lax.axis_index("core")
    pairs = []
    for k, block in enumerate(came):
        rows = block.shape[0] // 2
        x = lax.rem(chip - k - 1 + chips, chips)
        pairs.append((square_of(adj_ref, x, core, rows), block[rows:, :]))
    return pairs


def column_product(chips, hosts, adj_ref, far_ref, value_ref, came, recv_ref):
    rows = value_ref.shape[0]
    chip, core = lax.axis_index("chip"), lax.axis_index("core")
    halo = received(recv_ref, hosts, chips, 1 - core)
    pairs = [(square_of(adj_ref, chip, core, rows), value_ref[...])]
    pairs += other_chips(chips, adj_ref, came) + [(far_ref[:, : halo.shape[0]], halo)]
    return joint(pairs)


def there_kernel(chips, hosts, lent_ref, far_ref, value_ref, recv_ref, *refs):
    came, out_ref = refs[:-1], refs[-1]
    out_ref[...] = column_product(
        chips, hosts, lent_ref, far_ref, value_ref, came, recv_ref
    ).astype(BF16)


def here_kernel(
    chips, hosts, adj_ref, far_ref, sent_ref, recv_ref, value_ref, self_ref, bias_ref, up_ref,
    weight_ref, neigh_ref, mine_ref, place_ref, *refs
):
    came, (out_ref, grad_ref) = refs[:-2], refs[-2:]
    rows = mine_ref.shape[0]
    total = mine_ref[...] + returned(place_ref, recv_ref, hosts, chips)
    for block in came:
        total = total + block[:rows, :].astype(F32)
    grad = dot_nt(total.astype(BF16), neigh_ref[...])
    grad_ref[...] = grad + dot_nt(up_ref[...], weight_ref[...])
    out = column_product(chips, hosts, adj_ref, far_ref, sent_ref, came, recv_ref)
    out_ref[...] = out + dot(value_ref[...], self_ref[...]) + bias_ref[...].reshape(1, -1)


def add_rest(chips, rows, adj_ref, far_ref, agg, nodes_ref, shared_ref):
    chip, core = lax.axis_index("chip"), lax.axis_index("core")
    pairs = []
    for k in range(chips - 1):
        x = lax.rem(chip - k - 1 + chips, chips)
        block = nodes_ref[k * rows : (k + 1) * rows, :]
        pairs.append((square_of(adj_ref, x, 1 - core, rows), block))
    half = far_ref.shape[1] // 2
    pairs.append((far_ref[:, half:], shared_ref[:half, :]))
    return agg + joint(pairs)


def middle_kernel(
    chips,
    hosts,
    adj_ref,
    lent_ref,
    far_ref,
    far_two_ref,
    col_ref,
    col_two_ref,
    agg_ref,
    direct_ref,
    grad_ref,
    pick_ref,
    nodes_ref,
    shared_ref,
    neigh_two_ref,
    hidden_ref,
    sent_ref,
    grad_pre_ref,
    mine_ref,
    msg_ref,
    *rest,
):
    to_refs = rest
    far, rows = pick_ref.shape
    parts = [
        add_rest(
            chips, rows, ref, columns, agg_ref[i * rows : (i + 1) * rows, :], nodes_ref, shared_ref
        )
        for i, (ref, columns) in enumerate(((adj_ref, far_ref), (lent_ref, far_two_ref)))
    ]
    pre = direct_ref[...] + jnp.concatenate(parts, 0)
    sigmoid = jax.nn.sigmoid(pre)
    hidden = (pre[:rows] * sigmoid[:rows]).astype(BF16)
    hidden_ref[...] = hidden
    sent = dot(hidden, neigh_two_ref[...]).astype(BF16)
    sent_ref[...] = sent
    add = dot_nt(shared_ref[chips * far :, :], neigh_two_ref[...])
    grad = jnp.concatenate([grad_ref[:rows, :], grad_ref[rows:, :] + add], 0)
    grad_pre = (grad * sigmoid * (1.0 + pre * (1.0 - sigmoid))).astype(BF16)
    grad_pre_ref[...] = grad_pre[:rows]
    total = joint([(col_ref[...], grad_pre[:rows]), (col_two_ref[...], grad_pre[rows:])])
    picked = dot(pick_ref[...], sent)
    deal(chips, hosts, total, picked, sent, mine_ref, msg_ref, to_refs)


def last_kernel(here_ref, there_ref, output_ref):
    output_ref[...] = (here_ref[...] + there_ref[...].astype(F32)).astype(BF16)


def call(kernel, name, out_shape, in_specs, args, scratch=(), limit=32, flops=0):
    return pl.pallas_call(
        kernel,
        out_shape=out_shape,
        in_specs=in_specs,
        out_specs=jax.tree.map(lambda _: VMEM, out_shape),
        scratch_shapes=scratch,
        compiler_params=pltpu.CompilerParams(vmem_limit_bytes=limit * MIB),
        cost_estimate=pl.CostEstimate(
            flops=flops, bytes_accessed=flops // 1024, transcendentals=0
        ),
        name=name,
    )(*args)


def shift(value, axis, k):
    size = lax.axis_size(axis)
    return lax.ppermute(value, axis, [(i, (i + k) % size) for i in range(size)])


def shape(rows, width, kind=BF16):
    return jax.ShapeDtypeStruct((rows, width), kind)


def body(
    features,
    send_list,
    tile_dst,
    tile_src,
    tile_rows,
    tile_val,
    self_one,
    neigh_one,
    bias_one,
    self_two,
    neigh_two,
    bias_two,
    cotangent,
):
    chips = lax.axis_size("chip")
    hosts = lax.axis_size("hst")
    rows, width = features.shape
    tiles, blk = tile_val.shape[:2]
    send = send_list.shape[3]
    far = hosts * send
    all_rows = chips * CORES * (rows + far)
    count = chips * (rows + far)
    rows_shape = shape(rows, width)
    sum_shape = shape(rows, width, F32)
    both_shape = shape(CORES * rows, width, F32)
    square = 2 * rows * width * width
    far_shape = shape(rows, chips * CORES * far)
    dealt = (
        sum_shape,
        jax.ShapeDtypeStruct((chips * hosts * CORES, send, width), BF16),
    ) + (shape(2 * rows, width),) * (chips - 1)

    def across(msg, to):
        terms = [shift(block, "chip", k + 1) for k, block in enumerate(to)]
        recv = lax.all_to_all(msg, ("hst", "chip", "core"), split_axis=0, concat_axis=0, tiled=True)
        return terms, recv

    far_t = pltpu.VMEM((chips * CORES * far, rows), BF16)
    sums = jax.ShapeDtypeStruct(((rows // blk) * (all_rows // blk), blk // PARTS, blk), F32)
    give, pick, *sums = call(
        functools.partial(prep_kernel, chips),
        "prep",
        (shape(count, width), shape(far, rows)) + (sums,) * PARTS,
        [HBM] * 6,
        [
            pltpu.with_memory_space_constraint(value, pltpu.HBM)
            for value in (
                tile_dst,
                tile_src,
                tile_rows,
                send_list,
                tile_val,
                cotangent,
            )
        ],
        [
            pltpu.SMEM(tile_dst.shape, jnp.int32),
            pltpu.SMEM(tile_src.shape, jnp.int32),
            pltpu.SMEM(tile_rows.shape, jnp.int32),
            pltpu.SMEM(send_list.shape, jnp.int32),
            pltpu.VMEM(tile_val.shape, BF16),
            pltpu.VMEM(cotangent.shape, BF16),
            pltpu.VMEM((rows, rows), BF16),
            far_t,
            pltpu.VMEM((count, rows), BF16),
            pltpu.SemaphoreType.DMA((6 + CHUNKS,)),
        ],
    )
    came = shift(give, "core", 1)
    sent, picked, adj, col, keep, lend, place, columns = call(
        functools.partial(rest_kernel, chips),
        "rest",
        (
            rows_shape,
            shape(far, width),
            shape(all_rows, rows),
            shape(count, rows),
            shape(count, width),
            shape(all_rows + 2 * rows, width),
            shape(rows, chips * far),
            far_shape,
        ),
        [VMEM] * (4 + PARTS),
        (cotangent, features, pick, neigh_one, *sums),
        [far_t],
        flops=3 * square,
    )
    lent = shift(lend, "core", 1)
    mine, msg, *to = call(
        functools.partial(core_sum_kernel, chips, hosts),
        "core_sum",
        dealt,
        [VMEM] * 4,
        (keep, came, sent, picked),
        flops=60 * square,
    )
    terms, recv = across(msg, to)
    nodes, here, summed = call(
        functools.partial(merge_kernel, chips, hosts),
        "merge",
        (shape((chips - 1) * rows, width), shape(chips * far + rows, width), sum_shape),
        [VMEM] * (2 + chips),
        (recv, mine, place, *terms),
    )
    nodes = shift(nodes, "core", 1)
    shared = shift(here, "core", 1)
    agg, direct, grad, col_two, columns_two = call(
        functools.partial(early_one_kernel, chips),
        "early_one",
        (both_shape,) * 3 + (shape(count, rows), far_shape),
        [VMEM] * 9,
        (
            adj,
            lent,
            features,
            self_one,
            bias_one,
            cotangent,
            self_two,
            neigh_one,
            sent,
        ),
        [far_t],
        flops=8 * square,
    )
    agg, grad = call(
        functools.partial(mid_kernel, chips),
        "mid",
        (both_shape,) * 2,
        [VMEM] * (8 + chips),
        (adj, lent, columns, columns_two, agg, grad, summed, neigh_two, here, *terms),
        flops=3 * square,
    )
    hidden, sent, grad_pre, mine, msg, *to = call(
        functools.partial(middle_kernel, chips, hosts),
        "middle",
        (rows_shape,) * 3 + dealt,
        [VMEM] * 13,
        (
            adj,
            lent,
            columns,
            columns_two,
            col,
            col_two,
            agg,
            direct,
            grad,
            pick,
            nodes,
            shared,
            neigh_two,
        ),
        flops=12 * square,
    )
    terms, recv = across(msg, to)
    there = call(
        functools.partial(there_kernel, chips, hosts),
        "there",
        rows_shape,
        [VMEM] * (3 + chips),
        (lent, columns_two, sent, recv, *terms),
    )
    shared = shift(there, "core", 1)
    here, grad = call(
        functools.partial(here_kernel, chips, hosts),
        "here",
        (sum_shape,) * 2,
        [VMEM] * (11 + chips),
        (
            adj,
            columns,
            sent,
            recv,
            hidden,
            self_two,
            bias_two,
            grad_pre,
            self_one,
            neigh_one,
            mine,
            place,
            *terms,
        ),
        flops=7 * square,
    )
    output = call(last_kernel, "last", rows_shape, [VMEM] * 2, (here, shared))
    return output, grad


def solution(mesh):
    hosts, devs = mesh.devices.shape
    mesh = Mesh(mesh.devices.reshape(hosts, devs // CORES, CORES), ("hst", "chip", "core"))
    dev = ("chip", "core")
    every = ("hst", "chip", "core")
    return jax.shard_map(
        body,
        mesh=mesh,
        in_specs=(
            P(every, None),
            P("hst", dev, None, None),
            P(every),
            P(every),
            P(every),
            P(every, None, None),
            P(),
            P(),
            P(),
            P(),
            P(),
            P(),
            P(every, None),
        ),
        out_specs=(P(every, None), P(every, None)),
        check_vma=False,
    )
```

```python
import functools

import jax
import jax.numpy as jnp
from jax import lax
from jax.experimental import pallas as pl
from jax.experimental.pallas import tpu as pltpu
from jax.sharding import Mesh, PartitionSpec as P

F32 = jnp.float32
BF16 = jnp.bfloat16
MIB = 1024 * 1024
CHUNKS = 8
PARTS = 8
CORES = 2

VMEM = pl.BlockSpec(memory_space=pltpu.VMEM)
HBM = pl.BlockSpec(memory_space=pltpu.HBM)


def dot(a, b):
    return jnp.dot(a, b, preferred_element_type=F32)


def dot_nt(a, b):
    return lax.dot_general(a, b, (((1,), (1,)), ((), ())), preferred_element_type=F32)


def precise_nt(a, b):
    high = a.astype(BF16)
    low = (a - high.astype(F32)).astype(BF16)
    return dot_nt(high, b) + dot_nt(low, b)


def pick_matrix(send_ref, rows):
    hosts, send = send_ref.shape[2], send_ref.shape[3]
    place = lax.broadcasted_iota(jnp.int32, (send, rows), 0)
    column = lax.broadcasted_iota(jnp.int32, (send, rows), 1)
    parts = []
    for g in range(hosts):
        index = jnp.zeros((send, rows), jnp.int32)
        for s in range(send):
            index = jnp.where(place == s, send_ref[0, 0, g, s], index)
        parts.append(jnp.where(index == column, 1.0, 0.0).astype(F32))
    return jnp.concatenate(parts, 0).astype(BF16)


def column(chips, far, rows, side, adj_ref, far_t, out_ref):
    chip = lax.axis_index("chip")
    each = rows + far
    own_rows = chips * CORES * rows
    for j in range(far_t.shape[0] // rows):
        low = own_rows + j * rows
        far_t[j * rows : (j + 1) * rows, :] = adj_ref[low : low + rows, :].T
    for k in range(chips):
        d = lax.rem(chip + k, chips) * CORES + side
        at = k * each
        out_ref[at : at + rows, :] = adj_ref[pl.ds(pl.multiple_of(d * rows, rows), rows), :].T
        out_ref[at + rows : at + each, :] = far_t[pl.ds(pl.multiple_of(d * far, far), far), :]


def far_columns(chips, far_t, out_ref):
    far = far_t.shape[0] // (chips * CORES)
    core = lax.axis_index("core")
    parts = [
        far_t[pl.ds(pl.multiple_of((x * CORES + side) * far, far), far), :]
        for side in (1 - core, core)
        for x in range(chips)
    ]
    out_ref[...] = jnp.concatenate(parts, 0).T


def prep_kernel(
    chips,
    dst_hbm,
    src_hbm,
    rows_hbm,
    send_hbm,
    tile_hbm,
    cot_hbm,
    give_ref,
    pick_ref,
    cot_ref,
    *rest,
):
    accs, rest = rest[:PARTS], rest[PARTS:]
    (
        dst_ref,
        src_ref,
        rows_ref,
        send_ref,
        tile_buf,
        square,
        far_t,
        col,
        sems,
    ) = rest
    tiles, blk = tile_buf.shape[0], tile_buf.shape[1]
    each = tiles // CHUNKS
    cuts = [c * each for c in range(CHUNKS)] + [tiles - each // 2, tiles]
    chunks = [
        (tile_hbm.at[pl.ds(low, high - low)], tile_buf.at[pl.ds(low, high - low)])
        for low, high in zip(cuts, cuts[1:])
    ]
    pairs = [(send_hbm, send_ref), (dst_hbm, dst_ref), (src_hbm, src_ref), (rows_hbm, rows_ref)]
    pairs += chunks + [(cot_hbm, cot_ref)]
    copies = [pltpu.make_async_copy(a, b, sems.at[i]) for i, (a, b) in enumerate(pairs)]
    for copy in copies:
        copy.start()
    rows = cot_ref.shape[0]
    bpd = rows // blk
    sources = accs[0].shape[0] // bpd
    part = accs[0].shape[1]
    far = send_ref.shape[2] * send_ref.shape[3]
    for acc in accs:
        acc[...] = jnp.zeros_like(acc)
    place = lax.broadcasted_iota(jnp.int32, (part, blk), 0)

    def add(t, carry):
        slot = dst_ref[t] * sources + src_ref[t]
        for i, acc in enumerate(accs):
            value = tile_buf[t, i * part : (i + 1) * part, :].astype(F32)
            acc[slot] += jnp.where(place < rows_ref[t] - i * part, value, 0.0)
        return carry

    copies[0].wait()
    pick_ref[...] = pick_matrix(send_ref, rows)
    for copy in copies[1:4]:
        copy.wait()
    for copy, low, high in zip(copies[4:], cuts, cuts[1:]):
        copy.wait()
        lax.fori_loop(low, high, add, 0, unroll=True)
    copies[-1].wait()
    chip, side = lax.axis_index("chip"), 1 - lax.axis_index("core")
    base = chips * CORES
    for j in range(far_t.shape[0] // rows):
        put_square(accs, bpd, base + j, square, 0)
        far_t[j * rows : (j + 1) * rows, :] = square[...].T
    for k in range(chips):
        d = lax.rem(chip + k, chips) * CORES + side
        at = k * (rows + far)
        put_square(accs, bpd, d, square, 0)
        col[at : at + rows, :] = square[...].T
        low = pl.multiple_of(d * far, far)
        col[at + rows : at + rows + far, :] = far_t[pl.ds(low, far), :]
    give_ref[...] = dot(col[...], cot_ref[...]).astype(BF16)


def put_square(accs, bpd, d, out_ref, base):
    sources = accs[0].shape[0] // bpd
    part, blk = accs[0].shape[1:]
    for b in range(bpd):
        for j in range(bpd):
            for i, acc in enumerate(accs):
                low = base + b * blk + i * part
                value = acc[b * sources + d * bpd + j].astype(BF16)
                out_ref[low : low + part, j * blk : (j + 1) * blk] = value


def rest_kernel(chips, cot_ref, value_ref, pick_ref, neigh_ref, *refs):
    accs = refs[:PARTS]
    sent_ref, picked_ref, adj_ref, col_ref, keep_ref, lend_ref, place_ref, far_ref, far_t = refs[PARTS:]
    sent = dot(value_ref[...], neigh_ref[...]).astype(BF16)
    sent_ref[...] = sent
    picked_ref[...] = dot(pick_ref[...], sent).astype(BF16)
    rows = cot_ref.shape[0]
    bpd = rows // accs[0].shape[2]
    for d in range(adj_ref.shape[0] // rows):
        put_square(accs, bpd, d, adj_ref, d * rows)
    far = col_ref.shape[0] // chips - rows
    column(chips, far, rows, lax.axis_index("core"), adj_ref, far_t, col_ref)
    far_columns(chips, far_t, far_ref)
    keep_ref[...] = dot(col_ref[...], cot_ref[...]).astype(BF16)
    low = adj_ref.shape[0]
    lend_ref[:low, :] = adj_ref[...]
    lend_ref[low : low + rows, :] = cot_ref[...]
    lend_ref[low + rows :, :] = value_ref[...]
    place_ref[...] = jnp.concatenate([pick_ref[...]] * chips, 0).T


def deal(chips, hosts, total, picked, value, mine_ref, msg_ref, to_refs):
    rows = value.shape[0]
    far = picked.shape[0]
    send = far // hosts
    each = rows + far
    chip, core = lax.axis_index("chip"), lax.axis_index("core")
    mine_ref[...] = total[:rows]
    for k in range(chips):
        low = k * each + rows
        if k > 0:
            to_refs[k - 1][:rows, :] = total[k * each : low].astype(BF16)
            to_refs[k - 1][rows:, :] = value
        x = lax.rem(chip + k, chips)
        for g in range(hosts):
            at = low + g * send
            to = (g * chips + x) * CORES
            msg_ref[to + core] = total[at : at + send].astype(BF16)
            msg_ref[to + 1 - core] = picked[g * send : (g + 1) * send].astype(BF16)


def core_sum_kernel(
    chips, hosts, keep_ref, came_ref, value_ref, picked_ref, mine_ref, msg_ref, *rest
):
    total = keep_ref[...].astype(F32) + came_ref[...].astype(F32)
    picked = picked_ref[...].astype(F32)
    deal(chips, hosts, total, picked, value_ref[...], mine_ref, msg_ref, rest)


def received(recv_ref, hosts, chips, side):
    blocks = [
        recv_ref[(g * chips + x) * CORES + side].astype(F32)
        for x in range(chips)
        for g in range(hosts)
    ]
    return jnp.concatenate(blocks, 0).astype(BF16)


def merge_kernel(chips, hosts, recv_ref, mine_ref, place_ref, *refs):
    came, (out_ref, sum_ref) = refs[: chips - 1], refs[chips - 1 :]
    rows = mine_ref.shape[0]
    total = mine_ref[...]
    for k, ref in enumerate(came):
        total = total + ref[:rows, :].astype(F32)
        out_ref[k * rows : (k + 1) * rows, :] = ref[rows:, :]
    total = total + returned(place_ref, recv_ref, hosts, chips)
    sum_ref[...] = total
    low = len(came) * rows
    halo = received(recv_ref, hosts, chips, 1 - lax.axis_index("core"))
    high = low + halo.shape[0]
    out_ref[low:high, :] = halo
    out_ref[high:, :] = total.astype(BF16)


def returned(place_ref, recv_ref, hosts, chips):
    return dot(place_ref[...], received(recv_ref, hosts, chips, lax.axis_index("core")))


def joint(pairs):
    left = jnp.concatenate([a for a, _ in pairs], 1)
    return dot(left, jnp.concatenate([b for _, b in pairs], 0))


def square_of(adj_ref, x, side, rows):
    return adj_ref[pl.ds(pl.multiple_of((x * CORES + side) * rows, rows), rows), :]


def own_chip(adj_refs, blocks):
    chip, core = lax.axis_index("chip"), lax.axis_index("core")
    rows = blocks[0].shape[0]
    parts = [
        joint([(square_of(ref, chip, s, rows), b) for s, b in zip((core, 1 - core), blocks)])
        for ref in adj_refs
    ]
    return jnp.concatenate(parts, 0)


def early_one_kernel(
    chips, adj_ref, lent_ref, value_ref, self_ref, bias_ref, up_ref, weight_ref, neigh_ref, sent_ref,
    agg_ref, direct_ref, grad_ref, col_ref, far_ref, far_t,
):
    value = value_ref[...]
    rows = value.shape[0]
    low = adj_ref.shape[0]
    there = lent_ref[low + rows :, :]
    sent = dot(there, neigh_ref[...]).astype(BF16)
    agg_ref[...] = own_chip((adj_ref, lent_ref), (sent_ref[...], sent))
    both = jnp.concatenate([value, there], 0)
    direct_ref[...] = dot(both, self_ref[...]) + bias_ref[...].reshape(1, -1)
    both = jnp.concatenate([up_ref[...], lent_ref[low : low + rows, :]], 0)
    grad_ref[...] = dot_nt(both, weight_ref[...])
    far = col_ref.shape[0] // chips - rows
    column(chips, far, rows, lax.axis_index("core"), lent_ref, far_t, col_ref)
    far_columns(chips, far_t, far_ref)


def mid_kernel(
    chips, adj_ref, lent_ref, far_ref, far_two_ref, agg_ref, part_ref, sum_ref, neigh_ref, here_ref, *refs
):
    came, (agg_out, grad_ref) = refs[:-2], refs[-2:]
    rows = sum_ref.shape[0]
    halo = here_ref[(chips - 1) * rows : here_ref.shape[0] - rows, :]
    for i, (ref, columns) in enumerate(((adj_ref, far_ref), (lent_ref, far_two_ref))):
        pairs = other_chips(chips, ref, came) + [(columns[:, : halo.shape[0]], halo)]
        part = slice(i * rows, (i + 1) * rows)
        agg_out[part, :] = agg_ref[part, :] + joint(pairs)
    grad_ref[:rows, :] = part_ref[:rows, :] + precise_nt(sum_ref[...], neigh_ref[...])
    grad_ref[rows:, :] = part_ref[rows:, :]


def other_chips(chips, adj_ref, came):
    chip, core = lax.axis_index("chip"), lax.axis_index("core")
    pairs = []
    for k, block in enumerate(came):
        rows = block.shape[0] // 2
        x = lax.rem(chip - k - 1 + chips, chips)
        pairs.append((square_of(adj_ref, x, core, rows), block[rows:, :]))
    return pairs


def column_product(chips, hosts, adj_ref, far_ref, value_ref, came, recv_ref):
    rows = value_ref.shape[0]
    chip, core = lax.axis_index("chip"), lax.axis_index("core")
    halo = received(recv_ref, hosts, chips, 1 - core)
    pairs = [(square_of(adj_ref, chip, core, rows), value_ref[...])]
    pairs += other_chips(chips, adj_ref, came) + [(far_ref[:, : halo.shape[0]], halo)]
    return joint(pairs)


def there_kernel(chips, hosts, lent_ref, far_ref, value_ref, recv_ref, *refs):
    came, out_ref = refs[:-1], refs[-1]
    out_ref[...] = column_product(
        chips, hosts, lent_ref, far_ref, value_ref, came, recv_ref
    ).astype(BF16)


def here_kernel(
    chips, hosts, adj_ref, far_ref, sent_ref, recv_ref, value_ref, self_ref, bias_ref, up_ref,
    weight_ref, neigh_ref, mine_ref, place_ref, *refs
):
    came, (out_ref, grad_ref) = refs[:-2], refs[-2:]
    rows = mine_ref.shape[0]
    total = mine_ref[...] + returned(place_ref, recv_ref, hosts, chips)
    for block in came:
        total = total + block[:rows, :].astype(F32)
    grad = dot_nt(total.astype(BF16), neigh_ref[...])
    grad_ref[...] = grad + dot_nt(up_ref[...], weight_ref[...])
    out = column_product(chips, hosts, adj_ref, far_ref, sent_ref, came, recv_ref)
    out_ref[...] = out + dot(value_ref[...], self_ref[...]) + bias_ref[...].reshape(1, -1)


def add_rest(chips, rows, adj_ref, far_ref, agg, shared_ref):
    chip, core = lax.axis_index("chip"), lax.axis_index("core")
    pairs = []
    for k in range(chips - 1):
        x = lax.rem(chip - k - 1 + chips, chips)
        block = shared_ref[k * rows : (k + 1) * rows, :]
        pairs.append((square_of(adj_ref, x, 1 - core, rows), block))
    half = far_ref.shape[1] // 2
    low = (chips - 1) * rows
    pairs.append((far_ref[:, half:], shared_ref[low : low + half, :]))
    return agg + joint(pairs)


def middle_kernel(
    chips,
    hosts,
    adj_ref,
    lent_ref,
    far_ref,
    far_two_ref,
    col_ref,
    col_two_ref,
    agg_ref,
    direct_ref,
    grad_ref,
    pick_ref,
    shared_ref,
    neigh_two_ref,
    hidden_ref,
    sent_ref,
    grad_pre_ref,
    mine_ref,
    msg_ref,
    *rest,
):
    to_refs = rest
    far, rows = pick_ref.shape
    parts = [
        add_rest(chips, rows, ref, columns, agg_ref[i * rows : (i + 1) * rows, :], shared_ref)
        for i, (ref, columns) in enumerate(((adj_ref, far_ref), (lent_ref, far_two_ref)))
    ]
    pre = direct_ref[...] + jnp.concatenate(parts, 0)
    sigmoid = jax.nn.sigmoid(pre)
    hidden = (pre[:rows] * sigmoid[:rows]).astype(BF16)
    hidden_ref[...] = hidden
    sent = dot(hidden, neigh_two_ref[...]).astype(BF16)
    sent_ref[...] = sent
    low = (chips - 1) * rows + chips * far
    add = dot_nt(shared_ref[low:, :], neigh_two_ref[...])
    grad = jnp.concatenate([grad_ref[:rows, :], grad_ref[rows:, :] + add], 0)
    grad_pre = (grad * sigmoid * (1.0 + pre * (1.0 - sigmoid))).astype(BF16)
    grad_pre_ref[...] = grad_pre[:rows]
    total = joint([(col_ref[...], grad_pre[:rows]), (col_two_ref[...], grad_pre[rows:])])
    picked = dot(pick_ref[...], sent)
    deal(chips, hosts, total, picked, sent, mine_ref, msg_ref, to_refs)


def last_kernel(here_ref, there_ref, output_ref):
    output_ref[...] = (here_ref[...] + there_ref[...].astype(F32)).astype(BF16)


def call(kernel, name, out_shape, in_specs, args, scratch=(), limit=32, flops=0):
    return pl.pallas_call(
        kernel,
        out_shape=out_shape,
        in_specs=in_specs,
        out_specs=jax.tree.map(lambda _: VMEM, out_shape),
        scratch_shapes=scratch,
        compiler_params=pltpu.CompilerParams(vmem_limit_bytes=limit * MIB),
        cost_estimate=pl.CostEstimate(
            flops=flops, bytes_accessed=flops // 1024, transcendentals=0
        ),
        name=name,
    )(*args)


def shift(value, axis, k):
    size = lax.axis_size(axis)
    return lax.ppermute(value, axis, [(i, (i + k) % size) for i in range(size)])


def shape(rows, width, kind=BF16):
    return jax.ShapeDtypeStruct((rows, width), kind)


def body(
    features,
    send_list,
    tile_dst,
    tile_src,
    tile_rows,
    tile_val,
    self_one,
    neigh_one,
    bias_one,
    self_two,
    neigh_two,
    bias_two,
    cotangent,
):
    chips = lax.axis_size("chip")
    hosts = lax.axis_size("hst")
    rows, width = features.shape
    tiles, blk = tile_val.shape[:2]
    send = send_list.shape[3]
    far = hosts * send
    all_rows = chips * CORES * (rows + far)
    count = chips * (rows + far)
    rows_shape = shape(rows, width)
    sum_shape = shape(rows, width, F32)
    both_shape = shape(CORES * rows, width, F32)
    square = 2 * rows * width * width
    far_shape = shape(rows, chips * CORES * far)
    halo_rows = (chips - 1) * rows + chips * far
    dealt = (
        sum_shape,
        jax.ShapeDtypeStruct((chips * hosts * CORES, send, width), BF16),
    ) + (shape(2 * rows, width),) * (chips - 1)

    def across(msg, to):
        terms = [shift(block, "chip", k + 1) for k, block in enumerate(to)]
        recv = lax.all_to_all(msg, ("hst", "chip", "core"), split_axis=0, concat_axis=0, tiled=True)
        return terms, recv

    far_t = pltpu.VMEM((chips * CORES * far, rows), BF16)
    sums = jax.ShapeDtypeStruct(((rows // blk) * (all_rows // blk), blk // PARTS, blk), F32)
    give, pick, cot, *sums = call(
        functools.partial(prep_kernel, chips),
        "prep",
        (shape(count, width), shape(far, rows), rows_shape) + (sums,) * PARTS,
        [HBM] * 6,
        [
            pltpu.with_memory_space_constraint(value, pltpu.HBM)
            for value in (
                tile_dst,
                tile_src,
                tile_rows,
                send_list,
                tile_val,
                cotangent,
            )
        ],
        [
            pltpu.SMEM(tile_dst.shape, jnp.int32),
            pltpu.SMEM(tile_src.shape, jnp.int32),
            pltpu.SMEM(tile_rows.shape, jnp.int32),
            pltpu.SMEM(send_list.shape, jnp.int32),
            pltpu.VMEM(tile_val.shape, BF16),
            pltpu.VMEM((rows, rows), BF16),
            far_t,
            pltpu.VMEM((count, rows), BF16),
            pltpu.SemaphoreType.DMA((6 + CHUNKS,)),
        ],
    )
    came = shift(give, "core", 1)
    sent, picked, adj, col, keep, lend, place, columns = call(
        functools.partial(rest_kernel, chips),
        "rest",
        (
            rows_shape,
            shape(far, width),
            shape(all_rows, rows),
            shape(count, rows),
            shape(count, width),
            shape(all_rows + 2 * rows, width),
            shape(rows, chips * far),
            far_shape,
        ),
        [VMEM] * (4 + PARTS),
        (cot, features, pick, neigh_one, *sums),
        [far_t],
        flops=3 * square,
    )
    lent = shift(lend, "core", 1)
    mine, msg, *to = call(
        functools.partial(core_sum_kernel, chips, hosts),
        "core_sum",
        dealt,
        [VMEM] * 4,
        (keep, came, sent, picked),
        flops=60 * square,
    )
    terms, recv = across(msg, to)
    here, summed = call(
        functools.partial(merge_kernel, chips, hosts),
        "merge",
        (shape(halo_rows + rows, width), sum_shape),
        [VMEM] * (2 + chips),
        (recv, mine, place, *terms),
    )
    shared = shift(here, "core", 1)
    agg, direct, grad, col_two, columns_two = call(
        functools.partial(early_one_kernel, chips),
        "early_one",
        (both_shape,) * 3 + (shape(count, rows), far_shape),
        [VMEM] * 9,
        (
            adj,
            lent,
            features,
            self_one,
            bias_one,
            cot,
            self_two,
            neigh_one,
            sent,
        ),
        [far_t],
        flops=8 * square,
    )
    agg, grad = call(
        functools.partial(mid_kernel, chips),
        "mid",
        (both_shape,) * 2,
        [VMEM] * (8 + chips),
        (adj, lent, columns, columns_two, agg, grad, summed, neigh_two, here, *terms),
        flops=3 * square,
    )
    hidden, sent, grad_pre, mine, msg, *to = call(
        functools.partial(middle_kernel, chips, hosts),
        "middle",
        (rows_shape,) * 3 + dealt,
        [VMEM] * 12,
        (
            adj,
            lent,
            columns,
            columns_two,
            col,
            col_two,
            agg,
            direct,
            grad,
            pick,
            shared,
            neigh_two,
        ),
        flops=12 * square,
    )
    terms, recv = across(msg, to)
    there = call(
        functools.partial(there_kernel, chips, hosts),
        "there",
        rows_shape,
        [VMEM] * (3 + chips),
        (lent, columns_two, sent, recv, *terms),
    )
    shared = shift(there, "core", 1)
    here, grad = call(
        functools.partial(here_kernel, chips, hosts),
        "here",
        (sum_shape,) * 2,
        [VMEM] * (11 + chips),
        (
            adj,
            columns,
            sent,
            recv,
            hidden,
            self_two,
            bias_two,
            grad_pre,
            self_one,
            neigh_one,
            mine,
            place,
            *terms,
        ),
        flops=7 * square,
    )
    output = call(last_kernel, "last", rows_shape, [VMEM] * 2, (here, shared))
    return output, grad


def solution(mesh):
    hosts, devs = mesh.devices.shape
    mesh = Mesh(mesh.devices.reshape(hosts, devs // CORES, CORES), ("hst", "chip", "core"))
    dev = ("chip", "core")
    every = ("hst", "chip", "core")
    return jax.shard_map(
        body,
        mesh=mesh,
        in_specs=(
            P(every, None),
            P("hst", dev, None, None),
            P(every),
            P(every),
            P(every),
            P(every, None, None),
            P(),
            P(),
            P(),
            P(),
            P(),
            P(),
            P(every, None),
        ),
        out_specs=(P(every, None), P(every, None)),
        check_vma=False,
    )
```

```python
import functools

import jax
import jax.numpy as jnp
from jax import lax
from jax.experimental import pallas as pl
from jax.experimental.pallas import tpu as pltpu
from jax.sharding import Mesh, PartitionSpec as P

F32 = jnp.float32
BF16 = jnp.bfloat16
MIB = 1024 * 1024
CHUNKS = 8
PARTS = 4
CORES = 2

VMEM = pl.BlockSpec(memory_space=pltpu.VMEM)
HBM = pl.BlockSpec(memory_space=pltpu.HBM)


def dot(a, b):
    return jnp.dot(a, b, preferred_element_type=F32)


def dot_nt(a, b):
    return lax.dot_general(a, b, (((1,), (1,)), ((), ())), preferred_element_type=F32)


def precise_nt(a, b):
    high = a.astype(BF16)
    low = (a - high.astype(F32)).astype(BF16)
    return dot_nt(high, b) + dot_nt(low, b)


def pick_matrix(send_ref, rows):
    hosts, send = send_ref.shape[2], send_ref.shape[3]
    place = lax.broadcasted_iota(jnp.int32, (send, rows), 0)
    column = lax.broadcasted_iota(jnp.int32, (send, rows), 1)
    parts = []
    for g in range(hosts):
        index = jnp.zeros((send, rows), jnp.int32)
        for s in range(send):
            index = jnp.where(place == s, send_ref[0, 0, g, s], index)
        parts.append(jnp.where(index == column, 1.0, 0.0).astype(F32))
    return jnp.concatenate(parts, 0).astype(BF16)


def column(chips, far, rows, side, adj_ref, far_t, out_ref):
    chip = lax.axis_index("chip")
    each = rows + far
    own_rows = chips * CORES * rows
    for j in range(far_t.shape[0] // rows):
        low = own_rows + j * rows
        far_t[j * rows : (j + 1) * rows, :] = adj_ref[low : low + rows, :].T
    for k in range(chips):
        d = lax.rem(chip + k, chips) * CORES + side
        at = k * each
        out_ref[at : at + rows, :] = adj_ref[pl.ds(pl.multiple_of(d * rows, rows), rows), :].T
        out_ref[at + rows : at + each, :] = far_t[pl.ds(pl.multiple_of(d * far, far), far), :]


def far_columns(chips, far_t, out_ref):
    far = far_t.shape[0] // (chips * CORES)
    core = lax.axis_index("core")
    parts = [
        far_t[pl.ds(pl.multiple_of((x * CORES + side) * far, far), far), :]
        for side in (1 - core, core)
        for x in range(chips)
    ]
    out_ref[...] = jnp.concatenate(parts, 0).T


def prep_kernel(
    chips,
    dst_hbm,
    src_hbm,
    rows_hbm,
    send_hbm,
    tile_hbm,
    cot_hbm,
    give_ref,
    pick_ref,
    cot_ref,
    *rest,
):
    accs, rest = rest[:PARTS], rest[PARTS:]
    (
        dst_ref,
        src_ref,
        rows_ref,
        send_ref,
        tile_buf,
        square,
        far_t,
        col,
        sems,
    ) = rest
    tiles, blk = tile_buf.shape[0], tile_buf.shape[1]
    each = tiles // CHUNKS
    cuts = [c * each for c in range(CHUNKS)] + [tiles - each // 2, tiles]
    chunks = [
        (tile_hbm.at[pl.ds(low, high - low)], tile_buf.at[pl.ds(low, high - low)])
        for low, high in zip(cuts, cuts[1:])
    ]
    pairs = [(send_hbm, send_ref), (dst_hbm, dst_ref), (src_hbm, src_ref), (rows_hbm, rows_ref)]
    pairs += chunks + [(cot_hbm, cot_ref)]
    copies = [pltpu.make_async_copy(a, b, sems.at[i]) for i, (a, b) in enumerate(pairs)]
    for copy in copies:
        copy.start()
    rows = cot_ref.shape[0]
    bpd = rows // blk
    sources = accs[0].shape[0] // bpd
    part = accs[0].shape[1]
    far = send_ref.shape[2] * send_ref.shape[3]
    for acc in accs:
        acc[...] = jnp.zeros_like(acc)
    place = lax.broadcasted_iota(jnp.int32, (part, blk), 0)

    def add(t, carry):
        slot = dst_ref[t] * sources + src_ref[t]
        for i, acc in enumerate(accs):
            value = tile_buf[t, i * part : (i + 1) * part, :].astype(F32)
            acc[slot] += jnp.where(place < rows_ref[t] - i * part, value, 0.0)
        return carry

    copies[0].wait()
    pick_ref[...] = pick_matrix(send_ref, rows)
    for copy in copies[1:4]:
        copy.wait()
    for copy, low, high in zip(copies[4:], cuts, cuts[1:]):
        copy.wait()
        lax.fori_loop(low, high, add, 0, unroll=True)
    copies[-1].wait()
    chip, side = lax.axis_index("chip"), 1 - lax.axis_index("core")
    base = chips * CORES
    for j in range(far_t.shape[0] // rows):
        put_square(accs, bpd, base + j, square, 0)
        far_t[j * rows : (j + 1) * rows, :] = square[...].T
    for k in range(chips):
        d = lax.rem(chip + k, chips) * CORES + side
        at = k * (rows + far)
        put_square(accs, bpd, d, square, 0)
        col[at : at + rows, :] = square[...].T
        low = pl.multiple_of(d * far, far)
        col[at + rows : at + rows + far, :] = far_t[pl.ds(low, far), :]
    give_ref[...] = dot(col[...], cot_ref[...]).astype(BF16)


def put_square(accs, bpd, d, out_ref, base):
    sources = accs[0].shape[0] // bpd
    part, blk = accs[0].shape[1:]
    for b in range(bpd):
        for j in range(bpd):
            for i, acc in enumerate(accs):
                low = base + b * blk + i * part
                value = acc[b * sources + d * bpd + j].astype(BF16)
                out_ref[low : low + part, j * blk : (j + 1) * blk] = value


def rest_kernel(chips, cot_ref, value_ref, pick_ref, neigh_ref, *refs):
    accs = refs[:PARTS]
    sent_ref, picked_ref, adj_ref, col_ref, keep_ref, lend_ref, place_ref, far_ref, far_t = refs[PARTS:]
    sent = dot(value_ref[...], neigh_ref[...]).astype(BF16)
    sent_ref[...] = sent
    picked_ref[...] = dot(pick_ref[...], sent).astype(BF16)
    rows = cot_ref.shape[0]
    bpd = rows // accs[0].shape[2]
    for d in range(adj_ref.shape[0] // rows):
        put_square(accs, bpd, d, adj_ref, d * rows)
    far = col_ref.shape[0] // chips - rows
    column(chips, far, rows, lax.axis_index("core"), adj_ref, far_t, col_ref)
    far_columns(chips, far_t, far_ref)
    keep_ref[...] = dot(col_ref[...], cot_ref[...]).astype(BF16)
    low = adj_ref.shape[0]
    lend_ref[:low, :] = adj_ref[...]
    lend_ref[low : low + rows, :] = cot_ref[...]
    lend_ref[low + rows :, :] = value_ref[...]
    place_ref[...] = jnp.concatenate([pick_ref[...]] * chips, 0).T


def deal(chips, hosts, total, picked, value, mine_ref, msg_ref, to_refs):
    rows = value.shape[0]
    far = picked.shape[0]
    send = far // hosts
    each = rows + far
    chip, core = lax.axis_index("chip"), lax.axis_index("core")
    mine_ref[...] = total[:rows]
    for k in range(chips):
        low = k * each + rows
        if k > 0:
            to_refs[k - 1][:rows, :] = total[k * each : low].astype(BF16)
            to_refs[k - 1][rows:, :] = value
        x = lax.rem(chip + k, chips)
        for g in range(hosts):
            at = low + g * send
            to = (g * chips + x) * CORES
            msg_ref[to + core] = total[at : at + send].astype(BF16)
            msg_ref[to + 1 - core] = picked[g * send : (g + 1) * send].astype(BF16)


def core_sum_kernel(
    chips, hosts, keep_ref, came_ref, value_ref, picked_ref, mine_ref, msg_ref, *rest
):
    total = keep_ref[...].astype(F32) + came_ref[...].astype(F32)
    picked = picked_ref[...].astype(F32)
    deal(chips, hosts, total, picked, value_ref[...], mine_ref, msg_ref, rest)


def received(recv_ref, hosts, chips, side):
    blocks = [
        recv_ref[(g * chips + x) * CORES + side].astype(F32)
        for x in range(chips)
        for g in range(hosts)
    ]
    return jnp.concatenate(blocks, 0).astype(BF16)


def merge_kernel(chips, hosts, recv_ref, mine_ref, place_ref, *refs):
    came, (out_ref, sum_ref) = refs[: chips - 1], refs[chips - 1 :]
    rows = mine_ref.shape[0]
    total = mine_ref[...]
    for k, ref in enumerate(came):
        total = total + ref[:rows, :].astype(F32)
        out_ref[k * rows : (k + 1) * rows, :] = ref[rows:, :]
    total = total + returned(place_ref, recv_ref, hosts, chips)
    sum_ref[...] = total
    low = len(came) * rows
    halo = received(recv_ref, hosts, chips, 1 - lax.axis_index("core"))
    high = low + halo.shape[0]
    out_ref[low:high, :] = halo
    out_ref[high:, :] = total.astype(BF16)


def returned(place_ref, recv_ref, hosts, chips):
    return dot(place_ref[...], received(recv_ref, hosts, chips, lax.axis_index("core")))


def joint(pairs):
    left = jnp.concatenate([a for a, _ in pairs], 1)
    return dot(left, jnp.concatenate([b for _, b in pairs], 0))


def square_of(adj_ref, x, side, rows):
    return adj_ref[pl.ds(pl.multiple_of((x * CORES + side) * rows, rows), rows), :]


def own_chip(adj_refs, blocks):
    chip, core = lax.axis_index("chip"), lax.axis_index("core")
    rows = blocks[0].shape[0]
    parts = [
        joint([(square_of(ref, chip, s, rows), b) for s, b in zip((core, 1 - core), blocks)])
        for ref in adj_refs
    ]
    return jnp.concatenate(parts, 0)


def early_one_kernel(
    chips, adj_ref, lent_ref, value_ref, self_ref, bias_ref, up_ref, weight_ref, neigh_ref, sent_ref,
    agg_ref, direct_ref, grad_ref, col_ref, far_ref, far_t,
):
    value = value_ref[...]
    rows = value.shape[0]
    low = adj_ref.shape[0]
    there = lent_ref[low + rows :, :]
    sent = dot(there, neigh_ref[...]).astype(BF16)
    agg_ref[...] = own_chip((adj_ref, lent_ref), (sent_ref[...], sent))
    both = jnp.concatenate([value, there], 0)
    direct_ref[...] = dot(both, self_ref[...]) + bias_ref[...].reshape(1, -1)
    both = jnp.concatenate([up_ref[...], lent_ref[low : low + rows, :]], 0)
    grad_ref[...] = dot_nt(both, weight_ref[...])
    far = col_ref.shape[0] // chips - rows
    column(chips, far, rows, lax.axis_index("core"), lent_ref, far_t, col_ref)
    far_columns(chips, far_t, far_ref)


def mid_kernel(
    chips, adj_ref, lent_ref, far_ref, far_two_ref, agg_ref, part_ref, sum_ref, neigh_ref, here_ref, *refs
):
    came, (agg_out, grad_ref) = refs[:-2], refs[-2:]
    rows = sum_ref.shape[0]
    halo = here_ref[(chips - 1) * rows : here_ref.shape[0] - rows, :]
    for i, (ref, columns) in enumerate(((adj_ref, far_ref), (lent_ref, far_two_ref))):
        pairs = other_chips(chips, ref, came) + [(columns[:, : halo.shape[0]], halo)]
        part = slice(i * rows, (i + 1) * rows)
        agg_out[part, :] = agg_ref[part, :] + joint(pairs)
    grad_ref[:rows, :] = part_ref[:rows, :] + precise_nt(sum_ref[...], neigh_ref[...])
    grad_ref[rows:, :] = part_ref[rows:, :]


def other_chips(chips, adj_ref, came):
    chip, core = lax.axis_index("chip"), lax.axis_index("core")
    pairs = []
    for k, block in enumerate(came):
        rows = block.shape[0] // 2
        x = lax.rem(chip - k - 1 + chips, chips)
        pairs.append((square_of(adj_ref, x, core, rows), block[rows:, :]))
    return pairs


def column_product(chips, hosts, adj_ref, far_ref, value_ref, came, recv_ref):
    rows = value_ref.shape[0]
    chip, core = lax.axis_index("chip"), lax.axis_index("core")
    halo = received(recv_ref, hosts, chips, 1 - core)
    pairs = [(square_of(adj_ref, chip, core, rows), value_ref[...])]
    pairs += other_chips(chips, adj_ref, came) + [(far_ref[:, : halo.shape[0]], halo)]
    return joint(pairs)


def there_kernel(chips, hosts, lent_ref, far_ref, value_ref, recv_ref, *refs):
    came, out_ref = refs[:-1], refs[-1]
    out_ref[...] = column_product(
        chips, hosts, lent_ref, far_ref, value_ref, came, recv_ref
    ).astype(BF16)


def here_kernel(
    chips, hosts, adj_ref, far_ref, sent_ref, recv_ref, value_ref, self_ref, bias_ref, up_ref,
    weight_ref, neigh_ref, mine_ref, place_ref, *refs
):
    came, (out_ref, grad_ref) = refs[:-2], refs[-2:]
    rows = mine_ref.shape[0]
    total = mine_ref[...] + returned(place_ref, recv_ref, hosts, chips)
    for block in came:
        total = total + block[:rows, :].astype(F32)
    grad = dot_nt(total.astype(BF16), neigh_ref[...])
    grad_ref[...] = grad + dot_nt(up_ref[...], weight_ref[...])
    out = column_product(chips, hosts, adj_ref, far_ref, sent_ref, came, recv_ref)
    out_ref[...] = out + dot(value_ref[...], self_ref[...]) + bias_ref[...].reshape(1, -1)


def add_rest(chips, rows, adj_ref, far_ref, agg, shared_ref):
    chip, core = lax.axis_index("chip"), lax.axis_index("core")
    pairs = []
    for k in range(chips - 1):
        x = lax.rem(chip - k - 1 + chips, chips)
        block = shared_ref[k * rows : (k + 1) * rows, :]
        pairs.append((square_of(adj_ref, x, 1 - core, rows), block))
    half = far_ref.shape[1] // 2
    low = (chips - 1) * rows
    pairs.append((far_ref[:, half:], shared_ref[low : low + half, :]))
    return agg + joint(pairs)


def middle_kernel(
    chips,
    hosts,
    adj_ref,
    lent_ref,
    far_ref,
    far_two_ref,
    col_ref,
    col_two_ref,
    agg_ref,
    direct_ref,
    grad_ref,
    pick_ref,
    shared_ref,
    neigh_two_ref,
    hidden_ref,
    sent_ref,
    grad_pre_ref,
    mine_ref,
    msg_ref,
    *rest,
):
    to_refs = rest
    far, rows = pick_ref.shape
    parts = [
        add_rest(chips, rows, ref, columns, agg_ref[i * rows : (i + 1) * rows, :], shared_ref)
        for i, (ref, columns) in enumerate(((adj_ref, far_ref), (lent_ref, far_two_ref)))
    ]
    pre = direct_ref[...] + jnp.concatenate(parts, 0)
    sigmoid = jax.nn.sigmoid(pre)
    hidden = (pre[:rows] * sigmoid[:rows]).astype(BF16)
    hidden_ref[...] = hidden
    sent = dot(hidden, neigh_two_ref[...]).astype(BF16)
    sent_ref[...] = sent
    low = (chips - 1) * rows + chips * far
    add = dot_nt(shared_ref[low:, :], neigh_two_ref[...])
    grad = jnp.concatenate([grad_ref[:rows, :], grad_ref[rows:, :] + add], 0)
    grad_pre = (grad * sigmoid * (1.0 + pre * (1.0 - sigmoid))).astype(BF16)
    grad_pre_ref[...] = grad_pre[:rows]
    total = joint([(col_ref[...], grad_pre[:rows]), (col_two_ref[...], grad_pre[rows:])])
    picked = dot(pick_ref[...], sent)
    deal(chips, hosts, total, picked, sent, mine_ref, msg_ref, to_refs)


def last_kernel(here_ref, there_ref, output_ref):
    output_ref[...] = (here_ref[...] + there_ref[...].astype(F32)).astype(BF16)


def call(kernel, name, out_shape, in_specs, args, scratch=(), limit=32, flops=0):
    return pl.pallas_call(
        kernel,
        out_shape=out_shape,
        in_specs=in_specs,
        out_specs=jax.tree.map(lambda _: VMEM, out_shape),
        scratch_shapes=scratch,
        compiler_params=pltpu.CompilerParams(vmem_limit_bytes=limit * MIB),
        cost_estimate=pl.CostEstimate(
            flops=flops, bytes_accessed=flops // 1024, transcendentals=0
        ),
        name=name,
    )(*args)


def shift(value, axis, k):
    size = lax.axis_size(axis)
    return lax.ppermute(value, axis, [(i, (i + k) % size) for i in range(size)])


def shape(rows, width, kind=BF16):
    return jax.ShapeDtypeStruct((rows, width), kind)


def body(
    features,
    send_list,
    tile_dst,
    tile_src,
    tile_rows,
    tile_val,
    self_one,
    neigh_one,
    bias_one,
    self_two,
    neigh_two,
    bias_two,
    cotangent,
):
    chips = lax.axis_size("chip")
    hosts = lax.axis_size("hst")
    rows, width = features.shape
    tiles, blk = tile_val.shape[:2]
    send = send_list.shape[3]
    far = hosts * send
    all_rows = chips * CORES * (rows + far)
    count = chips * (rows + far)
    rows_shape = shape(rows, width)
    sum_shape = shape(rows, width, F32)
    both_shape = shape(CORES * rows, width, F32)
    square = 2 * rows * width * width
    far_shape = shape(rows, chips * CORES * far)
    halo_rows = (chips - 1) * rows + chips * far
    dealt = (
        sum_shape,
        jax.ShapeDtypeStruct((chips * hosts * CORES, send, width), BF16),
    ) + (shape(2 * rows, width),) * (chips - 1)

    def across(msg, to):
        terms = [shift(block, "chip", k + 1) for k, block in enumerate(to)]
        recv = lax.all_to_all(msg, ("hst", "chip", "core"), split_axis=0, concat_axis=0, tiled=True)
        return terms, recv

    far_t = pltpu.VMEM((chips * CORES * far, rows), BF16)
    sums = jax.ShapeDtypeStruct(((rows // blk) * (all_rows // blk), blk // PARTS, blk), F32)
    give, pick, cot, *sums = call(
        functools.partial(prep_kernel, chips),
        "prep",
        (shape(count, width), shape(far, rows), rows_shape) + (sums,) * PARTS,
        [HBM] * 6,
        [
            pltpu.with_memory_space_constraint(value, pltpu.HBM)
            for value in (
                tile_dst,
                tile_src,
                tile_rows,
                send_list,
                tile_val,
                cotangent,
            )
        ],
        [
            pltpu.SMEM(tile_dst.shape, jnp.int32),
            pltpu.SMEM(tile_src.shape, jnp.int32),
            pltpu.SMEM(tile_rows.shape, jnp.int32),
            pltpu.SMEM(send_list.shape, jnp.int32),
            pltpu.VMEM(tile_val.shape, BF16),
            pltpu.VMEM((rows, rows), BF16),
            far_t,
            pltpu.VMEM((count, rows), BF16),
            pltpu.SemaphoreType.DMA((6 + CHUNKS,)),
        ],
    )
    came = shift(give, "core", 1)
    sent, picked, adj, col, keep, lend, place, columns = call(
        functools.partial(rest_kernel, chips),
        "rest",
        (
            rows_shape,
            shape(far, width),
            shape(all_rows, rows),
            shape(count, rows),
            shape(count, width),
            shape(all_rows + 2 * rows, width),
            shape(rows, chips * far),
            far_shape,
        ),
        [VMEM] * (4 + PARTS),
        (cot, features, pick, neigh_one, *sums),
        [far_t],
        flops=3 * square,
    )
    lent = shift(lend, "core", 1)
    mine, msg, *to = call(
        functools.partial(core_sum_kernel, chips, hosts),
        "core_sum",
        dealt,
        [VMEM] * 4,
        (keep, came, sent, picked),
        flops=60 * square,
    )
    terms, recv = across(msg, to)
    here, summed = call(
        functools.partial(merge_kernel, chips, hosts),
        "merge",
        (shape(halo_rows + rows, width), sum_shape),
        [VMEM] * (2 + chips),
        (recv, mine, place, *terms),
    )
    shared = shift(here, "core", 1)
    agg, direct, grad, col_two, columns_two = call(
        functools.partial(early_one_kernel, chips),
        "early_one",
        (both_shape,) * 3 + (shape(count, rows), far_shape),
        [VMEM] * 9,
        (
            adj,
            lent,
            features,
            self_one,
            bias_one,
            cot,
            self_two,
            neigh_one,
            sent,
        ),
        [far_t],
        flops=8 * square,
    )
    agg, grad = call(
        functools.partial(mid_kernel, chips),
        "mid",
        (both_shape,) * 2,
        [VMEM] * (8 + chips),
        (adj, lent, columns, columns_two, agg, grad, summed, neigh_two, here, *terms),
        flops=3 * square,
    )
    hidden, sent, grad_pre, mine, msg, *to = call(
        functools.partial(middle_kernel, chips, hosts),
        "middle",
        (rows_shape,) * 3 + dealt,
        [VMEM] * 12,
        (
            adj,
            lent,
            columns,
            columns_two,
            col,
            col_two,
            agg,
            direct,
            grad,
            pick,
            shared,
            neigh_two,
        ),
        flops=12 * square,
    )
    terms, recv = across(msg, to)
    there = call(
        functools.partial(there_kernel, chips, hosts),
        "there",
        rows_shape,
        [VMEM] * (3 + chips),
        (lent, columns_two, sent, recv, *terms),
    )
    shared = shift(there, "core", 1)
    here, grad = call(
        functools.partial(here_kernel, chips, hosts),
        "here",
        (sum_shape,) * 2,
        [VMEM] * (11 + chips),
        (
            adj,
            columns,
            sent,
            recv,
            hidden,
            self_two,
            bias_two,
            grad_pre,
            self_one,
            neigh_one,
            mine,
            place,
            *terms,
        ),
        flops=7 * square,
    )
    output = call(last_kernel, "last", rows_shape, [VMEM] * 2, (here, shared))
    return output, grad


def solution(mesh):
    hosts, devs = mesh.devices.shape
    mesh = Mesh(mesh.devices.reshape(hosts, devs // CORES, CORES), ("hst", "chip", "core"))
    dev = ("chip", "core")
    every = ("hst", "chip", "core")
    return jax.shard_map(
        body,
        mesh=mesh,
        in_specs=(
            P(every, None),
            P("hst", dev, None, None),
            P(every),
            P(every),
            P(every),
            P(every, None, None),
            P(),
            P(),
            P(),
            P(),
            P(),
            P(),
            P(every, None),
        ),
        out_specs=(P(every, None), P(every, None)),
        check_vma=False,
    )
```

```python
import functools

import jax
import jax.numpy as jnp
from jax import lax
from jax.experimental import pallas as pl
from jax.experimental.pallas import tpu as pltpu
from jax.sharding import Mesh, PartitionSpec as P

F32 = jnp.float32
BF16 = jnp.bfloat16
MIB = 1024 * 1024
CHUNKS = 8
PARTS = 4
CORES = 2

VMEM = pl.BlockSpec(memory_space=pltpu.VMEM)
HBM = pl.BlockSpec(memory_space=pltpu.HBM)


def dot(a, b):
    return jnp.dot(a, b, preferred_element_type=F32)


def dot_nt(a, b):
    return lax.dot_general(a, b, (((1,), (1,)), ((), ())), preferred_element_type=F32)


def precise_nt(a, b):
    high = a.astype(BF16)
    low = (a - high.astype(F32)).astype(BF16)
    return dot_nt(high, b) + dot_nt(low, b)


def pick_matrix(send_ref, rows):
    hosts, send = send_ref.shape[2], send_ref.shape[3]
    place = lax.broadcasted_iota(jnp.int32, (send, rows), 0)
    column = lax.broadcasted_iota(jnp.int32, (send, rows), 1)
    parts = []
    for g in range(hosts):
        index = jnp.zeros((send, rows), jnp.int32)
        for s in range(send):
            index = jnp.where(place == s, send_ref[0, 0, g, s], index)
        parts.append(jnp.where(index == column, 1.0, 0.0).astype(F32))
    return jnp.concatenate(parts, 0).astype(BF16)


def column(chips, far, rows, side, adj_ref, far_t, out_ref):
    chip = lax.axis_index("chip")
    each = rows + far
    own_rows = chips * CORES * rows
    for j in range(far_t.shape[0] // rows):
        low = own_rows + j * rows
        far_t[j * rows : (j + 1) * rows, :] = adj_ref[low : low + rows, :].T
    for k in range(chips):
        d = lax.rem(chip + k, chips) * CORES + side
        at = k * each
        out_ref[at : at + rows, :] = adj_ref[pl.ds(pl.multiple_of(d * rows, rows), rows), :].T
        out_ref[at + rows : at + each, :] = far_t[pl.ds(pl.multiple_of(d * far, far), far), :]


def far_columns(chips, far_t, out_ref):
    far = far_t.shape[0] // (chips * CORES)
    core = lax.axis_index("core")
    parts = [
        far_t[pl.ds(pl.multiple_of((x * CORES + side) * far, far), far), :]
        for side in (1 - core, core)
        for x in range(chips)
    ]
    out_ref[...] = jnp.concatenate(parts, 0).T


def prep_kernel(
    chips,
    dst_hbm,
    src_hbm,
    rows_hbm,
    send_hbm,
    tile_hbm,
    cot_hbm,
    give_ref,
    pick_ref,
    cot_ref,
    *rest,
):
    accs, rest = rest[:PARTS], rest[PARTS:]
    (
        dst_ref,
        src_ref,
        rows_ref,
        send_ref,
        tile_buf,
        square,
        far_t,
        col,
        sems,
    ) = rest
    tiles, blk = tile_buf.shape[0], tile_buf.shape[1]
    each = tiles // CHUNKS
    cuts = [c * each for c in range(CHUNKS)] + [tiles]
    chunks = [
        (tile_hbm.at[pl.ds(low, high - low)], tile_buf.at[pl.ds(low, high - low)])
        for low, high in zip(cuts, cuts[1:])
    ]
    pairs = [(send_hbm, send_ref), (dst_hbm, dst_ref), (src_hbm, src_ref), (rows_hbm, rows_ref)]
    pairs += chunks + [(cot_hbm, cot_ref)]
    copies = [pltpu.make_async_copy(a, b, sems.at[i]) for i, (a, b) in enumerate(pairs)]
    for copy in copies:
        copy.start()
    rows = cot_ref.shape[0]
    bpd = rows // blk
    sources = accs[0].shape[0] // bpd
    part = accs[0].shape[1]
    far = send_ref.shape[2] * send_ref.shape[3]
    for acc in accs:
        acc[...] = jnp.zeros_like(acc)
    place = lax.broadcasted_iota(jnp.int32, (part, blk), 0)

    def add(t, carry):
        slot = dst_ref[t] * sources + src_ref[t]
        for i, acc in enumerate(accs):
            value = tile_buf[t, i * part : (i + 1) * part, :].astype(F32)
            acc[slot] += jnp.where(place < rows_ref[t] - i * part, value, 0.0)
        return carry

    copies[0].wait()
    pick_ref[...] = pick_matrix(send_ref, rows)
    for copy in copies[1:4]:
        copy.wait()
    for copy, low, high in zip(copies[4:], cuts, cuts[1:]):
        copy.wait()
        lax.fori_loop(low, high, add, 0, unroll=True)
    copies[-1].wait()
    chip, side = lax.axis_index("chip"), 1 - lax.axis_index("core")
    base = chips * CORES
    for j in range(far_t.shape[0] // rows):
        put_square(accs, bpd, base + j, square, 0)
        far_t[j * rows : (j + 1) * rows, :] = square[...].T
    for k in range(chips):
        d = lax.rem(chip + k, chips) * CORES + side
        at = k * (rows + far)
        put_square(accs, bpd, d, square, 0)
        col[at : at + rows, :] = square[...].T
        low = pl.multiple_of(d * far, far)
        col[at + rows : at + rows + far, :] = far_t[pl.ds(low, far), :]
    give_ref[...] = dot(col[...], cot_ref[...]).astype(BF16)


def put_square(accs, bpd, d, out_ref, base):
    sources = accs[0].shape[0] // bpd
    part, blk = accs[0].shape[1:]
    for b in range(bpd):
        for j in range(bpd):
            for i, acc in enumerate(accs):
                low = base + b * blk + i * part
                value = acc[b * sources + d * bpd + j].astype(BF16)
                out_ref[low : low + part, j * blk : (j + 1) * blk] = value


def rest_kernel(chips, cot_ref, value_ref, pick_ref, neigh_ref, *refs):
    accs = refs[:PARTS]
    sent_ref, picked_ref, adj_ref, col_ref, keep_ref, lend_ref, place_ref, far_ref, far_t = refs[PARTS:]
    sent = dot(value_ref[...], neigh_ref[...]).astype(BF16)
    sent_ref[...] = sent
    picked_ref[...] = dot(pick_ref[...], sent).astype(BF16)
    rows = cot_ref.shape[0]
    bpd = rows // accs[0].shape[2]
    for d in range(adj_ref.shape[0] // rows):
        put_square(accs, bpd, d, adj_ref, d * rows)
    far = col_ref.shape[0] // chips - rows
    column(chips, far, rows, lax.axis_index("core"), adj_ref, far_t, col_ref)
    far_columns(chips, far_t, far_ref)
    keep_ref[...] = dot(col_ref[...], cot_ref[...]).astype(BF16)
    low = adj_ref.shape[0]
    lend_ref[:low, :] = adj_ref[...]
    lend_ref[low : low + rows, :] = cot_ref[...]
    lend_ref[low + rows :, :] = value_ref[...]
    place_ref[...] = jnp.concatenate([pick_ref[...]] * chips, 0).T


def deal(chips, hosts, total, picked, value, mine_ref, msg_ref, to_refs):
    rows = value.shape[0]
    far = picked.shape[0]
    send = far // hosts
    each = rows + far
    chip, core = lax.axis_index("chip"), lax.axis_index("core")
    mine_ref[...] = total[:rows]
    for k in range(chips):
        low = k * each + rows
        if k > 0:
            to_refs[k - 1][:rows, :] = total[k * each : low].astype(BF16)
            to_refs[k - 1][rows:, :] = value
        x = lax.rem(chip + k, chips)
        for g in range(hosts):
            at = low + g * send
            to = (g * chips + x) * CORES
            msg_ref[to + core] = total[at : at + send].astype(BF16)
            msg_ref[to + 1 - core] = picked[g * send : (g + 1) * send].astype(BF16)


def core_sum_kernel(
    chips, hosts, keep_ref, came_ref, value_ref, picked_ref, mine_ref, msg_ref, *rest
):
    total = keep_ref[...].astype(F32) + came_ref[...].astype(F32)
    picked = picked_ref[...].astype(F32)
    deal(chips, hosts, total, picked, value_ref[...], mine_ref, msg_ref, rest)


def received(recv_ref, hosts, chips, side):
    blocks = [
        recv_ref[(g * chips + x) * CORES + side].astype(F32)
        for x in range(chips)
        for g in range(hosts)
    ]
    return jnp.concatenate(blocks, 0).astype(BF16)


def merge_kernel(chips, hosts, recv_ref, mine_ref, place_ref, *refs):
    came, (out_ref, sum_ref) = refs[: chips - 1], refs[chips - 1 :]
    rows = mine_ref.shape[0]
    total = mine_ref[...]
    for k, ref in enumerate(came):
        total = total + ref[:rows, :].astype(F32)
        out_ref[k * rows : (k + 1) * rows, :] = ref[rows:, :]
    total = total + returned(place_ref, recv_ref, hosts, chips)
    sum_ref[...] = total
    low = len(came) * rows
    halo = received(recv_ref, hosts, chips, 1 - lax.axis_index("core"))
    high = low + halo.shape[0]
    out_ref[low:high, :] = halo
    out_ref[high:, :] = total.astype(BF16)


def returned(place_ref, recv_ref, hosts, chips):
    return dot(place_ref[...], received(recv_ref, hosts, chips, lax.axis_index("core")))


def joint(pairs):
    left = jnp.concatenate([a for a, _ in pairs], 1)
    return dot(left, jnp.concatenate([b for _, b in pairs], 0))


def square_of(adj_ref, x, side, rows):
    return adj_ref[pl.ds(pl.multiple_of((x * CORES + side) * rows, rows), rows), :]


def own_chip(adj_refs, blocks):
    chip, core = lax.axis_index("chip"), lax.axis_index("core")
    rows = blocks[0].shape[0]
    parts = [
        joint([(square_of(ref, chip, s, rows), b) for s, b in zip((core, 1 - core), blocks)])
        for ref in adj_refs
    ]
    return jnp.concatenate(parts, 0)


def early_one_kernel(
    chips, adj_ref, lent_ref, value_ref, self_ref, bias_ref, up_ref, weight_ref, neigh_ref, sent_ref,
    agg_ref, direct_ref, grad_ref, col_ref, far_ref, far_t,
):
    value = value_ref[...]
    rows = value.shape[0]
    low = adj_ref.shape[0]
    there = lent_ref[low + rows :, :]
    sent = dot(there, neigh_ref[...]).astype(BF16)
    agg_ref[...] = own_chip((adj_ref, lent_ref), (sent_ref[...], sent))
    both = jnp.concatenate([value, there], 0)
    direct_ref[...] = dot(both, self_ref[...]) + bias_ref[...].reshape(1, -1)
    both = jnp.concatenate([up_ref[...], lent_ref[low : low + rows, :]], 0)
    grad_ref[...] = dot_nt(both, weight_ref[...])
    far = col_ref.shape[0] // chips - rows
    column(chips, far, rows, lax.axis_index("core"), lent_ref, far_t, col_ref)
    far_columns(chips, far_t, far_ref)


def mid_kernel(
    chips, adj_ref, lent_ref, far_ref, far_two_ref, agg_ref, part_ref, sum_ref, neigh_ref, here_ref, *refs
):
    came, (agg_out, grad_ref) = refs[:-2], refs[-2:]
    rows = sum_ref.shape[0]
    halo = here_ref[(chips - 1) * rows : here_ref.shape[0] - rows, :]
    for i, (ref, columns) in enumerate(((adj_ref, far_ref), (lent_ref, far_two_ref))):
        pairs = other_chips(chips, ref, came) + [(columns[:, : halo.shape[0]], halo)]
        part = slice(i * rows, (i + 1) * rows)
        agg_out[part, :] = agg_ref[part, :] + joint(pairs)
    grad_ref[:rows, :] = part_ref[:rows, :] + precise_nt(sum_ref[...], neigh_ref[...])
    grad_ref[rows:, :] = part_ref[rows:, :]


def other_chips(chips, adj_ref, came):
    chip, core = lax.axis_index("chip"), lax.axis_index("core")
    pairs = []
    for k, block in enumerate(came):
        rows = block.shape[0] // 2
        x = lax.rem(chip - k - 1 + chips, chips)
        pairs.append((square_of(adj_ref, x, core, rows), block[rows:, :]))
    return pairs


def column_product(chips, hosts, adj_ref, far_ref, value_ref, came, recv_ref):
    rows = value_ref.shape[0]
    chip, core = lax.axis_index("chip"), lax.axis_index("core")
    halo = received(recv_ref, hosts, chips, 1 - core)
    pairs = [(square_of(adj_ref, chip, core, rows), value_ref[...])]
    pairs += other_chips(chips, adj_ref, came) + [(far_ref[:, : halo.shape[0]], halo)]
    return joint(pairs)


def there_kernel(chips, hosts, lent_ref, far_ref, value_ref, recv_ref, *refs):
    came, out_ref = refs[:-1], refs[-1]
    out_ref[...] = column_product(
        chips, hosts, lent_ref, far_ref, value_ref, came, recv_ref
    ).astype(BF16)


def here_kernel(
    chips, hosts, adj_ref, far_ref, sent_ref, recv_ref, value_ref, self_ref, bias_ref, up_ref,
    weight_ref, neigh_ref, mine_ref, place_ref, *refs
):
    came, (out_ref, grad_ref) = refs[:-2], refs[-2:]
    rows = mine_ref.shape[0]
    total = mine_ref[...] + returned(place_ref, recv_ref, hosts, chips)
    for block in came:
        total = total + block[:rows, :].astype(F32)
    grad = dot_nt(total.astype(BF16), neigh_ref[...])
    grad_ref[...] = grad + dot_nt(up_ref[...], weight_ref[...])
    out = column_product(chips, hosts, adj_ref, far_ref, sent_ref, came, recv_ref)
    out_ref[...] = out + dot(value_ref[...], self_ref[...]) + bias_ref[...].reshape(1, -1)


def add_rest(chips, rows, adj_ref, far_ref, agg, shared_ref):
    chip, core = lax.axis_index("chip"), lax.axis_index("core")
    pairs = []
    for k in range(chips - 1):
        x = lax.rem(chip - k - 1 + chips, chips)
        block = shared_ref[k * rows : (k + 1) * rows, :]
        pairs.append((square_of(adj_ref, x, 1 - core, rows), block))
    half = far_ref.shape[1] // 2
    low = (chips - 1) * rows
    pairs.append((far_ref[:, half:], shared_ref[low : low + half, :]))
    return agg + joint(pairs)


def middle_kernel(
    chips,
    hosts,
    adj_ref,
    lent_ref,
    far_ref,
    far_two_ref,
    col_ref,
    col_two_ref,
    agg_ref,
    direct_ref,
    grad_ref,
    pick_ref,
    shared_ref,
    neigh_two_ref,
    hidden_ref,
    sent_ref,
    grad_pre_ref,
    mine_ref,
    msg_ref,
    *rest,
):
    to_refs = rest
    far, rows = pick_ref.shape
    parts = [
        add_rest(chips, rows, ref, columns, agg_ref[i * rows : (i + 1) * rows, :], shared_ref)
        for i, (ref, columns) in enumerate(((adj_ref, far_ref), (lent_ref, far_two_ref)))
    ]
    pre = direct_ref[...] + jnp.concatenate(parts, 0)
    sigmoid = jax.nn.sigmoid(pre)
    hidden = (pre[:rows] * sigmoid[:rows]).astype(BF16)
    hidden_ref[...] = hidden
    sent = dot(hidden, neigh_two_ref[...]).astype(BF16)
    sent_ref[...] = sent
    low = (chips - 1) * rows + chips * far
    add = dot_nt(shared_ref[low:, :], neigh_two_ref[...])
    grad = jnp.concatenate([grad_ref[:rows, :], grad_ref[rows:, :] + add], 0)
    grad_pre = (grad * sigmoid * (1.0 + pre * (1.0 - sigmoid))).astype(BF16)
    grad_pre_ref[...] = grad_pre[:rows]
    total = joint([(col_ref[...], grad_pre[:rows]), (col_two_ref[...], grad_pre[rows:])])
    picked = dot(pick_ref[...], sent)
    deal(chips, hosts, total, picked, sent, mine_ref, msg_ref, to_refs)


def last_kernel(here_ref, there_ref, output_ref):
    output_ref[...] = (here_ref[...] + there_ref[...].astype(F32)).astype(BF16)


def call(kernel, name, out_shape, in_specs, args, scratch=(), limit=32, flops=0):
    return pl.pallas_call(
        kernel,
        out_shape=out_shape,
        in_specs=in_specs,
        out_specs=jax.tree.map(lambda _: VMEM, out_shape),
        scratch_shapes=scratch,
        compiler_params=pltpu.CompilerParams(vmem_limit_bytes=limit * MIB),
        cost_estimate=pl.CostEstimate(
            flops=flops, bytes_accessed=flops // 1024, transcendentals=0
        ),
        name=name,
    )(*args)


def shift(value, axis, k):
    size = lax.axis_size(axis)
    return lax.ppermute(value, axis, [(i, (i + k) % size) for i in range(size)])


def shape(rows, width, kind=BF16):
    return jax.ShapeDtypeStruct((rows, width), kind)


def body(
    features,
    send_list,
    tile_dst,
    tile_src,
    tile_rows,
    tile_val,
    self_one,
    neigh_one,
    bias_one,
    self_two,
    neigh_two,
    bias_two,
    cotangent,
):
    chips = lax.axis_size("chip")
    hosts = lax.axis_size("hst")
    rows, width = features.shape
    tiles, blk = tile_val.shape[:2]
    send = send_list.shape[3]
    far = hosts * send
    all_rows = chips * CORES * (rows + far)
    count = chips * (rows + far)
    rows_shape = shape(rows, width)
    sum_shape = shape(rows, width, F32)
    both_shape = shape(CORES * rows, width, F32)
    square = 2 * rows * width * width
    far_shape = shape(rows, chips * CORES * far)
    halo_rows = (chips - 1) * rows + chips * far
    dealt = (
        sum_shape,
        jax.ShapeDtypeStruct((chips * hosts * CORES, send, width), BF16),
    ) + (shape(2 * rows, width),) * (chips - 1)

    def across(msg, to):
        terms = [shift(block, "chip", k + 1) for k, block in enumerate(to)]
        recv = lax.all_to_all(msg, ("hst", "chip", "core"), split_axis=0, concat_axis=0, tiled=True)
        return terms, recv

    far_t = pltpu.VMEM((chips * CORES * far, rows), BF16)
    sums = jax.ShapeDtypeStruct(((rows // blk) * (all_rows // blk), blk // PARTS, blk), F32)
    give, pick, cot, *sums = call(
        functools.partial(prep_kernel, chips),
        "prep",
        (shape(count, width), shape(far, rows), rows_shape) + (sums,) * PARTS,
        [HBM] * 6,
        [
            pltpu.with_memory_space_constraint(value, pltpu.HBM)
            for value in (
                tile_dst,
                tile_src,
                tile_rows,
                send_list,
                tile_val,
                cotangent,
            )
        ],
        [
            pltpu.SMEM(tile_dst.shape, jnp.int32),
            pltpu.SMEM(tile_src.shape, jnp.int32),
            pltpu.SMEM(tile_rows.shape, jnp.int32),
            pltpu.SMEM(send_list.shape, jnp.int32),
            pltpu.VMEM(tile_val.shape, BF16),
            pltpu.VMEM((rows, rows), BF16),
            far_t,
            pltpu.VMEM((count, rows), BF16),
            pltpu.SemaphoreType.DMA((5 + CHUNKS,)),
        ],
    )
    came = shift(give, "core", 1)
    sent, picked, adj, col, keep, lend, place, columns = call(
        functools.partial(rest_kernel, chips),
        "rest",
        (
            rows_shape,
            shape(far, width),
            shape(all_rows, rows),
            shape(count, rows),
            shape(count, width),
            shape(all_rows + 2 * rows, width),
            shape(rows, chips * far),
            far_shape,
        ),
        [VMEM] * (4 + PARTS),
        (cot, features, pick, neigh_one, *sums),
        [far_t],
        flops=3 * square,
    )
    lent = shift(lend, "core", 1)
    mine, msg, *to = call(
        functools.partial(core_sum_kernel, chips, hosts),
        "core_sum",
        dealt,
        [VMEM] * 4,
        (keep, came, sent, picked),
        flops=60 * square,
    )
    terms, recv = across(msg, to)
    here, summed = call(
        functools.partial(merge_kernel, chips, hosts),
        "merge",
        (shape(halo_rows + rows, width), sum_shape),
        [VMEM] * (2 + chips),
        (recv, mine, place, *terms),
    )
    shared = shift(here, "core", 1)
    agg, direct, grad, col_two, columns_two = call(
        functools.partial(early_one_kernel, chips),
        "early_one",
        (both_shape,) * 3 + (shape(count, rows), far_shape),
        [VMEM] * 9,
        (
            adj,
            lent,
            features,
            self_one,
            bias_one,
            cot,
            self_two,
            neigh_one,
            sent,
        ),
        [far_t],
        flops=8 * square,
    )
    agg, grad = call(
        functools.partial(mid_kernel, chips),
        "mid",
        (both_shape,) * 2,
        [VMEM] * (8 + chips),
        (adj, lent, columns, columns_two, agg, grad, summed, neigh_two, here, *terms),
        flops=3 * square,
    )
    hidden, sent, grad_pre, mine, msg, *to = call(
        functools.partial(middle_kernel, chips, hosts),
        "middle",
        (rows_shape,) * 3 + dealt,
        [VMEM] * 12,
        (
            adj,
            lent,
            columns,
            columns_two,
            col,
            col_two,
            agg,
            direct,
            grad,
            pick,
            shared,
            neigh_two,
        ),
        flops=12 * square,
    )
    terms, recv = across(msg, to)
    there = call(
        functools.partial(there_kernel, chips, hosts),
        "there",
        rows_shape,
        [VMEM] * (3 + chips),
        (lent, columns_two, sent, recv, *terms),
    )
    shared = shift(there, "core", 1)
    here, grad = call(
        functools.partial(here_kernel, chips, hosts),
        "here",
        (sum_shape,) * 2,
        [VMEM] * (11 + chips),
        (
            adj,
            columns,
            sent,
            recv,
            hidden,
            self_two,
            bias_two,
            grad_pre,
            self_one,
            neigh_one,
            mine,
            place,
            *terms,
        ),
        flops=7 * square,
    )
    output = call(last_kernel, "last", rows_shape, [VMEM] * 2, (here, shared))
    return output, grad


def solution(mesh):
    hosts, devs = mesh.devices.shape
    mesh = Mesh(mesh.devices.reshape(hosts, devs // CORES, CORES), ("hst", "chip", "core"))
    dev = ("chip", "core")
    every = ("hst", "chip", "core")
    return jax.shard_map(
        body,
        mesh=mesh,
        in_specs=(
            P(every, None),
            P("hst", dev, None, None),
            P(every),
            P(every),
            P(every),
            P(every, None, None),
            P(),
            P(),
            P(),
            P(),
            P(),
            P(),
            P(every, None),
        ),
        out_specs=(P(every, None), P(every, None)),
        check_vma=False,
    )
```
